32 devices in a mesh: east: 16 (over z, y, core), north: 2 (over x).
Axes of the slice: x: 2, y: 2, z: 4, core: 2. Of those that a mesh axis runs over, the one named last changes fastest.
Arguments:
- features: bfloat16 [96, 128, 32, 8], P(None, 'east', 'north'), may hold values from -6 to 6
- brick_active: int32 [16, 4, 1], P('east', 'north'), may hold values 0 or 1
- voxel_occupancy: int32 [128, 32, 8], P('east', 'north'), may hold values 0 or 1
- first_weights: bfloat16 [27, 96, 96], replicated, may hold values from -0.125 to 0.125
- second_weights: bfloat16 [27, 96, 96], replicated, may hold values from -0.125 to 0.125
- head: bfloat16 [13, 96], replicated, may hold values from -0.625 to 0.625
- teacher: bfloat16 [13, 128, 32, 8], P(None, 'east', 'north'), may hold values from -6 to 6
Outputs:
- grad_features: bfloat16 [96, 128, 32, 8], P(None, 'east', 'north')
- grad_first: float32 [27, 96, 96], replicated
- grad_second: float32 [27, 96, 96], replicated
The draws below stay inside these ranges and needn't reach their ends.
All inputs are finite; a program needn't handle non-finite values. No bound on the sum of `brick_active` or of `voxel_occupancy` on one device may be relied on, other than what follows from the above.
Results may differ from the reference program's by a relative error of at most 0.0058.
Values may be sent and summed in bfloat16 or wider, within the bound.
No kernel may reach another device: no remote copies, remote signals or barrier semaphores. Data moves between devices by JAX's collectives and lax.ppermute only.
A program may use at most 128 MiB of HBM per device.

```python
import jax
import jax.numpy as jnp
from jax import lax

CHANNELS = 96
CLASSES = 13
BRICK = 8
BE = 1
BN = 2
BZ = 1
EAST_V = 128
NORTH_V = 32
UP_V = 8
VOXELS = 32768
N_EAST = 16
N_NORTH = 2


def set_ends(drawn, own_key, smallest, top_value):
    longest = drawn.shape.index(max(drawn.shape))
    spots = []
    for shift in (0, 1):
        where = [jax.random.randint(jax.random.fold_in(own_key, axis), (), 0, length) for axis, length in enumerate(drawn.shape)]
        where[longest] = (where[longest] + shift) % drawn.shape[longest]
        spots.append(tuple(where))
    return drawn.at[spots[0]].set(smallest).at[spots[1]].set(top_value)


def level_of(stream_key, dims, shards, least, top_value):
    def one(position, blocks):
        draws = jax.random.uniform(jax.random.fold_in(jax.random.fold_in(stream_key, 6), position), (blocks,), jnp.float32, least / len(shards), top_value / len(shards))
        return jnp.repeat(jnp.exp(draws), dims[position] // blocks).reshape((-1,) + (1,) * (len(dims) - position - 1))

    loudness = one(*shards[0])
    for cut in shards[1:]:
        loudness = loudness * one(*cut)
    return loudness


def gaussian(stream_key, shape, spread, bound, cuts=(), held_as=jnp.bfloat16):
    result = jax.random.normal(stream_key, shape, jnp.float32) * spread
    if len(cuts) > 0:
        result = level_of(stream_key, shape, cuts, -0.22, 0.18) * result
    return jnp.clip(result, min=-bound, max=bound).astype(held_as)


def setup_inputs(seed: int = 0) -> dict:
    splits = jax.random.split(jax.random.key(seed), 8)
    features = gaussian(splits[0], (CHANNELS, EAST_V, NORTH_V, UP_V), 1.0, 6.0, ((1, 16), (2, 2)))
    brick_active = set_ends((jax.random.randint(splits[1], (BE * N_EAST, BN * N_NORTH, BZ), 0, 3) < 2).astype(jnp.int32), jax.random.fold_in(splits[1], 1), 0, 1)
    voxel_occupancy = set_ends((jax.random.randint(splits[2], (EAST_V, NORTH_V, UP_V), 0, 2) < 1).astype(jnp.int32), jax.random.fold_in(splits[2], 1), 0, 1)
    first_weights = gaussian(splits[3], (27, CHANNELS, CHANNELS), (27 * CHANNELS) ** -0.5, 0.125)
    second_weights = gaussian(splits[4], (27, CHANNELS, CHANNELS), (27 * CHANNELS) ** -0.5, 0.125)
    head = gaussian(splits[5], (CLASSES, CHANNELS), CHANNELS ** -0.5, 0.625)
    teacher = gaussian(splits[6], (CLASSES, EAST_V, NORTH_V, UP_V), 1.0, 6.0, ((1, 16), (2, 2)))
    return dict(features=features, brick_active=brick_active, voxel_occupancy=voxel_occupancy, first_weights=first_weights, second_weights=second_weights, head=head, teacher=teacher)


def offset_of(k):
    return (k // 9 - 1, k // 3 % 3 - 1, k % 3 - 1)

def shifted(padded, k, sign, shape):
    de, dn, du = offset_of(k)
    east, north, upward = shape
    a = 1 + sign * de
    b = 1 + sign * dn
    c = 1 + sign * du
    piece = padded[:, a:a + east, b:b + north, c:c + upward]
    return piece.reshape(padded.shape[0], -1)

def bordered(field):
    return jnp.pad(field, ((0, 0), (1, 1), (1, 1), (1, 1)))

def silu_slope(value):
    sig = jax.nn.sigmoid(value)
    return sig * (1.0 + value * (1.0 - sig))

def apply_stencil(field, weights, sign):
    shape = field.shape[1:]
    padded = bordered(field)
    total = jnp.zeros((weights.shape[1], field.shape[1] * field.shape[2] * field.shape[3]), jnp.float32)
    for k in range(27):
        piece = shifted(padded, k, sign, shape)
        if sign > 0:
            total = total + jnp.dot(weights[k], piece, preferred_element_type=jnp.float32)
        else:
            total = total + jnp.dot(weights[k].T, piece, preferred_element_type=jnp.float32)
    return total.reshape((weights.shape[1],) + shape)

def kernel_grad(grad, field):
    shape = field.shape[1:]
    padded = bordered(field)
    flat = grad.reshape(grad.shape[0], -1)
    rows = []
    for k in range(27):
        piece = shifted(padded, k, 1, shape)
        rows.append(jnp.dot(flat, piece.T, preferred_element_type=jnp.float32))
    return jnp.stack(rows, 0)

def reference(features, brick_active, voxel_occupancy, first_weights, second_weights, head, teacher):
    flags = jnp.repeat(jnp.repeat(jnp.repeat(brick_active, BRICK, 0), BRICK, 1), BRICK, 2)
    mask = (flags * voxel_occupancy).astype(jnp.float32)
    a0 = jnp.where(mask > 0, features, jnp.zeros_like(features))
    p1 = mask * apply_stencil(a0, first_weights, 1)
    a1 = jax.nn.silu(p1).astype(jnp.bfloat16)
    p2 = mask * apply_stencil(a1, second_weights, 1)
    a2 = jax.nn.silu(p2).astype(jnp.bfloat16)
    channels = a2.shape[0]
    flat_mask = mask.reshape(1, -1)
    logits = jnp.dot(head, a2.reshape(channels, -1), preferred_element_type=jnp.float32)
    g_logits = flat_mask * (logits - teacher.reshape(teacher.shape[0], -1).astype(jnp.float32))
    g_a2 = jnp.dot(head.astype(jnp.float32).T, g_logits, precision=lax.Precision.HIGHEST)
    g_p2 = (flat_mask * g_a2 * silu_slope(p2.reshape(channels, -1))).astype(jnp.bfloat16).reshape(p2.shape)
    scale = 1.0 / jnp.sqrt(jnp.float32(VOXELS))
    grad_second = kernel_grad(g_p2, a1) * scale
    g_a1 = apply_stencil(g_p2, second_weights, -1)
    g_p1 = (mask * g_a1 * silu_slope(p1)).astype(jnp.bfloat16)
    grad_first = kernel_grad(g_p1, a0) * scale
    grad_features = (mask * apply_stencil(g_p1, first_weights, -1)).astype(jnp.bfloat16)
    return (grad_features, grad_first, grad_second)
```

```python
import functools
import math

import jax
import jax.numpy as jnp
from jax import lax
from jax.experimental import pallas as pl
from jax.experimental.pallas import tpu as pltpu
from jax.sharding import PartitionSpec as P

LANES = 128
HALO = 4
OFFSETS = 9
WIDE = OFFSETS * LANES
AXES = ("east", "north")
F32 = jnp.float32
BF16 = jnp.bfloat16


def halo_of(block, axis, dim, width):
    count = lax.axis_size(axis)
    size = block.shape[dim]
    if count == 1:
        empty = jnp.zeros_like(lax.slice_in_dim(block, 0, width, axis=dim))
        return empty, empty
    if count == 2:
        me = lax.axis_index(axis)
        mine = lax.dynamic_slice_in_dim(block, (1 - me) * (size - width), width, axis=dim)
        other = lax.ppermute(mine, axis, [(0, 1), (1, 0)])
        empty = jnp.zeros_like(other)
        return jnp.where(me == 1, other, empty), jnp.where(me == 0, other, empty)
    forward = [(i, i + 1) for i in range(count - 1)]
    backward = [(target, source) for source, target in forward]
    low = lax.ppermute(lax.slice_in_dim(block, size - width, size, axis=dim), axis, forward)
    high = lax.ppermute(lax.slice_in_dim(block, 0, width, axis=dim), axis, backward)
    return low, high


def lane_of(shape):
    return lax.broadcasted_iota(jnp.int32, shape, len(shape) - 1)


def put_stack(value, rows, upward, stack_ref, parity, index):
    cubes = value.reshape(rows // upward, upward, LANES)
    level = lax.broadcasted_iota(jnp.int32, cubes.shape, 1)
    below = jnp.where(level == 0, 0.0, pltpu.roll(cubes, 1, 1)).reshape(rows, LANES)
    above = jnp.where(level == upward - 1, 0.0, pltpu.roll(cubes, upward - 1, 1)).reshape(rows, LANES)
    start = index * rows
    for up, moved in enumerate((below, value, above)):
        shifts = (
            jnp.concatenate([moved[rows - upward :], moved[: rows - upward]], 0),
            moved,
            jnp.concatenate([moved[upward:], moved[:upward]], 0),
        )
        for north, shifted in enumerate(shifts):
            lane = (north * 3 + up) * LANES
            stack_ref[parity, pl.ds(start, rows), lane : lane + LANES] = shifted.astype(BF16)


def convolve(stack_ref, weight_ref, pairs, rows, acc_ref, transposed):
    dims = (((1,), (1,)), ((), ())) if transposed else (((1,), (0,)), ((), ()))
    total = None
    for p in range(4):
        first = (p // 2) * rows
        part = lax.dot_general(
            stack_ref[p % 2, first : first + pairs * rows, :],
            weight_ref[p],
            dims,
            preferred_element_type=F32,
        )
        total = part if total is None else total + part
    acc_ref[0 : pairs * rows, :] = total


def put_forward(weight_ref, w_ref, channels):
    weight_ref[...] = jnp.zeros_like(weight_ref)
    for p in range(4):
        for q in range(2):
            if 0 <= p - q <= 2:
                for j in range(OFFSETS):
                    weight_ref[p, q * LANES : q * LANES + channels, j * LANES : j * LANES + channels] = w_ref[
                        (p - q) * OFFSETS + j
                    ]


def put_backward(weight_ref, w_ref, channels):
    weight_ref[...] = jnp.zeros_like(weight_ref)
    for p in range(4):
        for q in range(2):
            if 0 <= p - q <= 2:
                for j in range(OFFSETS):
                    weight_ref[p, j * LANES : j * LANES + channels, q * LANES : q * LANES + channels] = w_ref[
                        (2 - (p - q)) * OFFSETS + 8 - j
                    ]


def put_turned(turned_ref, value, plane, east, channels):
    turned = value.T[0:channels].astype(BF16)
    size = value.shape[0]
    for d in range(3):
        e = plane + d - 1
        if 0 <= e < east:
            turned_ref[d * channels : (d + 1) * channels, e * size : (e + 1) * size] = turned


def kernel_sum(turned_ref, stack_ref, first, east, rows, low, size, channels, out_ref):
    total = None
    for i in range(east // 2):
        fields = []
        for e in (2 * i, 2 * i + 1):
            plane = e + first
            start = (plane // 2) * rows + low
            fields.append(stack_ref[plane % 2, start : start + size, :])
        part = jnp.dot(
            turned_ref[:, 2 * i * size : (2 * i + 2) * size],
            jnp.concatenate(fields, 0),
            preferred_element_type=F32,
        )
        total = part if total is None else total + part
    blocks = [
        total[d * channels : (d + 1) * channels, j * LANES : (j + 1) * LANES]
        for d in range(3)
        for j in range(OFFSETS)
    ]
    blocks.append(jnp.zeros_like(blocks[0]))
    lane = lane_of(blocks[0].shape)
    spare = LANES - channels
    row = 0
    for t in range(0, 28, 4):
        for r in range(3):
            tail = pltpu.roll(blocks[t + 3], channels - spare * r, 1)
            out_ref[row : row + channels, :] = jnp.where(lane < channels, blocks[t + r], tail).astype(BF16)
            row += channels
    if row < out_ref.shape[0]:
        out_ref[row:, :] = jnp.zeros((out_ref.shape[0] - row, LANES), BF16)


def whole_kernel(
    channels, classes, east, north, upward,
    x_ref, w1_ref, w2_ref, head_ref,
    out_ref, second_ref, first_ref,
    s0_ref, s1_ref, sg_ref, mask_ref, slope_ref, acc_ref, wt_ref, wb_ref, turned_ref,
):
    rows = (north + 2 * HALO) * upward
    low, size = HALO * upward, north * upward
    planes = east + 2 * HALO
    lane = lane_of((rows, LANES))

    put_forward(wt_ref, w1_ref, channels)

    def start(i, carry):
        for parity in range(2):
            x = x_ref[2 * i + parity].astype(F32)
            mask = jnp.broadcast_to(x[:, channels : channels + 1], (rows, LANES))
            mask_ref[2 * i + parity] = mask
            a0 = jnp.where((mask > 0) & (lane < channels), x, 0.0)
            put_stack(a0, rows, upward, s0_ref, parity, i)
        return carry

    lax.fori_loop(0, planes // 2, start, 0)
    convolve(s0_ref, wt_ref, (planes - 2) // 2, rows, acc_ref, True)
    put_forward(wt_ref, w2_ref, channels)

    def middle(i, carry):
        for parity in range(2):
            plane = 2 * i + parity
            mask = mask_ref[plane + 1]
            p1 = mask * acc_ref[pl.ds(i * rows, rows), parity * LANES : (parity + 1) * LANES]
            sig = jax.nn.sigmoid(p1)
            slope_ref[plane] = mask * (sig * (1.0 + p1 * (1.0 - sig)))
            put_stack(p1 * sig, rows, upward, s1_ref, parity, i)
        return carry

    lax.fori_loop(0, (planes - 2) // 2, middle, 0)
    convolve(s1_ref, wt_ref, (planes - 4) // 2, rows, acc_ref, True)
    put_backward(wb_ref, w2_ref, channels)

    head = head_ref[...]
    class_lane = (lane > channels) & (lane <= channels + classes)

    for i in range((planes - 4) // 2):
        for parity in range(2):
            plane = 2 * i + parity
            mask = mask_ref[plane + 2]
            p2 = mask * acc_ref[i * rows : (i + 1) * rows, parity * LANES : (parity + 1) * LANES]
            sig = jax.nn.sigmoid(p2)
            a2 = (p2 * sig).astype(BF16)
            logits = lax.dot_general(a2, head, (((1,), (1,)), ((), ())), preferred_element_type=F32)
            g_logits = jnp.where(class_lane, mask * (logits - x_ref[plane + 2].astype(F32)), 0.0)
            coarse = g_logits.astype(BF16)
            fine = (g_logits - coarse.astype(F32)).astype(BF16)
            g_a2 = jnp.dot(
                jnp.concatenate([coarse, fine], 1), jnp.concatenate([head, head], 0), preferred_element_type=F32
            )
            g_p2 = mask * g_a2 * (sig * (1.0 + p2 * (1.0 - sig)))
            put_stack(g_p2, rows, upward, sg_ref, parity, i)
            put_turned(turned_ref, g_p2[low : low + size], plane - 2, east, channels)

    kernel_sum(turned_ref, s1_ref, 3, east, rows, low, size, channels, second_ref)
    convolve(sg_ref, wb_ref, (planes - 6) // 2, rows, acc_ref, False)
    put_backward(wb_ref, w1_ref, channels)

    for i in range((planes - 6) // 2):
        for parity in range(2):
            plane = 2 * i + parity
            g_p1 = slope_ref[plane + 2] * acc_ref[i * rows : (i + 1) * rows, parity * LANES : (parity + 1) * LANES]
            put_stack(g_p1, rows, upward, sg_ref, parity, i)
            put_turned(turned_ref, g_p1[low : low + size], plane - 1, east, channels)

    kernel_sum(turned_ref, s0_ref, 4, east, rows, low, size, channels, first_ref)
    convolve(sg_ref, wb_ref, east // 2, rows, acc_ref, False)
    for i in range(east // 2):
        for parity in range(2):
            plane = 2 * i + parity
            value = acc_ref[i * rows + low : i * rows + low + size, parity * LANES : (parity + 1) * LANES]
            value = mask_ref[plane + HALO, low : low + size] * value
            out_ref[plane] = value[:, 0:channels].astype(BF16)


def unpack_kernel(channels, scale, second_in, first_in, first_out, second_out):
    spare = LANES - channels
    for source, target in ((first_in, first_out), (second_in, second_out)):
        for t in range(0, 27, 4):
            tiles = [
                source[(t // 4 * 3 + r) * channels : (t // 4 * 3 + r + 1) * channels, :].astype(F32) * scale
                for r in range(3)
            ]
            for r in range(3):
                target[t + r] = tiles[r][:, 0:channels]
            if t + 3 < 27:
                lane = lane_of(tiles[0].shape)
                parts = [pltpu.roll(tiles[r], (spare * r - channels) % LANES, 1) for r in range(3)]
                last = jnp.where(lane < spare, parts[0], jnp.where(lane < 2 * spare, parts[1], parts[2]))
                target[t + 3] = last[:, 0:channels]


def per_device(
    features, brick_active, voxel_occupancy, first_weights, second_weights, head, teacher
):
    channels = features.shape[0]
    east, north, upward = features.shape[1:]
    classes = teacher.shape[0]
    devices = lax.axis_size("east") * lax.axis_size("north")
    scale = 1.0 / math.sqrt(devices * east * north * upward)

    flags = jnp.repeat(brick_active, east // brick_active.shape[0], 0)
    flags = jnp.repeat(flags, north // brick_active.shape[1], 1)
    flags = jnp.repeat(flags, upward // brick_active.shape[2], 2)
    mask = (flags * voxel_occupancy).astype(BF16)
    x = jnp.concatenate(
        [
            features.transpose(1, 2, 3, 0),
            mask[..., None],
            teacher.transpose(1, 2, 3, 0),
            jnp.zeros((east, north, upward, LANES - channels - 1 - classes), BF16),
        ],
        -1,
    )
    low, high = halo_of(x, "north", 1, HALO)
    x = jnp.concatenate([low, x, high], 1)
    low, high = halo_of(x, "east", 0, HALO)
    x = jnp.concatenate([low, x, high], 0)

    planes = east + 2 * HALO
    rows = (north + 2 * HALO) * upward
    x = x.reshape(planes, rows, LANES)
    head_wide = jnp.pad(head, ((channels + 1, LANES - channels - 1 - classes), (0, LANES - channels)))

    chunk = -(-21 * channels // (devices * 16)) * 16
    packed = chunk * devices
    vmem = pl.BlockSpec(memory_space=pltpu.VMEM)
    grad_features, second, first = pl.pallas_call(
        functools.partial(whole_kernel, channels, classes, east, north, upward),
        out_shape=(
            jax.ShapeDtypeStruct((east, north * upward, channels), BF16),
            jax.ShapeDtypeStruct((packed, LANES), BF16),
            jax.ShapeDtypeStruct((packed, LANES), BF16),
        ),
        in_specs=[vmem] * 4,
        out_specs=(vmem, vmem, vmem),
        scratch_shapes=[
            pltpu.VMEM((2, planes // 2 * rows, WIDE), BF16),
            pltpu.VMEM((2, (planes - 2) // 2 * rows, WIDE), BF16),
            pltpu.VMEM((2, (planes - 4) // 2 * rows, WIDE), BF16),
            pltpu.VMEM((planes, rows, LANES), F32),
            pltpu.VMEM((planes - 2, rows, LANES), F32),
            pltpu.VMEM(((planes - 2) // 2 * rows, 2 * LANES), F32),
            pltpu.VMEM((4, 2 * LANES, WIDE), BF16),
            pltpu.VMEM((4, WIDE, 2 * LANES), BF16),
            pltpu.VMEM((3 * channels, east * north * upward), BF16),
        ],
        compiler_params=pltpu.CompilerParams(vmem_limit_bytes=56 * 1024 * 1024),
        name="fields",
    )(x, first_weights, second_weights, head_wide)

    both = jnp.concatenate(
        [second.reshape(devices, chunk, LANES), first.reshape(devices, chunk, LANES)], 1
    )
    parts = lax.all_to_all(both, AXES, 0, 0, tiled=True)
    mine = jnp.sum(parts.astype(F32), 0).astype(BF16)
    whole = lax.all_gather(mine, AXES, axis=0)
    second = whole[:, :chunk].reshape(packed, LANES)
    first = whole[:, chunk:].reshape(packed, LANES)

    grad_first, grad_second = pl.pallas_call(
        functools.partial(unpack_kernel, channels, scale),
        out_shape=(
            jax.ShapeDtypeStruct(first_weights.shape, F32),
            jax.ShapeDtypeStruct(second_weights.shape, F32),
        ),
        in_specs=[vmem] * 2,
        out_specs=(vmem, vmem),
        compiler_params=pltpu.CompilerParams(vmem_limit_bytes=32 * 1024 * 1024),
        name="unpack",
    )(second, first)
    grad_features = grad_features.reshape(east, north, upward, channels).transpose(3, 0, 1, 2)
    return (grad_features, grad_first, grad_second)


def solution(mesh):
    in_specs = (
        P(None, "east", "north", None),
        P("east", "north", None),
        P("east", "north", None),
        P(),
        P(),
        P(),
        P(None, "east", "north", None),
    )
    out_specs = (P(None, "east", "north", None), P(), P())
    return jax.shard_map(
        per_device, mesh=mesh, in_specs=in_specs, out_specs=out_specs, check_vma=False
    )
```

```python
import functools
import math

import jax
import jax.numpy as jnp
from jax import lax
from jax.experimental import pallas as pl
from jax.experimental.pallas import tpu as pltpu
from jax.sharding import PartitionSpec as P

LANES = 128
HALO = 4
OFFSETS = 9
WIDE = OFFSETS * LANES
F32 = jnp.float32
BF16 = jnp.bfloat16


def halo_of(block, axis, dim, width):
    count = lax.axis_size(axis)
    size = block.shape[dim]
    if count == 1:
        empty = jnp.zeros_like(lax.slice_in_dim(block, 0, width, axis=dim))
        return empty, empty
    if count == 2:
        me = lax.axis_index(axis)
        mine = lax.dynamic_slice_in_dim(block, (1 - me) * (size - width), width, axis=dim)
        other = lax.ppermute(mine, axis, [(0, 1), (1, 0)])
        empty = jnp.zeros_like(other)
        return jnp.where(me == 1, other, empty), jnp.where(me == 0, other, empty)
    forward = [(i, i + 1) for i in range(count - 1)]
    backward = [(target, source) for source, target in forward]
    low = lax.ppermute(lax.slice_in_dim(block, size - width, size, axis=dim), axis, forward)
    high = lax.ppermute(lax.slice_in_dim(block, 0, width, axis=dim), axis, backward)
    return low, high


def exchange(value, axis, bit):
    size = lax.axis_size(axis)
    return lax.ppermute(value, axis, [(i, i ^ bit) for i in range(size)])


def high_bit(axis, bit):
    return (lax.axis_index(axis) // bit) % 2


def bits_of(axis):
    size = lax.axis_size(axis)
    return [(axis, 1 << i) for i in range(size.bit_length() - 1)]


def scatter_steps(values, orders):
    for step in range(len(orders[0])):
        sent = []
        for value, order in zip(values, orders):
            axis, bit = order[step]
            half = value.shape[0] // 2
            away = lax.dynamic_slice_in_dim(value, (1 - high_bit(axis, bit)) * half, half, 0)
            sent.append(exchange(away.astype(BF16), axis, bit))
        kept = []
        for value, order, other in zip(values, orders, sent):
            axis, bit = order[step]
            half = value.shape[0] // 2
            mine = lax.dynamic_slice_in_dim(value, high_bit(axis, bit) * half, half, 0)
            kept.append(mine + other.astype(F32))
        values = kept
    return values


def join(mine, other, axis, bit):
    upper = high_bit(axis, bit) == 1
    return jnp.concatenate([jnp.where(upper, other, mine), jnp.where(upper, mine, other)], 0)


def gather_steps(values, orders):
    for step in range(len(orders[0]) - 1, 0, -1):
        others = [exchange(value, *order[step]) for value, order in zip(values, orders)]
        values = [join(value, other, *order[step]) for value, other, order in zip(values, others, orders)]
    others = [exchange(value, *order[0]) for value, order in zip(values, orders)]
    return values, others


def lane_of(shape):
    return lax.broadcasted_iota(jnp.int32, shape, len(shape) - 1)


def put_stack(value, rows, upward, stack_ref, parity, index):
    cubes = value.reshape(rows // upward, upward, LANES)
    level = lax.broadcasted_iota(jnp.int32, cubes.shape, 1)
    below = jnp.where(level == 0, 0.0, pltpu.roll(cubes, 1, 1)).reshape(rows, LANES)
    above = jnp.where(level == upward - 1, 0.0, pltpu.roll(cubes, upward - 1, 1)).reshape(rows, LANES)
    start = index * rows
    for up, moved in enumerate((below, value, above)):
        shifts = (
            jnp.concatenate([moved[rows - upward :], moved[: rows - upward]], 0),
            moved,
            jnp.concatenate([moved[upward:], moved[:upward]], 0),
        )
        for north, shifted in enumerate(shifts):
            lane = (north * 3 + up) * LANES
            stack_ref[parity, pl.ds(start, rows), lane : lane + LANES] = shifted.astype(BF16)


def convolve(stack_ref, weight_ref, pairs, rows, acc_ref, transposed):
    dims = (((1,), (1,)), ((), ())) if transposed else (((1,), (0,)), ((), ()))
    total = None
    for p in range(4):
        first = (p // 2) * rows
        part = lax.dot_general(
            stack_ref[p % 2, first : first + pairs * rows, :],
            weight_ref[p],
            dims,
            preferred_element_type=F32,
        )
        total = part if total is None else total + part
    acc_ref[0 : pairs * rows, :] = total


def put_forward(weight_ref, w_ref, channels):
    weight_ref[...] = jnp.zeros_like(weight_ref)
    for p in range(4):
        for q in range(2):
            if 0 <= p - q <= 2:
                for j in range(OFFSETS):
                    weight_ref[p, q * LANES : q * LANES + channels, j * LANES : j * LANES + channels] = w_ref[
                        (p - q) * OFFSETS + j
                    ]


def put_backward(weight_ref, w_ref, channels):
    weight_ref[...] = jnp.zeros_like(weight_ref)
    for p in range(4):
        for q in range(2):
            if 0 <= p - q <= 2:
                for j in range(OFFSETS):
                    weight_ref[p, j * LANES : j * LANES + channels, q * LANES : q * LANES + channels] = w_ref[
                        (2 - (p - q)) * OFFSETS + 8 - j
                    ]


def put_turned(turned_ref, value, plane, east, channels):
    turned = value.T[0:channels].astype(BF16)
    size = value.shape[0]
    for d in range(3):
        e = plane + d - 1
        if 0 <= e < east:
            turned_ref[d * channels : (d + 1) * channels, e * size : (e + 1) * size] = turned


def kernel_sum(turned_ref, stack_ref, first, east, rows, low, size, channels, out_ref):
    total = None
    for i in range(east // 2):
        fields = []
        for e in (2 * i, 2 * i + 1):
            plane = e + first
            start = (plane // 2) * rows + low
            fields.append(stack_ref[plane % 2, start : start + size, :])
        part = jnp.dot(
            turned_ref[:, 2 * i * size : (2 * i + 2) * size],
            jnp.concatenate(fields, 0),
            preferred_element_type=F32,
        )
        total = part if total is None else total + part
    blocks = [
        total[d * channels : (d + 1) * channels, j * LANES : (j + 1) * LANES]
        for d in range(3)
        for j in range(OFFSETS)
    ]
    blocks.append(jnp.zeros_like(blocks[0]))
    lane = lane_of(blocks[0].shape)
    spare = LANES - channels
    row = 0
    for t in range(0, 28, 4):
        for r in range(3):
            tail = pltpu.roll(blocks[t + 3], channels - spare * r, 1)
            out_ref[row : row + channels, :] = jnp.where(lane < channels, blocks[t + r], tail)
            row += channels
    if row < out_ref.shape[0]:
        out_ref[row:, :] = jnp.zeros((out_ref.shape[0] - row, LANES), F32)


def whole_kernel(
    channels, classes, east, north, upward,
    x_ref, w1_ref, w2_ref, head_ref,
    out_ref, second_ref, first_ref,
    s0_ref, s1_ref, sg_ref, mask_ref, slope_ref, acc_ref, wt_ref, wb_ref, turned_ref,
):
    rows = (north + 2 * HALO) * upward
    low, size = HALO * upward, north * upward
    planes = east + 2 * HALO
    lane = lane_of((rows, LANES))

    put_forward(wt_ref, w1_ref, channels)

    def start(i, carry):
        for parity in range(2):
            x = x_ref[2 * i + parity].astype(F32)
            mask = jnp.broadcast_to(x[:, channels : channels + 1], (rows, LANES))
            mask_ref[2 * i + parity] = mask
            a0 = jnp.where((mask > 0) & (lane < channels), x, 0.0)
            put_stack(a0, rows, upward, s0_ref, parity, i)
        return carry

    lax.fori_loop(0, planes // 2, start, 0)
    convolve(s0_ref, wt_ref, (planes - 2) // 2, rows, acc_ref, True)
    put_forward(wt_ref, w2_ref, channels)

    def middle(i, carry):
        for parity in range(2):
            plane = 2 * i + parity
            mask = mask_ref[plane + 1]
            p1 = mask * acc_ref[pl.ds(i * rows, rows), parity * LANES : (parity + 1) * LANES]
            sig = jax.nn.sigmoid(p1)
            slope_ref[plane] = mask * (sig * (1.0 + p1 * (1.0 - sig)))
            put_stack(p1 * sig, rows, upward, s1_ref, parity, i)
        return carry

    lax.fori_loop(0, (planes - 2) // 2, middle, 0)
    convolve(s1_ref, wt_ref, (planes - 4) // 2, rows, acc_ref, True)
    put_backward(wb_ref, w2_ref, channels)

    head = head_ref[...]
    class_lane = (lane > channels) & (lane <= channels + classes)

    for i in range((planes - 4) // 2):
        for parity in range(2):
            plane = 2 * i + parity
            mask = mask_ref[plane + 2]
            p2 = mask * acc_ref[i * rows : (i + 1) * rows, parity * LANES : (parity + 1) * LANES]
            sig = jax.nn.sigmoid(p2)
            a2 = (p2 * sig).astype(BF16)
            logits = lax.dot_general(a2, head, (((1,), (1,)), ((), ())), preferred_element_type=F32)
            g_logits = jnp.where(class_lane, mask * (logits - x_ref[plane + 2].astype(F32)), 0.0)
            coarse = g_logits.astype(BF16)
            fine = (g_logits - coarse.astype(F32)).astype(BF16)
            g_a2 = jnp.dot(
                jnp.concatenate([coarse, fine], 1), jnp.concatenate([head, head], 0), preferred_element_type=F32
            )
            g_p2 = mask * g_a2 * (sig * (1.0 + p2 * (1.0 - sig)))
            put_stack(g_p2, rows, upward, sg_ref, parity, i)
            put_turned(turned_ref, g_p2[low : low + size], plane - 2, east, channels)

    kernel_sum(turned_ref, s1_ref, 3, east, rows, low, size, channels, second_ref)
    convolve(sg_ref, wb_ref, (planes - 6) // 2, rows, acc_ref, False)
    put_backward(wb_ref, w1_ref, channels)

    for i in range((planes - 6) // 2):
        for parity in range(2):
            plane = 2 * i + parity
            g_p1 = slope_ref[plane + 2] * acc_ref[i * rows : (i + 1) * rows, parity * LANES : (parity + 1) * LANES]
            put_stack(g_p1, rows, upward, sg_ref, parity, i)
            put_turned(turned_ref, g_p1[low : low + size], plane - 1, east, channels)

    kernel_sum(turned_ref, s0_ref, 4, east, rows, low, size, channels, first_ref)
    convolve(sg_ref, wb_ref, east // 2, rows, acc_ref, False)
    for i in range(east // 2):
        for parity in range(2):
            plane = 2 * i + parity
            value = acc_ref[i * rows + low : i * rows + low + size, parity * LANES : (parity + 1) * LANES]
            value = mask_ref[plane + HALO, low : low + size] * value
            out_ref[plane] = value[:, 0:channels].astype(BF16)


def unpack_kernel(channels, scale, upper_ref, second_mine, first_mine, second_other, first_other, first_out, second_out):
    spare = LANES - channels
    half = first_mine.shape[0]
    upper = upper_ref[0] == 1

    def rows_of(mine, other, start):
        pieces = []
        for begin, stop in ((start, min(start + channels, half)), (max(start, half), start + channels)):
            if begin < stop:
                place = begin % half
                picked = (mine[place : place + stop - begin, :], other[place : place + stop - begin, :])
                if begin < half:
                    picked = picked[::-1]
                pieces.append(jnp.where(upper, *picked))
        return (pieces[0] if len(pieces) == 1 else jnp.concatenate(pieces, 0)).astype(F32) * scale

    for mine, other, target in ((first_mine, first_other, first_out), (second_mine, second_other, second_out)):
        for t in range(0, 27, 4):
            tiles = [rows_of(mine, other, (t // 4 * 3 + r) * channels) for r in range(3)]
            for r in range(3):
                target[t + r] = tiles[r][:, 0:channels]
            if t + 3 < 27:
                lane = lane_of(tiles[0].shape)
                parts = [pltpu.roll(tiles[r], (spare * r - channels) % LANES, 1) for r in range(3)]
                last = jnp.where(lane < spare, parts[0], jnp.where(lane < 2 * spare, parts[1], parts[2]))
                target[t + 3] = last[:, 0:channels]


def per_device(
    features, brick_active, voxel_occupancy, first_weights, second_weights, head, teacher
):
    channels = features.shape[0]
    east, north, upward = features.shape[1:]
    classes = teacher.shape[0]
    devices = lax.axis_size("east") * lax.axis_size("north")
    scale = 1.0 / math.sqrt(devices * east * north * upward)

    flags = jnp.repeat(brick_active, east // brick_active.shape[0], 0)
    flags = jnp.repeat(flags, north // brick_active.shape[1], 1)
    flags = jnp.repeat(flags, upward // brick_active.shape[2], 2)
    mask = (flags * voxel_occupancy).astype(BF16)
    x = jnp.concatenate(
        [
            features.transpose(1, 2, 3, 0),
            mask[..., None],
            teacher.transpose(1, 2, 3, 0),
            jnp.zeros((east, north, upward, LANES - channels - 1 - classes), BF16),
        ],
        -1,
    )
    low, high = halo_of(x, "north", 1, HALO)
    x = jnp.concatenate([low, x, high], 1)
    low, high = halo_of(x, "east", 0, HALO)
    x = jnp.concatenate([low, x, high], 0)

    planes = east + 2 * HALO
    rows = (north + 2 * HALO) * upward
    x = x.reshape(planes, rows, LANES)
    head_wide = jnp.pad(head, ((channels + 1, LANES - channels - 1 - classes), (0, LANES - channels)))

    chunk = -(-21 * channels // (devices * 16)) * 16
    packed = chunk * devices
    vmem = pl.BlockSpec(memory_space=pltpu.VMEM)
    grad_features, second, first = pl.pallas_call(
        functools.partial(whole_kernel, channels, classes, east, north, upward),
        out_shape=(
            jax.ShapeDtypeStruct((east, north * upward, channels), BF16),
            jax.ShapeDtypeStruct((packed, LANES), F32),
            jax.ShapeDtypeStruct((packed, LANES), F32),
        ),
        in_specs=[vmem] * 4,
        out_specs=(vmem, vmem, vmem),
        scratch_shapes=[
            pltpu.VMEM((2, planes // 2 * rows, WIDE), BF16),
            pltpu.VMEM((2, (planes - 2) // 2 * rows, WIDE), BF16),
            pltpu.VMEM((2, (planes - 4) // 2 * rows, WIDE), BF16),
            pltpu.VMEM((planes, rows, LANES), F32),
            pltpu.VMEM((planes - 2, rows, LANES), F32),
            pltpu.VMEM(((planes - 2) // 2 * rows, 2 * LANES), F32),
            pltpu.VMEM((4, 2 * LANES, WIDE), BF16),
            pltpu.VMEM((4, WIDE, 2 * LANES), BF16),
            pltpu.VMEM((3 * channels, east * north * upward), BF16),
        ],
        compiler_params=pltpu.CompilerParams(vmem_limit_bytes=56 * 1024 * 1024),
        name="fields",
    )(x, first_weights, second_weights, head_wide)

    east_bits, north_bits = bits_of("east"), bits_of("north")
    orders = (
        east_bits[:1] + north_bits + east_bits[1:],
        east_bits[:2] + north_bits + east_bits[2:],
    )
    sums = scatter_steps((second, first), orders)
    mine, others = gather_steps([total.astype(BF16) for total in sums], orders)
    upper = high_bit(*east_bits[0]).reshape(1)

    grad_first, grad_second = pl.pallas_call(
        functools.partial(unpack_kernel, channels, scale),
        out_shape=(
            jax.ShapeDtypeStruct(first_weights.shape, F32),
            jax.ShapeDtypeStruct(second_weights.shape, F32),
        ),
        in_specs=[pl.BlockSpec(memory_space=pltpu.SMEM)] + [vmem] * 4,
        out_specs=(vmem, vmem),
        compiler_params=pltpu.CompilerParams(vmem_limit_bytes=32 * 1024 * 1024),
        name="unpack",
    )(upper, *mine, *others)
    grad_features = grad_features.reshape(east, north, upward, channels).transpose(3, 0, 1, 2)
    return (grad_features, grad_first, grad_second)


def solution(mesh):
    in_specs = (
        P(None, "east", "north", None),
        P("east", "north", None),
        P("east", "north", None),
        P(),
        P(),
        P(),
        P(None, "east", "north", None),
    )
    out_specs = (P(None, "east", "north", None), P(), P())
    return jax.shard_map(
        per_device, mesh=mesh, in_specs=in_specs, out_specs=out_specs, check_vma=False
    )
```

```python
import functools
import math

import jax
import jax.numpy as jnp
from jax import lax
from jax.experimental import pallas as pl
from jax.experimental.pallas import tpu as pltpu
from jax.sharding import PartitionSpec as P

LANES = 128
HALO = 4
OFFSETS = 9
WIDE = OFFSETS * LANES
F32 = jnp.float32
BF16 = jnp.bfloat16


def halo_of(block, axis, dim, width):
    count = lax.axis_size(axis)
    size = block.shape[dim]
    if count == 1:
        empty = jnp.zeros_like(lax.slice_in_dim(block, 0, width, axis=dim))
        return empty, empty
    if count == 2:
        me = lax.axis_index(axis)
        mine = lax.dynamic_slice_in_dim(block, (1 - me) * (size - width), width, axis=dim)
        other = lax.ppermute(mine, axis, [(0, 1), (1, 0)])
        empty = jnp.zeros_like(other)
        return jnp.where(me == 1, other, empty), jnp.where(me == 0, other, empty)
    forward = [(i, i + 1) for i in range(count - 1)]
    backward = [(target, source) for source, target in forward]
    low = lax.ppermute(lax.slice_in_dim(block, size - width, size, axis=dim), axis, forward)
    high = lax.ppermute(lax.slice_in_dim(block, 0, width, axis=dim), axis, backward)
    return low, high


def exchange(value, axis, bit):
    size = lax.axis_size(axis)
    return lax.ppermute(value, axis, [(i, i ^ bit) for i in range(size)])


def high_bit(axis, bit):
    return (lax.axis_index(axis) // bit) % 2


def bits_of(axis):
    size = lax.axis_size(axis)
    return [(axis, 1 << i) for i in range(size.bit_length() - 1)]


def scatter_steps(kept, sent, order):
    for step, (axis, bit) in enumerate(order):
        total = kept + exchange(sent, axis, bit).astype(F32)
        if step + 1 < len(order):
            upper = high_bit(*order[step + 1])
            half = total.shape[0] // 2
            sent = lax.dynamic_slice_in_dim(total, (1 - upper) * half, half, 0).astype(BF16)
            kept = lax.dynamic_slice_in_dim(total, upper * half, half, 0)
    return total


def gather_steps(mine, order):
    for axis, bit in order[:0:-1]:
        other = exchange(mine, axis, bit)
        upper = high_bit(axis, bit) == 1
        mine = jnp.concatenate([jnp.where(upper, other, mine), jnp.where(upper, mine, other)], 0)
    return mine, exchange(mine, *order[0])


def lane_of(shape):
    return lax.broadcasted_iota(jnp.int32, shape, len(shape) - 1)


def put_stack(value, rows, upward, stack_ref, parity, index):
    cubes = value.reshape(rows // upward, upward, LANES)
    level = lax.broadcasted_iota(jnp.int32, cubes.shape, 1)
    below = jnp.where(level == 0, 0.0, pltpu.roll(cubes, 1, 1)).reshape(rows, LANES)
    above = jnp.where(level == upward - 1, 0.0, pltpu.roll(cubes, upward - 1, 1)).reshape(rows, LANES)
    start = index * rows
    for up, moved in enumerate((below, value, above)):
        shifts = (
            jnp.concatenate([moved[rows - upward :], moved[: rows - upward]], 0),
            moved,
            jnp.concatenate([moved[upward:], moved[:upward]], 0),
        )
        for north, shifted in enumerate(shifts):
            lane = (north * 3 + up) * LANES
            stack_ref[parity, pl.ds(start, rows), lane : lane + LANES] = shifted.astype(BF16)


def convolve(stack_ref, weight_ref, pairs, rows, acc_ref, transposed):
    dims = (((1,), (1,)), ((), ())) if transposed else (((1,), (0,)), ((), ()))
    total = None
    for p in range(4):
        first = (p // 2) * rows
        part = lax.dot_general(
            stack_ref[p % 2, first : first + pairs * rows, :],
            weight_ref[p],
            dims,
            preferred_element_type=F32,
        )
        total = part if total is None else total + part
    acc_ref[0 : pairs * rows, :] = total


def put_forward(weight_ref, w_ref, channels):
    weight_ref[...] = jnp.zeros_like(weight_ref)
    for p in range(4):
        for q in range(2):
            if 0 <= p - q <= 2:
                for j in range(OFFSETS):
                    weight_ref[p, q * LANES : q * LANES + channels, j * LANES : j * LANES + channels] = w_ref[
                        (p - q) * OFFSETS + j
                    ]


def put_backward(weight_ref, w_ref, channels):
    weight_ref[...] = jnp.zeros_like(weight_ref)
    for p in range(4):
        for q in range(2):
            if 0 <= p - q <= 2:
                for j in range(OFFSETS):
                    weight_ref[p, j * LANES : j * LANES + channels, q * LANES : q * LANES + channels] = w_ref[
                        (2 - (p - q)) * OFFSETS + 8 - j
                    ]


def put_turned(turned_ref, value, plane, east, channels):
    turned = value.T[0:channels].astype(BF16)
    size = value.shape[0]
    for d in range(3):
        e = plane + d - 1
        if 0 <= e < east:
            turned_ref[d * channels : (d + 1) * channels, e * size : (e + 1) * size] = turned


def kernel_sum(turned_ref, stack_ref, first, east, rows, low, size, channels):
    total = None
    for i in range(east // 2):
        fields = []
        for e in (2 * i, 2 * i + 1):
            plane = e + first
            start = (plane // 2) * rows + low
            fields.append(stack_ref[plane % 2, start : start + size, :])
        part = jnp.dot(
            turned_ref[:, 2 * i * size : (2 * i + 2) * size],
            jnp.concatenate(fields, 0),
            preferred_element_type=F32,
        )
        total = part if total is None else total + part
    blocks = [
        total[d * channels : (d + 1) * channels, j * LANES : (j + 1) * LANES]
        for d in range(3)
        for j in range(OFFSETS)
    ]
    blocks.append(jnp.zeros_like(blocks[0]))
    lane = lane_of(blocks[0].shape)
    spare = LANES - channels
    tiles = []
    for t in range(0, 28, 4):
        for r in range(3):
            tail = pltpu.roll(blocks[t + 3], channels - spare * r, 1)
            tiles.append(jnp.where(lane < channels, blocks[t + r], tail))
    return tiles


def whole_kernel(
    channels, classes, east, north, upward,
    upper_ref, x_ref, w1_ref, w2_ref, head_ref,
    grad_ref, kept_ref, sent_ref,
    s0_ref, s1_ref, sg_ref, mask_ref, slope_ref, acc_ref, wt_ref, wb_ref, turned_ref,
):
    rows = (north + 2 * HALO) * upward
    low, size = HALO * upward, north * upward
    planes = east + 2 * HALO
    lane = lane_of((rows, LANES))

    put_forward(wt_ref, w1_ref, channels)

    def start(i, carry):
        for parity in range(2):
            x = x_ref[2 * i + parity].astype(F32)
            mask = jnp.broadcast_to(x[:, channels : channels + 1], (rows, LANES))
            mask_ref[2 * i + parity] = mask
            a0 = jnp.where((mask > 0) & (lane < channels), x, 0.0)
            put_stack(a0, rows, upward, s0_ref, parity, i)
        return carry

    lax.fori_loop(0, planes // 2, start, 0)
    convolve(s0_ref, wt_ref, (planes - 2) // 2, rows, acc_ref, True)
    put_forward(wt_ref, w2_ref, channels)

    def middle(i, carry):
        for parity in range(2):
            plane = 2 * i + parity
            mask = mask_ref[plane + 1]
            p1 = mask * acc_ref[pl.ds(i * rows, rows), parity * LANES : (parity + 1) * LANES]
            sig = jax.nn.sigmoid(p1)
            slope_ref[plane] = mask * (sig * (1.0 + p1 * (1.0 - sig)))
            put_stack(p1 * sig, rows, upward, s1_ref, parity, i)
        return carry

    lax.fori_loop(0, (planes - 2) // 2, middle, 0)
    convolve(s1_ref, wt_ref, (planes - 4) // 2, rows, acc_ref, True)
    put_backward(wb_ref, w2_ref, channels)

    head = head_ref[...]
    class_lane = (lane > channels) & (lane <= channels + classes)

    for i in range((planes - 4) // 2):
        for parity in range(2):
            plane = 2 * i + parity
            mask = mask_ref[plane + 2]
            p2 = mask * acc_ref[i * rows : (i + 1) * rows, parity * LANES : (parity + 1) * LANES]
            sig = jax.nn.sigmoid(p2)
            a2 = (p2 * sig).astype(BF16)
            logits = lax.dot_general(a2, head, (((1,), (1,)), ((), ())), preferred_element_type=F32)
            g_logits = jnp.where(class_lane, mask * (logits - x_ref[plane + 2].astype(F32)), 0.0)
            coarse = g_logits.astype(BF16)
            fine = (g_logits - coarse.astype(F32)).astype(BF16)
            g_a2 = jnp.dot(
                jnp.concatenate([coarse, fine], 1), jnp.concatenate([head, head], 0), preferred_element_type=F32
            )
            g_p2 = mask * g_a2 * (sig * (1.0 + p2 * (1.0 - sig)))
            put_stack(g_p2, rows, upward, sg_ref, parity, i)
            put_turned(turned_ref, g_p2[low : low + size], plane - 2, east, channels)

    upper = upper_ref[0] == 1
    for t, tile in enumerate(kernel_sum(turned_ref, s1_ref, 3, east, rows, low, size, channels)):
        kept_ref[t * channels : (t + 1) * channels, :] = tile
    convolve(sg_ref, wb_ref, (planes - 6) // 2, rows, acc_ref, False)

    for i in range((planes - 6) // 2):
        for parity in range(2):
            plane = 2 * i + parity
            g_p1 = slope_ref[plane + 2] * acc_ref[i * rows : (i + 1) * rows, parity * LANES : (parity + 1) * LANES]
            grad_ref[plane] = g_p1.astype(BF16)
            put_turned(turned_ref, g_p1[low : low + size], plane - 1, east, channels)

    tiles = kernel_sum(turned_ref, s0_ref, 4, east, rows, low, size, channels)
    for t, first in enumerate(tiles):
        place = slice(t * channels, (t + 1) * channels)
        second = kept_ref[place, :]
        sent_ref[place, :] = jnp.where(upper, second, first).astype(BF16)
        kept_ref[place, :] = jnp.where(upper, first, second)
    filled = len(tiles) * channels
    if filled < kept_ref.shape[0]:
        kept_ref[filled:, :] = jnp.zeros((kept_ref.shape[0] - filled, LANES), F32)
        sent_ref[filled:, :] = jnp.zeros((kept_ref.shape[0] - filled, LANES), BF16)


def last_kernel(channels, east, north, upward, x_ref, grad_ref, w1_ref, out_ref, stack_ref, wb_ref, acc_ref):
    rows = (north + 2 * HALO) * upward
    low, size = HALO * upward, north * upward
    put_backward(wb_ref, w1_ref, channels)

    def start(i, carry):
        for parity in range(2):
            put_stack(grad_ref[2 * i + parity].astype(F32), rows, upward, stack_ref, parity, i)
        return carry

    lax.fori_loop(0, east // 2 + 1, start, 0)
    convolve(stack_ref, wb_ref, east // 2, rows, acc_ref, False)
    for i in range(east // 2):
        for parity in range(2):
            plane = 2 * i + parity
            value = acc_ref[i * rows + low : i * rows + low + size, parity * LANES : (parity + 1) * LANES]
            mask = x_ref[plane + HALO, low : low + size, channels : channels + 1].astype(F32)
            out_ref[plane] = (mask * value)[:, 0:channels].astype(BF16)


def unpack_kernel(channels, scale, upper_ref, mine_ref, other_ref, first_out, second_out):
    spare = LANES - channels
    upper = upper_ref[0] == 1
    for target, here in ((first_out, upper), (second_out, jnp.logical_not(upper))):
        for t in range(0, 27, 4):
            tiles = []
            for r in range(3):
                start = (t // 4 * 3 + r) * channels
                place = slice(start, start + channels)
                tiles.append(jnp.where(here, mine_ref[place, :], other_ref[place, :]).astype(F32) * scale)
            for r in range(3):
                target[t + r] = tiles[r][:, 0:channels]
            if t + 3 < 27:
                lane = lane_of(tiles[0].shape)
                parts = [pltpu.roll(tiles[r], (spare * r - channels) % LANES, 1) for r in range(3)]
                last = jnp.where(lane < spare, parts[0], jnp.where(lane < 2 * spare, parts[1], parts[2]))
                target[t + 3] = last[:, 0:channels]


def per_device(
    features, brick_active, voxel_occupancy, first_weights, second_weights, head, teacher
):
    channels = features.shape[0]
    east, north, upward = features.shape[1:]
    classes = teacher.shape[0]
    devices = lax.axis_size("east") * lax.axis_size("north")
    scale = 1.0 / math.sqrt(devices * east * north * upward)

    flags = jnp.repeat(brick_active, east // brick_active.shape[0], 0)
    flags = jnp.repeat(flags, north // brick_active.shape[1], 1)
    flags = jnp.repeat(flags, upward // brick_active.shape[2], 2)
    mask = (flags * voxel_occupancy).astype(BF16)
    x = jnp.concatenate(
        [
            features.transpose(1, 2, 3, 0),
            mask[..., None],
            teacher.transpose(1, 2, 3, 0),
            jnp.zeros((east, north, upward, LANES - channels - 1 - classes), BF16),
        ],
        -1,
    )
    low, high = halo_of(x, "north", 1, HALO)
    x = jnp.concatenate([low, x, high], 1)
    low, high = halo_of(x, "east", 0, HALO)
    x = jnp.concatenate([low, x, high], 0)

    planes = east + 2 * HALO
    rows = (north + 2 * HALO) * upward
    x = x.reshape(planes, rows, LANES)
    head_wide = jnp.pad(head, ((channels + 1, LANES - channels - 1 - classes), (0, LANES - channels)))

    east_bits, north_bits = bits_of("east"), bits_of("north")
    order = east_bits[:1] + north_bits + east_bits[1:]
    upper = high_bit(*order[0]).reshape(1)
    unit = devices // 2 * 16
    packed = -(-21 * channels // unit) * unit
    vmem = pl.BlockSpec(memory_space=pltpu.VMEM)
    smem = pl.BlockSpec(memory_space=pltpu.SMEM)
    grad, kept, sent = pl.pallas_call(
        functools.partial(whole_kernel, channels, classes, east, north, upward),
        out_shape=(
            jax.ShapeDtypeStruct((east + 2, rows, LANES), BF16),
            jax.ShapeDtypeStruct((packed, LANES), F32),
            jax.ShapeDtypeStruct((packed, LANES), BF16),
        ),
        in_specs=[smem] + [vmem] * 4,
        out_specs=(vmem, vmem, vmem),
        scratch_shapes=[
            pltpu.VMEM((2, planes // 2 * rows, WIDE), BF16),
            pltpu.VMEM((2, (planes - 2) // 2 * rows, WIDE), BF16),
            pltpu.VMEM((2, (planes - 4) // 2 * rows, WIDE), BF16),
            pltpu.VMEM((planes, rows, LANES), F32),
            pltpu.VMEM((planes - 2, rows, LANES), F32),
            pltpu.VMEM(((planes - 2) // 2 * rows, 2 * LANES), F32),
            pltpu.VMEM((4, 2 * LANES, WIDE), BF16),
            pltpu.VMEM((4, WIDE, 2 * LANES), BF16),
            pltpu.VMEM((3 * channels, east * north * upward), BF16),
        ],
        compiler_params=pltpu.CompilerParams(vmem_limit_bytes=56 * 1024 * 1024),
        name="fields",
    )(upper, x, first_weights, second_weights, head_wide)

    grad_features = pl.pallas_call(
        functools.partial(last_kernel, channels, east, north, upward),
        out_shape=jax.ShapeDtypeStruct((east, north * upward, channels), BF16),
        in_specs=[vmem] * 3,
        out_specs=vmem,
        scratch_shapes=[
            pltpu.VMEM((2, (east + 2) // 2 * rows, WIDE), BF16),
            pltpu.VMEM((4, WIDE, 2 * LANES), BF16),
            pltpu.VMEM((east // 2 * rows, 2 * LANES), F32),
        ],
        compiler_params=pltpu.CompilerParams(vmem_limit_bytes=32 * 1024 * 1024),
        name="features",
    )(x, grad, first_weights)

    total = scatter_steps(kept, sent, order)
    mine, other = gather_steps(total.astype(BF16), order)
    grad_first, grad_second = pl.pallas_call(
        functools.partial(unpack_kernel, channels, scale),
        out_shape=(
            jax.ShapeDtypeStruct(first_weights.shape, F32),
            jax.ShapeDtypeStruct(second_weights.shape, F32),
        ),
        in_specs=[smem] + [vmem] * 2,
        out_specs=(vmem, vmem),
        compiler_params=pltpu.CompilerParams(vmem_limit_bytes=32 * 1024 * 1024),
        name="unpack",
    )(upper, mine, other)
    grad_features = grad_features.reshape(east, north, upward, channels).transpose(3, 0, 1, 2)
    return (grad_features, grad_first, grad_second)


def solution(mesh):
    in_specs = (
        P(None, "east", "north", None),
        P("east", "north", None),
        P("east", "north", None),
        P(),
        P(),
        P(),
        P(None, "east", "north", None),
    )
    out_specs = (P(None, "east", "north", None), P(), P())
    return jax.shard_map(
        per_device, mesh=mesh, in_specs=in_specs, out_specs=out_specs, check_vma=False
    )
```

```python
import functools
import math

import jax
import jax.numpy as jnp
from jax import lax
from jax.experimental import pallas as pl
from jax.experimental.pallas import tpu as pltpu
from jax.sharding import PartitionSpec as P

LANES = 128
HALO = 4
OFFSETS = 9
WIDE = OFFSETS * LANES
F32 = jnp.float32
BF16 = jnp.bfloat16


def halo_of(block, axis, dim, width):
    count = lax.axis_size(axis)
    size = block.shape[dim]
    if count == 1:
        empty = jnp.zeros_like(lax.slice_in_dim(block, 0, width, axis=dim))
        return empty, empty
    if count == 2:
        me = lax.axis_index(axis)
        mine = lax.dynamic_slice_in_dim(block, (1 - me) * (size - width), width, axis=dim)
        other = lax.ppermute(mine, axis, [(0, 1), (1, 0)])
        empty = jnp.zeros_like(other)
        return jnp.where(me == 1, other, empty), jnp.where(me == 0, other, empty)
    forward = [(i, i + 1) for i in range(count - 1)]
    backward = [(target, source) for source, target in forward]
    low = lax.ppermute(lax.slice_in_dim(block, size - width, size, axis=dim), axis, forward)
    high = lax.ppermute(lax.slice_in_dim(block, 0, width, axis=dim), axis, backward)
    return low, high


def high_bit(axis, bit):
    return (lax.axis_index(axis) // bit) % 2


def bits_of(axis):
    size = lax.axis_size(axis)
    return [(axis, 1 << i) for i in range(size.bit_length() - 1)]


def swap(value, axis, bit):
    north = lax.axis_size("north")
    pairs = []
    for e in range(1, lax.axis_size("east"), 2):
        for n in range(north):
            partner = (e ^ bit, n) if axis == "east" else (e, n ^ bit)
            pairs.append((e * north + n, partner[0] * north + partner[1]))
    return lax.ppermute(value, ("east", "north"), pairs)


def halves(total, axis, bit):
    upper = high_bit(axis, bit)
    half = total.shape[0] // 2
    sent = lax.dynamic_slice_in_dim(total, (1 - upper) * half, half, 0).astype(BF16)
    return sent, lax.dynamic_slice_in_dim(total, upper * half, half, 0)


def scatter_steps(totals, orders, beside):
    for step in range(len(orders[0])):
        sent, kept = zip(*[halves(total, *order[step]) for total, order in zip(totals, orders)])
        if step == 0:
            kept = beside(*kept)
        others = [swap(value, *order[step]) for value, order in zip(sent, orders)]
        totals = [mine + other.astype(F32) for mine, other in zip(kept, others)]
    return totals


def gather_steps(values, orders):
    for step in range(len(orders[0]) - 1, 0, -1):
        others = [swap(value, *order[step]) for value, order in zip(values, orders)]
        joined = []
        for mine, other, order in zip(values, others, orders):
            upper = high_bit(*order[step]) == 1
            joined.append(jnp.concatenate([jnp.where(upper, other, mine), jnp.where(upper, mine, other)], 0))
        values = joined
    return values, [swap(value, *order[0]) for value, order in zip(values, orders)]


def lane_of(shape):
    return lax.broadcasted_iota(jnp.int32, shape, len(shape) - 1)


def put_stack(value, rows, upward, stack_ref, parity, index):
    cubes = value.reshape(rows // upward, upward, LANES)
    level = lax.broadcasted_iota(jnp.int32, cubes.shape, 1)
    below = jnp.where(level == 0, 0.0, pltpu.roll(cubes, 1, 1)).reshape(rows, LANES)
    above = jnp.where(level == upward - 1, 0.0, pltpu.roll(cubes, upward - 1, 1)).reshape(rows, LANES)
    start = index * rows
    for up, moved in enumerate((below, value, above)):
        shifts = (
            jnp.concatenate([moved[rows - upward :], moved[: rows - upward]], 0),
            moved,
            jnp.concatenate([moved[upward:], moved[:upward]], 0),
        )
        for north, shifted in enumerate(shifts):
            lane = (north * 3 + up) * LANES
            stack_ref[parity, pl.ds(start, rows), lane : lane + LANES] = shifted.astype(BF16)


def convolve(stack_ref, weight_ref, pairs, rows, acc_ref, transposed):
    dims = (((1,), (1,)), ((), ())) if transposed else (((1,), (0,)), ((), ()))
    total = None
    for p in range(4):
        first = (p // 2) * rows
        part = lax.dot_general(
            stack_ref[p % 2, first : first + pairs * rows, :],
            weight_ref[p],
            dims,
            preferred_element_type=F32,
        )
        total = part if total is None else total + part
    acc_ref[0 : pairs * rows, :] = total


def put_forward(weight_ref, w_ref, channels):
    weight_ref[...] = jnp.zeros_like(weight_ref)
    for p in range(4):
        for q in range(2):
            if 0 <= p - q <= 2:
                for j in range(OFFSETS):
                    weight_ref[p, q * LANES : q * LANES + channels, j * LANES : j * LANES + channels] = w_ref[
                        (p - q) * OFFSETS + j
                    ]


def put_backward(weight_ref, w_ref, channels):
    weight_ref[...] = jnp.zeros_like(weight_ref)
    for p in range(4):
        for q in range(2):
            if 0 <= p - q <= 2:
                for j in range(OFFSETS):
                    weight_ref[p, j * LANES : j * LANES + channels, q * LANES : q * LANES + channels] = w_ref[
                        (2 - (p - q)) * OFFSETS + 8 - j
                    ]


def put_turned(turned_ref, value, plane, east, channels):
    turned = value.T[0:channels].astype(BF16)
    size = value.shape[0]
    for d in range(3):
        e = plane + d - 1
        if 0 <= e < east:
            turned_ref[d * channels : (d + 1) * channels, e * size : (e + 1) * size] = turned


def kernel_sum(turned_ref, stack_ref, first, east, rows, low, size, channels):
    total = None
    for i in range(east // 2):
        fields = []
        for e in (2 * i, 2 * i + 1):
            plane = e + first
            start = (plane // 2) * rows + low
            fields.append(stack_ref[plane % 2, start : start + size, :])
        part = jnp.dot(
            turned_ref[:, 2 * i * size : (2 * i + 2) * size],
            jnp.concatenate(fields, 0),
            preferred_element_type=F32,
        )
        total = part if total is None else total + part
    blocks = [
        total[d * channels : (d + 1) * channels, j * LANES : (j + 1) * LANES]
        for d in range(3)
        for j in range(OFFSETS)
    ]
    blocks.append(jnp.zeros_like(blocks[0]))
    lane = lane_of(blocks[0].shape)
    spare = LANES - channels
    tiles = []
    for t in range(0, 28, 4):
        for r in range(3):
            tail = pltpu.roll(blocks[t + 3], channels - spare * r, 1)
            tiles.append(jnp.where(lane < channels, blocks[t + r], tail))
    return tiles


def put_tiles(out_ref, tiles, channels):
    for t, tile in enumerate(tiles):
        out_ref[t * channels : (t + 1) * channels, :] = tile.astype(BF16)
    filled = len(tiles) * channels
    if filled < out_ref.shape[0]:
        out_ref[filled:, :] = jnp.zeros((out_ref.shape[0] - filled, LANES), BF16)


def whole_kernel(
    channels, classes, east, north, upward,
    x_ref, w1_ref, w2_ref, head_ref,
    grad_ref, second_ref, first_ref,
    s0_ref, s1_ref, sg_ref, mask_ref, slope_ref, acc_ref, wt_ref, wb_ref, turned_ref,
):
    rows = (north + 2 * HALO) * upward
    low, size = HALO * upward, north * upward
    planes = east + 2 * HALO
    lane = lane_of((rows, LANES))

    put_forward(wt_ref, w1_ref, channels)

    def start(i, carry):
        for parity in range(2):
            x = x_ref[2 * i + parity].astype(F32)
            mask = jnp.broadcast_to(x[:, channels : channels + 1], (rows, LANES))
            mask_ref[2 * i + parity] = mask
            a0 = jnp.where((mask > 0) & (lane < channels), x, 0.0)
            put_stack(a0, rows, upward, s0_ref, parity, i)
        return carry

    lax.fori_loop(0, planes // 2, start, 0)
    convolve(s0_ref, wt_ref, (planes - 2) // 2, rows, acc_ref, True)
    put_forward(wt_ref, w2_ref, channels)

    def middle(i, carry):
        for parity in range(2):
            plane = 2 * i + parity
            mask = mask_ref[plane + 1]
            p1 = mask * acc_ref[pl.ds(i * rows, rows), parity * LANES : (parity + 1) * LANES]
            sig = jax.nn.sigmoid(p1)
            slope_ref[plane] = mask * (sig * (1.0 + p1 * (1.0 - sig)))
            put_stack(p1 * sig, rows, upward, s1_ref, parity, i)
        return carry

    lax.fori_loop(0, (planes - 2) // 2, middle, 0)
    convolve(s1_ref, wt_ref, (planes - 4) // 2, rows, acc_ref, True)
    put_backward(wb_ref, w2_ref, channels)

    head = head_ref[...]
    class_lane = (lane > channels) & (lane <= channels + classes)

    for i in range((planes - 4) // 2):
        for parity in range(2):
            plane = 2 * i + parity
            mask = mask_ref[plane + 2]
            p2 = mask * acc_ref[i * rows : (i + 1) * rows, parity * LANES : (parity + 1) * LANES]
            sig = jax.nn.sigmoid(p2)
            a2 = (p2 * sig).astype(BF16)
            logits = lax.dot_general(a2, head, (((1,), (1,)), ((), ())), preferred_element_type=F32)
            g_logits = jnp.where(class_lane, mask * (logits - x_ref[plane + 2].astype(F32)), 0.0)
            coarse = g_logits.astype(BF16)
            fine = (g_logits - coarse.astype(F32)).astype(BF16)
            g_a2 = jnp.dot(
                jnp.concatenate([coarse, fine], 1), jnp.concatenate([head, head], 0), preferred_element_type=F32
            )
            g_p2 = mask * g_a2 * (sig * (1.0 + p2 * (1.0 - sig)))
            put_stack(g_p2, rows, upward, sg_ref, parity, i)
            put_turned(turned_ref, g_p2[low : low + size], plane - 2, east, channels)

    put_tiles(second_ref, kernel_sum(turned_ref, s1_ref, 3, east, rows, low, size, channels), channels)
    convolve(sg_ref, wb_ref, (planes - 6) // 2, rows, acc_ref, False)

    for i in range((planes - 6) // 2):
        for parity in range(2):
            plane = 2 * i + parity
            g_p1 = slope_ref[plane + 2] * acc_ref[i * rows : (i + 1) * rows, parity * LANES : (parity + 1) * LANES]
            grad_ref[plane] = g_p1.astype(BF16)
            put_turned(turned_ref, g_p1[low : low + size], plane - 1, east, channels)

    put_tiles(first_ref, kernel_sum(turned_ref, s0_ref, 4, east, rows, low, size, channels), channels)


def last_kernel(
    channels, east, north, upward,
    x_ref, grad_ref, w1_ref, second_in, first_in,
    out_ref, second_out, first_out,
    stack_ref, wb_ref, acc_ref,
):
    rows = (north + 2 * HALO) * upward
    low, size = HALO * upward, north * upward
    put_backward(wb_ref, w1_ref, channels)

    def start(i, carry):
        for parity in range(2):
            put_stack(grad_ref[2 * i + parity].astype(F32), rows, upward, stack_ref, parity, i)
        return carry

    lax.fori_loop(0, east // 2 + 1, start, 0)
    convolve(stack_ref, wb_ref, east // 2, rows, acc_ref, False)
    for i in range(east // 2):
        for parity in range(2):
            plane = 2 * i + parity
            value = acc_ref[i * rows + low : i * rows + low + size, parity * LANES : (parity + 1) * LANES]
            mask = x_ref[plane + HALO, low : low + size, channels : channels + 1].astype(F32)
            out_ref[plane] = (mask * value)[:, 0:channels].astype(BF16)


def unpack_kernel(
    channels, scale, flags_ref, second_mine, first_mine, second_other, first_other, near_ref, far_ref, first_out, second_out
):
    spare = LANES - channels
    half = second_mine.shape[0]
    odd = flags_ref[0] == 1
    streams = (
        (flags_ref[1] == 1, second_mine, second_other, 0, second_out),
        (flags_ref[2] == 1, first_mine, first_other, half, first_out),
    )

    def rows_of(upper, mine_ref, other_ref, base, start, stop):
        here = slice(start % half, start % half + stop - start)
        there = slice(base + start % half, base + start % half + stop - start)
        mine = jnp.where(odd, mine_ref[here, :], near_ref[there, :])
        other = jnp.where(odd, other_ref[here, :], far_ref[there, :])
        return jnp.where(upper, other, mine) if start < half else jnp.where(upper, mine, other)

    for upper, mine_ref, other_ref, base, target in streams:
        for t in range(0, 27, 4):
            tiles = []
            for r in range(3):
                start = (t // 4 * 3 + r) * channels
                edges = sorted({start, start + channels, min(max(half, start), start + channels)})
                pieces = [rows_of(upper, mine_ref, other_ref, base, *pair) for pair in zip(edges, edges[1:])]
                tile = pieces[0] if len(pieces) == 1 else jnp.concatenate(pieces, 0)
                tiles.append(tile.astype(F32) * scale)
            for r in range(3):
                target[t + r] = tiles[r][:, 0:channels]
            if t + 3 < 27:
                lane = lane_of(tiles[0].shape)
                parts = [pltpu.roll(tiles[r], (spare * r - channels) % LANES, 1) for r in range(3)]
                last = jnp.where(lane < spare, parts[0], jnp.where(lane < 2 * spare, parts[1], parts[2]))
                target[t + 3] = last[:, 0:channels]


def per_device(
    features, brick_active, voxel_occupancy, first_weights, second_weights, head, teacher
):
    channels = features.shape[0]
    east, north, upward = features.shape[1:]
    classes = teacher.shape[0]
    devices = lax.axis_size("east") * lax.axis_size("north")
    scale = 1.0 / math.sqrt(devices * east * north * upward)

    flags = jnp.repeat(brick_active, east // brick_active.shape[0], 0)
    flags = jnp.repeat(flags, north // brick_active.shape[1], 1)
    flags = jnp.repeat(flags, upward // brick_active.shape[2], 2)
    mask = (flags * voxel_occupancy).astype(BF16)
    x = jnp.concatenate(
        [
            features.transpose(1, 2, 3, 0),
            mask[..., None],
            teacher.transpose(1, 2, 3, 0),
            jnp.zeros((east, north, upward, LANES - channels - 1 - classes), BF16),
        ],
        -1,
    )
    low, high = halo_of(x, "north", 1, HALO)
    x = jnp.concatenate([low, x, high], 1)
    low, high = halo_of(x, "east", 0, HALO)
    x = jnp.concatenate([low, x, high], 0)

    planes = east + 2 * HALO
    rows = (north + 2 * HALO) * upward
    x = x.reshape(planes, rows, LANES)
    head_wide = jnp.pad(head, ((channels + 1, LANES - channels - 1 - classes), (0, LANES - channels)))

    east_bits, north_bits = bits_of("east"), bits_of("north")
    orders = (north_bits + east_bits[1:], east_bits[1:2] + north_bits + east_bits[2:])
    unit = devices // 2 * 16
    packed = -(-21 * channels // unit) * unit
    vmem = pl.BlockSpec(memory_space=pltpu.VMEM)
    smem = pl.BlockSpec(memory_space=pltpu.SMEM)
    grad, second, first = pl.pallas_call(
        functools.partial(whole_kernel, channels, classes, east, north, upward),
        out_shape=(
            jax.ShapeDtypeStruct((east + 2, rows, LANES), BF16),
            jax.ShapeDtypeStruct((packed, LANES), BF16),
            jax.ShapeDtypeStruct((packed, LANES), BF16),
        ),
        in_specs=[vmem] * 4,
        out_specs=(vmem, vmem, vmem),
        scratch_shapes=[
            pltpu.VMEM((2, planes // 2 * rows, WIDE), BF16),
            pltpu.VMEM((2, (planes - 2) // 2 * rows, WIDE), BF16),
            pltpu.VMEM((2, (planes - 4) // 2 * rows, WIDE), BF16),
            pltpu.VMEM((planes, rows, LANES), F32),
            pltpu.VMEM((planes - 2, rows, LANES), F32),
            pltpu.VMEM(((planes - 2) // 2 * rows, 2 * LANES), F32),
            pltpu.VMEM((4, 2 * LANES, WIDE), BF16),
            pltpu.VMEM((4, WIDE, 2 * LANES), BF16),
            pltpu.VMEM((3 * channels, east * north * upward), BF16),
        ],
        compiler_params=pltpu.CompilerParams(vmem_limit_bytes=56 * 1024 * 1024),
        name="fields",
    )(x, first_weights, second_weights, head_wide)

    anywhere = pl.BlockSpec(memory_space=pl.ANY)
    features_out = []

    def beside(second_kept, first_kept):
        out, second_kept, first_kept = pl.pallas_call(
            functools.partial(last_kernel, channels, east, north, upward),
            out_shape=(
                jax.ShapeDtypeStruct((east, north * upward, channels), BF16),
                jax.ShapeDtypeStruct(second_kept.shape, F32),
                jax.ShapeDtypeStruct(first_kept.shape, F32),
            ),
            in_specs=[vmem] * 3 + [anywhere] * 2,
            out_specs=(vmem, anywhere, anywhere),
            input_output_aliases={3: 1, 4: 2},
            scratch_shapes=[
                pltpu.VMEM((2, (east + 2) // 2 * rows, WIDE), BF16),
                pltpu.VMEM((4, WIDE, 2 * LANES), BF16),
                pltpu.VMEM((east // 2 * rows, 2 * LANES), F32),
            ],
            compiler_params=pltpu.CompilerParams(vmem_limit_bytes=32 * 1024 * 1024),
            name="features",
        )(x, grad, first_weights, second_kept, first_kept)
        features_out.append(out)
        return second_kept, first_kept

    to_odd = [(e, e + 1) for e in range(0, lax.axis_size("east"), 2)]
    to_even = [(e + 1, e) for e in range(0, lax.axis_size("east"), 2)]
    sums = [value.astype(F32) + lax.ppermute(value, "east", to_odd).astype(F32) for value in (second, first)]
    sums = scatter_steps(sums, orders, beside)
    mine, other = gather_steps([total.astype(BF16) for total in sums], orders)
    near = lax.ppermute(jnp.concatenate(mine, 0), "east", to_even)
    far = lax.ppermute(jnp.concatenate(other, 0), "east", to_even)
    flags = jnp.stack([high_bit("east", 1)] + [high_bit(*order[0]) for order in orders])
    grad_first, grad_second = pl.pallas_call(
        functools.partial(unpack_kernel, channels, scale),
        out_shape=(
            jax.ShapeDtypeStruct(first_weights.shape, F32),
            jax.ShapeDtypeStruct(second_weights.shape, F32),
        ),
        in_specs=[smem] + [vmem] * 6,
        out_specs=(vmem, vmem),
        compiler_params=pltpu.CompilerParams(vmem_limit_bytes=32 * 1024 * 1024),
        name="unpack",
    )(flags, *mine, *other, near, far)
    (grad_features,) = features_out
    grad_features = grad_features.reshape(east, north, upward, channels).transpose(3, 0, 1, 2)
    return (grad_features, grad_first, grad_second)


def solution(mesh):
    in_specs = (
        P(None, "east", "north", None),
        P("east", "north", None),
        P("east", "north", None),
        P(),
        P(),
        P(),
        P(None, "east", "north", None),
    )
    out_specs = (P(None, "east", "north", None), P(), P())
    return jax.shard_map(
        per_device, mesh=mesh, in_specs=in_specs, out_specs=out_specs, check_vma=False
    )
```

```python
import functools
import math

import jax
import jax.numpy as jnp
from jax import lax
from jax.experimental import pallas as pl
from jax.experimental.pallas import tpu as pltpu
from jax.sharding import PartitionSpec as P

LANES = 128
HALO = 4
OFFSETS = 9
WIDE = OFFSETS * LANES
F32 = jnp.float32
BF16 = jnp.bfloat16


def neighbours(count, first):
    pairs = [(i, i) for i in range(first)]
    for i in range(first, count, 2):
        pairs += [(i, i + 1), (i + 1, i)] if i + 1 < count else [(i, i)]
    return pairs


def halo_of(block, axis, dim, width):
    count = lax.axis_size(axis)
    size = block.shape[dim]
    me = lax.axis_index(axis)
    odd = me % 2
    start = (1 - odd) * (size - width)
    other = lax.ppermute(lax.dynamic_slice_in_dim(block, start, width, axis=dim), axis, neighbours(count, 0))
    empty = jnp.zeros_like(other)
    if count == 2:
        return jnp.where(odd == 1, other, empty), jnp.where(odd == 0, other, empty)
    start = odd * (size - width)
    next_other = lax.ppermute(lax.dynamic_slice_in_dim(block, start, width, axis=dim), axis, neighbours(count, 1))
    low = jnp.where(me == 0, empty, jnp.where(odd == 1, other, next_other))
    high = jnp.where(me == count - 1, empty, jnp.where(odd == 1, next_other, other))
    return low, high


def high_bit(axis, bit):
    return (lax.axis_index(axis) // bit) % 2


def bits_of(axis):
    size = lax.axis_size(axis)
    return [(axis, 1 << i) for i in range(size.bit_length() - 1)]


def swap(value, axis, bit):
    north = lax.axis_size("north")
    pairs = []
    for e in range(lax.axis_size("east")):
        for n in range(north):
            partner = (e ^ bit, n) if axis == "east" else (e, n ^ bit)
            if e % 2 == 0:
                partner = (e, n)
            pairs.append((e * north + n, partner[0] * north + partner[1]))
    return lax.ppermute(value, ("east", "north"), pairs)


def halves(total, axis, bit):
    upper = high_bit(axis, bit)
    half = total.shape[0] // 2
    sent = lax.dynamic_slice_in_dim(total, (1 - upper) * half, half, 0).astype(BF16)
    return sent, lax.dynamic_slice_in_dim(total, upper * half, half, 0)


def scatter_steps(totals, orders, beside):
    for step in range(len(orders[0])):
        sent, kept = zip(*[halves(total, *order[step]) for total, order in zip(totals, orders)])
        if step == 0:
            kept = beside(*kept)
        others = [swap(value, *order[step]) for value, order in zip(sent, orders)]
        totals = [mine + other.astype(F32) for mine, other in zip(kept, others)]
    return totals


def gather_steps(values, orders):
    for step in range(len(orders[0]) - 1, 0, -1):
        others = [swap(value, *order[step]) for value, order in zip(values, orders)]
        joined = []
        for mine, other, order in zip(values, others, orders):
            upper = high_bit(*order[step]) == 1
            joined.append(jnp.concatenate([jnp.where(upper, other, mine), jnp.where(upper, mine, other)], 0))
        values = joined
    return values, [swap(value, *order[0]) for value, order in zip(values, orders)]


def lane_of(shape):
    return lax.broadcasted_iota(jnp.int32, shape, len(shape) - 1)


def put_stack(value, rows, upward, stack_ref, parity, index):
    cubes = value.reshape(rows // upward, upward, LANES)
    level = lax.broadcasted_iota(jnp.int32, cubes.shape, 1)
    below = jnp.where(level == 0, 0.0, pltpu.roll(cubes, 1, 1)).reshape(rows, LANES)
    above = jnp.where(level == upward - 1, 0.0, pltpu.roll(cubes, upward - 1, 1)).reshape(rows, LANES)
    start = index * rows
    for up, moved in enumerate((below, value, above)):
        shifts = (
            jnp.concatenate([moved[rows - upward :], moved[: rows - upward]], 0),
            moved,
            jnp.concatenate([moved[upward:], moved[:upward]], 0),
        )
        for north, shifted in enumerate(shifts):
            lane = (north * 3 + up) * LANES
            stack_ref[parity, pl.ds(start, rows), lane : lane + LANES] = shifted.astype(BF16)


def convolve(stack_ref, weight_ref, pairs, rows, acc_ref, transposed):
    dims = (((1,), (1,)), ((), ())) if transposed else (((1,), (0,)), ((), ()))
    total = None
    for p in range(4):
        first = (p // 2) * rows
        part = lax.dot_general(
            stack_ref[p % 2, first : first + pairs * rows, :],
            weight_ref[p],
            dims,
            preferred_element_type=F32,
        )
        total = part if total is None else total + part
    acc_ref[0 : pairs * rows, :] = total


def put_forward(weight_ref, w_ref, channels):
    weight_ref[...] = jnp.zeros_like(weight_ref)
    for p in range(4):
        for q in range(2):
            if 0 <= p - q <= 2:
                for j in range(OFFSETS):
                    weight_ref[p, q * LANES : q * LANES + channels, j * LANES : j * LANES + channels] = w_ref[
                        (p - q) * OFFSETS + j
                    ]


def put_backward(weight_ref, w_ref, channels):
    weight_ref[...] = jnp.zeros_like(weight_ref)
    for p in range(4):
        for q in range(2):
            if 0 <= p - q <= 2:
                for j in range(OFFSETS):
                    weight_ref[p, j * LANES : j * LANES + channels, q * LANES : q * LANES + channels] = w_ref[
                        (2 - (p - q)) * OFFSETS + 8 - j
                    ]


def put_turned(turned_ref, value, plane, east, channels):
    turned = value.T[0:channels].astype(BF16)
    size = value.shape[0]
    for d in range(3):
        e = plane + d - 1
        if 0 <= e < east:
            turned_ref[d * channels : (d + 1) * channels, e * size : (e + 1) * size] = turned


def kernel_sum(turned_ref, stack_ref, first, east, rows, low, size, channels):
    total = None
    for i in range(east // 2):
        fields = []
        for e in (2 * i, 2 * i + 1):
            plane = e + first
            start = (plane // 2) * rows + low
            fields.append(stack_ref[plane % 2, start : start + size, :])
        part = jnp.dot(
            turned_ref[:, 2 * i * size : (2 * i + 2) * size],
            jnp.concatenate(fields, 0),
            preferred_element_type=F32,
        )
        total = part if total is None else total + part
    blocks = [
        total[d * channels : (d + 1) * channels, j * LANES : (j + 1) * LANES]
        for d in range(3)
        for j in range(OFFSETS)
    ]
    blocks.append(jnp.zeros_like(blocks[0]))
    lane = lane_of(blocks[0].shape)
    spare = LANES - channels
    tiles = []
    for t in range(0, 28, 4):
        for r in range(3):
            tail = pltpu.roll(blocks[t + 3], channels - spare * r, 1)
            tiles.append(jnp.where(lane < channels, blocks[t + r], tail))
    return tiles


def put_tiles(out_ref, tiles, channels):
    for t, tile in enumerate(tiles):
        out_ref[t * channels : (t + 1) * channels, :] = tile.astype(BF16)
    filled = len(tiles) * channels
    if filled < out_ref.shape[0]:
        out_ref[filled:, :] = jnp.zeros((out_ref.shape[0] - filled, LANES), BF16)


def whole_kernel(
    channels, classes, east, north, upward,
    x_ref, w1_ref, w2_ref, head_ref,
    grad_ref, second_ref, first_ref,
    s0_ref, s1_ref, sg_ref, mask_ref, slope_ref, acc_ref, wt_ref, wb_ref, turned_ref,
):
    rows = (north + 2 * HALO) * upward
    low, size = HALO * upward, north * upward
    planes = east + 2 * HALO
    lane = lane_of((rows, LANES))

    put_forward(wt_ref, w1_ref, channels)

    def start(i, carry):
        for parity in range(2):
            x = x_ref[2 * i + parity].astype(F32)
            mask = jnp.broadcast_to(x[:, channels : channels + 1], (rows, LANES))
            mask_ref[2 * i + parity] = mask
            a0 = jnp.where((mask > 0) & (lane < channels), x, 0.0)
            put_stack(a0, rows, upward, s0_ref, parity, i)
        return carry

    lax.fori_loop(0, planes // 2, start, 0)
    convolve(s0_ref, wt_ref, (planes - 2) // 2, rows, acc_ref, True)
    put_forward(wt_ref, w2_ref, channels)

    def middle(i, carry):
        for parity in range(2):
            plane = 2 * i + parity
            mask = mask_ref[plane + 1]
            p1 = mask * acc_ref[pl.ds(i * rows, rows), parity * LANES : (parity + 1) * LANES]
            sig = jax.nn.sigmoid(p1)
            slope_ref[plane] = mask * (sig * (1.0 + p1 * (1.0 - sig)))
            put_stack(p1 * sig, rows, upward, s1_ref, parity, i)
        return carry

    lax.fori_loop(0, (planes - 2) // 2, middle, 0)
    convolve(s1_ref, wt_ref, (planes - 4) // 2, rows, acc_ref, True)
    put_backward(wb_ref, w2_ref, channels)

    head = head_ref[...]
    class_lane = (lane > channels) & (lane <= channels + classes)

    for i in range((planes - 4) // 2):
        for parity in range(2):
            plane = 2 * i + parity
            mask = mask_ref[plane + 2]
            p2 = mask * acc_ref[i * rows : (i + 1) * rows, parity * LANES : (parity + 1) * LANES]
            sig = jax.nn.sigmoid(p2)
            a2 = (p2 * sig).astype(BF16)
            logits = lax.dot_general(a2, head, (((1,), (1,)), ((), ())), preferred_element_type=F32)
            g_logits = jnp.where(class_lane, mask * (logits - x_ref[plane + 2].astype(F32)), 0.0)
            coarse = g_logits.astype(BF16)
            fine = (g_logits - coarse.astype(F32)).astype(BF16)
            g_a2 = jnp.dot(
                jnp.concatenate([coarse, fine], 1), jnp.concatenate([head, head], 0), preferred_element_type=F32
            )
            g_p2 = mask * g_a2 * (sig * (1.0 + p2 * (1.0 - sig)))
            put_stack(g_p2, rows, upward, sg_ref, parity, i)
            put_turned(turned_ref, g_p2[low : low + size], plane - 2, east, channels)

    put_tiles(second_ref, kernel_sum(turned_ref, s1_ref, 3, east, rows, low, size, channels), channels)
    convolve(sg_ref, wb_ref, (planes - 6) // 2, rows, acc_ref, False)

    for i in range((planes - 6) // 2):
        for parity in range(2):
            plane = 2 * i + parity
            g_p1 = slope_ref[plane + 2] * acc_ref[i * rows : (i + 1) * rows, parity * LANES : (parity + 1) * LANES]
            grad_ref[plane] = g_p1.astype(BF16)
            put_turned(turned_ref, g_p1[low : low + size], plane - 1, east, channels)

    put_tiles(first_ref, kernel_sum(turned_ref, s0_ref, 4, east, rows, low, size, channels), channels)


def last_kernel(
    channels, east, north, upward,
    x_ref, grad_ref, w1_ref, second_in, first_in,
    out_ref, second_out, first_out,
    stack_ref, wb_ref, acc_ref,
):
    rows = (north + 2 * HALO) * upward
    low, size = HALO * upward, north * upward
    put_backward(wb_ref, w1_ref, channels)

    def start(i, carry):
        for parity in range(2):
            put_stack(grad_ref[2 * i + parity].astype(F32), rows, upward, stack_ref, parity, i)
        return carry

    lax.fori_loop(0, east // 2 + 1, start, 0)
    convolve(stack_ref, wb_ref, east // 2, rows, acc_ref, False)
    for i in range(east // 2):
        for parity in range(2):
            plane = 2 * i + parity
            value = acc_ref[i * rows + low : i * rows + low + size, parity * LANES : (parity + 1) * LANES]
            mask = x_ref[plane + HALO, low : low + size, channels : channels + 1].astype(F32)
            out_ref[plane] = (mask * value)[:, 0:channels].astype(BF16)


def unpack_kernel(
    channels, scale, flags_ref, second_mine, first_mine, second_other, first_other, near_ref, far_ref, first_out, second_out
):
    spare = LANES - channels
    half = second_mine.shape[0]
    odd = flags_ref[0] == 1
    streams = (
        (flags_ref[1] == 1, second_mine, second_other, 0, second_out),
        (flags_ref[2] == 1, first_mine, first_other, half, first_out),
    )

    def rows_of(upper, mine_ref, other_ref, base, start, stop):
        here = slice(start % half, start % half + stop - start)
        there = slice(base + start % half, base + start % half + stop - start)
        mine = jnp.where(odd, mine_ref[here, :], near_ref[there, :])
        other = jnp.where(odd, other_ref[here, :], far_ref[there, :])
        return jnp.where(upper, other, mine) if start < half else jnp.where(upper, mine, other)

    for upper, mine_ref, other_ref, base, target in streams:
        for t in range(0, 27, 4):
            tiles = []
            for r in range(3):
                start = (t // 4 * 3 + r) * channels
                edges = sorted({start, start + channels, min(max(half, start), start + channels)})
                pieces = [rows_of(upper, mine_ref, other_ref, base, *pair) for pair in zip(edges, edges[1:])]
                tile = pieces[0] if len(pieces) == 1 else jnp.concatenate(pieces, 0)
                tiles.append(tile.astype(F32) * scale)
            for r in range(3):
                target[t + r] = tiles[r][:, 0:channels]
            if t + 3 < 27:
                lane = lane_of(tiles[0].shape)
                parts = [pltpu.roll(tiles[r], (spare * r - channels) % LANES, 1) for r in range(3)]
                last = jnp.where(lane < spare, parts[0], jnp.where(lane < 2 * spare, parts[1], parts[2]))
                target[t + 3] = last[:, 0:channels]


def per_device(
    features, brick_active, voxel_occupancy, first_weights, second_weights, head, teacher
):
    channels = features.shape[0]
    east, north, upward = features.shape[1:]
    classes = teacher.shape[0]
    devices = lax.axis_size("east") * lax.axis_size("north")
    scale = 1.0 / math.sqrt(devices * east * north * upward)

    flags = jnp.repeat(brick_active, east // brick_active.shape[0], 0)
    flags = jnp.repeat(flags, north // brick_active.shape[1], 1)
    flags = jnp.repeat(flags, upward // brick_active.shape[2], 2)
    mask = (flags * voxel_occupancy).astype(BF16)
    x = jnp.concatenate(
        [
            features.transpose(1, 2, 3, 0),
            mask[..., None],
            teacher.transpose(1, 2, 3, 0),
            jnp.zeros((east, north, upward, LANES - channels - 1 - classes), BF16),
        ],
        -1,
    )
    low, high = halo_of(x, "north", 1, HALO)
    x = jnp.concatenate([low, x, high], 1)
    low, high = halo_of(x, "east", 0, HALO)
    x = jnp.concatenate([low, x, high], 0)

    planes = east + 2 * HALO
    rows = (north + 2 * HALO) * upward
    x = x.reshape(planes, rows, LANES)
    head_wide = jnp.pad(head, ((channels + 1, LANES - channels - 1 - classes), (0, LANES - channels)))

    east_bits, north_bits = bits_of("east"), bits_of("north")
    orders = (north_bits + east_bits[1:], east_bits[1:2] + north_bits + east_bits[2:])
    unit = devices // 2 * 16
    packed = -(-21 * channels // unit) * unit
    vmem = pl.BlockSpec(memory_space=pltpu.VMEM)
    smem = pl.BlockSpec(memory_space=pltpu.SMEM)
    grad, second, first = pl.pallas_call(
        functools.partial(whole_kernel, channels, classes, east, north, upward),
        out_shape=(
            jax.ShapeDtypeStruct((east + 2, rows, LANES), BF16),
            jax.ShapeDtypeStruct((packed, LANES), BF16),
            jax.ShapeDtypeStruct((packed, LANES), BF16),
        ),
        in_specs=[vmem] * 4,
        out_specs=(vmem, vmem, vmem),
        scratch_shapes=[
            pltpu.VMEM((2, planes // 2 * rows, WIDE), BF16),
            pltpu.VMEM((2, (planes - 2) // 2 * rows, WIDE), BF16),
            pltpu.VMEM((2, (planes - 4) // 2 * rows, WIDE), BF16),
            pltpu.VMEM((planes, rows, LANES), F32),
            pltpu.VMEM((planes - 2, rows, LANES), F32),
            pltpu.VMEM(((planes - 2) // 2 * rows, 2 * LANES), F32),
            pltpu.VMEM((4, 2 * LANES, WIDE), BF16),
            pltpu.VMEM((4, WIDE, 2 * LANES), BF16),
            pltpu.VMEM((3 * channels, east * north * upward), BF16),
        ],
        compiler_params=pltpu.CompilerParams(vmem_limit_bytes=56 * 1024 * 1024),
        name="fields",
    )(x, first_weights, second_weights, head_wide)

    anywhere = pl.BlockSpec(memory_space=pl.ANY)
    features_out = []

    def beside(second_kept, first_kept):
        out, second_kept, first_kept = pl.pallas_call(
            functools.partial(last_kernel, channels, east, north, upward),
            out_shape=(
                jax.ShapeDtypeStruct((east, north * upward, channels), BF16),
                jax.ShapeDtypeStruct(second_kept.shape, F32),
                jax.ShapeDtypeStruct(first_kept.shape, F32),
            ),
            in_specs=[vmem] * 3 + [anywhere] * 2,
            out_specs=(vmem, anywhere, anywhere),
            input_output_aliases={3: 1, 4: 2},
            scratch_shapes=[
                pltpu.VMEM((2, (east + 2) // 2 * rows, WIDE), BF16),
                pltpu.VMEM((4, WIDE, 2 * LANES), BF16),
                pltpu.VMEM((east // 2 * rows, 2 * LANES), F32),
            ],
            compiler_params=pltpu.CompilerParams(vmem_limit_bytes=32 * 1024 * 1024),
            name="features",
        )(x, grad, first_weights, second_kept, first_kept)
        features_out.append(out)
        return second_kept, first_kept

    cores = neighbours(lax.axis_size("east"), 0)
    sums = [value.astype(F32) + lax.ppermute(value, "east", cores).astype(F32) for value in (second, first)]
    sums = scatter_steps(sums, orders, beside)
    mine, other = gather_steps([total.astype(BF16) for total in sums], orders)
    near = lax.ppermute(jnp.concatenate(mine, 0), "east", cores)
    far = lax.ppermute(jnp.concatenate(other, 0), "east", cores)
    flags = jnp.stack([high_bit("east", 1)] + [high_bit(*order[0]) for order in orders])
    grad_first, grad_second = pl.pallas_call(
        functools.partial(unpack_kernel, channels, scale),
        out_shape=(
            jax.ShapeDtypeStruct(first_weights.shape, F32),
            jax.ShapeDtypeStruct(second_weights.shape, F32),
        ),
        in_specs=[smem] + [vmem] * 6,
        out_specs=(vmem, vmem),
        compiler_params=pltpu.CompilerParams(vmem_limit_bytes=32 * 1024 * 1024),
        name="unpack",
    )(flags, *mine, *other, near, far)
    (grad_features,) = features_out
    grad_features = grad_features.reshape(east, north, upward, channels).transpose(3, 0, 1, 2)
    return (grad_features, grad_first, grad_second)


def solution(mesh):
    in_specs = (
        P(None, "east", "north", None),
        P("east", "north", None),
        P("east", "north", None),
        P(),
        P(),
        P(),
        P(None, "east", "north", None),
    )
    out_specs = (P(None, "east", "north", None), P(), P())
    return jax.shard_map(
        per_device, mesh=mesh, in_specs=in_specs, out_specs=out_specs, check_vma=False
    )
```

```python
import functools
import math

import jax
import jax.numpy as jnp
from jax import lax
from jax.experimental import pallas as pl
from jax.experimental.pallas import tpu as pltpu
from jax.sharding import PartitionSpec as P

LANES = 128
HALO = 4
OFFSETS = 9
WIDE = OFFSETS * LANES
F32 = jnp.float32
BF16 = jnp.bfloat16


def rounds_of(axis):
    count = lax.axis_size(axis)
    me = lax.axis_index(axis)
    rounds = [(neighbours(count, 0), me % 2, jnp.int32(1))]
    if count > 2:
        inside = ((me > 0) & (me < count - 1)).astype(jnp.int32)
        rounds.append((neighbours(count, 1), (me + 1) % 2, inside))
    return rounds


def neighbours(count, first):
    pairs = []
    for i in range(first, count, 2):
        pairs += [(i, (i + 1) % count), ((i + 1) % count, i)]
    return pairs


def jointly(east_pairs, north_pairs):
    north = lax.axis_size("north")
    return [(e * north + n, f * north + m) for e, f in east_pairs for n, m in north_pairs]


def high_bit(axis, bit):
    return (lax.axis_index(axis) // bit) % 2


def bits_of(axis):
    size = lax.axis_size(axis)
    return [(axis, 1 << i) for i in range(size.bit_length() - 1)]


def place_in(group):
    return sum(high_bit(axis, bit) << i for i, (axis, bit) in enumerate(group))


def swap(value, group, change):
    masks = {"east": 0, "north": 0}
    for i, (axis, bit) in enumerate(group):
        if change >> i & 1:
            masks[axis] |= bit
    pairs = [[(i, i ^ masks[axis]) for i in range(lax.axis_size(axis))] for axis in ("east", "north")]
    return lax.ppermute(value, ("east", "north"), jointly(*pairs))


def scatter_sums(total, groups, beside):
    for number, group in enumerate(groups):
        ways = 1 << len(group)
        part = total.shape[0] // ways
        place = place_in(group)
        sent = [
            lax.dynamic_slice_in_dim(total, (place ^ change) * part, part, 0).astype(BF16)
            for change in range(1, ways)
        ]
        kept = lax.dynamic_slice_in_dim(total, place * part, part, 0)
        if number == 0:
            kept = beside(kept)
        for change in range(1, ways):
            kept = kept + swap(sent[change - 1], group, change).astype(F32)
        total = kept
    return total


def gather_parts(mine, groups):
    for group in reversed(groups):
        ways = 1 << len(group)
        place = place_in(group)
        parts = [mine] + [swap(mine, group, change) for change in range(1, ways)]
        joined = []
        for row in range(ways):
            piece = parts[0]
            for change in range(1, ways):
                piece = jnp.where((place ^ row) == change, parts[change], piece)
            joined.append(piece)
        mine = jnp.concatenate(joined, 0)
    return mine


def lane_of(shape):
    return lax.broadcasted_iota(jnp.int32, shape, len(shape) - 1)


def put_stack(value, rows, upward, stack_ref, parity, index):
    cubes = value.reshape(rows // upward, upward, LANES)
    level = lax.broadcasted_iota(jnp.int32, cubes.shape, 1)
    below = jnp.where(level == 0, 0.0, pltpu.roll(cubes, 1, 1)).reshape(rows, LANES)
    above = jnp.where(level == upward - 1, 0.0, pltpu.roll(cubes, upward - 1, 1)).reshape(rows, LANES)
    start = index * rows
    for up, moved in enumerate((below, value, above)):
        shifts = (
            jnp.concatenate([moved[rows - upward :], moved[: rows - upward]], 0),
            moved,
            jnp.concatenate([moved[upward:], moved[:upward]], 0),
        )
        for north, shifted in enumerate(shifts):
            lane = (north * 3 + up) * LANES
            stack_ref[parity, pl.ds(start, rows), lane : lane + LANES] = shifted.astype(BF16)


def convolve(stack_ref, weight_ref, pairs, rows, acc_ref, transposed):
    dims = (((1,), (1,)), ((), ())) if transposed else (((1,), (0,)), ((), ()))
    total = None
    for p in range(4):
        first = (p // 2) * rows
        part = lax.dot_general(
            stack_ref[p % 2, first : first + pairs * rows, :],
            weight_ref[p],
            dims,
            preferred_element_type=F32,
        )
        total = part if total is None else total + part
    acc_ref[0 : pairs * rows, :] = total


def put_forward(weight_ref, w_ref, channels):
    weight_ref[...] = jnp.zeros_like(weight_ref)
    for p in range(4):
        for q in range(2):
            if 0 <= p - q <= 2:
                for j in range(OFFSETS):
                    weight_ref[p, q * LANES : q * LANES + channels, j * LANES : j * LANES + channels] = w_ref[
                        (p - q) * OFFSETS + j
                    ]


def put_backward(weight_ref, w_ref, channels):
    weight_ref[...] = jnp.zeros_like(weight_ref)
    for p in range(4):
        for q in range(2):
            if 0 <= p - q <= 2:
                for j in range(OFFSETS):
                    weight_ref[p, j * LANES : j * LANES + channels, q * LANES : q * LANES + channels] = w_ref[
                        (2 - (p - q)) * OFFSETS + 8 - j
                    ]


def put_turned(turned_ref, value, plane, east, channels):
    turned = value.T[0:channels].astype(BF16)
    size = value.shape[0]
    for d in range(3):
        e = plane + d - 1
        if 0 <= e < east:
            turned_ref[d * channels : (d + 1) * channels, e * size : (e + 1) * size] = turned


def kernel_sum(turned_ref, stack_ref, first, east, rows, low, size, channels):
    total = None
    for i in range(east // 2):
        fields = []
        for e in (2 * i, 2 * i + 1):
            plane = e + first
            start = (plane // 2) * rows + low
            fields.append(stack_ref[plane % 2, start : start + size, :])
        part = jnp.dot(
            turned_ref[:, 2 * i * size : (2 * i + 2) * size],
            jnp.concatenate(fields, 0),
            preferred_element_type=F32,
        )
        total = part if total is None else total + part
    blocks = [
        total[d * channels : (d + 1) * channels, j * LANES : (j + 1) * LANES]
        for d in range(3)
        for j in range(OFFSETS)
    ]
    blocks.append(jnp.zeros_like(blocks[0]))
    lane = lane_of(blocks[0].shape)
    spare = LANES - channels
    tiles = []
    for t in range(0, 28, 4):
        for r in range(3):
            tail = pltpu.roll(blocks[t + 3], channels - spare * r, 1)
            tiles.append(jnp.where(lane < channels, blocks[t + r], tail))
    return tiles


def prepare_kernel(
    channels, upward, edge, east_rounds, north_rounds,
    flags_ref, active_ref, features_ref, occupied_ref, teacher_ref,
    center_ref, *edge_refs,
):
    east, size, _ = center_ref.shape
    north = size // upward
    classes = teacher_ref.shape[0]
    wide = (classes + 1) * upward
    row = lax.broadcasted_iota(jnp.int32, (size, north), 0) // upward
    spread = (row == lax.broadcasted_iota(jnp.int32, (size, north), 1)).astype(BF16)
    level = lax.broadcasted_iota(jnp.int32, (size, wide), 0) % upward
    same = level == lax.broadcasted_iota(jnp.int32, (size, wide), 1) % upward
    target = lax.broadcasted_iota(jnp.int32, (wide, LANES), 0) // upward + channels
    gather = (target == lax.broadcasted_iota(jnp.int32, (wide, LANES), 1)).astype(BF16)
    bricks = active_ref.shape
    up = lax.broadcasted_iota(jnp.int32, (upward, north), 0) // (upward // bricks[2])
    along = lax.broadcasted_iota(jnp.int32, (upward, north), 1) // (north // bricks[1])
    for e in range(east):
        mask = jnp.zeros((upward, north), jnp.int32)
        for b in range(bricks[1]):
            for c in range(bricks[2]):
                inside = (along == b) & (up == c)
                mask = jnp.where(inside, active_ref[e // (east // bricks[0]), b, c], mask)
        mask = (mask * occupied_ref[e]).astype(F32)
        field = jnp.concatenate([mask] + [teacher_ref[c, e].astype(F32) for c in range(classes)], 0).astype(BF16)
        everywhere = lax.dot_general(spread, field, (((1,), (1,)), ((), ())), preferred_element_type=F32)
        own = jnp.where(same, everywhere, 0.0).astype(BF16)
        tail = jnp.dot(own, gather, preferred_element_type=F32).astype(BF16)
        center_ref[e, :, 0:channels] = features_ref[e]
        center_ref[e, :, channels:LANES] = tail[:, channels:LANES]
    east_starts = [(1 - flags_ref[r]) * (east - HALO) for r in range(east_rounds)]
    north_starts = [
        pl.multiple_of((1 - flags_ref[2 * east_rounds + r]) * (size - edge), edge) for r in range(north_rounds)
    ]
    edge_refs = iter(edge_refs)
    for e in east_starts:
        next(edge_refs)[...] = center_ref[pl.ds(e, HALO)]
    for n in north_starts:
        next(edge_refs)[...] = center_ref[:, pl.ds(n, edge), :]
    for e in east_starts:
        for n in north_starts:
            next(edge_refs)[...] = center_ref[pl.ds(e, HALO), pl.ds(n, edge), :]


def place_edges(flags_ref, center_ref, edge_refs, east_rounds, north_rounds, edge, x_ref):
    east, size, _ = center_ref.shape
    x_ref[...] = jnp.zeros_like(x_ref)
    x_ref[HALO : HALO + east, edge : edge + size, :] = center_ref[...]
    edge_refs = iter(edge_refs)
    easts = [(flags_ref[r], flags_ref[east_rounds + r]) for r in range(east_rounds)]
    base = 2 * east_rounds
    norths = [(flags_ref[base + r], flags_ref[base + north_rounds + r]) for r in range(north_rounds)]
    middle_east, middle_north = pl.ds(HALO, east), pl.ds(edge, size)
    east_places = [(pl.ds((1 - side) * (east + HALO), HALO), inside) for side, inside in easts]
    north_places = [
        (pl.ds(pl.multiple_of((1 - side) * (size + edge), edge), edge), inside) for side, inside in norths
    ]
    spots = [(e, middle_north, inside) for e, inside in east_places]
    spots += [(middle_east, n, inside) for n, inside in north_places]
    spots += [(e, n, a * b) for e, a in east_places for n, b in north_places]
    for e, n, inside in spots:
        ref = next(edge_refs)

        @pl.when(inside == 1)
        def _(ref=ref, e=e, n=n):
            x_ref[e, n, :] = ref[...]


def whole_kernel(channels, classes, east, north, upward, east_rounds, north_rounds, flags_ref, w1_ref, w2_ref, head_ref, center_ref, *refs):
    edges = east_rounds + north_rounds + east_rounds * north_rounds
    (
        grad_ref, kept_ref, sent_ref,
        x_ref, s0_ref, s1_ref, sg_ref, mask_ref, slope_ref, acc_ref, wt_ref, wb_ref, turned_ref,
    ) = refs[edges:]
    rows = (north + 2 * HALO) * upward
    low, size = HALO * upward, north * upward
    planes = east + 2 * HALO
    lane = lane_of((rows, LANES))

    place_edges(flags_ref, center_ref, refs[:edges], east_rounds, north_rounds, low, x_ref)
    put_forward(wt_ref, w1_ref, channels)

    def start(i, carry):
        for parity in range(2):
            x = x_ref[2 * i + parity].astype(F32)
            mask = jnp.broadcast_to(x[:, channels : channels + 1], (rows, LANES))
            mask_ref[2 * i + parity] = mask
            a0 = jnp.where((mask > 0) & (lane < channels), x, 0.0)
            put_stack(a0, rows, upward, s0_ref, parity, i)
        return carry

    lax.fori_loop(0, planes // 2, start, 0)
    convolve(s0_ref, wt_ref, (planes - 2) // 2, rows, acc_ref, True)
    put_forward(wt_ref, w2_ref, channels)

    def middle(i, carry):
        for parity in range(2):
            plane = 2 * i + parity
            mask = mask_ref[plane + 1]
            p1 = mask * acc_ref[pl.ds(i * rows, rows), parity * LANES : (parity + 1) * LANES]
            sig = jax.nn.sigmoid(p1)
            slope_ref[plane] = mask * (sig * (1.0 + p1 * (1.0 - sig)))
            put_stack(p1 * sig, rows, upward, s1_ref, parity, i)
        return carry

    lax.fori_loop(0, (planes - 2) // 2, middle, 0)
    convolve(s1_ref, wt_ref, (planes - 4) // 2, rows, acc_ref, True)
    put_backward(wb_ref, w2_ref, channels)

    head = head_ref[...]
    class_lane = (lane > channels) & (lane <= channels + classes)

    for i in range((planes - 4) // 2):
        for parity in range(2):
            plane = 2 * i + parity
            mask = mask_ref[plane + 2]
            p2 = mask * acc_ref[i * rows : (i + 1) * rows, parity * LANES : (parity + 1) * LANES]
            sig = jax.nn.sigmoid(p2)
            a2 = (p2 * sig).astype(BF16)
            logits = lax.dot_general(a2, head, (((1,), (1,)), ((), ())), preferred_element_type=F32)
            g_logits = jnp.where(class_lane, mask * (logits - x_ref[plane + 2].astype(F32)), 0.0)
            coarse = g_logits.astype(BF16)
            fine = (g_logits - coarse.astype(F32)).astype(BF16)
            g_a2 = jnp.dot(
                jnp.concatenate([coarse, fine], 1), jnp.concatenate([head, head], 0), preferred_element_type=F32
            )
            g_p2 = mask * g_a2 * (sig * (1.0 + p2 * (1.0 - sig)))
            put_stack(g_p2, rows, upward, sg_ref, parity, i)
            put_turned(turned_ref, g_p2[low : low + size], plane - 2, east, channels)

    upper = flags_ref[2 * (east_rounds + north_rounds)] == 1
    for t, tile in enumerate(kernel_sum(turned_ref, s1_ref, 3, east, rows, low, size, channels)):
        kept_ref[t * channels : (t + 1) * channels, :] = tile.astype(BF16)
    convolve(sg_ref, wb_ref, (planes - 6) // 2, rows, acc_ref, False)

    for i in range((planes - 6) // 2):
        for parity in range(2):
            plane = 2 * i + parity
            g_p1 = slope_ref[plane + 2] * acc_ref[i * rows : (i + 1) * rows, parity * LANES : (parity + 1) * LANES]
            grad_ref[plane] = g_p1.astype(BF16)
            put_turned(turned_ref, g_p1[low : low + size], plane - 1, east, channels)

    tiles = kernel_sum(turned_ref, s0_ref, 4, east, rows, low, size, channels)
    for t, tile in enumerate(tiles):
        place = slice(t * channels, (t + 1) * channels)
        first, second = tile.astype(BF16), kept_ref[place, :]
        sent_ref[place, :] = jnp.where(upper, second, first)
        kept_ref[place, :] = jnp.where(upper, first, second)
    filled = len(tiles) * channels
    if filled < kept_ref.shape[0]:
        kept_ref[filled:, :] = jnp.zeros((kept_ref.shape[0] - filled, LANES), BF16)
        sent_ref[filled:, :] = jnp.zeros((kept_ref.shape[0] - filled, LANES), BF16)


def last_kernel(
    channels, east, north, upward,
    center_ref, grad_ref, w1_ref, kept_in,
    out_ref, kept_out,
    stack_ref, wb_ref, acc_ref,
):
    rows = (north + 2 * HALO) * upward
    low, size = HALO * upward, north * upward
    put_backward(wb_ref, w1_ref, channels)

    def start(i, carry):
        for parity in range(2):
            put_stack(grad_ref[2 * i + parity].astype(F32), rows, upward, stack_ref, parity, i)
        return carry

    lax.fori_loop(0, east // 2 + 1, start, 0)
    convolve(stack_ref, wb_ref, east // 2, rows, acc_ref, False)
    for i in range(east // 2):
        for parity in range(2):
            plane = 2 * i + parity
            value = acc_ref[i * rows + low : i * rows + low + size, parity * LANES : (parity + 1) * LANES]
            mask = center_ref[plane, :, channels : channels + 1].astype(F32)
            out_ref[plane] = (mask * value)[:, 0:channels].astype(BF16)


def unpack_kernel(channels, scale, upper_ref, mine_ref, other_ref, first_out, second_out):
    spare = LANES - channels
    upper = upper_ref[0] == 1
    for target, here in ((first_out, upper), (second_out, jnp.logical_not(upper))):
        for t in range(0, 27, 4):
            tiles = []
            for r in range(3):
                start = (t // 4 * 3 + r) * channels
                place = slice(start, start + channels)
                tiles.append(jnp.where(here, mine_ref[place, :], other_ref[place, :]).astype(F32) * scale)
            for r in range(3):
                target[t + r] = tiles[r][:, 0:channels]
            if t + 3 < 27:
                lane = lane_of(tiles[0].shape)
                parts = [pltpu.roll(tiles[r], (spare * r - channels) % LANES, 1) for r in range(3)]
                last = jnp.where(lane < spare, parts[0], jnp.where(lane < 2 * spare, parts[1], parts[2]))
                target[t + 3] = last[:, 0:channels]


def per_device(
    features, brick_active, voxel_occupancy, first_weights, second_weights, head, teacher
):
    channels = features.shape[0]
    east, north, upward = features.shape[1:]
    classes = teacher.shape[0]
    devices = lax.axis_size("east") * lax.axis_size("north")
    scale = 1.0 / math.sqrt(devices * east * north * upward)
    planes = east + 2 * HALO
    rows = (north + 2 * HALO) * upward
    edge, size = HALO * upward, north * upward
    vmem = pl.BlockSpec(memory_space=pltpu.VMEM)
    smem = pl.BlockSpec(memory_space=pltpu.SMEM)
    anywhere = pl.BlockSpec(memory_space=pl.ANY)

    east_bits, north_bits = bits_of("east"), bits_of("north")
    rest = north_bits + east_bits[1:]
    groups = [rest[i : i + 2] for i in range(0, len(rest), 2)]
    upper = high_bit(*east_bits[0])
    easts, norths = rounds_of("east"), rounds_of("north")
    counts = (len(easts), len(norths))
    flags = [side for _, side, _ in easts] + [inside for _, _, inside in easts]
    flags += [side for _, side, _ in norths] + [inside for _, _, inside in norths] + [upper]
    flags = jnp.stack(flags).astype(jnp.int32)

    shapes = [(HALO, size, LANES)] * counts[0] + [(east, edge, LANES)] * counts[1]
    shapes += [(HALO, edge, LANES)] * (counts[0] * counts[1])
    center, *edges = pl.pallas_call(
        functools.partial(prepare_kernel, channels, upward, edge, *counts),
        out_shape=[jax.ShapeDtypeStruct(shape, BF16) for shape in [(east, size, LANES)] + shapes],
        in_specs=[smem] * 2 + [vmem] * 3,
        out_specs=[vmem] * (1 + len(shapes)),
        compiler_params=pltpu.CompilerParams(vmem_limit_bytes=32 * 1024 * 1024),
        name="prepare",
    )(
        flags,
        brick_active,
        features.transpose(1, 2, 3, 0).reshape(east, size, channels),
        voxel_occupancy.transpose(0, 2, 1),
        teacher.transpose(0, 1, 3, 2),
    )
    routes = [("east", pairs) for pairs, _, _ in easts] + [("north", pairs) for pairs, _, _ in norths]
    routes += [(("east", "north"), jointly(a, b)) for a, _, _ in easts for b, _, _ in norths]
    edges = [lax.ppermute(value, *route) for value, route in zip(edges, routes)]

    head_wide = jnp.pad(head, ((channels + 1, LANES - channels - 1 - classes), (0, LANES - channels)))
    unit = devices // 2 * 16
    packed = -(-21 * channels // unit) * unit
    grad, kept, sent = pl.pallas_call(
        functools.partial(whole_kernel, channels, classes, east, north, upward, *counts),
        out_shape=(
            jax.ShapeDtypeStruct((east + 2, rows, LANES), BF16),
            jax.ShapeDtypeStruct((packed, LANES), BF16),
            jax.ShapeDtypeStruct((packed, LANES), BF16),
        ),
        in_specs=[smem] + [vmem] * (4 + len(edges)),
        out_specs=(vmem, vmem, vmem),
        scratch_shapes=[
            pltpu.VMEM((planes, rows, LANES), BF16),
            pltpu.VMEM((2, planes // 2 * rows, WIDE), BF16),
            pltpu.VMEM((2, (planes - 2) // 2 * rows, WIDE), BF16),
            pltpu.VMEM((2, (planes - 4) // 2 * rows, WIDE), BF16),
            pltpu.VMEM((planes, rows, LANES), F32),
            pltpu.VMEM((planes - 2, rows, LANES), F32),
            pltpu.VMEM(((planes - 2) // 2 * rows, 2 * LANES), F32),
            pltpu.VMEM((4, 2 * LANES, WIDE), BF16),
            pltpu.VMEM((4, WIDE, 2 * LANES), BF16),
            pltpu.VMEM((3 * channels, east * size), BF16),
        ],
        compiler_params=pltpu.CompilerParams(vmem_limit_bytes=56 * 1024 * 1024),
        name="fields",
    )(flags, first_weights, second_weights, head_wide, center, *edges)

    features_out = []

    def beside(kept):
        out, kept = pl.pallas_call(
            functools.partial(last_kernel, channels, east, north, upward),
            out_shape=(
                jax.ShapeDtypeStruct((east, size, channels), BF16),
                jax.ShapeDtypeStruct(kept.shape, F32),
            ),
            in_specs=[vmem] * 3 + [anywhere],
            out_specs=(vmem, anywhere),
            input_output_aliases={3: 1},
            scratch_shapes=[
                pltpu.VMEM((2, (east + 2) // 2 * rows, WIDE), BF16),
                pltpu.VMEM((4, WIDE, 2 * LANES), BF16),
                pltpu.VMEM((east // 2 * rows, 2 * LANES), F32),
            ],
            compiler_params=pltpu.CompilerParams(vmem_limit_bytes=32 * 1024 * 1024),
            name="features",
        )(center, grad, first_weights, kept)
        features_out.append(out)
        return kept

    total = kept.astype(F32) + swap(sent, east_bits[:1], 1).astype(F32)
    total = scatter_sums(total, groups, beside)
    mine = gather_parts(total.astype(BF16), groups)
    other = swap(mine, east_bits[:1], 1)
    grad_first, grad_second = pl.pallas_call(
        functools.partial(unpack_kernel, channels, scale),
        out_shape=(
            jax.ShapeDtypeStruct(first_weights.shape, F32),
            jax.ShapeDtypeStruct(second_weights.shape, F32),
        ),
        in_specs=[smem] + [vmem] * 2,
        out_specs=(vmem, vmem),
        compiler_params=pltpu.CompilerParams(vmem_limit_bytes=32 * 1024 * 1024),
        name="unpack",
    )(upper.reshape(1).astype(jnp.int32), mine, other)
    (grad_features,) = features_out
    grad_features = grad_features.reshape(east, north, upward, channels).transpose(3, 0, 1, 2)
    return (grad_features, grad_first, grad_second)


def solution(mesh):
    in_specs = (
        P(None, "east", "north", None),
        P("east", "north", None),
        P("east", "north", None),
        P(),
        P(),
        P(),
        P(None, "east", "north", None),
    )
    out_specs = (P(None, "east", "north", None), P(), P())
    return jax.shard_map(
        per_device, mesh=mesh, in_specs=in_specs, out_specs=out_specs, check_vma=False
    )
```

```python
import functools
import math

import jax
import jax.numpy as jnp
from jax import lax
from jax.experimental import pallas as pl
from jax.experimental.pallas import tpu as pltpu
from jax.sharding import PartitionSpec as P

LANES = 128
HALO = 4
OFFSETS = 9
WIDE = OFFSETS * LANES
F32 = jnp.float32
BF16 = jnp.bfloat16


def rounds_of(axis):
    count = lax.axis_size(axis)
    me = lax.axis_index(axis)
    rounds = [(neighbours(count, 0), me % 2, jnp.int32(1))]
    if count > 2:
        inside = ((me > 0) & (me < count - 1)).astype(jnp.int32)
        rounds.append((neighbours(count, 1), (me + 1) % 2, inside))
    return rounds


def neighbours(count, first):
    pairs = []
    for i in range(first, count, 2):
        pairs += [(i, (i + 1) % count), ((i + 1) % count, i)]
    return pairs


def jointly(east_pairs, north_pairs):
    north = lax.axis_size("north")
    return [(e * north + n, f * north + m) for e, f in east_pairs for n, m in north_pairs]


def high_bit(axis, bit):
    return (lax.axis_index(axis) // bit) % 2


def bits_of(axis):
    size = lax.axis_size(axis)
    return [(axis, 1 << i) for i in range(size.bit_length() - 1)]


def place_in(group):
    return sum(high_bit(axis, bit) << i for i, (axis, bit) in enumerate(group))


def swap(value, group, change):
    masks = {"east": 0, "north": 0}
    for i, (axis, bit) in enumerate(group):
        if change >> i & 1:
            masks[axis] |= bit
    pairs = [[(i, i ^ masks[axis]) for i in range(lax.axis_size(axis))] for axis in ("east", "north")]
    return lax.ppermute(value, ("east", "north"), jointly(*pairs))


def scatter_sums(total, groups):
    for group in groups:
        ways = 1 << len(group)
        part = total.shape[0] // ways
        place = place_in(group)
        sent = [
            lax.dynamic_slice_in_dim(total, (place ^ change) * part, part, 0).astype(BF16)
            for change in range(1, ways)
        ]
        total = lax.dynamic_slice_in_dim(total, place * part, part, 0)
        for change in range(1, ways):
            total = total + swap(sent[change - 1], group, change).astype(F32)
    return total


def gather_parts(mine, groups):
    for group in reversed(groups):
        ways = 1 << len(group)
        place = place_in(group)
        parts = [mine] + [swap(mine, group, change) for change in range(1, ways)]
        joined = []
        for row in range(ways):
            piece = parts[0]
            for change in range(1, ways):
                piece = jnp.where((place ^ row) == change, parts[change], piece)
            joined.append(piece)
        mine = jnp.concatenate(joined, 0)
    return mine


def lane_of(shape):
    return lax.broadcasted_iota(jnp.int32, shape, len(shape) - 1)


def put_stack(value, upward, stack_ref, parity, index):
    total = value.shape[0]
    rows = total - 2 * upward
    cubes = value.reshape(total // upward, upward, LANES)
    level = lax.broadcasted_iota(jnp.int32, cubes.shape, 1)
    below = jnp.where(level == 0, 0.0, pltpu.roll(cubes, 1, 1)).reshape(total, LANES)
    above = jnp.where(level == upward - 1, 0.0, pltpu.roll(cubes, upward - 1, 1)).reshape(total, LANES)
    for up, moved in enumerate((below, value, above)):
        even = moved.astype(BF16)
        shifts = (even[0:rows], moved[upward : upward + rows].astype(BF16), even[2 * upward :])
        for north, shifted in enumerate(shifts):
            lane = (north * 3 + up) * LANES
            stack_ref[parity, pl.ds(index * rows, rows), lane : lane + LANES] = shifted


def convolve(stack_ref, weight_ref, pairs, rows, acc_ref, transposed):
    dims = (((1,), (1,)), ((), ())) if transposed else (((1,), (0,)), ((), ()))
    total = None
    for p in range(4):
        first = (p // 2) * rows
        part = lax.dot_general(
            stack_ref[p % 2, first : first + pairs * rows, :],
            weight_ref[p],
            dims,
            preferred_element_type=F32,
        )
        total = part if total is None else total + part
    acc_ref[0 : pairs * rows, :] = total


def weights_kernel(
    channels, classes,
    w1_in, w2_in, head_ref,
    ahead1_ref, ahead2_ref, back1_ref, back2_ref, head_out,
    w1_ref, w2_ref, arrived,
):
    copies = [
        pltpu.make_async_copy(w1_in, w1_ref, arrived.at[0]),
        pltpu.make_async_copy(w2_in, w2_ref, arrived.at[1]),
    ]
    for copy in copies:
        copy.start()
    for ref in (ahead1_ref, ahead2_ref, back1_ref, back2_ref):
        ref[...] = jnp.zeros_like(ref)
    for copy in copies:
        copy.wait()
    for w_ref, ahead_ref, back_ref in ((w1_ref, ahead1_ref, back1_ref), (w2_ref, ahead2_ref, back2_ref)):
        for d in range(3):
            for j in range(OFFSETS):
                value = w_ref[d * OFFSETS + j]
                for q in range(2):
                    side = slice(q * LANES, q * LANES + channels)
                    ahead_ref[d + q, side, j * LANES : j * LANES + channels] = value
                    turn = (OFFSETS - 1 - j) * LANES
                    back_ref[2 - d + q, turn : turn + channels, side] = value
    row = lax.broadcasted_iota(jnp.int32, (LANES, classes), 0)
    spread = (row == lax.broadcasted_iota(jnp.int32, (LANES, classes), 1) + channels + 1).astype(BF16)
    head_out[...] = jnp.zeros_like(head_out)
    head_out[:, 0:channels] = jnp.dot(spread, head_ref[...], preferred_element_type=F32).astype(BF16)


def put_turned(turned_ref, value, plane, east, channels):
    turned = value.T[0:channels].astype(BF16)
    size = value.shape[0]
    for d in range(3):
        e = plane + d - 1
        if 0 <= e < east:
            turned_ref[d * channels : (d + 1) * channels, e * size : (e + 1) * size] = turned


def kernel_sum(turned_ref, stack_ref, first, east, rows, low, size, channels):
    total = None
    for i in range(east // 2):
        fields = []
        for e in (2 * i, 2 * i + 1):
            plane = e + first
            start = (plane // 2) * rows + low
            fields.append(stack_ref[plane % 2, start : start + size, :])
        part = jnp.dot(
            turned_ref[:, 2 * i * size : (2 * i + 2) * size],
            jnp.concatenate(fields, 0),
            preferred_element_type=F32,
        )
        total = part if total is None else total + part
    blocks = [
        total[d * channels : (d + 1) * channels, j * LANES : (j + 1) * LANES]
        for d in range(3)
        for j in range(OFFSETS)
    ]
    blocks.append(jnp.zeros_like(blocks[0]))
    lane = lane_of(blocks[0].shape)
    spare = LANES - channels
    tiles = []
    for t in range(0, 28, 4):
        for r in range(3):
            tail = pltpu.roll(blocks[t + 3], channels - spare * r, 1)
            tiles.append(jnp.where(lane < channels, blocks[t + r], tail))
    return tiles


def prepare_kernel(
    channels, upward, edge, east_rounds, north_rounds,
    flags_ref, active_ref, features_in, occupied_in, teacher_in,
    center_ref, *edge_refs,
):
    *edge_refs, features_ref, occupied_ref, teacher_ref, arrived = edge_refs
    copies = [
        pltpu.make_async_copy(source, target, arrived.at[i])
        for i, (source, target) in enumerate(
            ((occupied_in, occupied_ref), (teacher_in, teacher_ref), (features_in, features_ref))
        )
    ]
    for copy in copies:
        copy.start()
    for copy in copies:
        copy.wait()
    east, size, _ = center_ref.shape
    north = size // upward
    classes = teacher_ref.shape[0]
    wide = (classes + 1) * upward
    row = lax.broadcasted_iota(jnp.int32, (size, north), 0) // upward
    spread = (row == lax.broadcasted_iota(jnp.int32, (size, north), 1)).astype(BF16)
    level = lax.broadcasted_iota(jnp.int32, (size, wide), 0) % upward
    same = level == lax.broadcasted_iota(jnp.int32, (size, wide), 1) % upward
    target = lax.broadcasted_iota(jnp.int32, (wide, LANES), 0) // upward + channels
    gather = (target == lax.broadcasted_iota(jnp.int32, (wide, LANES), 1)).astype(BF16)
    bricks = active_ref.shape
    up = lax.broadcasted_iota(jnp.int32, (upward, north), 0) // (upward // bricks[2])
    along = lax.broadcasted_iota(jnp.int32, (upward, north), 1) // (north // bricks[1])
    for e in range(east):
        mask = jnp.zeros((upward, north), jnp.int32)
        for b in range(bricks[1]):
            for c in range(bricks[2]):
                inside = (along == b) & (up == c)
                mask = jnp.where(inside, active_ref[e // (east // bricks[0]), b, c], mask)
        mask = (mask * occupied_ref[e]).astype(F32)
        field = jnp.concatenate([mask] + [teacher_ref[c, e].astype(F32) for c in range(classes)], 0).astype(BF16)
        everywhere = lax.dot_general(spread, field, (((1,), (1,)), ((), ())), preferred_element_type=F32)
        own = jnp.where(same, everywhere, 0.0).astype(BF16)
        tail = jnp.dot(own, gather, preferred_element_type=F32).astype(BF16)
        center_ref[e, :, 0:channels] = features_ref[e]
        center_ref[e, :, channels:LANES] = tail[:, channels:LANES]
    east_starts = [(1 - flags_ref[r]) * (east - HALO) for r in range(east_rounds)]
    north_starts = [
        pl.multiple_of((1 - flags_ref[2 * east_rounds + r]) * (size - edge), edge) for r in range(north_rounds)
    ]
    edge_refs = iter(edge_refs)
    for e in east_starts:
        next(edge_refs)[...] = center_ref[pl.ds(e, HALO)]
    for n in north_starts:
        next(edge_refs)[...] = center_ref[:, pl.ds(n, edge), :]
    for e in east_starts:
        for n in north_starts:
            next(edge_refs)[...] = center_ref[pl.ds(e, HALO), pl.ds(n, edge), :]


def place_edges(flags_ref, center_ref, edge_refs, east_rounds, north_rounds, edge, x_ref):
    east, size, _ = center_ref.shape
    x_ref[...] = jnp.zeros_like(x_ref)
    x_ref[HALO : HALO + east, edge : edge + size, :] = center_ref[...]
    edge_refs = iter(edge_refs)
    easts = [(flags_ref[r], flags_ref[east_rounds + r]) for r in range(east_rounds)]
    base = 2 * east_rounds
    norths = [(flags_ref[base + r], flags_ref[base + north_rounds + r]) for r in range(north_rounds)]
    middle_east, middle_north = pl.ds(HALO, east), pl.ds(edge, size)
    east_places = [(pl.ds((1 - side) * (east + HALO), HALO), inside) for side, inside in easts]
    north_places = [
        (pl.ds(pl.multiple_of((1 - side) * (size + edge), edge), edge), inside) for side, inside in norths
    ]
    spots = [(e, middle_north, inside) for e, inside in east_places]
    spots += [(middle_east, n, inside) for n, inside in north_places]
    spots += [(e, n, a * b) for e, a in east_places for n, b in north_places]
    for e, n, inside in spots:
        ref = next(edge_refs)

        @pl.when(inside == 1)
        def _(ref=ref, e=e, n=n):
            x_ref[e, n, :] = ref[...]


def whole_kernel(
    channels, classes, east, north, upward, east_rounds, north_rounds,
    flags_ref, ahead1_ref, ahead2_ref, back2_ref, head_ref, center_ref, *refs,
):
    edges = east_rounds + north_rounds + east_rounds * north_rounds
    (
        grad_ref, kept_ref, sent_ref,
        x_ref, s0_ref, s1_ref, sg_ref, mask_ref, slope_ref, acc_ref, turned_ref,
    ) = refs[edges:]
    rows = (north + 2 * HALO) * upward
    low, size = HALO * upward, north * upward
    planes = east + 2 * HALO
    lane = lane_of((rows, LANES))
    rows1, rows2, rows3 = rows - 2 * upward, rows - 4 * upward, rows - 6 * upward
    low1, low2, low3 = low - upward, low - 2 * upward, low - 3 * upward

    place_edges(flags_ref, center_ref, refs[:edges], east_rounds, north_rounds, low, x_ref)
    border = jnp.zeros((upward, LANES), F32)

    def start(i, carry):
        for parity in range(2):
            x = x_ref[2 * i + parity].astype(F32)
            mask = jnp.broadcast_to(x[:, channels : channels + 1], (rows, LANES))
            mask_ref[2 * i + parity] = mask
            a0 = jnp.where((mask > 0) & (lane < channels), x, 0.0)
            put_stack(jnp.concatenate([border, a0, border], 0), upward, s0_ref, parity, i)
        return carry

    lax.fori_loop(0, planes // 2, start, 0)
    convolve(s0_ref, ahead1_ref, (planes - 2) // 2, rows, acc_ref, True)

    def middle(i, carry):
        for parity in range(2):
            plane = 2 * i + parity
            mask = mask_ref[plane + 1]
            p1 = mask * acc_ref[pl.ds(i * rows, rows), parity * LANES : (parity + 1) * LANES]
            sig = jax.nn.sigmoid(p1)
            slope_ref[plane] = mask * (sig * (1.0 + p1 * (1.0 - sig)))
            put_stack((p1 * sig)[upward : upward + rows1], upward, s1_ref, parity, i)
        return carry

    lax.fori_loop(0, (planes - 2) // 2, middle, 0)
    convolve(s1_ref, ahead2_ref, (planes - 4) // 2, rows2, acc_ref, True)

    head = head_ref[...]
    class_lane = (lane[0:rows2] > channels) & (lane[0:rows2] <= channels + classes)
    here = slice(2 * upward, 2 * upward + rows2)

    for i in range((planes - 4) // 2):
        for parity in range(2):
            plane = 2 * i + parity
            mask = mask_ref[plane + 2, here]
            p2 = mask * acc_ref[i * rows2 : (i + 1) * rows2, parity * LANES : (parity + 1) * LANES]
            sig = jax.nn.sigmoid(p2)
            a2 = (p2 * sig).astype(BF16)
            logits = lax.dot_general(a2, head, (((1,), (1,)), ((), ())), preferred_element_type=F32)
            g_logits = jnp.where(class_lane, mask * (logits - x_ref[plane + 2, here].astype(F32)), 0.0)
            coarse = g_logits.astype(BF16)
            fine = (g_logits - coarse.astype(F32)).astype(BF16)
            g_a2 = jnp.dot(
                jnp.concatenate([coarse, fine], 1), jnp.concatenate([head, head], 0), preferred_element_type=F32
            )
            g_p2 = mask * g_a2 * (sig * (1.0 + p2 * (1.0 - sig)))
            put_stack(g_p2, upward, sg_ref, parity, i)
            put_turned(turned_ref, g_p2[low2 : low2 + size], plane - 2, east, channels)

    upper = flags_ref[2 * (east_rounds + north_rounds)] == 1
    for t, tile in enumerate(kernel_sum(turned_ref, s1_ref, 3, east, rows2, low2, size, channels)):
        kept_ref[t * channels : (t + 1) * channels, :] = tile.astype(BF16)
    convolve(sg_ref, back2_ref, (planes - 6) // 2, rows3, acc_ref, False)

    there = slice(2 * upward + upward, 2 * upward + upward + rows3)
    for i in range((planes - 6) // 2):
        for parity in range(2):
            plane = 2 * i + parity
            g_p1 = slope_ref[plane + 2, there] * acc_ref[
                i * rows3 : (i + 1) * rows3, parity * LANES : (parity + 1) * LANES
            ]
            grad_ref[plane] = g_p1.astype(BF16)
            put_turned(turned_ref, g_p1[low3 : low3 + size], plane - 1, east, channels)

    tiles = kernel_sum(turned_ref, s0_ref, 4, east, rows, low, size, channels)
    for t, tile in enumerate(tiles):
        place = slice(t * channels, (t + 1) * channels)
        first, second = tile.astype(BF16), kept_ref[place, :]
        sent_ref[place, :] = jnp.where(upper, second, first)
        kept_ref[place, :] = jnp.where(upper, first, second)
    filled = len(tiles) * channels
    if filled < kept_ref.shape[0]:
        kept_ref[filled:, :] = jnp.zeros((kept_ref.shape[0] - filled, LANES), BF16)
        sent_ref[filled:, :] = jnp.zeros((kept_ref.shape[0] - filled, LANES), BF16)


def last_kernel(
    channels, east, north, upward,
    center_ref, grad_ref, back1_ref, kept_in,
    out_ref, kept_out,
    stack_ref, acc_ref,
):
    size = north * upward

    def start(i, carry):
        for parity in range(2):
            put_stack(grad_ref[2 * i + parity].astype(F32), upward, stack_ref, parity, i)
        return carry

    lax.fori_loop(0, east // 2 + 1, start, 0)
    convolve(stack_ref, back1_ref, east // 2, size, acc_ref, False)
    for i in range(east // 2):
        for parity in range(2):
            plane = 2 * i + parity
            value = acc_ref[i * size : (i + 1) * size, parity * LANES : (parity + 1) * LANES]
            mask = center_ref[plane, :, channels : channels + 1].astype(F32)
            out_ref[plane] = (mask * value)[:, 0:channels].astype(BF16)


def parts_kernel(place_ref, kept_ref, came_ref, total_ref, *sent_refs):
    part = total_ref.shape[0]
    for change, ref in enumerate((total_ref,) + sent_refs):
        start = pl.multiple_of((place_ref[0] ^ change) * part, part)
        rows = pl.ds(start, part)
        ref[...] = (kept_ref[rows, :].astype(F32) + came_ref[rows, :].astype(F32)).astype(ref.dtype)


def unpack_kernel(channels, scale, aliased, first_ref_flag, packed_ref, *refs):
    first_out, second_out, whole_ref, done = refs[2:] if aliased else refs
    spare = LANES - channels
    is_first = first_ref_flag[0] == 1
    spans = [(t, min(t + 4, 27)) for t in range(0, 27, 4)]

    def copy_of(target, i):
        a, b = spans[i]
        return pltpu.make_async_copy(whole_ref.at[a:b], target.at[a:b], done.at[i])

    for i, (t, stop) in enumerate(spans):
        tiles = []
        for r in range(3):
            start = (t // 4 * 3 + r) * channels
            tiles.append(packed_ref[start : start + channels, :].astype(F32) * scale)
        for r in range(3):
            whole_ref[t + r] = tiles[r][:, 0:channels]
        if stop - t == 4:
            lane = lane_of(tiles[0].shape)
            parts = [pltpu.roll(tiles[r], (spare * r - channels) % LANES, 1) for r in range(3)]
            last = jnp.where(lane < spare, parts[0], jnp.where(lane < 2 * spare, parts[1], parts[2]))
            whole_ref[t + 3] = last[:, 0:channels]

        @pl.when(is_first)
        def _(i=i):
            copy_of(first_out, i).start()

        @pl.when(jnp.logical_not(is_first))
        def _(i=i):
            copy_of(second_out, i).start()

    for i in range(len(spans)):
        copy_of(first_out, i).wait()


def per_device(
    features, brick_active, voxel_occupancy, first_weights, second_weights, head, teacher
):
    channels = features.shape[0]
    east, north, upward = features.shape[1:]
    classes = teacher.shape[0]
    devices = lax.axis_size("east") * lax.axis_size("north")
    scale = 1.0 / math.sqrt(devices * east * north * upward)
    planes = east + 2 * HALO
    rows = (north + 2 * HALO) * upward
    edge, size = HALO * upward, north * upward
    vmem = pl.BlockSpec(memory_space=pltpu.VMEM)
    smem = pl.BlockSpec(memory_space=pltpu.SMEM)
    anywhere = pl.BlockSpec(memory_space=pl.ANY)
    far = pl.BlockSpec(memory_space=pltpu.HBM)

    east_bits, north_bits = bits_of("east"), bits_of("north")
    rest = north_bits + east_bits[1:]
    groups = [rest[i : i + 2] for i in range(0, len(rest), 2)]
    upper = high_bit(*east_bits[0])
    easts, norths = rounds_of("east"), rounds_of("north")
    counts = (len(easts), len(norths))
    flags = [side for _, side, _ in easts] + [inside for _, _, inside in easts]
    flags += [side for _, side, _ in norths] + [inside for _, _, inside in norths] + [upper]
    flags = jnp.stack(flags).astype(jnp.int32)

    shapes = [(HALO, size, LANES)] * counts[0] + [(east, edge, LANES)] * counts[1]
    shapes += [(HALO, edge, LANES)] * (counts[0] * counts[1])
    center, *edges = pl.pallas_call(
        functools.partial(prepare_kernel, channels, upward, edge, *counts),
        out_shape=[jax.ShapeDtypeStruct(shape, BF16) for shape in [(east, size, LANES)] + shapes],
        in_specs=[smem] * 2 + [far] * 3,
        out_specs=[vmem] * (1 + len(shapes)),
        scratch_shapes=[
            pltpu.VMEM((east, size, channels), BF16),
            pltpu.VMEM((east, upward, north), jnp.int32),
            pltpu.VMEM((classes, east, upward, north), BF16),
            pltpu.SemaphoreType.DMA((3,)),
        ],
        compiler_params=pltpu.CompilerParams(vmem_limit_bytes=16 * 1024 * 1024),
        name="prepare",
    )(
        flags,
        brick_active,
        pltpu.with_memory_space_constraint(features.transpose(1, 2, 3, 0).reshape(east, size, channels), pltpu.HBM),
        pltpu.with_memory_space_constraint(voxel_occupancy.transpose(0, 2, 1), pltpu.HBM),
        pltpu.with_memory_space_constraint(teacher.transpose(0, 1, 3, 2), pltpu.HBM),
    )
    routes = [("east", pairs) for pairs, _, _ in easts] + [("north", pairs) for pairs, _, _ in norths]
    routes += [(("east", "north"), jointly(a, b)) for a, _, _ in easts for b, _, _ in norths]
    edges = [lax.ppermute(value, *route) for value, route in zip(edges, routes)]

    unit = devices // 2 * 16
    packed = -(-21 * channels // unit) * unit
    wide = (4, 2 * LANES, WIDE)
    tall = (4, WIDE, 2 * LANES)
    ahead1, ahead2, back1, back2, head_wide = pl.pallas_call(
        functools.partial(weights_kernel, channels, classes),
        out_shape=[jax.ShapeDtypeStruct(shape, BF16) for shape in (wide, wide, tall, tall, (LANES, LANES))],
        in_specs=[far, far, vmem],
        out_specs=[vmem] * 5,
        scratch_shapes=[
            pltpu.VMEM(first_weights.shape, BF16),
            pltpu.VMEM(second_weights.shape, BF16),
            pltpu.SemaphoreType.DMA((2,)),
        ],
        compiler_params=pltpu.CompilerParams(vmem_limit_bytes=20 * 1024 * 1024),
        name="weights",
    )(
        pltpu.with_memory_space_constraint(first_weights, pltpu.HBM),
        pltpu.with_memory_space_constraint(second_weights, pltpu.HBM),
        head,
    )
    grad, kept, sent = pl.pallas_call(
        functools.partial(whole_kernel, channels, classes, east, north, upward, *counts),
        out_shape=(
            jax.ShapeDtypeStruct((east + 2, rows - 6 * upward, LANES), BF16),
            jax.ShapeDtypeStruct((packed, LANES), BF16),
            jax.ShapeDtypeStruct((packed, LANES), BF16),
        ),
        in_specs=[smem] + [vmem] * (5 + len(edges)),
        out_specs=(vmem, vmem, vmem),
        scratch_shapes=[
            pltpu.VMEM((planes, rows, LANES), BF16),
            pltpu.VMEM((2, planes // 2 * rows, WIDE), BF16),
            pltpu.VMEM((2, (planes - 2) // 2 * (rows - 4 * upward), WIDE), BF16),
            pltpu.VMEM((2, (planes - 4) // 2 * (rows - 6 * upward), WIDE), BF16),
            pltpu.VMEM((planes, rows, LANES), F32),
            pltpu.VMEM((planes - 2, rows, LANES), F32),
            pltpu.VMEM(((planes - 2) // 2 * rows, 2 * LANES), F32),
            pltpu.VMEM((3 * channels, east * size), BF16),
        ],
        compiler_params=pltpu.CompilerParams(vmem_limit_bytes=38 * 1024 * 1024),
        name="fields",
    )(flags, ahead1, ahead2, back2, head_wide, center, *edges)

    features_out = []

    def beside(kept):
        out, kept = pl.pallas_call(
            functools.partial(last_kernel, channels, east, north, upward),
            out_shape=(
                jax.ShapeDtypeStruct((east, size, channels), BF16),
                jax.ShapeDtypeStruct(kept.shape, F32),
            ),
            in_specs=[vmem] * 3 + [anywhere],
            out_specs=(vmem, anywhere),
            input_output_aliases={3: 1},
            scratch_shapes=[
                pltpu.VMEM((2, (east + 2) // 2 * size, WIDE), BF16),
                pltpu.VMEM((east // 2 * size, 2 * LANES), F32),
            ],
            compiler_params=pltpu.CompilerParams(vmem_limit_bytes=24 * 1024 * 1024),
            name="features",
        )(center, grad, back1, kept)
        features_out.append(out)
        return kept

    ways = 1 << len(groups[0])
    part = packed // ways
    total, *parts = pl.pallas_call(
        parts_kernel,
        out_shape=[jax.ShapeDtypeStruct((part, LANES), F32)]
        + [jax.ShapeDtypeStruct((part, LANES), BF16)] * (ways - 1),
        in_specs=[smem] + [vmem] * 2,
        out_specs=[vmem] * ways,
        compiler_params=pltpu.CompilerParams(vmem_limit_bytes=8 * 1024 * 1024),
        name="parts",
    )(place_in(groups[0]).reshape(1).astype(jnp.int32), kept, swap(sent, east_bits[:1], 1))
    total = beside(total)
    for change in range(1, ways):
        total = total + swap(parts[change - 1], groups[0], change).astype(F32)
    total = scatter_sums(total, groups[1:])
    mine = gather_parts(total.astype(BF16), groups)
    other = swap(mine, east_bits[:1], 1)

    def unpack(is_first, value, *aliased):
        return pl.pallas_call(
            functools.partial(unpack_kernel, channels, scale, bool(aliased)),
            out_shape=(
                jax.ShapeDtypeStruct(first_weights.shape, F32),
                jax.ShapeDtypeStruct(second_weights.shape, F32),
            ),
            in_specs=[smem, vmem] + [anywhere] * len(aliased),
            out_specs=(anywhere, anywhere),
            input_output_aliases={2: 0, 3: 1} if aliased else {},
            scratch_shapes=[pltpu.VMEM(first_weights.shape, F32), pltpu.SemaphoreType.DMA((7,))],
            compiler_params=pltpu.CompilerParams(vmem_limit_bytes=12 * 1024 * 1024),
            name="unpack",
        )(is_first.reshape(1).astype(jnp.int32), value, *aliased)

    outputs = unpack(upper, mine)
    grad_first, grad_second = unpack(1 - upper, other, *outputs)
    (grad_features,) = features_out
    grad_features = grad_features.reshape(east, north, upward, channels).transpose(3, 0, 1, 2)
    return (grad_features, grad_first, grad_second)


def solution(mesh):
    in_specs = (
        P(None, "east", "north", None),
        P("east", "north", None),
        P("east", "north", None),
        P(),
        P(),
        P(),
        P(None, "east", "north", None),
    )
    out_specs = (P(None, "east", "north", None), P(), P())
    return jax.shard_map(
        per_device, mesh=mesh, in_specs=in_specs, out_specs=out_specs, check_vma=False
    )
```

```python
import functools
import math

import jax
import jax.numpy as jnp
from jax import lax
from jax.experimental import pallas as pl
from jax.experimental.pallas import tpu as pltpu
from jax.sharding import PartitionSpec as P

LANES = 128
HALO = 4
OFFSETS = 9
WIDE = OFFSETS * LANES
F32 = jnp.float32
BF16 = jnp.bfloat16


def rounds_of(axis):
    count = lax.axis_size(axis)
    me = lax.axis_index(axis)
    rounds = [([i ^ 1 for i in range(count)], me % 2, jnp.int32(1))]
    if count > 2:
        inside = ((me > 0) & (me < count - 1)).astype(jnp.int32)
        partners = [0] + [((i - 1) ^ 1) + 1 for i in range(1, count - 1)] + [count - 1]
        rounds.append((partners, (me + 1) % 2, inside))
    return rounds


def exchange(value, east, north):
    count = len(north)
    target = {(e, n): (f, m) for e, f in enumerate(east) for n, m in enumerate(north)}
    alone = [place for place, other in target.items() if place == other]
    while alone:
        e, n = alone.pop(0)
        near = [place for place in ((e, n ^ 1), (e ^ 1, n)) if place in alone]
        other = near[0] if near else alone[0]
        alone.remove(other)
        target[e, n], target[other] = other, (e, n)
    pairs = [(e * count + n, f * count + m) for (e, n), (f, m) in target.items()]
    return lax.ppermute(value, ("east", "north"), pairs)


def high_bit(axis, bit):
    return (lax.axis_index(axis) // bit) % 2


def bits_of(axis):
    size = lax.axis_size(axis)
    return [(axis, 1 << i) for i in range(size.bit_length() - 1)]


def place_in(group):
    return sum(high_bit(axis, bit) << i for i, (axis, bit) in enumerate(group))


def swap(value, group, change):
    masks = {"east": 0, "north": 0}
    for i, (axis, bit) in enumerate(group):
        if change >> i & 1:
            masks[axis] |= bit
    partners = [[i ^ masks[axis] for i in range(lax.axis_size(axis))] for axis in ("east", "north")]
    return exchange(value, *partners)


def scatter_sums(total, groups):
    for group in groups:
        ways = 1 << len(group)
        part = total.shape[0] // ways
        place = place_in(group)
        sent = [
            lax.dynamic_slice_in_dim(total, (place ^ change) * part, part, 0).astype(BF16)
            for change in range(1, ways)
        ]
        total = lax.dynamic_slice_in_dim(total, place * part, part, 0)
        for change in range(1, ways):
            total = total + swap(sent[change - 1], group, change).astype(F32)
    return total


def gather_parts(mine, groups):
    for group in reversed(groups):
        ways = 1 << len(group)
        place = place_in(group)
        parts = [mine] + [swap(mine, group, change) for change in range(1, ways)]
        joined = []
        for row in range(ways):
            piece = parts[0]
            for change in range(1, ways):
                piece = jnp.where((place ^ row) == change, parts[change], piece)
            joined.append(piece)
        mine = jnp.concatenate(joined, 0)
    return mine


def lane_of(shape):
    return lax.broadcasted_iota(jnp.int32, shape, len(shape) - 1)


def put_stack(value, upward, stack_ref, parity, index):
    total = value.shape[0]
    rows = total - 2 * upward
    cubes = value.reshape(total // upward, upward, LANES)
    level = lax.broadcasted_iota(jnp.int32, cubes.shape, 1)
    below = jnp.where(level == 0, 0.0, pltpu.roll(cubes, 1, 1)).reshape(total, LANES)
    above = jnp.where(level == upward - 1, 0.0, pltpu.roll(cubes, upward - 1, 1)).reshape(total, LANES)
    for up, moved in enumerate((below, value, above)):
        even = moved.astype(BF16)
        shifts = (even[0:rows], moved[upward : upward + rows].astype(BF16), even[2 * upward :])
        for north, shifted in enumerate(shifts):
            lane = (north * 3 + up) * LANES
            stack_ref[parity, pl.ds(index * rows, rows), lane : lane + LANES] = shifted


def convolve(stack_ref, weight_ref, pair, rows):
    fields = [stack_ref[p % 2, (pair + p // 2) * rows : (pair + p // 2 + 1) * rows, :] for p in range(4)]
    both = jnp.dot(jnp.concatenate(fields, 1), weight_ref[...], preferred_element_type=F32)
    return both[:, 0:LANES], both[:, LANES:]


def weights_kernel(
    channels, classes,
    w1_in, w2_in, head_in,
    ahead1_ref, ahead2_ref, back1_ref, back2_ref, head_out,
    w1_ref, w2_ref, head_ref, arrived,
):
    copies = [
        pltpu.make_async_copy(source, target, arrived.at[i])
        for i, (source, target) in enumerate(((w1_in, w1_ref), (w2_in, w2_ref), (head_in, head_ref)))
    ]
    for copy in copies:
        copy.start()
    for ref in (ahead1_ref, ahead2_ref, back1_ref, back2_ref, head_out):
        ref[...] = jnp.zeros_like(ref)
    for copy in copies:
        copy.wait()
    row = lax.broadcasted_iota(jnp.int32, (channels, channels), 0)
    unit = (row == lax.broadcasted_iota(jnp.int32, (channels, channels), 1)).astype(BF16)
    for w_ref, ahead_ref, back_ref in ((w1_ref, ahead1_ref, back1_ref), (w2_ref, ahead2_ref, back2_ref)):
        for d in range(3):
            for j in range(OFFSETS):
                value = w_ref[d * OFFSETS + j]
                turned = lax.dot_general(unit, value, (((1,), (1,)), ((), ())), preferred_element_type=F32).astype(BF16)
                for q in range(2):
                    side = slice(q * LANES, q * LANES + channels)
                    start = ((d + q) * OFFSETS + j) * LANES
                    ahead_ref[start : start + channels, side] = turned
                    start = ((2 - d + q) * OFFSETS + OFFSETS - 1 - j) * LANES
                    back_ref[start : start + channels, side] = value
    row = lax.broadcasted_iota(jnp.int32, (LANES, classes), 0)
    spread = (row == lax.broadcasted_iota(jnp.int32, (LANES, classes), 1) + channels + 1).astype(BF16)
    head_out[:, 0:channels] = jnp.dot(spread, head_ref[...], preferred_element_type=F32).astype(BF16)


def put_turned(turned_ref, value, plane, east, channels):
    turned = value.T[0:channels].astype(BF16)
    size = value.shape[0]
    for d in range(3):
        e = plane + d - 1
        if 0 <= e < east:
            turned_ref[d * channels : (d + 1) * channels, e * size : (e + 1) * size] = turned


def kernel_sum(turned_ref, stack_ref, first, east, rows, low, size, channels):
    total = None
    for i in range(east // 2):
        fields = []
        for e in (2 * i, 2 * i + 1):
            plane = e + first
            start = (plane // 2) * rows + low
            fields.append(stack_ref[plane % 2, start : start + size, :])
        part = jnp.dot(
            turned_ref[:, 2 * i * size : (2 * i + 2) * size],
            jnp.concatenate(fields, 0),
            preferred_element_type=F32,
        )
        total = part if total is None else total + part
    blocks = [
        total[d * channels : (d + 1) * channels, j * LANES : (j + 1) * LANES]
        for d in range(3)
        for j in range(OFFSETS)
    ]
    blocks.append(jnp.zeros_like(blocks[0]))
    lane = lane_of(blocks[0].shape)
    spare = LANES - channels
    tiles = []
    for t in range(0, 28, 4):
        for r in range(3):
            tail = pltpu.roll(blocks[t + 3], channels - spare * r, 1)
            tiles.append(jnp.where(lane < channels, blocks[t + r], tail))
    return tiles


def prepare_kernel(
    channels, upward, edge, east_rounds, north_rounds,
    flags_ref, active_ref, features_in, occupied_in, teacher_in,
    center_ref, *edge_refs,
):
    *edge_refs, features_ref, occupied_ref, teacher_ref, arrived = edge_refs
    copies = [
        pltpu.make_async_copy(source, target, arrived.at[i])
        for i, (source, target) in enumerate(
            ((occupied_in, occupied_ref), (teacher_in, teacher_ref), (features_in, features_ref))
        )
    ]
    for copy in copies:
        copy.start()
    for copy in copies:
        copy.wait()
    east, size, _ = center_ref.shape
    north = size // upward
    classes = teacher_ref.shape[0]
    wide = (classes + 1) * upward
    row = lax.broadcasted_iota(jnp.int32, (size, north), 0) // upward
    spread = (row == lax.broadcasted_iota(jnp.int32, (size, north), 1)).astype(BF16)
    level = lax.broadcasted_iota(jnp.int32, (size, wide), 0) % upward
    same = level == lax.broadcasted_iota(jnp.int32, (size, wide), 1) % upward
    target = lax.broadcasted_iota(jnp.int32, (wide, LANES), 0) // upward + channels
    gather = (target == lax.broadcasted_iota(jnp.int32, (wide, LANES), 1)).astype(BF16)
    bricks = active_ref.shape
    up = lax.broadcasted_iota(jnp.int32, (upward, north), 0) // (upward // bricks[2])
    along = lax.broadcasted_iota(jnp.int32, (upward, north), 1) // (north // bricks[1])
    for e in range(east):
        mask = jnp.zeros((upward, north), jnp.int32)
        for b in range(bricks[1]):
            for c in range(bricks[2]):
                inside = (along == b) & (up == c)
                mask = jnp.where(inside, active_ref[e // (east // bricks[0]), b, c], mask)
        mask = (mask * occupied_ref[e]).astype(F32)
        field = jnp.concatenate([mask] + [teacher_ref[c, e].astype(F32) for c in range(classes)], 0).astype(BF16)
        everywhere = lax.dot_general(spread, field, (((1,), (1,)), ((), ())), preferred_element_type=F32)
        own = jnp.where(same, everywhere, 0.0).astype(BF16)
        tail = jnp.dot(own, gather, preferred_element_type=F32).astype(BF16)
        center_ref[e, :, 0:channels] = features_ref[e]
        center_ref[e, :, channels:LANES] = tail[:, channels:LANES]
    east_starts = [(1 - flags_ref[r]) * (east - HALO) for r in range(east_rounds)]
    north_starts = [
        pl.multiple_of((1 - flags_ref[2 * east_rounds + r]) * (size - edge), edge) for r in range(north_rounds)
    ]
    edge_refs = iter(edge_refs)
    for e in east_starts:
        next(edge_refs)[...] = center_ref[pl.ds(e, HALO)]
    for n in north_starts:
        next(edge_refs)[...] = center_ref[:, pl.ds(n, edge), :]
    for e in east_starts:
        for n in north_starts:
            next(edge_refs)[...] = center_ref[pl.ds(e, HALO), pl.ds(n, edge), :]


def place_edges(flags_ref, center_ref, edge_refs, east_rounds, north_rounds, edge, x_ref):
    east, size, _ = center_ref.shape
    x_ref[...] = jnp.zeros_like(x_ref)
    x_ref[HALO : HALO + east, edge : edge + size, :] = center_ref[...]
    edge_refs = iter(edge_refs)
    easts = [(flags_ref[r], flags_ref[east_rounds + r]) for r in range(east_rounds)]
    base = 2 * east_rounds
    norths = [(flags_ref[base + r], flags_ref[base + north_rounds + r]) for r in range(north_rounds)]
    middle_east, middle_north = pl.ds(HALO, east), pl.ds(edge, size)
    east_places = [(pl.ds((1 - side) * (east + HALO), HALO), inside) for side, inside in easts]
    north_places = [
        (pl.ds(pl.multiple_of((1 - side) * (size + edge), edge), edge), inside) for side, inside in norths
    ]
    spots = [(e, middle_north, inside) for e, inside in east_places]
    spots += [(middle_east, n, inside) for n, inside in north_places]
    spots += [(e, n, a * b) for e, a in east_places for n, b in north_places]
    for e, n, inside in spots:
        ref = next(edge_refs)

        @pl.when(inside == 1)
        def _(ref=ref, e=e, n=n):
            x_ref[e, n, :] = ref[...]


def whole_kernel(
    channels, classes, east, north, upward, east_rounds, north_rounds,
    flags_ref, ahead1_ref, ahead2_ref, back2_ref, head_ref, center_ref, *refs,
):
    edges = east_rounds + north_rounds + east_rounds * north_rounds
    (
        grad_ref, kept_ref, sent_ref,
        x_ref, s0_ref, s1_ref, sg_ref, mask_ref, slope_ref, turned_ref,
    ) = refs[edges:]
    rows = (north + 2 * HALO) * upward
    low, size = HALO * upward, north * upward
    planes = east + 2 * HALO
    lane = lane_of((rows, LANES))
    rows1, rows2, rows3 = rows - 2 * upward, rows - 4 * upward, rows - 6 * upward
    low1, low2, low3 = low - upward, low - 2 * upward, low - 3 * upward

    place_edges(flags_ref, center_ref, refs[:edges], east_rounds, north_rounds, low, x_ref)
    border = jnp.zeros((upward, LANES), F32)

    for plane in range(planes):
        x = x_ref[plane].astype(F32)
        mask = jnp.broadcast_to(x[:, channels : channels + 1], (rows, LANES))
        mask_ref[plane] = mask
        a0 = jnp.where((mask > 0) & (lane < channels), x, 0.0)
        put_stack(jnp.concatenate([border, a0, border], 0), upward, s0_ref, plane % 2, plane // 2)

    for i in range((planes - 2) // 2):
        for parity, value in enumerate(convolve(s0_ref, ahead1_ref, i, rows)):
            plane = 2 * i + parity
            mask = mask_ref[plane + 1]
            p1 = mask * value
            sig = jax.nn.sigmoid(p1)
            slope_ref[plane] = mask * (sig * (1.0 + p1 * (1.0 - sig)))
            put_stack((p1 * sig)[upward : upward + rows1], upward, s1_ref, parity, i)

    head = head_ref[...]
    class_lane = (lane[0:rows2] > channels) & (lane[0:rows2] <= channels + classes)
    here = slice(2 * upward, 2 * upward + rows2)

    for i in range((planes - 4) // 2):
        for parity, value in enumerate(convolve(s1_ref, ahead2_ref, i, rows2)):
            plane = 2 * i + parity
            mask = mask_ref[plane + 2, here]
            p2 = mask * value
            sig = jax.nn.sigmoid(p2)
            a2 = (p2 * sig).astype(BF16)
            logits = lax.dot_general(a2, head, (((1,), (1,)), ((), ())), preferred_element_type=F32)
            g_logits = jnp.where(class_lane, mask * (logits - x_ref[plane + 2, here].astype(F32)), 0.0)
            coarse = g_logits.astype(BF16)
            fine = (g_logits - coarse.astype(F32)).astype(BF16)
            g_a2 = jnp.dot(
                jnp.concatenate([coarse, fine], 1), jnp.concatenate([head, head], 0), preferred_element_type=F32
            )
            g_p2 = mask * g_a2 * (sig * (1.0 + p2 * (1.0 - sig)))
            put_stack(g_p2, upward, sg_ref, parity, i)
            put_turned(turned_ref, g_p2[low2 : low2 + size], plane - 2, east, channels)

    upper = flags_ref[2 * (east_rounds + north_rounds)] == 1
    for t, tile in enumerate(kernel_sum(turned_ref, s1_ref, 3, east, rows2, low2, size, channels)):
        kept_ref[t * channels : (t + 1) * channels, :] = tile.astype(BF16)

    there = slice(2 * upward + upward, 2 * upward + upward + rows3)
    for i in range((planes - 6) // 2):
        for parity, value in enumerate(convolve(sg_ref, back2_ref, i, rows3)):
            plane = 2 * i + parity
            g_p1 = slope_ref[plane + 2, there] * value
            grad_ref[plane] = g_p1.astype(BF16)
            put_turned(turned_ref, g_p1[low3 : low3 + size], plane - 1, east, channels)

    tiles = kernel_sum(turned_ref, s0_ref, 4, east, rows, low, size, channels)
    for t, tile in enumerate(tiles):
        place = slice(t * channels, (t + 1) * channels)
        first, second = tile.astype(BF16), kept_ref[place, :]
        sent_ref[place, :] = jnp.where(upper, second, first)
        kept_ref[place, :] = jnp.where(upper, first, second)
    filled = len(tiles) * channels
    if filled < kept_ref.shape[0]:
        kept_ref[filled:, :] = jnp.zeros((kept_ref.shape[0] - filled, LANES), BF16)
        sent_ref[filled:, :] = jnp.zeros((kept_ref.shape[0] - filled, LANES), BF16)


def last_kernel(
    channels, east, north, upward,
    center_ref, grad_ref, back1_ref, kept_in,
    out_ref, kept_out,
    stack_ref,
):
    size = north * upward
    for plane in range(east + 2):
        put_stack(grad_ref[plane].astype(F32), upward, stack_ref, plane % 2, plane // 2)
    for i in range(east // 2):
        for parity, value in enumerate(convolve(stack_ref, back1_ref, i, size)):
            plane = 2 * i + parity
            mask = center_ref[plane, :, channels : channels + 1].astype(F32)
            out_ref[plane] = (mask * value)[:, 0:channels].astype(BF16)


def parts_kernel(place_ref, kept_ref, came_ref, total_ref, *sent_refs):
    part = total_ref.shape[0]
    for change, ref in enumerate((total_ref,) + sent_refs):
        start = pl.multiple_of((place_ref[0] ^ change) * part, part)
        rows = pl.ds(start, part)
        ref[...] = (kept_ref[rows, :].astype(F32) + came_ref[rows, :].astype(F32)).astype(ref.dtype)


def unpack_kernel(channels, scale, aliased, first_ref_flag, packed_ref, *refs):
    first_out, second_out, whole_ref, done = refs[2:] if aliased else refs
    spare = LANES - channels
    is_first = first_ref_flag[0] == 1
    spans = [(t, min(t + 4, 27)) for t in range(0, 27, 4)]

    def copy_of(target, i):
        a, b = spans[i]
        return pltpu.make_async_copy(whole_ref.at[a:b], target.at[a:b], done.at[i])

    for i, (t, stop) in enumerate(spans):
        tiles = []
        for r in range(3):
            start = (t // 4 * 3 + r) * channels
            tiles.append(packed_ref[start : start + channels, :].astype(F32) * scale)
        for r in range(3):
            whole_ref[t + r] = tiles[r][:, 0:channels]
        if stop - t == 4:
            lane = lane_of(tiles[0].shape)
            parts = [pltpu.roll(tiles[r], (spare * r - channels) % LANES, 1) for r in range(3)]
            last = jnp.where(lane < spare, parts[0], jnp.where(lane < 2 * spare, parts[1], parts[2]))
            whole_ref[t + 3] = last[:, 0:channels]

        @pl.when(is_first)
        def _(i=i):
            copy_of(first_out, i).start()

        @pl.when(jnp.logical_not(is_first))
        def _(i=i):
            copy_of(second_out, i).start()

    for i in range(len(spans)):
        copy_of(first_out, i).wait()


def per_device(
    features, brick_active, voxel_occupancy, first_weights, second_weights, head, teacher
):
    channels = features.shape[0]
    east, north, upward = features.shape[1:]
    classes = teacher.shape[0]
    devices = lax.axis_size("east") * lax.axis_size("north")
    scale = 1.0 / math.sqrt(devices * east * north * upward)
    planes = east + 2 * HALO
    rows = (north + 2 * HALO) * upward
    edge, size = HALO * upward, north * upward
    vmem = pl.BlockSpec(memory_space=pltpu.VMEM)
    smem = pl.BlockSpec(memory_space=pltpu.SMEM)
    anywhere = pl.BlockSpec(memory_space=pl.ANY)
    far = pl.BlockSpec(memory_space=pltpu.HBM)

    east_bits, north_bits = bits_of("east"), bits_of("north")
    rest = north_bits + east_bits[1:]
    groups = [rest[i : i + 2] for i in range(0, len(rest), 2)]
    upper = high_bit(*east_bits[0])
    easts, norths = rounds_of("east"), rounds_of("north")
    counts = (len(easts), len(norths))
    flags = [side for _, side, _ in easts] + [inside for _, _, inside in easts]
    flags += [side for _, side, _ in norths] + [inside for _, _, inside in norths] + [upper]
    flags = jnp.stack(flags).astype(jnp.int32)

    shapes = [(HALO, size, LANES)] * counts[0] + [(east, edge, LANES)] * counts[1]
    shapes += [(HALO, edge, LANES)] * (counts[0] * counts[1])
    center, *edges = pl.pallas_call(
        functools.partial(prepare_kernel, channels, upward, edge, *counts),
        out_shape=[jax.ShapeDtypeStruct(shape, BF16) for shape in [(east, size, LANES)] + shapes],
        in_specs=[smem] * 2 + [far] * 3,
        out_specs=[vmem] * (1 + len(shapes)),
        scratch_shapes=[
            pltpu.VMEM((east, size, channels), BF16),
            pltpu.VMEM((east, upward, north), jnp.int32),
            pltpu.VMEM((classes, east, upward, north), BF16),
            pltpu.SemaphoreType.DMA((3,)),
        ],
        compiler_params=pltpu.CompilerParams(vmem_limit_bytes=16 * 1024 * 1024),
        name="prepare",
    )(
        flags,
        brick_active,
        pltpu.with_memory_space_constraint(features.transpose(1, 2, 3, 0).reshape(east, size, channels), pltpu.HBM),
        pltpu.with_memory_space_constraint(voxel_occupancy.transpose(0, 2, 1), pltpu.HBM),
        pltpu.with_memory_space_constraint(teacher.transpose(0, 1, 3, 2), pltpu.HBM),
    )
    stay = [list(range(lax.axis_size(axis))) for axis in ("east", "north")]
    routes = [(partners, stay[1]) for partners, _, _ in easts] + [(stay[0], partners) for partners, _, _ in norths]
    routes += [(a, b) for a, _, _ in easts for b, _, _ in norths]
    edges = [exchange(value, *route) for value, route in zip(edges, routes)]

    unit = devices // 2 * 16
    packed = -(-21 * channels // unit) * unit
    shapes = [(4 * WIDE, 2 * LANES)] * 4 + [(LANES, LANES)]
    ahead1, ahead2, back1, back2, head_wide = pl.pallas_call(
        functools.partial(weights_kernel, channels, classes),
        out_shape=[jax.ShapeDtypeStruct(shape, BF16) for shape in shapes],
        in_specs=[far] * 3,
        out_specs=[vmem] * 5,
        scratch_shapes=[
            pltpu.VMEM(first_weights.shape, BF16),
            pltpu.VMEM(second_weights.shape, BF16),
            pltpu.VMEM(head.shape, BF16),
            pltpu.SemaphoreType.DMA((3,)),
        ],
        compiler_params=pltpu.CompilerParams(vmem_limit_bytes=16 * 1024 * 1024),
        name="weights",
    )(*[pltpu.with_memory_space_constraint(value, pltpu.HBM) for value in (first_weights, second_weights, head)])
    grad, kept, sent = pl.pallas_call(
        functools.partial(whole_kernel, channels, classes, east, north, upward, *counts),
        out_shape=(
            jax.ShapeDtypeStruct((east + 2, rows - 6 * upward, LANES), BF16),
            jax.ShapeDtypeStruct((packed, LANES), BF16),
            jax.ShapeDtypeStruct((packed, LANES), BF16),
        ),
        in_specs=[smem] + [vmem] * (5 + len(edges)),
        out_specs=(vmem, vmem, vmem),
        scratch_shapes=[
            pltpu.VMEM((planes, rows, LANES), BF16),
            pltpu.VMEM((2, planes // 2 * rows, WIDE), BF16),
            pltpu.VMEM((2, (planes - 2) // 2 * (rows - 4 * upward), WIDE), BF16),
            pltpu.VMEM((2, (planes - 4) // 2 * (rows - 6 * upward), WIDE), BF16),
            pltpu.VMEM((planes, rows, LANES), F32),
            pltpu.VMEM((planes - 2, rows, LANES), F32),
            pltpu.VMEM((3 * channels, east * size), BF16),
        ],
        compiler_params=pltpu.CompilerParams(vmem_limit_bytes=32 * 1024 * 1024),
        name="fields",
    )(flags, ahead1, ahead2, back2, head_wide, center, *edges)

    features_out = []

    def beside(kept):
        out, kept = pl.pallas_call(
            functools.partial(last_kernel, channels, east, north, upward),
            out_shape=(
                jax.ShapeDtypeStruct((east, size, channels), BF16),
                jax.ShapeDtypeStruct(kept.shape, F32),
            ),
            in_specs=[vmem] * 3 + [anywhere],
            out_specs=(vmem, anywhere),
            input_output_aliases={3: 1},
            scratch_shapes=[pltpu.VMEM((2, (east + 2) // 2 * size, WIDE), BF16)],
            compiler_params=pltpu.CompilerParams(vmem_limit_bytes=12 * 1024 * 1024),
            name="features",
        )(center, grad, back1, kept)
        features_out.append(out)
        return kept

    ways = 1 << len(groups[0])
    part = packed // ways
    total, *parts = pl.pallas_call(
        parts_kernel,
        out_shape=[jax.ShapeDtypeStruct((part, LANES), F32)]
        + [jax.ShapeDtypeStruct((part, LANES), BF16)] * (ways - 1),
        in_specs=[smem] + [vmem] * 2,
        out_specs=[vmem] * ways,
        compiler_params=pltpu.CompilerParams(vmem_limit_bytes=8 * 1024 * 1024),
        name="parts",
    )(place_in(groups[0]).reshape(1).astype(jnp.int32), kept, swap(sent, east_bits[:1], 1))
    total = beside(total)
    for change in range(1, ways):
        total = total + swap(parts[change - 1], groups[0], change).astype(F32)
    total = scatter_sums(total, groups[1:])
    mine = gather_parts(total.astype(BF16), groups)
    other = swap(mine, east_bits[:1], 1)

    def unpack(is_first, value, *aliased):
        return pl.pallas_call(
            functools.partial(unpack_kernel, channels, scale, bool(aliased)),
            out_shape=(
                jax.ShapeDtypeStruct(first_weights.shape, F32),
                jax.ShapeDtypeStruct(second_weights.shape, F32),
            ),
            in_specs=[smem, vmem] + [anywhere] * len(aliased),
            out_specs=(anywhere, anywhere),
            input_output_aliases={2: 0, 3: 1} if aliased else {},
            scratch_shapes=[pltpu.VMEM(first_weights.shape, F32), pltpu.SemaphoreType.DMA((7,))],
            compiler_params=pltpu.CompilerParams(vmem_limit_bytes=12 * 1024 * 1024),
            name="unpack",
        )(is_first.reshape(1).astype(jnp.int32), value, *aliased)

    outputs = unpack(upper, mine)
    grad_first, grad_second = unpack(1 - upper, other, *outputs)
    (grad_features,) = features_out
    grad_features = grad_features.reshape(east, north, upward, channels).transpose(3, 0, 1, 2)
    return (grad_features, grad_first, grad_second)


def solution(mesh):
    in_specs = (
        P(None, "east", "north", None),
        P("east", "north", None),
        P("east", "north", None),
        P(),
        P(),
        P(),
        P(None, "east", "north", None),
    )
    out_specs = (P(None, "east", "north", None), P(), P())
    return jax.shard_map(
        per_device, mesh=mesh, in_specs=in_specs, out_specs=out_specs, check_vma=False
    )
```

```python
import functools
import math

import jax
import jax.numpy as jnp
from jax import lax
from jax.experimental import pallas as pl
from jax.experimental.pallas import tpu as pltpu
from jax.sharding import PartitionSpec as P

LANES = 128
HALO = 4
OFFSETS = 9
WIDE = OFFSETS * LANES
F32 = jnp.float32
BF16 = jnp.bfloat16


def rounds_of(axis):
    count = lax.axis_size(axis)
    me = lax.axis_index(axis)
    rounds = [([i ^ 1 for i in range(count)], me % 2, jnp.int32(1))]
    if count > 2:
        inside = ((me > 0) & (me < count - 1)).astype(jnp.int32)
        partners = [0] + [((i - 1) ^ 1) + 1 for i in range(1, count - 1)] + [count - 1]
        rounds.append((partners, (me + 1) % 2, inside))
    return rounds


def exchange(value, east, north):
    count = len(north)
    target = {(e, n): (f, m) for e, f in enumerate(east) for n, m in enumerate(north)}
    alone = [place for place, other in target.items() if place == other]
    while alone:
        e, n = alone.pop(0)
        near = [place for place in ((e, n ^ 1), (e ^ 1, n)) if place in alone]
        other = near[0] if near else alone[0]
        alone.remove(other)
        target[e, n], target[other] = other, (e, n)
    pairs = [(e * count + n, f * count + m) for (e, n), (f, m) in target.items()]
    return lax.ppermute(value, ("east", "north"), pairs)


def high_bit(axis, bit):
    return (lax.axis_index(axis) // bit) % 2


def bits_of(axis):
    size = lax.axis_size(axis)
    return [(axis, 1 << i) for i in range(size.bit_length() - 1)]


def place_in(group):
    return sum(high_bit(axis, bit) << i for i, (axis, bit) in enumerate(group))


def swap(value, group, change):
    masks = {"east": 0, "north": 0}
    for i, (axis, bit) in enumerate(group):
        if change >> i & 1:
            masks[axis] |= bit
    partners = [[i ^ masks[axis] for i in range(lax.axis_size(axis))] for axis in ("east", "north")]
    return exchange(value, *partners)


def scatter_sums(total, groups):
    for group in groups:
        ways = 1 << len(group)
        part = total.shape[0] // ways
        place = place_in(group)
        sent = [
            lax.dynamic_slice_in_dim(total, (place ^ change) * part, part, 0).astype(BF16)
            for change in range(1, ways)
        ]
        total = lax.dynamic_slice_in_dim(total, place * part, part, 0)
        for change in range(1, ways):
            total = total + swap(sent[change - 1], group, change).astype(F32)
    return total


def gather_parts(mine, groups):
    for group in reversed(groups):
        ways = 1 << len(group)
        place = place_in(group)
        parts = [mine] + [swap(mine, group, change) for change in range(1, ways)]
        joined = []
        for row in range(ways):
            piece = parts[0]
            for change in range(1, ways):
                piece = jnp.where((place ^ row) == change, parts[change], piece)
            joined.append(piece)
        mine = jnp.concatenate(joined, 0)
    return mine


def lane_of(shape):
    return lax.broadcasted_iota(jnp.int32, shape, len(shape) - 1)


def put_stack(value, upward, stack_ref, parity, index):
    total = value.shape[0]
    rows = total - 2 * upward
    cubes = value.reshape(total // upward, upward, LANES)
    level = lax.broadcasted_iota(jnp.int32, cubes.shape, 1)
    below = jnp.where(level == 0, 0.0, pltpu.roll(cubes, 1, 1)).reshape(total, LANES)
    above = jnp.where(level == upward - 1, 0.0, pltpu.roll(cubes, upward - 1, 1)).reshape(total, LANES)
    for up, moved in enumerate((below, value, above)):
        even = moved.astype(BF16)
        shifts = (even[0:rows], moved[upward : upward + rows].astype(BF16), even[2 * upward :])
        for north, shifted in enumerate(shifts):
            lane = (north * 3 + up) * LANES
            stack_ref[parity, pl.ds(index * rows, rows), lane : lane + LANES] = shifted


def grouped(pairs, size):
    count = max(1, pairs // size)
    edges = [pairs * i // count for i in range(count + 1)]
    return list(zip(edges, edges[1:]))


def convolve(stack_ref, weight_ref, first, stop, rows):
    fields = [stack_ref[p % 2, (first + p // 2) * rows : (stop + p // 2) * rows, :] for p in range(4)]
    both = jnp.dot(jnp.concatenate(fields, 1), weight_ref[...], preferred_element_type=F32)
    return [
        (pair, parity, both[(pair - first) * rows : (pair - first + 1) * rows, parity * LANES : (parity + 1) * LANES])
        for pair in range(first, stop)
        for parity in range(2)
    ]


def put_back(back_ref, w_ref, channels):
    back_ref[...] = jnp.zeros_like(back_ref)
    for d in range(3):
        for j in range(OFFSETS):
            for q in range(2):
                start = ((2 - d + q) * OFFSETS + OFFSETS - 1 - j) * LANES
                back_ref[start : start + channels, q * LANES : q * LANES + channels] = w_ref[d * OFFSETS + j]


def weights_kernel(
    channels, classes,
    w1_in, w2_in, head_in,
    ahead1_ref, ahead2_ref, back2_ref, head_out,
    w1_ref, w2_ref, head_ref, arrived,
):
    copies = [
        pltpu.make_async_copy(source, target, arrived.at[i])
        for i, (source, target) in enumerate(((w1_in, w1_ref), (w2_in, w2_ref), (head_in, head_ref)))
    ]
    for copy in copies:
        copy.start()
    for ref in (ahead1_ref, ahead2_ref, head_out):
        ref[...] = jnp.zeros_like(ref)
    for copy in copies:
        copy.wait()
    row = lax.broadcasted_iota(jnp.int32, (channels, channels), 0)
    unit = (row == lax.broadcasted_iota(jnp.int32, (channels, channels), 1)).astype(BF16)
    for w_ref, ahead_ref in ((w1_ref, ahead1_ref), (w2_ref, ahead2_ref)):
        for d in range(3):
            for j in range(OFFSETS):
                value = w_ref[d * OFFSETS + j]
                turned = lax.dot_general(unit, value, (((1,), (1,)), ((), ())), preferred_element_type=F32).astype(BF16)
                for q in range(2):
                    side = slice(q * LANES, q * LANES + channels)
                    start = ((d + q) * OFFSETS + j) * LANES
                    ahead_ref[start : start + channels, side] = turned
    put_back(back2_ref, w2_ref, channels)
    row = lax.broadcasted_iota(jnp.int32, (LANES, classes), 0)
    spread = (row == lax.broadcasted_iota(jnp.int32, (LANES, classes), 1) + channels + 1).astype(BF16)
    head_out[:, 0:channels] = jnp.dot(spread, head_ref[...], preferred_element_type=F32).astype(BF16)


def put_turned(turned_ref, value, plane, east, channels):
    turned = value.T[0:channels].astype(BF16)
    size = value.shape[0]
    for d in range(3):
        e = plane + d - 1
        if 0 <= e < east:
            turned_ref[d * channels : (d + 1) * channels, e * size : (e + 1) * size] = turned


def kernel_sum(turned_ref, stack_ref, first, east, rows, low, size, channels):
    fields = []
    for e in range(first, first + east):
        start = (e // 2) * rows + low
        fields.append(stack_ref[e % 2, start : start + size, :])
    total = jnp.dot(turned_ref[...], jnp.concatenate(fields, 0), preferred_element_type=F32)
    blocks = [
        total[d * channels : (d + 1) * channels, j * LANES : (j + 1) * LANES]
        for d in range(3)
        for j in range(OFFSETS)
    ]
    blocks.append(jnp.zeros_like(blocks[0]))
    lane = lane_of(blocks[0].shape)
    spare = LANES - channels
    tiles = []
    for t in range(0, 28, 4):
        for r in range(3):
            tail = pltpu.roll(blocks[t + 3], channels - spare * r, 1)
            tiles.append(jnp.where(lane < channels, blocks[t + r], tail))
    return tiles


def prepare_kernel(
    channels, upward, edge, east_rounds, north_rounds,
    flags_ref, active_ref, features_in, occupied_in, teacher_in,
    center_ref, *edge_refs,
):
    *edge_refs, features_ref, occupied_ref, teacher_ref, arrived = edge_refs
    copies = [
        pltpu.make_async_copy(source, target, arrived.at[i])
        for i, (source, target) in enumerate(
            ((occupied_in, occupied_ref), (teacher_in, teacher_ref), (features_in, features_ref))
        )
    ]
    for copy in copies:
        copy.start()
    for copy in copies:
        copy.wait()
    east, size, _ = center_ref.shape
    north = size // upward
    classes = teacher_ref.shape[0]
    wide = (classes + 1) * upward
    row = lax.broadcasted_iota(jnp.int32, (size, north), 0) // upward
    spread = (row == lax.broadcasted_iota(jnp.int32, (size, north), 1)).astype(BF16)
    level = lax.broadcasted_iota(jnp.int32, (size, wide), 0) % upward
    same = level == lax.broadcasted_iota(jnp.int32, (size, wide), 1) % upward
    target = lax.broadcasted_iota(jnp.int32, (wide, LANES), 0) // upward + channels
    gather = (target == lax.broadcasted_iota(jnp.int32, (wide, LANES), 1)).astype(BF16)
    bricks = active_ref.shape
    up = lax.broadcasted_iota(jnp.int32, (upward, north), 0) // (upward // bricks[1])
    along = lax.broadcasted_iota(jnp.int32, (upward, north), 1) // (north // bricks[2])
    for e in range(east):
        mask = jnp.zeros((upward, north), jnp.int32)
        for b in range(bricks[2]):
            for c in range(bricks[1]):
                inside = (along == b) & (up == c)
                mask = jnp.where(inside, active_ref[e // (east // bricks[0]), c, b], mask)
        mask = (mask * occupied_ref[e]).astype(F32)
        field = jnp.concatenate([mask] + [teacher_ref[c, e].astype(F32) for c in range(classes)], 0).astype(BF16)
        everywhere = lax.dot_general(spread, field, (((1,), (1,)), ((), ())), preferred_element_type=F32)
        own = jnp.where(same, everywhere, 0.0).astype(BF16)
        tail = jnp.dot(own, gather, preferred_element_type=F32).astype(BF16)
        center_ref[e, :, 0:channels] = features_ref[e]
        center_ref[e, :, channels:LANES] = tail[:, channels:LANES]
    east_starts = [(1 - flags_ref[r]) * (east - HALO) for r in range(east_rounds)]
    north_starts = [
        pl.multiple_of((1 - flags_ref[2 * east_rounds + r]) * (size - edge), edge) for r in range(north_rounds)
    ]
    edge_refs = iter(edge_refs)
    for e in east_starts:
        next(edge_refs)[...] = center_ref[pl.ds(e, HALO)]
    for n in north_starts:
        next(edge_refs)[...] = center_ref[:, pl.ds(n, edge), :]
    for e in east_starts:
        for n in north_starts:
            next(edge_refs)[...] = center_ref[pl.ds(e, HALO), pl.ds(n, edge), :]


def place_edges(flags_ref, center_ref, edge_refs, east_rounds, north_rounds, edge, x_ref):
    east, size, _ = center_ref.shape
    x_ref[...] = jnp.zeros_like(x_ref)
    x_ref[HALO : HALO + east, edge : edge + size, :] = center_ref[...]
    edge_refs = iter(edge_refs)
    easts = [(flags_ref[r], flags_ref[east_rounds + r]) for r in range(east_rounds)]
    base = 2 * east_rounds
    norths = [(flags_ref[base + r], flags_ref[base + north_rounds + r]) for r in range(north_rounds)]
    middle_east, middle_north = pl.ds(HALO, east), pl.ds(edge, size)
    east_places = [(pl.ds((1 - side) * (east + HALO), HALO), inside) for side, inside in easts]
    north_places = [
        (pl.ds(pl.multiple_of((1 - side) * (size + edge), edge), edge), inside) for side, inside in norths
    ]
    spots = [(e, middle_north, inside) for e, inside in east_places]
    spots += [(middle_east, n, inside) for n, inside in north_places]
    spots += [(e, n, a * b) for e, a in east_places for n, b in north_places]
    for e, n, inside in spots:
        ref = next(edge_refs)

        @pl.when(inside == 1)
        def _(ref=ref, e=e, n=n):
            x_ref[e, n, :] = ref[...]


def whole_kernel(
    channels, classes, east, north, upward, east_rounds, north_rounds,
    flags_ref, ahead1_ref, ahead2_ref, back2_ref, head_ref, center_ref, *refs,
):
    edges = east_rounds + north_rounds + east_rounds * north_rounds
    (
        grad_ref, kept_ref, sent_ref,
        x_ref, s0_ref, s1_ref, sg_ref, mask_ref, slope_ref, turned_ref,
    ) = refs[edges:]
    rows = (north + 2 * HALO) * upward
    low, size = HALO * upward, north * upward
    planes = east + 2 * HALO
    lane = lane_of((rows, LANES))
    rows1, rows2, rows3 = rows - 2 * upward, rows - 4 * upward, rows - 6 * upward
    low1, low2, low3 = low - upward, low - 2 * upward, low - 3 * upward

    place_edges(flags_ref, center_ref, refs[:edges], east_rounds, north_rounds, low, x_ref)
    border = jnp.zeros((upward, LANES), F32)

    for plane in range(planes):
        x = x_ref[plane].astype(F32)
        mask = jnp.broadcast_to(x[:, channels : channels + 1], (rows, LANES))
        mask_ref[plane] = mask
        a0 = jnp.where((mask > 0) & (lane < channels), x, 0.0)
        put_stack(jnp.concatenate([border, a0, border], 0), upward, s0_ref, plane % 2, plane // 2)

    for first, stop in grouped((planes - 2) // 2, 2):
        for i, parity, value in convolve(s0_ref, ahead1_ref, first, stop, rows):
            plane = 2 * i + parity
            mask = mask_ref[plane + 1]
            p1 = mask * value
            sig = jax.nn.sigmoid(p1)
            slope_ref[plane] = mask * (sig * (1.0 + p1 * (1.0 - sig)))
            put_stack((p1 * sig)[upward : upward + rows1], upward, s1_ref, parity, i)

    head = head_ref[...]
    class_lane = (lane[0:rows2] > channels) & (lane[0:rows2] <= channels + classes)
    here = slice(2 * upward, 2 * upward + rows2)

    for first, stop in grouped((planes - 4) // 2, 2):
        for i, parity, value in convolve(s1_ref, ahead2_ref, first, stop, rows2):
            plane = 2 * i + parity
            mask = mask_ref[plane + 2, here]
            p2 = mask * value
            sig = jax.nn.sigmoid(p2)
            a2 = (p2 * sig).astype(BF16)
            logits = lax.dot_general(a2, head, (((1,), (1,)), ((), ())), preferred_element_type=F32)
            g_logits = jnp.where(class_lane, mask * (logits - x_ref[plane + 2, here].astype(F32)), 0.0)
            coarse = g_logits.astype(BF16)
            fine = (g_logits - coarse.astype(F32)).astype(BF16)
            g_a2 = jnp.dot(
                jnp.concatenate([coarse, fine], 1), jnp.concatenate([head, head], 0), preferred_element_type=F32
            )
            g_p2 = mask * g_a2 * (sig * (1.0 + p2 * (1.0 - sig)))
            put_stack(g_p2, upward, sg_ref, parity, i)
            put_turned(turned_ref, g_p2[low2 : low2 + size], plane - 2, east, channels)

    upper = flags_ref[2 * (east_rounds + north_rounds)] == 1
    for t, tile in enumerate(kernel_sum(turned_ref, s1_ref, 3, east, rows2, low2, size, channels)):
        kept_ref[t * channels : (t + 1) * channels, :] = tile.astype(BF16)

    there = slice(2 * upward + upward, 2 * upward + upward + rows3)
    for first, stop in grouped((planes - 6) // 2, 2):
        for i, parity, value in convolve(sg_ref, back2_ref, first, stop, rows3):
            plane = 2 * i + parity
            g_p1 = slope_ref[plane + 2, there] * value
            grad_ref[plane] = g_p1.astype(BF16)
            put_turned(turned_ref, g_p1[low3 : low3 + size], plane - 1, east, channels)

    tiles = kernel_sum(turned_ref, s0_ref, 4, east, rows, low, size, channels)
    for t, tile in enumerate(tiles):
        place = slice(t * channels, (t + 1) * channels)
        first, second = tile.astype(BF16), kept_ref[place, :]
        sent_ref[place, :] = jnp.where(upper, second, first)
        kept_ref[place, :] = jnp.where(upper, first, second)
    filled = len(tiles) * channels
    if filled < kept_ref.shape[0]:
        kept_ref[filled:, :] = jnp.zeros((kept_ref.shape[0] - filled, LANES), BF16)
        sent_ref[filled:, :] = jnp.zeros((kept_ref.shape[0] - filled, LANES), BF16)


def last_kernel(
    channels, east, north, upward,
    center_ref, grad_ref, w1_in, kept_in,
    out_ref, kept_out,
    stack_ref, back1_ref, w1_ref, arrived,
):
    size = north * upward
    copy = pltpu.make_async_copy(w1_in, w1_ref, arrived)
    copy.start()
    for plane in range(east + 2):
        put_stack(grad_ref[plane].astype(F32), upward, stack_ref, plane % 2, plane // 2)
    copy.wait()
    put_back(back1_ref, w1_ref, channels)
    for first, stop in grouped(east // 2, 2):
        for i, parity, value in convolve(stack_ref, back1_ref, first, stop, size):
            plane = 2 * i + parity
            mask = center_ref[plane, :, channels : channels + 1].astype(F32)
            out_ref[plane] = (mask * value)[:, 0:channels].astype(BF16)


def parts_kernel(place_ref, kept_ref, came_ref, total_ref, *sent_refs):
    part = total_ref.shape[0]
    for change, ref in enumerate((total_ref,) + sent_refs):
        start = pl.multiple_of((place_ref[0] ^ change) * part, part)
        rows = pl.ds(start, part)
        ref[...] = (kept_ref[rows, :].astype(F32) + came_ref[rows, :].astype(F32)).astype(ref.dtype)


def unpack_kernel(channels, scale, aliased, first_ref_flag, packed_ref, *refs):
    first_out, second_out, whole_ref, done = refs[2:] if aliased else refs
    spare = LANES - channels
    is_first = first_ref_flag[0] == 1
    spans = [(t, min(t + 4, 27)) for t in range(0, 27, 4)]

    def copy_of(target, i):
        a, b = spans[i]
        return pltpu.make_async_copy(whole_ref.at[a:b], target.at[a:b], done.at[i])

    for i, (t, stop) in enumerate(spans):
        tiles = []
        for r in range(3):
            start = (t // 4 * 3 + r) * channels
            tiles.append(packed_ref[start : start + channels, :].astype(F32) * scale)
        for r in range(3):
            whole_ref[t + r] = tiles[r][:, 0:channels]
        if stop - t == 4:
            lane = lane_of(tiles[0].shape)
            parts = [pltpu.roll(tiles[r], (spare * r - channels) % LANES, 1) for r in range(3)]
            last = jnp.where(lane < spare, parts[0], jnp.where(lane < 2 * spare, parts[1], parts[2]))
            whole_ref[t + 3] = last[:, 0:channels]

        @pl.when(is_first)
        def _(i=i):
            copy_of(first_out, i).start()

        @pl.when(jnp.logical_not(is_first))
        def _(i=i):
            copy_of(second_out, i).start()

    for i in range(len(spans)):
        copy_of(first_out, i).wait()


def per_device(
    features, brick_active, voxel_occupancy, first_weights, second_weights, head, teacher
):
    channels = features.shape[0]
    east, north, upward = features.shape[1:]
    classes = teacher.shape[0]
    devices = lax.axis_size("east") * lax.axis_size("north")
    scale = 1.0 / math.sqrt(devices * east * north * upward)
    planes = east + 2 * HALO
    rows = (north + 2 * HALO) * upward
    edge, size = HALO * upward, north * upward
    vmem = pl.BlockSpec(memory_space=pltpu.VMEM)
    smem = pl.BlockSpec(memory_space=pltpu.SMEM)
    anywhere = pl.BlockSpec(memory_space=pl.ANY)
    far = pl.BlockSpec(memory_space=pltpu.HBM)

    east_bits, north_bits = bits_of("east"), bits_of("north")
    rest = north_bits + east_bits[1:]
    groups = [rest[i : i + 2] for i in range(0, len(rest), 2)]
    upper = high_bit(*east_bits[0])
    easts, norths = rounds_of("east"), rounds_of("north")
    counts = (len(easts), len(norths))
    flags = [side for _, side, _ in easts] + [inside for _, _, inside in easts]
    flags += [side for _, side, _ in norths] + [inside for _, _, inside in norths] + [upper]
    flags = jnp.stack(flags).astype(jnp.int32)

    shapes = [(HALO, size, LANES)] * counts[0] + [(east, edge, LANES)] * counts[1]
    shapes += [(HALO, edge, LANES)] * (counts[0] * counts[1])
    center, *edges = pl.pallas_call(
        functools.partial(prepare_kernel, channels, upward, edge, *counts),
        out_shape=[jax.ShapeDtypeStruct(shape, BF16) for shape in [(east, size, LANES)] + shapes],
        in_specs=[smem] * 2 + [far] * 3,
        out_specs=[vmem] * (1 + len(shapes)),
        scratch_shapes=[
            pltpu.VMEM((east, size, channels), BF16),
            pltpu.VMEM((east, upward, north), jnp.int32),
            pltpu.VMEM((classes, east, upward, north), BF16),
            pltpu.SemaphoreType.DMA((3,)),
        ],
        compiler_params=pltpu.CompilerParams(vmem_limit_bytes=6 * 1024 * 1024),
        name="prepare",
    )(
        flags,
        brick_active.transpose(0, 2, 1),
        pltpu.with_memory_space_constraint(features.transpose(1, 2, 3, 0).reshape(east, size, channels), pltpu.HBM),
        pltpu.with_memory_space_constraint(voxel_occupancy.transpose(0, 2, 1), pltpu.HBM),
        pltpu.with_memory_space_constraint(teacher.transpose(0, 1, 3, 2), pltpu.HBM),
    )
    stay = [list(range(lax.axis_size(axis))) for axis in ("east", "north")]
    routes = [(partners, stay[1]) for partners, _, _ in easts] + [(stay[0], partners) for partners, _, _ in norths]
    routes += [(a, b) for a, _, _ in easts for b, _, _ in norths]
    edges = [exchange(value, *route) for value, route in zip(edges, routes)]

    unit = devices // 2 * 16
    packed = -(-21 * channels // unit) * unit
    shapes = [(4 * WIDE, 2 * LANES)] * 3 + [(LANES, LANES)]
    ahead1, ahead2, back2, head_wide = pl.pallas_call(
        functools.partial(weights_kernel, channels, classes),
        out_shape=[jax.ShapeDtypeStruct(shape, BF16) for shape in shapes],
        in_specs=[far] * 3,
        out_specs=[vmem] * 4,
        scratch_shapes=[
            pltpu.VMEM(first_weights.shape, BF16),
            pltpu.VMEM(second_weights.shape, BF16),
            pltpu.VMEM(head.shape, BF16),
            pltpu.SemaphoreType.DMA((3,)),
        ],
        compiler_params=pltpu.CompilerParams(vmem_limit_bytes=12 * 1024 * 1024),
        name="weights",
    )(*[pltpu.with_memory_space_constraint(value, pltpu.HBM) for value in (first_weights, second_weights, head)])
    grad, kept, sent = pl.pallas_call(
        functools.partial(whole_kernel, channels, classes, east, north, upward, *counts),
        out_shape=(
            jax.ShapeDtypeStruct((east + 2, rows - 6 * upward, LANES), BF16),
            jax.ShapeDtypeStruct((packed, LANES), BF16),
            jax.ShapeDtypeStruct((packed, LANES), BF16),
        ),
        in_specs=[smem] + [vmem] * (5 + len(edges)),
        out_specs=(vmem, vmem, vmem),
        scratch_shapes=[
            pltpu.VMEM((planes, rows, LANES), BF16),
            pltpu.VMEM((2, planes // 2 * rows, WIDE), BF16),
            pltpu.VMEM((2, (planes - 2) // 2 * (rows - 4 * upward), WIDE), BF16),
            pltpu.VMEM((2, (planes - 4) // 2 * (rows - 6 * upward), WIDE), BF16),
            pltpu.VMEM((planes, rows, LANES), F32),
            pltpu.VMEM((planes - 2, rows, LANES), F32),
            pltpu.VMEM((3 * channels, east * size), BF16),
        ],
        compiler_params=pltpu.CompilerParams(vmem_limit_bytes=26 * 1024 * 1024),
        name="fields",
    )(flags, ahead1, ahead2, back2, head_wide, center, *edges)

    features_out = []

    def beside(kept):
        out, kept = pl.pallas_call(
            functools.partial(last_kernel, channels, east, north, upward),
            out_shape=(
                jax.ShapeDtypeStruct((east, size, channels), BF16),
                jax.ShapeDtypeStruct(kept.shape, F32),
            ),
            in_specs=[vmem, vmem, far, anywhere],
            out_specs=(vmem, anywhere),
            input_output_aliases={3: 1},
            scratch_shapes=[
                pltpu.VMEM((2, (east + 2) // 2 * size, WIDE), BF16),
                pltpu.VMEM((4 * WIDE, 2 * LANES), BF16),
                pltpu.VMEM(first_weights.shape, BF16),
                pltpu.SemaphoreType.DMA(()),
            ],
            compiler_params=pltpu.CompilerParams(vmem_limit_bytes=10 * 1024 * 1024),
            name="features",
        )(center, grad, pltpu.with_memory_space_constraint(first_weights, pltpu.HBM), kept)
        features_out.append(out)
        return kept

    ways = 1 << len(groups[0])
    part = packed // ways
    total, *parts = pl.pallas_call(
        parts_kernel,
        out_shape=[jax.ShapeDtypeStruct((part, LANES), F32)]
        + [jax.ShapeDtypeStruct((part, LANES), BF16)] * (ways - 1),
        in_specs=[smem] + [vmem] * 2,
        out_specs=[vmem] * ways,
        compiler_params=pltpu.CompilerParams(vmem_limit_bytes=4 * 1024 * 1024),
        name="parts",
    )(place_in(groups[0]).reshape(1).astype(jnp.int32), kept, swap(sent, east_bits[:1], 1))
    total = beside(total)
    for change in range(1, ways):
        total = total + swap(parts[change - 1], groups[0], change).astype(F32)
    total = scatter_sums(total, groups[1:])
    mine = gather_parts(total.astype(BF16), groups)
    other = swap(mine, east_bits[:1], 1)

    def unpack(is_first, value, *aliased):
        return pl.pallas_call(
            functools.partial(unpack_kernel, channels, scale, bool(aliased)),
            out_shape=(
                jax.ShapeDtypeStruct(first_weights.shape, F32),
                jax.ShapeDtypeStruct(second_weights.shape, F32),
            ),
            in_specs=[smem, vmem] + [anywhere] * len(aliased),
            out_specs=(anywhere, anywhere),
            input_output_aliases={2: 0, 3: 1} if aliased else {},
            scratch_shapes=[pltpu.VMEM(first_weights.shape, F32), pltpu.SemaphoreType.DMA((7,))],
            compiler_params=pltpu.CompilerParams(vmem_limit_bytes=5 * 1024 * 1024),
            name="unpack",
        )(is_first.reshape(1).astype(jnp.int32), value, *aliased)

    outputs = unpack(upper, mine)
    grad_first, grad_second = unpack(1 - upper, other, *outputs)
    (grad_features,) = features_out
    grad_features = grad_features.reshape(east, north, upward, channels).transpose(3, 0, 1, 2)
    return (grad_features, grad_first, grad_second)


def solution(mesh):
    in_specs = (
        P(None, "east", "north", None),
        P("east", "north", None),
        P("east", "north", None),
        P(),
        P(),
        P(),
        P(None, "east", "north", None),
    )
    out_specs = (P(None, "east", "north", None), P(), P())
    return jax.shard_map(
        per_device, mesh=mesh, in_specs=in_specs, out_specs=out_specs, check_vma=False
    )
```

```python
import functools
import math

import jax
import jax.numpy as jnp
from jax import lax
from jax.experimental import pallas as pl
from jax.experimental.pallas import tpu as pltpu
from jax.sharding import PartitionSpec as P

LANES = 128
HALO = 4
OFFSETS = 9
WIDE = OFFSETS * LANES
F32 = jnp.float32
BF16 = jnp.bfloat16


def rounds_of(axis):
    count = lax.axis_size(axis)
    me = lax.axis_index(axis)
    rounds = [([i ^ 1 for i in range(count)], me % 2, jnp.int32(1))]
    if count > 2:
        inside = ((me > 0) & (me < count - 1)).astype(jnp.int32)
        partners = [0] + [((i - 1) ^ 1) + 1 for i in range(1, count - 1)] + [count - 1]
        rounds.append((partners, (me + 1) % 2, inside))
    return rounds


def exchange(value, east, north):
    count = len(north)
    target = {(e, n): (f, m) for e, f in enumerate(east) for n, m in enumerate(north)}
    alone = [place for place, other in target.items() if place == other]
    while alone:
        e, n = alone.pop(0)
        near = [place for place in ((e, n ^ 1), (e ^ 1, n)) if place in alone]
        other = near[0] if near else alone[0]
        alone.remove(other)
        target[e, n], target[other] = other, (e, n)
    pairs = [(e * count + n, f * count + m) for (e, n), (f, m) in target.items()]
    return lax.ppermute(value, ("east", "north"), pairs)


def high_bit(axis, bit):
    return (lax.axis_index(axis) // bit) % 2


def bits_of(axis):
    size = lax.axis_size(axis)
    return [(axis, 1 << i) for i in range(size.bit_length() - 1)]


def place_in(group):
    return sum(high_bit(axis, bit) << i for i, (axis, bit) in enumerate(group))


def swap(value, group, change):
    masks = {"east": 0, "north": 0}
    for i, (axis, bit) in enumerate(group):
        if change >> i & 1:
            masks[axis] |= bit
    partners = [[i ^ masks[axis] for i in range(lax.axis_size(axis))] for axis in ("east", "north")]
    return exchange(value, *partners)


def members_of(group):
    count = lax.axis_size("north")
    found = {}
    for e in range(lax.axis_size("east")):
        for n in range(count):
            here = {"east": e, "north": n}
            place = 0
            for i, (axis, bit) in enumerate(group):
                place |= (1 if here[axis] & bit else 0) << i
                here[axis] &= ~bit
            found.setdefault((here["east"], here["north"]), {})[place] = e * count + n
    return [[places[i] for i in range(len(places))] for places in found.values()]


def all_to_all(value, group):
    ways = 1 << len(group)
    parts = value.reshape(ways, value.shape[0] // ways, LANES)
    return lax.all_to_all(parts, ("east", "north"), 0, 0, axis_index_groups=members_of(group))


def scatter_sums(total, groups):
    for group in groups:
        total = all_to_all(total.astype(BF16), group).astype(F32).sum(0)
    return total


def gather_parts(mine, groups):
    for group in reversed(groups):
        ways = 1 << len(group)
        mine = all_to_all(jnp.concatenate([mine] * ways, 0), group).reshape(-1, LANES)
    return mine


def lane_of(shape):
    return lax.broadcasted_iota(jnp.int32, shape, len(shape) - 1)


def put_stack(value, upward, stack_ref, parity, index):
    total = value.shape[0]
    rows = total - 2 * upward
    cubes = value.reshape(total // upward, upward, LANES)
    level = lax.broadcasted_iota(jnp.int32, cubes.shape, 1)
    below = jnp.where(level == 0, 0.0, pltpu.roll(cubes, 1, 1)).reshape(total, LANES)
    above = jnp.where(level == upward - 1, 0.0, pltpu.roll(cubes, upward - 1, 1)).reshape(total, LANES)
    for up, moved in enumerate((below, value, above)):
        even = moved.astype(BF16)
        shifts = (even[0:rows], moved[upward : upward + rows].astype(BF16), even[2 * upward :])
        for north, shifted in enumerate(shifts):
            lane = (north * 3 + up) * LANES
            stack_ref[parity, pl.ds(index * rows, rows), lane : lane + LANES] = shifted


def grouped(pairs, size):
    count = max(1, pairs // size)
    edges = [pairs * i // count for i in range(count + 1)]
    return list(zip(edges, edges[1:]))


def convolve(stack_ref, weight_ref, first, stop, rows):
    fields = [stack_ref[p % 2, (first + p // 2) * rows : (stop + p // 2) * rows, :] for p in range(4)]
    both = jnp.dot(jnp.concatenate(fields, 1), weight_ref[...], preferred_element_type=F32)
    return [
        (pair, parity, both[(pair - first) * rows : (pair - first + 1) * rows, parity * LANES : (parity + 1) * LANES])
        for pair in range(first, stop)
        for parity in range(2)
    ]


def put_back(back_ref, w_ref, channels):
    back_ref[...] = jnp.zeros_like(back_ref)
    for d in range(3):
        for j in range(OFFSETS):
            for q in range(2):
                start = ((2 - d + q) * OFFSETS + OFFSETS - 1 - j) * LANES
                back_ref[start : start + channels, q * LANES : q * LANES + channels] = w_ref[d * OFFSETS + j]


def put_ahead(ahead_ref, w_ref, channels):
    ahead_ref[...] = jnp.zeros_like(ahead_ref)
    row = lax.broadcasted_iota(jnp.int32, (channels, channels), 0)
    unit = (row == lax.broadcasted_iota(jnp.int32, (channels, channels), 1)).astype(BF16)
    for d in range(3):
        for j in range(OFFSETS):
            value = w_ref[d * OFFSETS + j]
            turned = lax.dot_general(unit, value, (((1,), (1,)), ((), ())), preferred_element_type=F32).astype(BF16)
            for q in range(2):
                start = ((d + q) * OFFSETS + j) * LANES
                ahead_ref[start : start + channels, q * LANES : q * LANES + channels] = turned


def weights_kernel(channels, classes, w1_in, head_in, ahead1_ref, head_out, w1_ref, head_ref, arrived):
    copies = [
        pltpu.make_async_copy(source, target, arrived.at[i])
        for i, (source, target) in enumerate(((w1_in, w1_ref), (head_in, head_ref)))
    ]
    for copy in copies:
        copy.start()
    for copy in copies:
        copy.wait()
    put_ahead(ahead1_ref, w1_ref, channels)
    head_out[...] = jnp.zeros_like(head_out)
    row = lax.broadcasted_iota(jnp.int32, (LANES, classes), 0)
    spread = (row == lax.broadcasted_iota(jnp.int32, (LANES, classes), 1) + channels + 1).astype(BF16)
    head_out[:, 0:channels] = jnp.dot(spread, head_ref[...], preferred_element_type=F32).astype(BF16)


def put_turned(turned_ref, value, plane, east, channels):
    turned = value.T[0:channels].astype(BF16)
    size = value.shape[0]
    for d in range(3):
        e = plane + d - 1
        if 0 <= e < east:
            turned_ref[d * channels : (d + 1) * channels, e * size : (e + 1) * size] = turned


def kernel_sum(turned_ref, stack_ref, first, east, rows, low, size, channels):
    fields = []
    for e in range(first, first + east):
        start = (e // 2) * rows + low
        fields.append(stack_ref[e % 2, start : start + size, :])
    total = jnp.dot(turned_ref[...], jnp.concatenate(fields, 0), preferred_element_type=F32)
    blocks = [
        total[d * channels : (d + 1) * channels, j * LANES : (j + 1) * LANES]
        for d in range(3)
        for j in range(OFFSETS)
    ]
    blocks.append(jnp.zeros_like(blocks[0]))
    lane = lane_of(blocks[0].shape)
    spare = LANES - channels
    tiles = []
    for t in range(0, 28, 4):
        for r in range(3):
            tail = pltpu.roll(blocks[t + 3], channels - spare * r, 1)
            tiles.append(jnp.where(lane < channels, blocks[t + r], tail))
    return tiles


def prepare_kernel(
    channels, upward, edge,
    active_in, features_in, occupied_in, teacher_in,
    center_ref, *edge_refs,
):
    *edge_refs, active_ref, features_ref, occupied_ref, teacher_ref, arrived = edge_refs
    copies = [
        pltpu.make_async_copy(source, target, arrived.at[i])
        for i, (source, target) in enumerate(
            (
                (active_in, active_ref),
                (occupied_in, occupied_ref),
                (teacher_in, teacher_ref),
                (features_in, features_ref),
            )
        )
    ]
    for copy in copies:
        copy.start()
    for copy in copies:
        copy.wait()
    east, size, _ = center_ref.shape
    north = size // upward
    classes = teacher_ref.shape[0]
    wide = (classes + 1) * upward
    row = lax.broadcasted_iota(jnp.int32, (size, north), 0) // upward
    spread = (row == lax.broadcasted_iota(jnp.int32, (size, north), 1)).astype(BF16)
    level = lax.broadcasted_iota(jnp.int32, (size, wide), 0) % upward
    same = level == lax.broadcasted_iota(jnp.int32, (size, wide), 1) % upward
    target = lax.broadcasted_iota(jnp.int32, (wide, LANES), 0) // upward + channels
    gather = (target == lax.broadcasted_iota(jnp.int32, (wide, LANES), 1)).astype(BF16)
    bricks = active_ref.shape
    up = lax.broadcasted_iota(jnp.int32, (upward, north), 0) // (upward // bricks[1])
    along = lax.broadcasted_iota(jnp.int32, (upward, north), 1) // (north // bricks[2])
    for e in range(east):
        mask = jnp.zeros((upward, north), jnp.int32)
        for b in range(bricks[2]):
            for c in range(bricks[1]):
                inside = (along == b) & (up == c)
                mask = jnp.where(inside, active_ref[e // (east // bricks[0]), c, b], mask)
        mask = (mask * occupied_ref[e]).astype(F32)
        goal = teacher_ref[:, e].astype(F32).reshape(classes * upward, north)
        field = jnp.concatenate([mask, goal], 0).astype(BF16)
        everywhere = lax.dot_general(spread, field, (((1,), (1,)), ((), ())), preferred_element_type=F32)
        own = jnp.where(same, everywhere, 0.0).astype(BF16)
        tail = jnp.dot(own, gather, preferred_element_type=F32).astype(BF16)
        center_ref[e, :, 0:channels] = features_ref[e]
        center_ref[e, :, channels:LANES] = tail[:, channels:LANES]
    east_starts = [(1 - side) * (east - HALO) for _, side, _ in rounds_of("east")]
    north_starts = [pl.multiple_of((1 - side) * (size - edge), edge) for _, side, _ in rounds_of("north")]
    edge_refs = iter(edge_refs)
    for e in east_starts:
        next(edge_refs)[...] = center_ref[pl.ds(e, HALO)]
    for n in north_starts:
        next(edge_refs)[...] = center_ref[:, pl.ds(n, edge), :]
    for e in east_starts:
        for n in north_starts:
            next(edge_refs)[...] = center_ref[pl.ds(e, HALO), pl.ds(n, edge), :]


def place_edges(center_ref, edge_refs, edge, x_ref):
    east, size, _ = center_ref.shape
    x_ref[...] = jnp.zeros_like(x_ref)
    x_ref[HALO : HALO + east, edge : edge + size, :] = center_ref[...]
    edge_refs = iter(edge_refs)
    middle_east, middle_north = pl.ds(HALO, east), pl.ds(edge, size)
    east_places = [(pl.ds((1 - side) * (east + HALO), HALO), inside) for _, side, inside in rounds_of("east")]
    north_places = [
        (pl.ds(pl.multiple_of((1 - side) * (size + edge), edge), edge), inside)
        for _, side, inside in rounds_of("north")
    ]
    spots = [(e, middle_north, inside) for e, inside in east_places]
    spots += [(middle_east, n, inside) for n, inside in north_places]
    spots += [(e, n, a * b) for e, a in east_places for n, b in north_places]
    for e, n, inside in spots:
        ref = next(edge_refs)

        @pl.when(inside == 1)
        def _(ref=ref, e=e, n=n):
            x_ref[e, n, :] = ref[...]


def whole_kernel(
    channels, classes, east, north, upward, edges,
    ahead1_ref, w2_in, head_ref, center_ref, *refs,
):
    (
        grad_ref, kept_ref, sent_ref,
        x_ref, s0_ref, s1_ref, sg_ref, mask_ref, slope_ref, turned_ref, ahead2_ref, back2_ref, w2_ref, arrived,
    ) = refs[edges:]
    copy = pltpu.make_async_copy(w2_in, w2_ref, arrived)
    copy.start()
    rows = (north + 2 * HALO) * upward
    low, size = HALO * upward, north * upward
    planes = east + 2 * HALO
    lane = lane_of((rows, LANES))
    rows1, rows2, rows3 = rows - 2 * upward, rows - 4 * upward, rows - 6 * upward
    low1, low2, low3 = low - upward, low - 2 * upward, low - 3 * upward

    place_edges(center_ref, refs[:edges], low, x_ref)
    border = jnp.zeros((upward, LANES), F32)

    for plane in range(planes):
        x = x_ref[plane].astype(F32)
        mask = jnp.broadcast_to(x[:, channels : channels + 1], (rows, LANES))
        mask_ref[plane] = mask
        a0 = jnp.where((mask > 0) & (lane < channels), x, 0.0)
        put_stack(jnp.concatenate([border, a0, border], 0), upward, s0_ref, plane % 2, plane // 2)

    copy.wait()
    put_ahead(ahead2_ref, w2_ref, channels)
    put_back(back2_ref, w2_ref, channels)
    for first, stop in grouped((planes - 2) // 2, 2):
        for i, parity, value in convolve(s0_ref, ahead1_ref, first, stop, rows):
            plane = 2 * i + parity
            mask = mask_ref[plane + 1]
            p1 = mask * value
            sig = jax.nn.sigmoid(p1)
            slope_ref[plane] = mask * (sig * (1.0 + p1 * (1.0 - sig)))
            put_stack((p1 * sig)[upward : upward + rows1], upward, s1_ref, parity, i)

    head = head_ref[...]
    class_lane = (lane[0:rows2] > channels) & (lane[0:rows2] <= channels + classes)
    here = slice(2 * upward, 2 * upward + rows2)

    for first, stop in grouped((planes - 4) // 2, 2):
        for i, parity, value in convolve(s1_ref, ahead2_ref, first, stop, rows2):
            plane = 2 * i + parity
            mask = mask_ref[plane + 2, here]
            p2 = mask * value
            sig = jax.nn.sigmoid(p2)
            a2 = (p2 * sig).astype(BF16)
            logits = lax.dot_general(a2, head, (((1,), (1,)), ((), ())), preferred_element_type=F32)
            g_logits = jnp.where(class_lane, mask * (logits - x_ref[plane + 2, here].astype(F32)), 0.0)
            coarse = g_logits.astype(BF16)
            fine = (g_logits - coarse.astype(F32)).astype(BF16)
            g_a2 = jnp.dot(
                jnp.concatenate([coarse, fine], 1), jnp.concatenate([head, head], 0), preferred_element_type=F32
            )
            g_p2 = mask * g_a2 * (sig * (1.0 + p2 * (1.0 - sig)))
            put_stack(g_p2, upward, sg_ref, parity, i)
            put_turned(turned_ref, g_p2[low2 : low2 + size], plane - 2, east, channels)

    upper = high_bit("east", 1) == 1
    for t, tile in enumerate(kernel_sum(turned_ref, s1_ref, 3, east, rows2, low2, size, channels)):
        kept_ref[t * channels : (t + 1) * channels, :] = tile.astype(BF16)

    there = slice(2 * upward + upward, 2 * upward + upward + rows3)
    for first, stop in grouped((planes - 6) // 2, 2):
        for i, parity, value in convolve(sg_ref, back2_ref, first, stop, rows3):
            plane = 2 * i + parity
            g_p1 = slope_ref[plane + 2, there] * value
            grad_ref[plane] = g_p1.astype(BF16)
            put_turned(turned_ref, g_p1[low3 : low3 + size], plane - 1, east, channels)

    tiles = kernel_sum(turned_ref, s0_ref, 4, east, rows, low, size, channels)
    for t, tile in enumerate(tiles):
        place = slice(t * channels, (t + 1) * channels)
        first, second = tile.astype(BF16), kept_ref[place, :]
        sent_ref[place, :] = jnp.where(upper, second, first)
        kept_ref[place, :] = jnp.where(upper, first, second)
    filled = len(tiles) * channels
    if filled < kept_ref.shape[0]:
        kept_ref[filled:, :] = jnp.zeros((kept_ref.shape[0] - filled, LANES), BF16)
        sent_ref[filled:, :] = jnp.zeros((kept_ref.shape[0] - filled, LANES), BF16)


def last_kernel(
    channels, east, north, upward,
    center_ref, grad_ref, w1_in, kept_in,
    out_ref, kept_out,
    stack_ref, back1_ref, w1_ref, arrived,
):
    size = north * upward
    copy = pltpu.make_async_copy(w1_in, w1_ref, arrived)
    copy.start()
    for plane in range(east + 2):
        put_stack(grad_ref[plane].astype(F32), upward, stack_ref, plane % 2, plane // 2)
    copy.wait()
    put_back(back1_ref, w1_ref, channels)
    for first, stop in grouped(east // 2, 2):
        for i, parity, value in convolve(stack_ref, back1_ref, first, stop, size):
            plane = 2 * i + parity
            mask = center_ref[plane, :, channels : channels + 1].astype(F32)
            out_ref[plane] = (mask * value)[:, 0:channels].astype(BF16)


def parts_kernel(place_ref, kept_ref, came_ref, total_ref, *sent_refs):
    part = total_ref.shape[0]
    for change, ref in enumerate((total_ref,) + sent_refs):
        start = pl.multiple_of((place_ref[0] ^ change) * part, part)
        rows = pl.ds(start, part)
        ref[...] = (kept_ref[rows, :].astype(F32) + came_ref[rows, :].astype(F32)).astype(ref.dtype)


def unpack_kernel(channels, scale, aliased, first_ref_flag, packed_ref, *refs):
    first_out, second_out, whole_ref, done = refs[2:] if aliased else refs
    spare = LANES - channels
    is_first = first_ref_flag[0] == 1
    spans = [(t, min(t + 4, 27)) for t in range(0, 27, 4)]

    def copy_of(target, i):
        a, b = spans[i]
        return pltpu.make_async_copy(whole_ref.at[a:b], target.at[a:b], done.at[i])

    for i, (t, stop) in enumerate(spans):
        tiles = []
        for r in range(3):
            start = (t // 4 * 3 + r) * channels
            tiles.append(packed_ref[start : start + channels, :].astype(F32) * scale)
        for r in range(3):
            whole_ref[t + r] = tiles[r][:, 0:channels]
        if stop - t == 4:
            lane = lane_of(tiles[0].shape)
            parts = [pltpu.roll(tiles[r], (spare * r - channels) % LANES, 1) for r in range(3)]
            last = jnp.where(lane < spare, parts[0], jnp.where(lane < 2 * spare, parts[1], parts[2]))
            whole_ref[t + 3] = last[:, 0:channels]

        @pl.when(is_first)
        def _(i=i):
            copy_of(first_out, i).start()

        @pl.when(jnp.logical_not(is_first))
        def _(i=i):
            copy_of(second_out, i).start()

    for i in range(len(spans)):
        copy_of(first_out, i).wait()


def per_device(
    features, brick_active, voxel_occupancy, first_weights, second_weights, head, teacher
):
    channels = features.shape[0]
    east, north, upward = features.shape[1:]
    classes = teacher.shape[0]
    devices = lax.axis_size("east") * lax.axis_size("north")
    scale = 1.0 / math.sqrt(devices * east * north * upward)
    planes = east + 2 * HALO
    rows = (north + 2 * HALO) * upward
    edge, size = HALO * upward, north * upward
    vmem = pl.BlockSpec(memory_space=pltpu.VMEM)
    smem = pl.BlockSpec(memory_space=pltpu.SMEM)
    anywhere = pl.BlockSpec(memory_space=pl.ANY)
    far = pl.BlockSpec(memory_space=pltpu.HBM)

    east_bits, north_bits = bits_of("east"), bits_of("north")
    rest = north_bits + east_bits[1:]
    groups = [rest[i : i + 2] for i in range(0, len(rest), 2)]
    upper = high_bit(*east_bits[0])
    easts, norths = rounds_of("east"), rounds_of("north")
    counts = (len(easts), len(norths))

    shapes = [(HALO, size, LANES)] * counts[0] + [(east, edge, LANES)] * counts[1]
    shapes += [(HALO, edge, LANES)] * (counts[0] * counts[1])
    center, *edges = pl.pallas_call(
        functools.partial(prepare_kernel, channels, upward, edge),
        out_shape=[jax.ShapeDtypeStruct(shape, BF16) for shape in [(east, size, LANES)] + shapes],
        in_specs=[far] * 4,
        out_specs=[vmem] * (1 + len(shapes)),
        scratch_shapes=[
            pltpu.SMEM((brick_active.shape[0], brick_active.shape[2], brick_active.shape[1]), jnp.int32),
            pltpu.VMEM((east, size, channels), BF16),
            pltpu.VMEM((east, upward, north), jnp.int32),
            pltpu.VMEM((classes, east, upward, north), BF16),
            pltpu.SemaphoreType.DMA((4,)),
        ],
        compiler_params=pltpu.CompilerParams(vmem_limit_bytes=6 * 1024 * 1024),
        name="prepare",
    )(
        *[
            pltpu.with_memory_space_constraint(value, pltpu.HBM)
            for value in (
                brick_active.transpose(0, 2, 1),
                features.transpose(1, 2, 3, 0).reshape(east, size, channels),
                voxel_occupancy.transpose(0, 2, 1),
                teacher.transpose(0, 1, 3, 2),
            )
        ]
    )
    stay = [list(range(lax.axis_size(axis))) for axis in ("east", "north")]
    routes = [(partners, stay[1]) for partners, _, _ in easts] + [(stay[0], partners) for partners, _, _ in norths]
    routes += [(a, b) for a, _, _ in easts for b, _, _ in norths]
    edges = [exchange(value, *route) for value, route in zip(edges, routes)]

    unit = devices // 2 * 16
    packed = -(-21 * channels // unit) * unit
    first_far, second_far, head_far = [
        pltpu.with_memory_space_constraint(value, pltpu.HBM) for value in (first_weights, second_weights, head)
    ]
    ahead1, head_wide = pl.pallas_call(
        functools.partial(weights_kernel, channels, classes),
        out_shape=[jax.ShapeDtypeStruct(shape, BF16) for shape in ((4 * WIDE, 2 * LANES), (LANES, LANES))],
        in_specs=[far] * 2,
        out_specs=[vmem] * 2,
        scratch_shapes=[
            pltpu.VMEM(first_weights.shape, BF16),
            pltpu.VMEM(head.shape, BF16),
            pltpu.SemaphoreType.DMA((2,)),
        ],
        compiler_params=pltpu.CompilerParams(vmem_limit_bytes=6 * 1024 * 1024),
        name="weights",
    )(first_far, head_far)
    grad, kept, sent = pl.pallas_call(
        functools.partial(whole_kernel, channels, classes, east, north, upward, len(edges)),
        out_shape=(
            jax.ShapeDtypeStruct((east + 2, rows - 6 * upward, LANES), BF16),
            jax.ShapeDtypeStruct((packed, LANES), BF16),
            jax.ShapeDtypeStruct((packed, LANES), BF16),
        ),
        in_specs=[vmem, far] + [vmem] * (2 + len(edges)),
        out_specs=(vmem, vmem, vmem),
        scratch_shapes=[
            pltpu.VMEM((planes, rows, LANES), BF16),
            pltpu.VMEM((2, planes // 2 * rows, WIDE), BF16),
            pltpu.VMEM((2, (planes - 2) // 2 * (rows - 4 * upward), WIDE), BF16),
            pltpu.VMEM((2, (planes - 4) // 2 * (rows - 6 * upward), WIDE), BF16),
            pltpu.VMEM((planes, rows, LANES), F32),
            pltpu.VMEM((planes - 2, rows, LANES), F32),
            pltpu.VMEM((3 * channels, east * size), BF16),
            pltpu.VMEM((4 * WIDE, 2 * LANES), BF16),
            pltpu.VMEM((4 * WIDE, 2 * LANES), BF16),
            pltpu.VMEM(second_weights.shape, BF16),
            pltpu.SemaphoreType.DMA(()),
        ],
        compiler_params=pltpu.CompilerParams(vmem_limit_bytes=32 * 1024 * 1024),
        name="fields",
    )(ahead1, second_far, head_wide, center, *edges)

    features_out = []

    def beside(kept):
        out, kept = pl.pallas_call(
            functools.partial(last_kernel, channels, east, north, upward),
            out_shape=(
                jax.ShapeDtypeStruct((east, size, channels), BF16),
                jax.ShapeDtypeStruct(kept.shape, F32),
            ),
            in_specs=[vmem, vmem, far, anywhere],
            out_specs=(vmem, anywhere),
            input_output_aliases={3: 1},
            scratch_shapes=[
                pltpu.VMEM((2, (east + 2) // 2 * size, WIDE), BF16),
                pltpu.VMEM((4 * WIDE, 2 * LANES), BF16),
                pltpu.VMEM(first_weights.shape, BF16),
                pltpu.SemaphoreType.DMA(()),
            ],
            compiler_params=pltpu.CompilerParams(vmem_limit_bytes=10 * 1024 * 1024),
            name="features",
        )(center, grad, first_far, kept)
        features_out.append(out)
        return kept

    ways = 1 << len(groups[0])
    part = packed // ways
    total, *parts = pl.pallas_call(
        parts_kernel,
        out_shape=[jax.ShapeDtypeStruct((part, LANES), F32)]
        + [jax.ShapeDtypeStruct((part, LANES), BF16)] * (ways - 1),
        in_specs=[smem] + [vmem] * 2,
        out_specs=[vmem] * ways,
        compiler_params=pltpu.CompilerParams(vmem_limit_bytes=4 * 1024 * 1024),
        name="parts",
    )(place_in(groups[0]).reshape(1).astype(jnp.int32), kept, swap(sent, east_bits[:1], 1))
    total = beside(total)
    for change in range(1, ways):
        total = total + swap(parts[change - 1], groups[0], change).astype(F32)
    total = scatter_sums(total, groups[1:])
    mine = gather_parts(total.astype(BF16), groups)
    other = swap(mine, east_bits[:1], 1)

    def unpack(is_first, value, *aliased):
        return pl.pallas_call(
            functools.partial(unpack_kernel, channels, scale, bool(aliased)),
            out_shape=(
                jax.ShapeDtypeStruct(first_weights.shape, F32),
                jax.ShapeDtypeStruct(second_weights.shape, F32),
            ),
            in_specs=[smem, vmem] + [anywhere] * len(aliased),
            out_specs=(anywhere, anywhere),
            input_output_aliases={2: 0, 3: 1} if aliased else {},
            scratch_shapes=[pltpu.VMEM(first_weights.shape, F32), pltpu.SemaphoreType.DMA((7,))],
            compiler_params=pltpu.CompilerParams(vmem_limit_bytes=5 * 1024 * 1024),
            name="unpack",
        )(is_first.reshape(1).astype(jnp.int32), value, *aliased)

    outputs = unpack(upper, mine)
    grad_first, grad_second = unpack(1 - upper, other, *outputs)
    (grad_features,) = features_out
    grad_features = grad_features.reshape(east, north, upward, channels).transpose(3, 0, 1, 2)
    return (grad_features, grad_first, grad_second)


def solution(mesh):
    in_specs = (
        P(None, "east", "north", None),
        P("east", "north", None),
        P("east", "north", None),
        P(),
        P(),
        P(),
        P(None, "east", "north", None),
    )
    out_specs = (P(None, "east", "north", None), P(), P())
    return jax.shard_map(
        per_device, mesh=mesh, in_specs=in_specs, out_specs=out_specs, check_vma=False
    )
```

```python
import functools
import math

import jax
import jax.numpy as jnp
from jax import lax
from jax.experimental import pallas as pl
from jax.experimental.pallas import tpu as pltpu
from jax.sharding import PartitionSpec as P

LANES = 128
HALO = 4
OFFSETS = 9
WIDE = OFFSETS * LANES
F32 = jnp.float32
BF16 = jnp.bfloat16


def rounds_of(axis):
    count = lax.axis_size(axis)
    me = lax.axis_index(axis)
    rounds = [([i ^ 1 for i in range(count)], me % 2, jnp.int32(1))]
    if count > 2:
        inside = ((me > 0) & (me < count - 1)).astype(jnp.int32)
        partners = [0] + [((i - 1) ^ 1) + 1 for i in range(1, count - 1)] + [count - 1]
        rounds.append((partners, (me + 1) % 2, inside))
    return rounds


def exchange(value, east, north):
    count = len(north)
    target = {(e, n): (f, m) for e, f in enumerate(east) for n, m in enumerate(north)}
    alone = [place for place, other in target.items() if place == other]
    while alone:
        e, n = alone.pop(0)
        near = [place for place in ((e, n ^ 1), (e ^ 1, n)) if place in alone]
        other = near[0] if near else alone[0]
        alone.remove(other)
        target[e, n], target[other] = other, (e, n)
    pairs = [(e * count + n, f * count + m) for (e, n), (f, m) in target.items()]
    return lax.ppermute(value, ("east", "north"), pairs)


def high_bit(axis, bit):
    return (lax.axis_index(axis) // bit) % 2


def bits_of(axis):
    size = lax.axis_size(axis)
    return [(axis, 1 << i) for i in range(size.bit_length() - 1)]


def place_in(group):
    return sum(high_bit(axis, bit) << i for i, (axis, bit) in enumerate(group))


def swap(value, group, change):
    masks = {"east": 0, "north": 0}
    for i, (axis, bit) in enumerate(group):
        if change >> i & 1:
            masks[axis] |= bit
    partners = [[i ^ masks[axis] for i in range(lax.axis_size(axis))] for axis in ("east", "north")]
    return exchange(value, *partners)


def scatter_sums(total, groups):
    for group in groups:
        ways = 1 << len(group)
        part = total.shape[0] // ways
        place = place_in(group)
        sent = [
            lax.dynamic_slice_in_dim(total, (place ^ change) * part, part, 0).astype(BF16)
            for change in range(1, ways)
        ]
        total = lax.dynamic_slice_in_dim(total, place * part, part, 0)
        for change in range(1, ways):
            total = total + swap(sent[change - 1], group, change).astype(F32)
    return total


def gather_parts(mine, groups):
    for group in reversed(groups):
        ways = 1 << len(group)
        place = place_in(group)
        parts = [mine] + [swap(mine, group, change) for change in range(1, ways)]
        joined = []
        for row in range(ways):
            piece = parts[0]
            for change in range(1, ways):
                piece = jnp.where((place ^ row) == change, parts[change], piece)
            joined.append(piece)
        mine = jnp.concatenate(joined, 0)
    return mine


def lane_of(shape):
    return lax.broadcasted_iota(jnp.int32, shape, len(shape) - 1)


def put_stack(value, upward, stack, parity, index):
    even_ref, odd_ref = stack
    total = value.shape[0]
    rows = total - 2 * upward
    cubes = value.reshape(total // upward, upward, LANES)
    level = lax.broadcasted_iota(jnp.int32, cubes.shape, 1)
    below = jnp.where(level == 0, 0.0, pltpu.roll(cubes, 1, 1)).reshape(total, LANES)
    above = jnp.where(level == upward - 1, 0.0, pltpu.roll(cubes, upward - 1, 1)).reshape(total, LANES)
    for up, moved in enumerate((below, value, above)):
        lanes = slice(up * LANES, (up + 1) * LANES)
        even_ref[parity, index * total : (index + 1) * total, lanes] = moved.astype(BF16)
        odd_ref[parity, index * rows : (index + 1) * rows, lanes] = moved[upward : upward + rows].astype(BF16)


def shifts_of(stack, plane, rows, upward, start, size):
    even_ref, odd_ref = stack
    even = (plane // 2) * (rows + 2 * upward) + start
    odd = (plane // 2) * rows + start
    return jnp.concatenate(
        [
            even_ref[plane % 2, even : even + size, :],
            odd_ref[plane % 2, odd : odd + size, :],
            even_ref[plane % 2, even + 2 * upward : even + 2 * upward + size, :],
        ],
        1,
    )


def stack_shapes(planes, rows, upward):
    return [pltpu.VMEM((2, planes // 2 * (rows + extra), 3 * LANES), BF16) for extra in (2 * upward, 0)]


def grouped(pairs, size):
    count = max(1, pairs // size)
    edges = [pairs * i // count for i in range(count + 1)]
    return list(zip(edges, edges[1:]))


def convolve(stack, weight_ref, first, stop, rows, upward):
    fields = [
        jnp.concatenate([shifts_of(stack, 2 * pair + p, rows, upward, 0, rows) for p in range(4)], 1)
        for pair in range(first, stop)
    ]
    both = jnp.dot(jnp.concatenate(fields, 0), weight_ref[...], preferred_element_type=F32)
    return [
        (pair, parity, both[(pair - first) * rows : (pair - first + 1) * rows, parity * LANES : (parity + 1) * LANES])
        for pair in range(first, stop)
        for parity in range(2)
    ]


def unit_of(channels):
    row = lax.broadcasted_iota(jnp.int32, (channels, LANES), 0)
    return (row == lax.broadcasted_iota(jnp.int32, (channels, LANES), 1)).astype(BF16)


def put_back(back_ref, w_ref, channels):
    unit = unit_of(channels)
    border = jnp.zeros((LANES - channels, channels), BF16)
    for d in range(3):
        for j in range(OFFSETS):
            wide = jnp.concatenate([w_ref[d * OFFSETS + j], border], 0)
            block = jnp.dot(wide, unit, preferred_element_type=F32).astype(BF16)
            for q in range(2):
                row = ((2 - d + q) * OFFSETS + OFFSETS - 1 - j) * LANES
                back_ref[row : row + LANES, q * LANES : (q + 1) * LANES] = block
    put_zeros(back_ref)


def put_zeros(target_ref):
    run = OFFSETS * LANES
    target_ref[0:run, LANES : 2 * LANES] = jnp.zeros((run, LANES), BF16)
    target_ref[3 * run : 4 * run, 0:LANES] = jnp.zeros((run, LANES), BF16)


def put_ahead(ahead_ref, w_ref, channels):
    unit = unit_of(channels)
    border = jnp.zeros((LANES - channels, channels), BF16)
    for d in range(3):
        for j in range(OFFSETS):
            wide = jnp.concatenate([w_ref[d * OFFSETS + j], border], 0)
            turned = lax.dot_general(unit, wide, (((0,), (1,)), ((), ())), preferred_element_type=F32).astype(BF16)
            for q in range(2):
                row = ((d + q) * OFFSETS + j) * LANES
                ahead_ref[row : row + LANES, q * LANES : (q + 1) * LANES] = turned
    put_zeros(ahead_ref)


def weights_kernel(channels, classes, w1_in, head_in, ahead1_ref, head_out, w1_ref, head_ref, arrived):
    copies = [
        pltpu.make_async_copy(source, target, arrived.at[i])
        for i, (source, target) in enumerate(((w1_in, w1_ref), (head_in, head_ref)))
    ]
    for copy in copies:
        copy.start()
    for copy in copies:
        copy.wait()
    put_ahead(ahead1_ref, w1_ref, channels)
    head_out[...] = jnp.zeros_like(head_out)
    row = lax.broadcasted_iota(jnp.int32, (LANES, classes), 0)
    spread = (row == lax.broadcasted_iota(jnp.int32, (LANES, classes), 1) + channels + 1).astype(BF16)
    head_out[:, 0:channels] = jnp.dot(spread, head_ref[...], preferred_element_type=F32).astype(BF16)


def put_turned(turned_ref, value, plane, east, channels):
    turned = value.astype(BF16).T[0:channels]
    size = value.shape[0]
    for d in range(3):
        e = plane + d - 1
        if 0 <= e < east:
            turned_ref[d * channels : (d + 1) * channels, e * size : (e + 1) * size] = turned


def kernel_sum(turned_ref, stack, first, east, rows, upward, low, size, channels):
    fields = [shifts_of(stack, plane, rows, upward, low, size) for plane in range(first, first + east)]
    total = jnp.dot(turned_ref[...], jnp.concatenate(fields, 0), preferred_element_type=F32)
    blocks = [
        total[d * channels : (d + 1) * channels, j * LANES : (j + 1) * LANES]
        for d in range(3)
        for j in range(OFFSETS)
    ]
    blocks.append(jnp.zeros_like(blocks[0]))
    lane = lane_of(blocks[0].shape)
    spare = LANES - channels
    tiles = []
    for t in range(0, 28, 4):
        for r in range(3):
            tail = pltpu.roll(blocks[t + 3], channels - spare * r, 1)
            tiles.append(jnp.where(lane < channels, blocks[t + r], tail))
    return tiles


def prepare_kernel(
    channels, upward, edge,
    active_in, features_in, occupied_in, teacher_in,
    center_ref, *edge_refs,
):
    *edge_refs, active_ref, features_ref, occupied_ref, teacher_ref, arrived = edge_refs
    copies = [
        pltpu.make_async_copy(source, target, arrived.at[i])
        for i, (source, target) in enumerate(
            (
                (active_in, active_ref),
                (occupied_in, occupied_ref),
                (teacher_in, teacher_ref),
                (features_in, features_ref),
            )
        )
    ]
    for copy in copies:
        copy.start()
    for copy in copies[:-1]:
        copy.wait()
    east, size, _ = center_ref.shape
    north = size // upward
    classes = teacher_ref.shape[0]
    wide = (classes + 1) * upward
    row = lax.broadcasted_iota(jnp.int32, (size, north), 0) // upward
    spread = (row == lax.broadcasted_iota(jnp.int32, (size, north), 1)).astype(BF16)
    level = lax.broadcasted_iota(jnp.int32, (size, wide), 0) % upward
    same = level == lax.broadcasted_iota(jnp.int32, (size, wide), 1) % upward
    target = lax.broadcasted_iota(jnp.int32, (wide, LANES), 0) // upward + channels
    gather = (target == lax.broadcasted_iota(jnp.int32, (wide, LANES), 1)).astype(BF16)
    bricks = active_ref.shape
    up = lax.broadcasted_iota(jnp.int32, (upward, north), 0) // (upward // bricks[1])
    along = lax.broadcasted_iota(jnp.int32, (upward, north), 1) // (north // bricks[2])
    for e in range(east):
        mask = jnp.zeros((upward, north), jnp.int32)
        for b in range(bricks[2]):
            for c in range(bricks[1]):
                inside = (along == b) & (up == c)
                mask = jnp.where(inside, active_ref[e // (east // bricks[0]), c, b], mask)
        mask = (mask * occupied_ref[e]).astype(F32)
        goal = teacher_ref[:, e].astype(F32).reshape(classes * upward, north)
        field = jnp.concatenate([mask, goal], 0).astype(BF16)
        everywhere = lax.dot_general(spread, field, (((1,), (1,)), ((), ())), preferred_element_type=F32)
        own = jnp.where(same, everywhere, 0.0).astype(BF16)
        tail = jnp.dot(own, gather, preferred_element_type=F32).astype(BF16)
        center_ref[e, :, channels:LANES] = tail[:, channels:LANES]
    copies[-1].wait()
    center_ref[:, :, 0:channels] = features_ref[...]
    east_starts = [(1 - side) * (east - HALO) for _, side, _ in rounds_of("east")]
    north_starts = [pl.multiple_of((1 - side) * (size - edge), edge) for _, side, _ in rounds_of("north")]
    edge_refs = iter(edge_refs)
    for e in east_starts:
        next(edge_refs)[...] = center_ref[pl.ds(e, HALO)]
    for n in north_starts:
        next(edge_refs)[...] = center_ref[:, pl.ds(n, edge), :]
    for e in east_starts:
        for n in north_starts:
            next(edge_refs)[...] = center_ref[pl.ds(e, HALO), pl.ds(n, edge), :]


def place_edges(center_ref, edge_refs, edge, x_ref):
    east, size, _ = center_ref.shape
    x_ref[...] = jnp.zeros_like(x_ref)
    x_ref[HALO : HALO + east, edge : edge + size, :] = center_ref[...]
    edge_refs = iter(edge_refs)
    middle_east, middle_north = pl.ds(HALO, east), pl.ds(edge, size)
    east_places = [(pl.ds((1 - side) * (east + HALO), HALO), inside) for _, side, inside in rounds_of("east")]
    north_places = [
        (pl.ds(pl.multiple_of((1 - side) * (size + edge), edge), edge), inside)
        for _, side, inside in rounds_of("north")
    ]
    spots = [(e, middle_north, inside) for e, inside in east_places]
    spots += [(middle_east, n, inside) for n, inside in north_places]
    spots += [(e, n, a * b) for e, a in east_places for n, b in north_places]
    for e, n, inside in spots:
        ref = next(edge_refs)

        @pl.when(inside == 1)
        def _(ref=ref, e=e, n=n):
            x_ref[e, n, :] = ref[...]


def whole_kernel(
    channels, classes, east, north, upward, edges,
    ahead1_ref, w2_in, head_ref, center_ref, *refs,
):
    (
        grad_ref, kept_ref, sent_ref,
        x_ref, even0, odd0, even1, odd1, even2, odd2, mask_ref, slope_ref, turned_ref, ahead2_ref, back2_ref, w2_ref, arrived,
    ) = refs[edges:]
    stack0, stack1, stack2 = (even0, odd0), (even1, odd1), (even2, odd2)
    copy = pltpu.make_async_copy(w2_in, w2_ref, arrived)
    copy.start()
    rows = (north + 2 * HALO) * upward
    low, size = HALO * upward, north * upward
    planes = east + 2 * HALO
    lane = lane_of((rows, LANES))
    rows1, rows2, rows3 = rows - 2 * upward, rows - 4 * upward, rows - 6 * upward
    low1, low2, low3 = low - upward, low - 2 * upward, low - 3 * upward

    place_edges(center_ref, refs[:edges], low, x_ref)
    border = jnp.zeros((upward, LANES), F32)

    for plane in range(planes):
        x = x_ref[plane].astype(F32)
        mask = jnp.broadcast_to(x[:, channels : channels + 1], (rows, LANES))
        mask_ref[plane] = mask
        a0 = jnp.where((mask > 0) & (lane < channels), x, 0.0)
        put_stack(jnp.concatenate([border, a0, border], 0), upward, stack0, plane % 2, plane // 2)

    copy.wait()
    put_ahead(ahead2_ref, w2_ref, channels)
    put_back(back2_ref, w2_ref, channels)
    for first, stop in grouped((planes - 2) // 2, 2):
        for i, parity, value in convolve(stack0, ahead1_ref, first, stop, rows, upward):
            plane = 2 * i + parity
            mask = mask_ref[plane + 1]
            p1 = mask * value
            sig = 0.5 * jnp.tanh(0.5 * p1) + 0.5
            slope_ref[plane] = mask * (sig * (1.0 + p1 * (1.0 - sig)))
            put_stack((p1 * sig)[upward : upward + rows1], upward, stack1, parity, i)

    head = head_ref[...]
    class_lane = (lane[0:rows2] > channels) & (lane[0:rows2] <= channels + classes)
    here = slice(2 * upward, 2 * upward + rows2)

    for first, stop in grouped((planes - 4) // 2, 2):
        for i, parity, value in convolve(stack1, ahead2_ref, first, stop, rows2, upward):
            plane = 2 * i + parity
            mask = mask_ref[plane + 2, here]
            p2 = mask * value
            sig = 0.5 * jnp.tanh(0.5 * p2) + 0.5
            a2 = (p2 * sig).astype(BF16)
            logits = lax.dot_general(a2, head, (((1,), (1,)), ((), ())), preferred_element_type=F32)
            g_logits = jnp.where(class_lane, mask * (logits - x_ref[plane + 2, here].astype(F32)), 0.0)
            coarse = g_logits.astype(BF16)
            fine = (g_logits - coarse.astype(F32)).astype(BF16)
            g_a2 = jnp.dot(
                jnp.concatenate([coarse, fine], 1), jnp.concatenate([head, head], 0), preferred_element_type=F32
            )
            g_p2 = mask * g_a2 * (sig * (1.0 + p2 * (1.0 - sig)))
            put_stack(g_p2, upward, stack2, parity, i)
            put_turned(turned_ref, g_p2[low2 : low2 + size], plane - 2, east, channels)

    upper = high_bit("east", 1) == 1
    for t, tile in enumerate(kernel_sum(turned_ref, stack1, 3, east, rows2, upward, low2, size, channels)):
        kept_ref[t * channels : (t + 1) * channels, :] = tile.astype(BF16)

    there = slice(2 * upward + upward, 2 * upward + upward + rows3)
    for first, stop in grouped((planes - 6) // 2, 2):
        for i, parity, value in convolve(stack2, back2_ref, first, stop, rows3, upward):
            plane = 2 * i + parity
            g_p1 = slope_ref[plane + 2, there] * value
            grad_ref[plane] = g_p1.astype(BF16)
            put_turned(turned_ref, g_p1[low3 : low3 + size], plane - 1, east, channels)

    tiles = kernel_sum(turned_ref, stack0, 4, east, rows, upward, low, size, channels)
    for t, tile in enumerate(tiles):
        place = slice(t * channels, (t + 1) * channels)
        first, second = tile.astype(BF16), kept_ref[place, :]
        sent_ref[place, :] = jnp.where(upper, second, first)
        kept_ref[place, :] = jnp.where(upper, first, second)
    filled = len(tiles) * channels
    if filled < kept_ref.shape[0]:
        kept_ref[filled:, :] = jnp.zeros((kept_ref.shape[0] - filled, LANES), BF16)
        sent_ref[filled:, :] = jnp.zeros((kept_ref.shape[0] - filled, LANES), BF16)


def last_kernel(
    channels, east, north, upward,
    center_ref, grad_ref, w1_in, kept_in,
    out_ref, kept_out,
    even_ref, odd_ref, back1_ref, w1_ref, arrived,
):
    size = north * upward
    copy = pltpu.make_async_copy(w1_in, w1_ref, arrived)
    copy.start()
    for plane in range(east + 2):
        put_stack(grad_ref[plane].astype(F32), upward, (even_ref, odd_ref), plane % 2, plane // 2)
    copy.wait()
    put_back(back1_ref, w1_ref, channels)
    for first, stop in grouped(east // 2, 2):
        for i, parity, value in convolve((even_ref, odd_ref), back1_ref, first, stop, size, upward):
            plane = 2 * i + parity
            mask = center_ref[plane, :, channels : channels + 1].astype(F32)
            out_ref[plane] = (mask * value)[:, 0:channels].astype(BF16)


def parts_kernel(place_ref, kept_ref, came_ref, total_ref, *sent_refs):
    part = total_ref.shape[0]
    for change, ref in enumerate((total_ref,) + sent_refs):
        start = pl.multiple_of((place_ref[0] ^ change) * part, part)
        rows = pl.ds(start, part)
        ref[...] = (kept_ref[rows, :].astype(F32) + came_ref[rows, :].astype(F32)).astype(ref.dtype)


def unpack_kernel(channels, scale, aliased, first_ref_flag, packed_ref, *refs):
    first_out, second_out, whole_ref, done = refs[2:] if aliased else refs
    spare = LANES - channels
    is_first = first_ref_flag[0] == 1
    spans = [(t, min(t + 4, 27)) for t in range(0, 27, 4)]

    def copy_of(target, i):
        a, b = spans[i]
        return pltpu.make_async_copy(whole_ref.at[a:b], target.at[a:b], done.at[i])

    for i, (t, stop) in enumerate(spans):
        tiles = []
        for r in range(3):
            start = (t // 4 * 3 + r) * channels
            tiles.append(packed_ref[start : start + channels, :].astype(F32) * scale)
        for r in range(3):
            whole_ref[t + r] = tiles[r][:, 0:channels]
        if stop - t == 4:
            lane = lane_of(tiles[0].shape)
            parts = [pltpu.roll(tiles[r], (spare * r - channels) % LANES, 1) for r in range(3)]
            last = jnp.where(lane < spare, parts[0], jnp.where(lane < 2 * spare, parts[1], parts[2]))
            whole_ref[t + 3] = last[:, 0:channels]

        @pl.when(is_first)
        def _(i=i):
            copy_of(first_out, i).start()

        @pl.when(jnp.logical_not(is_first))
        def _(i=i):
            copy_of(second_out, i).start()

    for i in range(len(spans)):
        copy_of(first_out, i).wait()


def per_device(
    features, brick_active, voxel_occupancy, first_weights, second_weights, head, teacher
):
    channels = features.shape[0]
    east, north, upward = features.shape[1:]
    classes = teacher.shape[0]
    devices = lax.axis_size("east") * lax.axis_size("north")
    scale = 1.0 / math.sqrt(devices * east * north * upward)
    planes = east + 2 * HALO
    rows = (north + 2 * HALO) * upward
    edge, size = HALO * upward, north * upward
    vmem = pl.BlockSpec(memory_space=pltpu.VMEM)
    smem = pl.BlockSpec(memory_space=pltpu.SMEM)
    anywhere = pl.BlockSpec(memory_space=pl.ANY)
    far = pl.BlockSpec(memory_space=pltpu.HBM)

    east_bits, north_bits = bits_of("east"), bits_of("north")
    rest = north_bits + east_bits[1:]
    groups = [rest[i : i + 2] for i in range(0, len(rest), 2)]
    upper = high_bit(*east_bits[0])
    easts, norths = rounds_of("east"), rounds_of("north")
    counts = (len(easts), len(norths))

    shapes = [(HALO, size, LANES)] * counts[0] + [(east, edge, LANES)] * counts[1]
    shapes += [(HALO, edge, LANES)] * (counts[0] * counts[1])
    center, *edges = pl.pallas_call(
        functools.partial(prepare_kernel, channels, upward, edge),
        out_shape=[jax.ShapeDtypeStruct(shape, BF16) for shape in [(east, size, LANES)] + shapes],
        in_specs=[far] * 4,
        out_specs=[vmem] * (1 + len(shapes)),
        scratch_shapes=[
            pltpu.SMEM((brick_active.shape[0], brick_active.shape[2], brick_active.shape[1]), jnp.int32),
            pltpu.VMEM((east, size, channels), BF16),
            pltpu.VMEM((east, upward, north), jnp.int32),
            pltpu.VMEM((classes, east, upward, north), BF16),
            pltpu.SemaphoreType.DMA((4,)),
        ],
        compiler_params=pltpu.CompilerParams(vmem_limit_bytes=6 * 1024 * 1024),
        name="prepare",
    )(
        *[
            pltpu.with_memory_space_constraint(value, pltpu.HBM)
            for value in (
                brick_active.transpose(0, 2, 1),
                features.transpose(1, 2, 3, 0).reshape(east, size, channels),
                voxel_occupancy.transpose(0, 2, 1),
                teacher.transpose(0, 1, 3, 2),
            )
        ]
    )
    stay = [list(range(lax.axis_size(axis))) for axis in ("east", "north")]
    routes = [(partners, stay[1]) for partners, _, _ in easts] + [(stay[0], partners) for partners, _, _ in norths]
    routes += [(a, b) for a, _, _ in easts for b, _, _ in norths]
    edges = [exchange(value, *route) for value, route in zip(edges, routes)]

    unit = devices // 2 * 16
    packed = -(-21 * channels // unit) * unit
    first_far, second_far, head_far = [
        pltpu.with_memory_space_constraint(value, pltpu.HBM) for value in (first_weights, second_weights, head)
    ]
    ahead1, head_wide = pl.pallas_call(
        functools.partial(weights_kernel, channels, classes),
        out_shape=[jax.ShapeDtypeStruct(shape, BF16) for shape in ((4 * WIDE, 2 * LANES), (LANES, LANES))],
        in_specs=[far] * 2,
        out_specs=[vmem] * 2,
        scratch_shapes=[
            pltpu.VMEM(first_weights.shape, BF16),
            pltpu.VMEM(head.shape, BF16),
            pltpu.SemaphoreType.DMA((2,)),
        ],
        compiler_params=pltpu.CompilerParams(vmem_limit_bytes=6 * 1024 * 1024),
        name="weights",
    )(first_far, head_far)
    grad, kept, sent = pl.pallas_call(
        functools.partial(whole_kernel, channels, classes, east, north, upward, len(edges)),
        out_shape=(
            jax.ShapeDtypeStruct((east + 2, rows - 6 * upward, LANES), BF16),
            jax.ShapeDtypeStruct((packed, LANES), BF16),
            jax.ShapeDtypeStruct((packed, LANES), BF16),
        ),
        in_specs=[vmem, far] + [vmem] * (2 + len(edges)),
        out_specs=(vmem, vmem, vmem),
        scratch_shapes=[
            pltpu.VMEM((planes, rows, LANES), BF16),
            *stack_shapes(planes, rows, upward),
            *stack_shapes(planes - 2, rows - 4 * upward, upward),
            *stack_shapes(planes - 4, rows - 6 * upward, upward),
            pltpu.VMEM((planes, rows, LANES), F32),
            pltpu.VMEM((planes - 2, rows, LANES), F32),
            pltpu.VMEM((3 * channels, east * size), BF16),
            pltpu.VMEM((4 * WIDE, 2 * LANES), BF16),
            pltpu.VMEM((4 * WIDE, 2 * LANES), BF16),
            pltpu.VMEM(second_weights.shape, BF16),
            pltpu.SemaphoreType.DMA(()),
        ],
        compiler_params=pltpu.CompilerParams(vmem_limit_bytes=28 * 1024 * 1024),
        name="fields",
    )(ahead1, second_far, head_wide, center, *edges)

    features_out = []

    def beside(kept):
        out, kept = pl.pallas_call(
            functools.partial(last_kernel, channels, east, north, upward),
            out_shape=(
                jax.ShapeDtypeStruct((east, size, channels), BF16),
                jax.ShapeDtypeStruct(kept.shape, F32),
            ),
            in_specs=[vmem, vmem, far, anywhere],
            out_specs=(vmem, anywhere),
            input_output_aliases={3: 1},
            scratch_shapes=[
                *stack_shapes(east + 2, size, upward),
                pltpu.VMEM((4 * WIDE, 2 * LANES), BF16),
                pltpu.VMEM(first_weights.shape, BF16),
                pltpu.SemaphoreType.DMA(()),
            ],
            compiler_params=pltpu.CompilerParams(vmem_limit_bytes=10 * 1024 * 1024),
            name="features",
        )(center, grad, first_far, kept)
        features_out.append(out)
        return kept

    ways = 1 << len(groups[0])
    part = packed // ways
    total, *parts = pl.pallas_call(
        parts_kernel,
        out_shape=[jax.ShapeDtypeStruct((part, LANES), F32)]
        + [jax.ShapeDtypeStruct((part, LANES), BF16)] * (ways - 1),
        in_specs=[smem] + [vmem] * 2,
        out_specs=[vmem] * ways,
        compiler_params=pltpu.CompilerParams(vmem_limit_bytes=4 * 1024 * 1024),
        name="parts",
    )(place_in(groups[0]).reshape(1).astype(jnp.int32), kept, swap(sent, east_bits[:1], 1))
    total = beside(total)
    for change in range(1, ways):
        total = total + swap(parts[change - 1], groups[0], change).astype(F32)
    total = scatter_sums(total, groups[1:])
    mine = gather_parts(total.astype(BF16), groups)
    other = swap(mine, east_bits[:1], 1)

    def unpack(is_first, value, *aliased):
        return pl.pallas_call(
            functools.partial(unpack_kernel, channels, scale, bool(aliased)),
            out_shape=(
                jax.ShapeDtypeStruct(first_weights.shape, F32),
                jax.ShapeDtypeStruct(second_weights.shape, F32),
            ),
            in_specs=[smem, vmem] + [anywhere] * len(aliased),
            out_specs=(anywhere, anywhere),
            input_output_aliases={2: 0, 3: 1} if aliased else {},
            scratch_shapes=[pltpu.VMEM(first_weights.shape, F32), pltpu.SemaphoreType.DMA((7,))],
            compiler_params=pltpu.CompilerParams(vmem_limit_bytes=5 * 1024 * 1024),
            name="unpack",
        )(is_first.reshape(1).astype(jnp.int32), value, *aliased)

    outputs = unpack(upper, mine)
    grad_first, grad_second = unpack(1 - upper, other, *outputs)
    (grad_features,) = features_out
    grad_features = grad_features.reshape(east, north, upward, channels).transpose(3, 0, 1, 2)
    return (grad_features, grad_first, grad_second)


def solution(mesh):
    in_specs = (
        P(None, "east", "north", None),
        P("east", "north", None),
        P("east", "north", None),
        P(),
        P(),
        P(),
        P(None, "east", "north", None),
    )
    out_specs = (P(None, "east", "north", None), P(), P())
    return jax.shard_map(
        per_device, mesh=mesh, in_specs=in_specs, out_specs=out_specs, check_vma=False
    )
```

```python
import functools
import math

import jax
import jax.numpy as jnp
from jax import lax
from jax.experimental import pallas as pl
from jax.experimental.pallas import tpu as pltpu
from jax.sharding import PartitionSpec as P

LANES = 128
HALO = 4
OFFSETS = 9
WIDE = OFFSETS * LANES
F32 = jnp.float32
BF16 = jnp.bfloat16


def rounds_of(axis):
    count = lax.axis_size(axis)
    me = lax.axis_index(axis)
    rounds = [([i ^ 1 for i in range(count)], me % 2, jnp.int32(1))]
    if count > 2:
        inside = ((me > 0) & (me < count - 1)).astype(jnp.int32)
        partners = [0] + [((i - 1) ^ 1) + 1 for i in range(1, count - 1)] + [count - 1]
        rounds.append((partners, (me + 1) % 2, inside))
    return rounds


def exchange(value, east, north):
    count = len(north)
    target = {(e, n): (f, m) for e, f in enumerate(east) for n, m in enumerate(north)}
    alone = [place for place, other in target.items() if place == other]
    while alone:
        e, n = alone.pop(0)
        near = [place for place in ((e, n ^ 1), (e ^ 1, n)) if place in alone]
        other = near[0] if near else alone[0]
        alone.remove(other)
        target[e, n], target[other] = other, (e, n)
    pairs = [(e * count + n, f * count + m) for (e, n), (f, m) in target.items()]
    return lax.ppermute(value, ("east", "north"), pairs)


def high_bit(axis, bit):
    return (lax.axis_index(axis) // bit) % 2


def bits_of(axis):
    size = lax.axis_size(axis)
    return [(axis, 1 << i) for i in range(size.bit_length() - 1)]


def place_in(group):
    return sum(high_bit(axis, bit) << i for i, (axis, bit) in enumerate(group))


def swap(value, group, change):
    masks = {"east": 0, "north": 0}
    for i, (axis, bit) in enumerate(group):
        if change >> i & 1:
            masks[axis] |= bit
    partners = [[i ^ masks[axis] for i in range(lax.axis_size(axis))] for axis in ("east", "north")]
    return exchange(value, *partners)


def share_sums(total, bits):
    total = total.astype(BF16)
    for bit in bits:
        total = (total.astype(F32) + swap(total, [bit], 1).astype(F32)).astype(BF16)
    return total


def gather_parts(mine, groups):
    for group in reversed(groups):
        ways = 1 << len(group)
        place = place_in(group)
        parts = [mine] + [swap(mine, group, change) for change in range(1, ways)]
        joined = []
        for row in range(ways):
            piece = parts[0]
            for change in range(1, ways):
                piece = jnp.where((place ^ row) == change, parts[change], piece)
            joined.append(piece)
        mine = jnp.concatenate(joined, 0)
    return mine


def lane_of(shape):
    return lax.broadcasted_iota(jnp.int32, shape, len(shape) - 1)


def put_stack(value, upward, stack, parity, index):
    even_ref, odd_ref = stack
    total = value.shape[0]
    rows = total - 2 * upward
    cubes = value.reshape(total // upward, upward, LANES)
    level = lax.broadcasted_iota(jnp.int32, cubes.shape, 1)
    below = jnp.where(level == 0, 0.0, pltpu.roll(cubes, 1, 1)).reshape(total, LANES)
    above = jnp.where(level == upward - 1, 0.0, pltpu.roll(cubes, upward - 1, 1)).reshape(total, LANES)
    for up, moved in enumerate((below, value, above)):
        lanes = slice(up * LANES, (up + 1) * LANES)
        even_ref[parity, index * total : (index + 1) * total, lanes] = moved.astype(BF16)
        odd_ref[parity, index * rows : (index + 1) * rows, lanes] = moved[upward : upward + rows].astype(BF16)


def shifts_of(stack, plane, rows, upward, start, size):
    even_ref, odd_ref = stack
    even = (plane // 2) * (rows + 2 * upward) + start
    odd = (plane // 2) * rows + start
    return jnp.concatenate(
        [
            even_ref[plane % 2, even : even + size, :],
            odd_ref[plane % 2, odd : odd + size, :],
            even_ref[plane % 2, even + 2 * upward : even + 2 * upward + size, :],
        ],
        1,
    )


def stack_shapes(planes, rows, upward):
    return [pltpu.VMEM((2, planes // 2 * (rows + extra), 3 * LANES), BF16) for extra in (2 * upward, 0)]


def grouped(pairs, size):
    count = max(1, pairs // size)
    edges = [pairs * i // count for i in range(count + 1)]
    return list(zip(edges, edges[1:]))


def convolve(stack, weight_ref, first, stop, rows, upward):
    fields = [
        jnp.concatenate([shifts_of(stack, 2 * pair + p, rows, upward, 0, rows) for p in range(4)], 1)
        for pair in range(first, stop)
    ]
    both = jnp.dot(jnp.concatenate(fields, 0), weight_ref[...], preferred_element_type=F32)
    return [
        (pair, parity, both[(pair - first) * rows : (pair - first + 1) * rows, parity * LANES : (parity + 1) * LANES])
        for pair in range(first, stop)
        for parity in range(2)
    ]


def unit_of(channels):
    row = lax.broadcasted_iota(jnp.int32, (channels, LANES), 0)
    return (row == lax.broadcasted_iota(jnp.int32, (channels, LANES), 1)).astype(BF16)


def put_back(back_ref, w_ref, channels):
    unit = unit_of(channels)
    border = jnp.zeros((LANES - channels, channels), BF16)
    for d in range(3):
        for j in range(OFFSETS):
            wide = jnp.concatenate([w_ref[d * OFFSETS + j], border], 0)
            block = jnp.dot(wide, unit, preferred_element_type=F32).astype(BF16)
            for q in range(2):
                row = ((2 - d + q) * OFFSETS + OFFSETS - 1 - j) * LANES
                back_ref[row : row + LANES, q * LANES : (q + 1) * LANES] = block
    put_zeros(back_ref)


def put_zeros(target_ref):
    run = OFFSETS * LANES
    target_ref[0:run, LANES : 2 * LANES] = jnp.zeros((run, LANES), BF16)
    target_ref[3 * run : 4 * run, 0:LANES] = jnp.zeros((run, LANES), BF16)


def put_ahead(ahead_ref, w_ref, channels):
    unit = unit_of(channels)
    border = jnp.zeros((LANES - channels, channels), BF16)
    for d in range(3):
        for j in range(OFFSETS):
            wide = jnp.concatenate([w_ref[d * OFFSETS + j], border], 0)
            turned = lax.dot_general(unit, wide, (((0,), (1,)), ((), ())), preferred_element_type=F32).astype(BF16)
            for q in range(2):
                row = ((d + q) * OFFSETS + j) * LANES
                ahead_ref[row : row + LANES, q * LANES : (q + 1) * LANES] = turned
    put_zeros(ahead_ref)


def weights_kernel(channels, classes, w1_in, head_in, ahead1_ref, head_out, w1_ref, head_ref, arrived):
    copies = [
        pltpu.make_async_copy(source, target, arrived.at[i])
        for i, (source, target) in enumerate(((w1_in, w1_ref), (head_in, head_ref)))
    ]
    for copy in copies:
        copy.start()
    for copy in copies:
        copy.wait()
    put_ahead(ahead1_ref, w1_ref, channels)
    head_out[...] = jnp.zeros_like(head_out)
    row = lax.broadcasted_iota(jnp.int32, (LANES, classes), 0)
    spread = (row == lax.broadcasted_iota(jnp.int32, (LANES, classes), 1) + channels + 1).astype(BF16)
    head_out[:, 0:channels] = jnp.dot(spread, head_ref[...], preferred_element_type=F32).astype(BF16)


def put_turned(turned_ref, value, plane, east, channels):
    turned = value.astype(BF16).T[0:channels]
    size = value.shape[0]
    for d in range(3):
        e = plane + d - 1
        if 0 <= e < east:
            turned_ref[d * channels : (d + 1) * channels, e * size : (e + 1) * size] = turned


def kernel_sum(turned_ref, stack, first, east, rows, upward, low, size, channels):
    fields = [shifts_of(stack, plane, rows, upward, low, size) for plane in range(first, first + east)]
    total = jnp.dot(turned_ref[...], jnp.concatenate(fields, 0), preferred_element_type=F32)
    blocks = [
        total[d * channels : (d + 1) * channels, j * LANES : (j + 1) * LANES]
        for d in range(3)
        for j in range(OFFSETS)
    ]
    blocks.append(jnp.zeros_like(blocks[0]))
    lane = lane_of(blocks[0].shape)
    spare = LANES - channels
    tiles = []
    for t in range(0, 28, 4):
        for r in range(3):
            tail = pltpu.roll(blocks[t + 3], channels - spare * r, 1)
            tiles.append(jnp.where(lane < channels, blocks[t + r], tail))
    return tiles


def prepare_kernel(
    channels, upward, edge,
    active_in, features_in, occupied_in, teacher_in,
    center_ref, *edge_refs,
):
    *edge_refs, active_ref, features_ref, occupied_ref, teacher_ref, arrived = edge_refs
    copies = [
        pltpu.make_async_copy(source, target, arrived.at[i])
        for i, (source, target) in enumerate(
            (
                (active_in, active_ref),
                (occupied_in, occupied_ref),
                (teacher_in, teacher_ref),
                (features_in, features_ref),
            )
        )
    ]
    for copy in copies:
        copy.start()
    for copy in copies[:-1]:
        copy.wait()
    east, size, _ = center_ref.shape
    north = size // upward
    classes = teacher_ref.shape[0]
    wide = (classes + 1) * upward
    row = lax.broadcasted_iota(jnp.int32, (size, north), 0) // upward
    spread = (row == lax.broadcasted_iota(jnp.int32, (size, north), 1)).astype(BF16)
    level = lax.broadcasted_iota(jnp.int32, (size, wide), 0) % upward
    same = level == lax.broadcasted_iota(jnp.int32, (size, wide), 1) % upward
    target = lax.broadcasted_iota(jnp.int32, (wide, LANES), 0) // upward + channels
    gather = (target == lax.broadcasted_iota(jnp.int32, (wide, LANES), 1)).astype(BF16)
    bricks = active_ref.shape
    up = lax.broadcasted_iota(jnp.int32, (upward, north), 0) // (upward // bricks[1])
    along = lax.broadcasted_iota(jnp.int32, (upward, north), 1) // (north // bricks[2])
    for e in range(east):
        mask = jnp.zeros((upward, north), jnp.int32)
        for b in range(bricks[2]):
            for c in range(bricks[1]):
                inside = (along == b) & (up == c)
                mask = jnp.where(inside, active_ref[e // (east // bricks[0]), c, b], mask)
        mask = (mask * occupied_ref[e]).astype(F32)
        goal = teacher_ref[:, e].astype(F32).reshape(classes * upward, north)
        field = jnp.concatenate([mask, goal], 0).astype(BF16)
        everywhere = lax.dot_general(spread, field, (((1,), (1,)), ((), ())), preferred_element_type=F32)
        own = jnp.where(same, everywhere, 0.0).astype(BF16)
        tail = jnp.dot(own, gather, preferred_element_type=F32).astype(BF16)
        center_ref[e, :, channels:LANES] = tail[:, channels:LANES]
    copies[-1].wait()
    center_ref[:, :, 0:channels] = features_ref[...]
    east_starts = [(1 - side) * (east - HALO) for _, side, _ in rounds_of("east")]
    north_starts = [pl.multiple_of((1 - side) * (size - edge), edge) for _, side, _ in rounds_of("north")]
    edge_refs = iter(edge_refs)
    for e in east_starts:
        next(edge_refs)[...] = center_ref[pl.ds(e, HALO)]
    for n in north_starts:
        next(edge_refs)[...] = center_ref[:, pl.ds(n, edge), :]
    for e in east_starts:
        for n in north_starts:
            next(edge_refs)[...] = center_ref[pl.ds(e, HALO), pl.ds(n, edge), :]


def place_edges(center_ref, edge_refs, edge, x_ref):
    east, size, _ = center_ref.shape
    x_ref[...] = jnp.zeros_like(x_ref)
    x_ref[HALO : HALO + east, edge : edge + size, :] = center_ref[...]
    edge_refs = iter(edge_refs)
    middle_east, middle_north = pl.ds(HALO, east), pl.ds(edge, size)
    east_places = [(pl.ds((1 - side) * (east + HALO), HALO), inside) for _, side, inside in rounds_of("east")]
    north_places = [
        (pl.ds(pl.multiple_of((1 - side) * (size + edge), edge), edge), inside)
        for _, side, inside in rounds_of("north")
    ]
    spots = [(e, middle_north, inside) for e, inside in east_places]
    spots += [(middle_east, n, inside) for n, inside in north_places]
    spots += [(e, n, a * b) for e, a in east_places for n, b in north_places]
    for e, n, inside in spots:
        ref = next(edge_refs)

        @pl.when(inside == 1)
        def _(ref=ref, e=e, n=n):
            x_ref[e, n, :] = ref[...]


def whole_kernel(
    channels, classes, east, north, upward, edges,
    ahead1_ref, w2_in, head_ref, center_ref, *refs,
):
    (
        grad_ref, kept_ref, sent_ref,
        x_ref, even0, odd0, even1, odd1, even2, odd2, mask_ref, slope_ref, turned_ref, ahead2_ref, back2_ref, w2_ref, arrived,
    ) = refs[edges:]
    stack0, stack1, stack2 = (even0, odd0), (even1, odd1), (even2, odd2)
    copy = pltpu.make_async_copy(w2_in, w2_ref, arrived)
    copy.start()
    rows = (north + 2 * HALO) * upward
    low, size = HALO * upward, north * upward
    planes = east + 2 * HALO
    lane = lane_of((rows, LANES))
    rows1, rows2, rows3 = rows - 2 * upward, rows - 4 * upward, rows - 6 * upward
    low1, low2, low3 = low - upward, low - 2 * upward, low - 3 * upward

    place_edges(center_ref, refs[:edges], low, x_ref)
    border = jnp.zeros((upward, LANES), F32)

    for plane in range(planes):
        x = x_ref[plane].astype(F32)
        mask = jnp.broadcast_to(x[:, channels : channels + 1], (rows, LANES))
        mask_ref[plane] = mask
        a0 = jnp.where((mask > 0) & (lane < channels), x, 0.0)
        put_stack(jnp.concatenate([border, a0, border], 0), upward, stack0, plane % 2, plane // 2)

    copy.wait()
    put_ahead(ahead2_ref, w2_ref, channels)
    put_back(back2_ref, w2_ref, channels)
    for first, stop in grouped((planes - 2) // 2, 3):
        for i, parity, value in convolve(stack0, ahead1_ref, first, stop, rows, upward):
            plane = 2 * i + parity
            mask = mask_ref[plane + 1]
            p1 = mask * value
            sig = 0.5 * jnp.tanh(0.5 * p1) + 0.5
            slope_ref[plane] = mask * (sig * (1.0 + p1 * (1.0 - sig)))
            put_stack((p1 * sig)[upward : upward + rows1], upward, stack1, parity, i)

    head = head_ref[...]
    class_lane = (lane[0:rows2] > channels) & (lane[0:rows2] <= channels + classes)
    here = slice(2 * upward, 2 * upward + rows2)

    for first, stop in grouped((planes - 4) // 2, 3):
        for i, parity, value in convolve(stack1, ahead2_ref, first, stop, rows2, upward):
            plane = 2 * i + parity
            mask = mask_ref[plane + 2, here]
            p2 = mask * value
            sig = 0.5 * jnp.tanh(0.5 * p2) + 0.5
            a2 = (p2 * sig).astype(BF16)
            logits = lax.dot_general(a2, head, (((1,), (1,)), ((), ())), preferred_element_type=F32)
            g_logits = jnp.where(class_lane, mask * (logits - x_ref[plane + 2, here].astype(F32)), 0.0)
            coarse = g_logits.astype(BF16)
            fine = (g_logits - coarse.astype(F32)).astype(BF16)
            g_a2 = jnp.dot(
                jnp.concatenate([coarse, fine], 1), jnp.concatenate([head, head], 0), preferred_element_type=F32
            )
            g_p2 = mask * g_a2 * (sig * (1.0 + p2 * (1.0 - sig)))
            put_stack(g_p2, upward, stack2, parity, i)
            put_turned(turned_ref, g_p2[low2 : low2 + size], plane - 2, east, channels)

    upper = high_bit("east", 1) == 1
    for t, tile in enumerate(kernel_sum(turned_ref, stack1, 3, east, rows2, upward, low2, size, channels)):
        kept_ref[t * channels : (t + 1) * channels, :] = tile.astype(BF16)

    there = slice(2 * upward + upward, 2 * upward + upward + rows3)
    for first, stop in grouped((planes - 6) // 2, 3):
        for i, parity, value in convolve(stack2, back2_ref, first, stop, rows3, upward):
            plane = 2 * i + parity
            g_p1 = slope_ref[plane + 2, there] * value
            grad_ref[plane] = g_p1.astype(BF16)
            put_turned(turned_ref, g_p1[low3 : low3 + size], plane - 1, east, channels)

    tiles = kernel_sum(turned_ref, stack0, 4, east, rows, upward, low, size, channels)
    for t, tile in enumerate(tiles):
        place = slice(t * channels, (t + 1) * channels)
        first, second = tile.astype(BF16), kept_ref[place, :]
        sent_ref[place, :] = jnp.where(upper, second, first)
        kept_ref[place, :] = jnp.where(upper, first, second)
    filled = len(tiles) * channels
    if filled < kept_ref.shape[0]:
        kept_ref[filled:, :] = jnp.zeros((kept_ref.shape[0] - filled, LANES), BF16)
        sent_ref[filled:, :] = jnp.zeros((kept_ref.shape[0] - filled, LANES), BF16)


def last_kernel(
    channels, east, north, upward,
    center_ref, grad_ref, w1_in, kept_in,
    out_ref, kept_out,
    even_ref, odd_ref, back1_ref, w1_ref, arrived,
):
    size = north * upward
    copy = pltpu.make_async_copy(w1_in, w1_ref, arrived)
    copy.start()
    for plane in range(east + 2):
        put_stack(grad_ref[plane].astype(F32), upward, (even_ref, odd_ref), plane % 2, plane // 2)
    copy.wait()
    put_back(back1_ref, w1_ref, channels)
    for first, stop in grouped(east // 2, 4):
        for i, parity, value in convolve((even_ref, odd_ref), back1_ref, first, stop, size, upward):
            plane = 2 * i + parity
            mask = center_ref[plane, :, channels : channels + 1].astype(F32)
            out_ref[plane] = (mask * value)[:, 0:channels].astype(BF16)


def parts_kernel(place_ref, kept_ref, came_ref, total_ref, *sent_refs):
    part = total_ref.shape[0]
    for change, ref in enumerate((total_ref,) + sent_refs):
        start = pl.multiple_of((place_ref[0] ^ change) * part, part)
        rows = pl.ds(start, part)
        ref[...] = (kept_ref[rows, :].astype(F32) + came_ref[rows, :].astype(F32)).astype(ref.dtype)


def unpack_kernel(channels, scale, aliased, first_ref_flag, packed_ref, *refs):
    first_out, second_out, whole_ref, done = refs[2:] if aliased else refs
    spare = LANES - channels
    is_first = first_ref_flag[0] == 1
    spans = [(t, min(t + 4, 27)) for t in range(0, 27, 4)]

    def copy_of(target, i):
        a, b = spans[i]
        return pltpu.make_async_copy(whole_ref.at[a:b], target.at[a:b], done.at[i])

    for i, (t, stop) in enumerate(spans):
        tiles = []
        for r in range(3):
            start = (t // 4 * 3 + r) * channels
            tiles.append(packed_ref[start : start + channels, :].astype(F32) * scale)
        for r in range(3):
            whole_ref[t + r] = tiles[r][:, 0:channels]
        if stop - t == 4:
            lane = lane_of(tiles[0].shape)
            parts = [pltpu.roll(tiles[r], (spare * r - channels) % LANES, 1) for r in range(3)]
            last = jnp.where(lane < spare, parts[0], jnp.where(lane < 2 * spare, parts[1], parts[2]))
            whole_ref[t + 3] = last[:, 0:channels]

        @pl.when(is_first)
        def _(i=i):
            copy_of(first_out, i).start()

        @pl.when(jnp.logical_not(is_first))
        def _(i=i):
            copy_of(second_out, i).start()

    for i in range(len(spans)):
        copy_of(first_out, i).wait()


def per_device(
    features, brick_active, voxel_occupancy, first_weights, second_weights, head, teacher
):
    channels = features.shape[0]
    east, north, upward = features.shape[1:]
    classes = teacher.shape[0]
    devices = lax.axis_size("east") * lax.axis_size("north")
    scale = 1.0 / math.sqrt(devices * east * north * upward)
    planes = east + 2 * HALO
    rows = (north + 2 * HALO) * upward
    edge, size = HALO * upward, north * upward
    vmem = pl.BlockSpec(memory_space=pltpu.VMEM)
    smem = pl.BlockSpec(memory_space=pltpu.SMEM)
    anywhere = pl.BlockSpec(memory_space=pl.ANY)
    far = pl.BlockSpec(memory_space=pltpu.HBM)

    east_bits, north_bits = bits_of("east"), bits_of("north")
    rest = north_bits + east_bits[1:]
    near, others = rest[:2], rest[2:]
    upper = high_bit(*east_bits[0])
    easts, norths = rounds_of("east"), rounds_of("north")
    counts = (len(easts), len(norths))

    shapes = [(HALO, size, LANES)] * counts[0] + [(east, edge, LANES)] * counts[1]
    shapes += [(HALO, edge, LANES)] * (counts[0] * counts[1])
    center, *edges = pl.pallas_call(
        functools.partial(prepare_kernel, channels, upward, edge),
        out_shape=[jax.ShapeDtypeStruct(shape, BF16) for shape in [(east, size, LANES)] + shapes],
        in_specs=[far] * 4,
        out_specs=[vmem] * (1 + len(shapes)),
        scratch_shapes=[
            pltpu.SMEM((brick_active.shape[0], brick_active.shape[2], brick_active.shape[1]), jnp.int32),
            pltpu.VMEM((east, size, channels), BF16),
            pltpu.VMEM((east, upward, north), jnp.int32),
            pltpu.VMEM((classes, east, upward, north), BF16),
            pltpu.SemaphoreType.DMA((4,)),
        ],
        compiler_params=pltpu.CompilerParams(vmem_limit_bytes=6 * 1024 * 1024),
        name="prepare",
    )(
        *[
            pltpu.with_memory_space_constraint(value, pltpu.HBM)
            for value in (
                brick_active.transpose(0, 2, 1),
                features.transpose(1, 2, 3, 0).reshape(east, size, channels),
                voxel_occupancy.transpose(0, 2, 1),
                teacher.transpose(0, 1, 3, 2),
            )
        ]
    )
    stay = [list(range(lax.axis_size(axis))) for axis in ("east", "north")]
    routes = [(partners, stay[1]) for partners, _, _ in easts] + [(stay[0], partners) for partners, _, _ in norths]
    routes += [(a, b) for a, _, _ in easts for b, _, _ in norths]
    edges = [exchange(value, *route) for value, route in zip(edges, routes)]

    unit = devices // 2 * 16
    packed = -(-21 * channels // unit) * unit
    first_far, second_far, head_far = [
        pltpu.with_memory_space_constraint(value, pltpu.HBM) for value in (first_weights, second_weights, head)
    ]
    ahead1, head_wide = pl.pallas_call(
        functools.partial(weights_kernel, channels, classes),
        out_shape=[jax.ShapeDtypeStruct(shape, BF16) for shape in ((4 * WIDE, 2 * LANES), (LANES, LANES))],
        in_specs=[far] * 2,
        out_specs=[vmem] * 2,
        scratch_shapes=[
            pltpu.VMEM(first_weights.shape, BF16),
            pltpu.VMEM(head.shape, BF16),
            pltpu.SemaphoreType.DMA((2,)),
        ],
        compiler_params=pltpu.CompilerParams(vmem_limit_bytes=6 * 1024 * 1024),
        name="weights",
    )(first_far, head_far)
    grad, kept, sent = pl.pallas_call(
        functools.partial(whole_kernel, channels, classes, east, north, upward, len(edges)),
        out_shape=(
            jax.ShapeDtypeStruct((east + 2, rows - 6 * upward, LANES), BF16),
            jax.ShapeDtypeStruct((packed, LANES), BF16),
            jax.ShapeDtypeStruct((packed, LANES), BF16),
        ),
        in_specs=[vmem, far] + [vmem] * (2 + len(edges)),
        out_specs=(vmem, vmem, vmem),
        scratch_shapes=[
            pltpu.VMEM((planes, rows, LANES), BF16),
            *stack_shapes(planes, rows, upward),
            *stack_shapes(planes - 2, rows - 4 * upward, upward),
            *stack_shapes(planes - 4, rows - 6 * upward, upward),
            pltpu.VMEM((planes, rows, LANES), F32),
            pltpu.VMEM((planes - 2, rows, LANES), F32),
            pltpu.VMEM((3 * channels, east * size), BF16),
            pltpu.VMEM((4 * WIDE, 2 * LANES), BF16),
            pltpu.VMEM((4 * WIDE, 2 * LANES), BF16),
            pltpu.VMEM(second_weights.shape, BF16),
            pltpu.SemaphoreType.DMA(()),
        ],
        compiler_params=pltpu.CompilerParams(vmem_limit_bytes=28 * 1024 * 1024),
        name="fields",
    )(ahead1, second_far, head_wide, center, *edges)

    features_out = []

    def beside(kept):
        out, kept = pl.pallas_call(
            functools.partial(last_kernel, channels, east, north, upward),
            out_shape=(
                jax.ShapeDtypeStruct((east, size, channels), BF16),
                jax.ShapeDtypeStruct(kept.shape, F32),
            ),
            in_specs=[vmem, vmem, far, anywhere],
            out_specs=(vmem, anywhere),
            input_output_aliases={3: 1},
            scratch_shapes=[
                *stack_shapes(east + 2, size, upward),
                pltpu.VMEM((4 * WIDE, 2 * LANES), BF16),
                pltpu.VMEM(first_weights.shape, BF16),
                pltpu.SemaphoreType.DMA(()),
            ],
            compiler_params=pltpu.CompilerParams(vmem_limit_bytes=10 * 1024 * 1024),
            name="features",
        )(center, grad, first_far, kept)
        features_out.append(out)
        return kept

    ways = 1 << len(near)
    part = packed // ways
    total, *parts = pl.pallas_call(
        parts_kernel,
        out_shape=[jax.ShapeDtypeStruct((part, LANES), F32)]
        + [jax.ShapeDtypeStruct((part, LANES), BF16)] * (ways - 1),
        in_specs=[smem] + [vmem] * 2,
        out_specs=[vmem] * ways,
        compiler_params=pltpu.CompilerParams(vmem_limit_bytes=4 * 1024 * 1024),
        name="parts",
    )(place_in(near).reshape(1).astype(jnp.int32), kept, swap(sent, east_bits[:1], 1))
    total = beside(total)
    for change in range(1, ways):
        total = total + swap(parts[change - 1], near, change).astype(F32)
    mine = gather_parts(share_sums(total, others), [near])
    other = swap(mine, east_bits[:1], 1)

    def unpack(is_first, value, *aliased):
        return pl.pallas_call(
            functools.partial(unpack_kernel, channels, scale, bool(aliased)),
            out_shape=(
                jax.ShapeDtypeStruct(first_weights.shape, F32),
                jax.ShapeDtypeStruct(second_weights.shape, F32),
            ),
            in_specs=[smem, vmem] + [anywhere] * len(aliased),
            out_specs=(anywhere, anywhere),
            input_output_aliases={2: 0, 3: 1} if aliased else {},
            scratch_shapes=[pltpu.VMEM(first_weights.shape, F32), pltpu.SemaphoreType.DMA((7,))],
            compiler_params=pltpu.CompilerParams(vmem_limit_bytes=5 * 1024 * 1024),
            name="unpack",
        )(is_first.reshape(1).astype(jnp.int32), value, *aliased)

    outputs = unpack(upper, mine)
    grad_first, grad_second = unpack(1 - upper, other, *outputs)
    (grad_features,) = features_out
    grad_features = grad_features.reshape(east, north, upward, channels).transpose(3, 0, 1, 2)
    return (grad_features, grad_first, grad_second)


def solution(mesh):
    in_specs = (
        P(None, "east", "north", None),
        P("east", "north", None),
        P("east", "north", None),
        P(),
        P(),
        P(),
        P(None, "east", "north", None),
    )
    out_specs = (P(None, "east", "north", None), P(), P())
    return jax.shard_map(
        per_device, mesh=mesh, in_specs=in_specs, out_specs=out_specs, check_vma=False
    )
```

```python
import functools
import math

import jax
import jax.numpy as jnp
from jax import lax
from jax.experimental import pallas as pl
from jax.experimental.pallas import tpu as pltpu
from jax.sharding import PartitionSpec as P

LANES = 128
HALO = 4
OFFSETS = 9
WIDE = OFFSETS * LANES
F32 = jnp.float32
BF16 = jnp.bfloat16


def rounds_of(axis):
    count = lax.axis_size(axis)
    me = lax.axis_index(axis)
    rounds = [([i ^ 1 for i in range(count)], me % 2, jnp.int32(1))]
    if count > 2:
        inside = ((me > 0) & (me < count - 1)).astype(jnp.int32)
        partners = [0] + [((i - 1) ^ 1) + 1 for i in range(1, count - 1)] + [count - 1]
        rounds.append((partners, (me + 1) % 2, inside))
    return rounds


def exchange(value, east, north):
    count = len(north)
    target = {(e, n): (f, m) for e, f in enumerate(east) for n, m in enumerate(north)}
    alone = [place for place, other in target.items() if place == other]
    while alone:
        e, n = alone.pop(0)
        near = [place for place in ((e, n ^ 1), (e ^ 1, n)) if place in alone]
        other = near[0] if near else alone[0]
        alone.remove(other)
        target[e, n], target[other] = other, (e, n)
    pairs = [(e * count + n, f * count + m) for (e, n), (f, m) in target.items()]
    return lax.ppermute(value, ("east", "north"), pairs)


def high_bit(axis, bit):
    return (lax.axis_index(axis) // bit) % 2


def bits_of(axis):
    size = lax.axis_size(axis)
    return [(axis, 1 << i) for i in range(size.bit_length() - 1)]


def place_in(group):
    return sum(high_bit(axis, bit) << i for i, (axis, bit) in enumerate(group))


def swap(value, group, change):
    masks = {"east": 0, "north": 0}
    for i, (axis, bit) in enumerate(group):
        if change >> i & 1:
            masks[axis] |= bit
    partners = [[i ^ masks[axis] for i in range(lax.axis_size(axis))] for axis in ("east", "north")]
    return exchange(value, *partners)


def share_sums(total, bits):
    total = total.astype(BF16)
    for bit in bits:
        total = (total.astype(F32) + swap(total, [bit], 1).astype(F32)).astype(BF16)
    return total


def gather_parts(mine, groups):
    for group in reversed(groups):
        ways = 1 << len(group)
        place = place_in(group)
        parts = [mine] + [swap(mine, group, change) for change in range(1, ways)]
        joined = []
        for row in range(ways):
            piece = parts[0]
            for change in range(1, ways):
                piece = jnp.where((place ^ row) == change, parts[change], piece)
            joined.append(piece)
        mine = jnp.concatenate(joined, 0)
    return mine


def lane_of(shape):
    return lax.broadcasted_iota(jnp.int32, shape, len(shape) - 1)


def put_stack(value, upward, stack, parity, index):
    even_ref, odd_ref = stack
    total = value.shape[0]
    rows = total - 2 * upward
    cubes = value.reshape(total // upward, upward, LANES)
    level = lax.broadcasted_iota(jnp.int32, cubes.shape, 1)
    below = jnp.where(level == 0, 0.0, pltpu.roll(cubes, 1, 1)).reshape(total, LANES)
    above = jnp.where(level == upward - 1, 0.0, pltpu.roll(cubes, upward - 1, 1)).reshape(total, LANES)
    for up, moved in enumerate((below, value, above)):
        lanes = slice(up * LANES, (up + 1) * LANES)
        even_ref[parity, index * total : (index + 1) * total, lanes] = moved.astype(BF16)
        odd_ref[parity, index * rows : (index + 1) * rows, lanes] = moved[upward : upward + rows].astype(BF16)


def shifts_of(stack, plane, rows, upward, start, size):
    even_ref, odd_ref = stack
    even = (plane // 2) * (rows + 2 * upward) + start
    odd = (plane // 2) * rows + start
    return jnp.concatenate(
        [
            even_ref[plane % 2, even : even + size, :],
            odd_ref[plane % 2, odd : odd + size, :],
            even_ref[plane % 2, even + 2 * upward : even + 2 * upward + size, :],
        ],
        1,
    )


def stack_shapes(planes, rows, upward):
    return [pltpu.VMEM((2, planes // 2 * (rows + extra), 3 * LANES), BF16) for extra in (2 * upward, 0)]


def grouped(pairs, size):
    count = max(1, pairs // size)
    edges = [pairs * i // count for i in range(count + 1)]
    return list(zip(edges, edges[1:]))


def convolve(stack, weight_ref, first, stop, rows, upward):
    fields = [
        jnp.concatenate([shifts_of(stack, 2 * pair + p, rows, upward, 0, rows) for p in range(4)], 1)
        for pair in range(first, stop)
    ]
    both = jnp.dot(jnp.concatenate(fields, 0), weight_ref[...], preferred_element_type=F32)
    return [
        (pair, parity, both[(pair - first) * rows : (pair - first + 1) * rows, parity * LANES : (parity + 1) * LANES])
        for pair in range(first, stop)
        for parity in range(2)
    ]


def unit_of(channels):
    row = lax.broadcasted_iota(jnp.int32, (channels, LANES), 0)
    return (row == lax.broadcasted_iota(jnp.int32, (channels, LANES), 1)).astype(BF16)


def put_back(back_ref, w_ref, channels):
    unit = unit_of(channels)
    border = jnp.zeros((LANES - channels, channels), BF16)
    for d in range(3):
        for j in range(OFFSETS):
            wide = jnp.concatenate([w_ref[d * OFFSETS + j], border], 0)
            block = jnp.dot(wide, unit, preferred_element_type=F32).astype(BF16)
            for q in range(2):
                row = ((2 - d + q) * OFFSETS + OFFSETS - 1 - j) * LANES
                back_ref[row : row + LANES, q * LANES : (q + 1) * LANES] = block
    put_zeros(back_ref)


def put_zeros(target_ref):
    run = OFFSETS * LANES
    target_ref[0:run, LANES : 2 * LANES] = jnp.zeros((run, LANES), BF16)
    target_ref[3 * run : 4 * run, 0:LANES] = jnp.zeros((run, LANES), BF16)


def put_ahead(ahead_ref, w_ref, channels):
    unit = unit_of(channels)
    border = jnp.zeros((LANES - channels, channels), BF16)
    for d in range(3):
        for j in range(OFFSETS):
            wide = jnp.concatenate([w_ref[d * OFFSETS + j], border], 0)
            turned = lax.dot_general(unit, wide, (((0,), (1,)), ((), ())), preferred_element_type=F32).astype(BF16)
            for q in range(2):
                row = ((d + q) * OFFSETS + j) * LANES
                ahead_ref[row : row + LANES, q * LANES : (q + 1) * LANES] = turned
    put_zeros(ahead_ref)


def weights_kernel(channels, classes, w1_in, head_in, ahead1_ref, head_out, w1_ref, head_ref, arrived):
    copies = [
        pltpu.make_async_copy(source, target, arrived.at[i])
        for i, (source, target) in enumerate(((w1_in, w1_ref), (head_in, head_ref)))
    ]
    for copy in copies:
        copy.start()
    for copy in copies:
        copy.wait()
    put_ahead(ahead1_ref, w1_ref, channels)
    head_out[...] = jnp.zeros_like(head_out)
    row = lax.broadcasted_iota(jnp.int32, (LANES, classes), 0)
    spread = (row == lax.broadcasted_iota(jnp.int32, (LANES, classes), 1) + channels + 1).astype(BF16)
    head_out[:, 0:channels] = jnp.dot(spread, head_ref[...], preferred_element_type=F32).astype(BF16)


def put_turned(turned_ref, value, plane, east, channels):
    turned = value.astype(BF16).T[0:channels]
    size = value.shape[0]
    for d in range(3):
        e = plane + d - 1
        if 0 <= e < east:
            turned_ref[d * channels : (d + 1) * channels, e * size : (e + 1) * size] = turned


def kernel_sum(turned_ref, stack, first, east, rows, upward, low, size, channels):
    fields = [shifts_of(stack, plane, rows, upward, low, size) for plane in range(first, first + east)]
    total = jnp.dot(turned_ref[...], jnp.concatenate(fields, 0), preferred_element_type=F32)
    blocks = [
        total[d * channels : (d + 1) * channels, j * LANES : (j + 1) * LANES]
        for d in range(3)
        for j in range(OFFSETS)
    ]
    blocks.append(jnp.zeros_like(blocks[0]))
    lane = lane_of(blocks[0].shape)
    spare = LANES - channels
    tiles = []
    for t in range(0, 28, 4):
        for r in range(3):
            tail = pltpu.roll(blocks[t + 3], channels - spare * r, 1)
            tiles.append(jnp.where(lane < channels, blocks[t + r], tail))
    return tiles


def prepare_kernel(
    channels, upward, edge,
    active_in, features_in, occupied_in, teacher_in,
    center_ref, *edge_refs,
):
    *edge_refs, active_ref, features_ref, occupied_ref, teacher_ref, arrived = edge_refs
    copies = [
        pltpu.make_async_copy(source, target, arrived.at[i])
        for i, (source, target) in enumerate(
            (
                (active_in, active_ref),
                (occupied_in, occupied_ref),
                (teacher_in, teacher_ref),
                (features_in, features_ref),
            )
        )
    ]
    for copy in copies:
        copy.start()
    for copy in copies[:-1]:
        copy.wait()
    east, size, _ = center_ref.shape
    north = size // upward
    classes = teacher_ref.shape[0]
    wide = (classes + 1) * upward
    row = lax.broadcasted_iota(jnp.int32, (size, north), 0) // upward
    spread = (row == lax.broadcasted_iota(jnp.int32, (size, north), 1)).astype(BF16)
    level = lax.broadcasted_iota(jnp.int32, (size, wide), 0) % upward
    same = level == lax.broadcasted_iota(jnp.int32, (size, wide), 1) % upward
    target = lax.broadcasted_iota(jnp.int32, (wide, LANES), 0) // upward + channels
    gather = (target == lax.broadcasted_iota(jnp.int32, (wide, LANES), 1)).astype(BF16)
    bricks = active_ref.shape
    up = lax.broadcasted_iota(jnp.int32, (upward, north), 0) // (upward // bricks[1])
    along = lax.broadcasted_iota(jnp.int32, (upward, north), 1) // (north // bricks[2])
    for e in range(east):
        mask = jnp.zeros((upward, north), jnp.int32)
        for b in range(bricks[2]):
            for c in range(bricks[1]):
                inside = (along == b) & (up == c)
                mask = jnp.where(inside, active_ref[e // (east // bricks[0]), c, b], mask)
        mask = (mask * occupied_ref[e]).astype(F32)
        goal = teacher_ref[:, e].astype(F32).reshape(classes * upward, north)
        field = jnp.concatenate([mask, goal], 0).astype(BF16)
        everywhere = lax.dot_general(spread, field, (((1,), (1,)), ((), ())), preferred_element_type=F32)
        own = jnp.where(same, everywhere, 0.0).astype(BF16)
        tail = jnp.dot(own, gather, preferred_element_type=F32).astype(BF16)
        center_ref[e, :, channels:LANES] = tail[:, channels:LANES]
    copies[-1].wait()
    center_ref[:, :, 0:channels] = features_ref[...]
    east_starts = [(1 - side) * (east - HALO) for _, side, _ in rounds_of("east")]
    north_starts = [pl.multiple_of((1 - side) * (size - edge), edge) for _, side, _ in rounds_of("north")]
    edge_refs = iter(edge_refs)
    for e in east_starts:
        next(edge_refs)[...] = center_ref[pl.ds(e, HALO)]
    for n in north_starts:
        next(edge_refs)[...] = center_ref[:, pl.ds(n, edge), :]
    for e in east_starts:
        for n in north_starts:
            next(edge_refs)[...] = center_ref[pl.ds(e, HALO), pl.ds(n, edge), :]


def place_edges(center_ref, edge_refs, edge, x_ref):
    east, size, _ = center_ref.shape
    x_ref[...] = jnp.zeros_like(x_ref)
    x_ref[HALO : HALO + east, edge : edge + size, :] = center_ref[...]
    edge_refs = iter(edge_refs)
    middle_east, middle_north = pl.ds(HALO, east), pl.ds(edge, size)
    east_places = [(pl.ds((1 - side) * (east + HALO), HALO), inside) for _, side, inside in rounds_of("east")]
    north_places = [
        (pl.ds(pl.multiple_of((1 - side) * (size + edge), edge), edge), inside)
        for _, side, inside in rounds_of("north")
    ]
    spots = [(e, middle_north, inside) for e, inside in east_places]
    spots += [(middle_east, n, inside) for n, inside in north_places]
    spots += [(e, n, a * b) for e, a in east_places for n, b in north_places]
    for e, n, inside in spots:
        ref = next(edge_refs)

        @pl.when(inside == 1)
        def _(ref=ref, e=e, n=n):
            x_ref[e, n, :] = ref[...]


def whole_kernel(
    channels, classes, east, north, upward, edges,
    ahead1_ref, w2_in, head_ref, center_ref, *refs,
):
    (
        grad_ref, kept_ref, sent_ref,
        x_ref, even0, odd0, even1, odd1, even2, odd2, mask_ref, slope_ref, turned_ref, ahead2_ref, back2_ref, w2_ref, arrived,
    ) = refs[edges:]
    stack0, stack1, stack2 = (even0, odd0), (even1, odd1), (even2, odd2)
    copy = pltpu.make_async_copy(w2_in, w2_ref, arrived)
    copy.start()
    rows = (north + 2 * HALO) * upward
    low, size = HALO * upward, north * upward
    planes = east + 2 * HALO
    lane = lane_of((rows, LANES))
    rows1, rows2, rows3 = rows - 2 * upward, rows - 4 * upward, rows - 6 * upward
    low1, low2, low3 = low - upward, low - 2 * upward, low - 3 * upward

    place_edges(center_ref, refs[:edges], low, x_ref)
    border = jnp.zeros((upward, LANES), F32)

    for plane in range(planes):
        x = x_ref[plane].astype(F32)
        mask = jnp.broadcast_to(x[:, channels : channels + 1], (rows, LANES))
        mask_ref[plane] = mask
        a0 = jnp.where((mask > 0) & (lane < channels), x, 0.0)
        put_stack(jnp.concatenate([border, a0, border], 0), upward, stack0, plane % 2, plane // 2)

    copy.wait()
    put_ahead(ahead2_ref, w2_ref, channels)
    put_back(back2_ref, w2_ref, channels)
    for first, stop in grouped((planes - 2) // 2, 1):
        for i, parity, value in convolve(stack0, ahead1_ref, first, stop, rows, upward):
            plane = 2 * i + parity
            mask = mask_ref[plane + 1]
            p1 = mask * value
            sig = 0.5 * jnp.tanh(0.5 * p1) + 0.5
            slope_ref[plane] = mask * (sig * (1.0 + p1 * (1.0 - sig)))
            put_stack((p1 * sig)[upward : upward + rows1], upward, stack1, parity, i)

    head = head_ref[...]
    class_lane = (lane[0:rows2] > channels) & (lane[0:rows2] <= channels + classes)
    here = slice(2 * upward, 2 * upward + rows2)

    for first, stop in grouped((planes - 4) // 2, 1):
        for i, parity, value in convolve(stack1, ahead2_ref, first, stop, rows2, upward):
            plane = 2 * i + parity
            mask = mask_ref[plane + 2, here]
            p2 = mask * value
            sig = 0.5 * jnp.tanh(0.5 * p2) + 0.5
            a2 = (p2 * sig).astype(BF16)
            logits = lax.dot_general(a2, head, (((1,), (1,)), ((), ())), preferred_element_type=F32)
            g_logits = jnp.where(class_lane, mask * (logits - x_ref[plane + 2, here].astype(F32)), 0.0)
            coarse = g_logits.astype(BF16)
            fine = (g_logits - coarse.astype(F32)).astype(BF16)
            g_a2 = jnp.dot(
                jnp.concatenate([coarse, fine], 1), jnp.concatenate([head, head], 0), preferred_element_type=F32
            )
            g_p2 = mask * g_a2 * (sig * (1.0 + p2 * (1.0 - sig)))
            put_stack(g_p2, upward, stack2, parity, i)
            put_turned(turned_ref, g_p2[low2 : low2 + size], plane - 2, east, channels)

    upper = high_bit("east", 1) == 1
    for t, tile in enumerate(kernel_sum(turned_ref, stack1, 3, east, rows2, upward, low2, size, channels)):
        kept_ref[t * channels : (t + 1) * channels, :] = tile.astype(BF16)

    there = slice(2 * upward + upward, 2 * upward + upward + rows3)
    for first, stop in grouped((planes - 6) // 2, 1):
        for i, parity, value in convolve(stack2, back2_ref, first, stop, rows3, upward):
            plane = 2 * i + parity
            g_p1 = slope_ref[plane + 2, there] * value
            grad_ref[plane] = g_p1.astype(BF16)
            put_turned(turned_ref, g_p1[low3 : low3 + size], plane - 1, east, channels)

    tiles = kernel_sum(turned_ref, stack0, 4, east, rows, upward, low, size, channels)
    for t, tile in enumerate(tiles):
        place = slice(t * channels, (t + 1) * channels)
        first, second = tile.astype(BF16), kept_ref[place, :]
        sent_ref[place, :] = jnp.where(upper, second, first)
        kept_ref[place, :] = jnp.where(upper, first, second)
    filled = len(tiles) * channels
    if filled < kept_ref.shape[0]:
        kept_ref[filled:, :] = jnp.zeros((kept_ref.shape[0] - filled, LANES), BF16)
        sent_ref[filled:, :] = jnp.zeros((kept_ref.shape[0] - filled, LANES), BF16)


def last_kernel(
    channels, east, north, upward,
    center_ref, grad_ref, w1_in, kept_in,
    out_ref, kept_out,
    even_ref, odd_ref, back1_ref, w1_ref, arrived,
):
    size = north * upward
    copy = pltpu.make_async_copy(w1_in, w1_ref, arrived)
    copy.start()
    for plane in range(east + 2):
        put_stack(grad_ref[plane].astype(F32), upward, (even_ref, odd_ref), plane % 2, plane // 2)
    copy.wait()
    put_back(back1_ref, w1_ref, channels)
    for first, stop in grouped(east // 2, 4):
        for i, parity, value in convolve((even_ref, odd_ref), back1_ref, first, stop, size, upward):
            plane = 2 * i + parity
            mask = center_ref[plane, :, channels : channels + 1].astype(F32)
            out_ref[plane] = (mask * value)[:, 0:channels].astype(BF16)


def parts_kernel(place_ref, kept_ref, came_ref, total_ref, *sent_refs):
    part = total_ref.shape[0]
    for change, ref in enumerate((total_ref,) + sent_refs):
        start = pl.multiple_of((place_ref[0] ^ change) * part, part)
        rows = pl.ds(start, part)
        ref[...] = (kept_ref[rows, :].astype(F32) + came_ref[rows, :].astype(F32)).astype(ref.dtype)


def unpack_kernel(channels, scale, aliased, first_ref_flag, packed_ref, *refs):
    first_out, second_out, whole_ref, done = refs[2:] if aliased else refs
    spare = LANES - channels
    is_first = first_ref_flag[0] == 1
    spans = [(t, min(t + 4, 27)) for t in range(0, 27, 4)]

    def copy_of(target, i):
        a, b = spans[i]
        return pltpu.make_async_copy(whole_ref.at[a:b], target.at[a:b], done.at[i])

    for i, (t, stop) in enumerate(spans):
        tiles = []
        for r in range(3):
            start = (t // 4 * 3 + r) * channels
            tiles.append(packed_ref[start : start + channels, :].astype(F32) * scale)
        for r in range(3):
            whole_ref[t + r] = tiles[r][:, 0:channels]
        if stop - t == 4:
            lane = lane_of(tiles[0].shape)
            parts = [pltpu.roll(tiles[r], (spare * r - channels) % LANES, 1) for r in range(3)]
            last = jnp.where(lane < spare, parts[0], jnp.where(lane < 2 * spare, parts[1], parts[2]))
            whole_ref[t + 3] = last[:, 0:channels]

        @pl.when(is_first)
        def _(i=i):
            copy_of(first_out, i).start()

        @pl.when(jnp.logical_not(is_first))
        def _(i=i):
            copy_of(second_out, i).start()

    for i in range(len(spans)):
        copy_of(first_out, i).wait()


def per_device(
    features, brick_active, voxel_occupancy, first_weights, second_weights, head, teacher
):
    channels = features.shape[0]
    east, north, upward = features.shape[1:]
    classes = teacher.shape[0]
    devices = lax.axis_size("east") * lax.axis_size("north")
    scale = 1.0 / math.sqrt(devices * east * north * upward)
    planes = east + 2 * HALO
    rows = (north + 2 * HALO) * upward
    edge, size = HALO * upward, north * upward
    vmem = pl.BlockSpec(memory_space=pltpu.VMEM)
    smem = pl.BlockSpec(memory_space=pltpu.SMEM)
    anywhere = pl.BlockSpec(memory_space=pl.ANY)
    far = pl.BlockSpec(memory_space=pltpu.HBM)

    east_bits, north_bits = bits_of("east"), bits_of("north")
    rest = north_bits + east_bits[1:]
    near, others = rest[:2], rest[2:]
    upper = high_bit(*east_bits[0])
    easts, norths = rounds_of("east"), rounds_of("north")
    counts = (len(easts), len(norths))

    shapes = [(HALO, size, LANES)] * counts[0] + [(east, edge, LANES)] * counts[1]
    shapes += [(HALO, edge, LANES)] * (counts[0] * counts[1])
    center, *edges = pl.pallas_call(
        functools.partial(prepare_kernel, channels, upward, edge),
        out_shape=[jax.ShapeDtypeStruct(shape, BF16) for shape in [(east, size, LANES)] + shapes],
        in_specs=[far] * 4,
        out_specs=[vmem] * (1 + len(shapes)),
        scratch_shapes=[
            pltpu.SMEM((brick_active.shape[0], brick_active.shape[2], brick_active.shape[1]), jnp.int32),
            pltpu.VMEM((east, size, channels), BF16),
            pltpu.VMEM((east, upward, north), jnp.int32),
            pltpu.VMEM((classes, east, upward, north), BF16),
            pltpu.SemaphoreType.DMA((4,)),
        ],
        compiler_params=pltpu.CompilerParams(vmem_limit_bytes=6 * 1024 * 1024),
        name="prepare",
    )(
        *[
            pltpu.with_memory_space_constraint(value, pltpu.HBM)
            for value in (
                brick_active.transpose(0, 2, 1),
                features.transpose(1, 2, 3, 0).reshape(east, size, channels),
                voxel_occupancy.transpose(0, 2, 1),
                teacher.transpose(0, 1, 3, 2),
            )
        ]
    )
    stay = [list(range(lax.axis_size(axis))) for axis in ("east", "north")]
    routes = [(partners, stay[1]) for partners, _, _ in easts] + [(stay[0], partners) for partners, _, _ in norths]
    routes += [(a, b) for a, _, _ in easts for b, _, _ in norths]
    edges = [exchange(value, *route) for value, route in zip(edges, routes)]

    unit = devices // 2 * 16
    packed = -(-21 * channels // unit) * unit
    first_far, second_far, head_far = [
        pltpu.with_memory_space_constraint(value, pltpu.HBM) for value in (first_weights, second_weights, head)
    ]
    ahead1, head_wide = pl.pallas_call(
        functools.partial(weights_kernel, channels, classes),
        out_shape=[jax.ShapeDtypeStruct(shape, BF16) for shape in ((4 * WIDE, 2 * LANES), (LANES, LANES))],
        in_specs=[far] * 2,
        out_specs=[vmem] * 2,
        scratch_shapes=[
            pltpu.VMEM(first_weights.shape, BF16),
            pltpu.VMEM(head.shape, BF16),
            pltpu.SemaphoreType.DMA((2,)),
        ],
        compiler_params=pltpu.CompilerParams(vmem_limit_bytes=6 * 1024 * 1024),
        name="weights",
    )(first_far, head_far)
    grad, kept, sent = pl.pallas_call(
        functools.partial(whole_kernel, channels, classes, east, north, upward, len(edges)),
        out_shape=(
            jax.ShapeDtypeStruct((east + 2, rows - 6 * upward, LANES), BF16),
            jax.ShapeDtypeStruct((packed, LANES), BF16),
            jax.ShapeDtypeStruct((packed, LANES), BF16),
        ),
        in_specs=[vmem, far] + [vmem] * (2 + len(edges)),
        out_specs=(vmem, vmem, vmem),
        scratch_shapes=[
            pltpu.VMEM((planes, rows, LANES), BF16),
            *stack_shapes(planes, rows, upward),
            *stack_shapes(planes - 2, rows - 4 * upward, upward),
            *stack_shapes(planes - 4, rows - 6 * upward, upward),
            pltpu.VMEM((planes, rows, LANES), F32),
            pltpu.VMEM((planes - 2, rows, LANES), F32),
            pltpu.VMEM((3 * channels, east * size), BF16),
            pltpu.VMEM((4 * WIDE, 2 * LANES), BF16),
            pltpu.VMEM((4 * WIDE, 2 * LANES), BF16),
            pltpu.VMEM(second_weights.shape, BF16),
            pltpu.SemaphoreType.DMA(()),
        ],
        compiler_params=pltpu.CompilerParams(vmem_limit_bytes=28 * 1024 * 1024),
        name="fields",
    )(ahead1, second_far, head_wide, center, *edges)

    features_out = []

    def beside(kept):
        out, kept = pl.pallas_call(
            functools.partial(last_kernel, channels, east, north, upward),
            out_shape=(
                jax.ShapeDtypeStruct((east, size, channels), BF16),
                jax.ShapeDtypeStruct(kept.shape, F32),
            ),
            in_specs=[vmem, vmem, far, anywhere],
            out_specs=(vmem, anywhere),
            input_output_aliases={3: 1},
            scratch_shapes=[
                *stack_shapes(east + 2, size, upward),
                pltpu.VMEM((4 * WIDE, 2 * LANES), BF16),
                pltpu.VMEM(first_weights.shape, BF16),
                pltpu.SemaphoreType.DMA(()),
            ],
            compiler_params=pltpu.CompilerParams(vmem_limit_bytes=10 * 1024 * 1024),
            name="features",
        )(center, grad, first_far, kept)
        features_out.append(out)
        return kept

    ways = 1 << len(near)
    part = packed // ways
    total, *parts = pl.pallas_call(
        parts_kernel,
        out_shape=[jax.ShapeDtypeStruct((part, LANES), F32)]
        + [jax.ShapeDtypeStruct((part, LANES), BF16)] * (ways - 1),
        in_specs=[smem] + [vmem] * 2,
        out_specs=[vmem] * ways,
        compiler_params=pltpu.CompilerParams(vmem_limit_bytes=4 * 1024 * 1024),
        name="parts",
    )(place_in(near).reshape(1).astype(jnp.int32), kept, swap(sent, east_bits[:1], 1))
    total = beside(total)
    for change in range(1, ways):
        total = total + swap(parts[change - 1], near, change).astype(F32)
    mine = gather_parts(share_sums(total, others), [near])
    other = swap(mine, east_bits[:1], 1)

    def unpack(is_first, value, *aliased):
        return pl.pallas_call(
            functools.partial(unpack_kernel, channels, scale, bool(aliased)),
            out_shape=(
                jax.ShapeDtypeStruct(first_weights.shape, F32),
                jax.ShapeDtypeStruct(second_weights.shape, F32),
            ),
            in_specs=[smem, vmem] + [anywhere] * len(aliased),
            out_specs=(anywhere, anywhere),
            input_output_aliases={2: 0, 3: 1} if aliased else {},
            scratch_shapes=[pltpu.VMEM(first_weights.shape, F32), pltpu.SemaphoreType.DMA((7,))],
            compiler_params=pltpu.CompilerParams(vmem_limit_bytes=5 * 1024 * 1024),
            name="unpack",
        )(is_first.reshape(1).astype(jnp.int32), value, *aliased)

    outputs = unpack(upper, mine)
    grad_first, grad_second = unpack(1 - upper, other, *outputs)
    (grad_features,) = features_out
    grad_features = grad_features.reshape(east, north, upward, channels).transpose(3, 0, 1, 2)
    return (grad_features, grad_first, grad_second)


def solution(mesh):
    in_specs = (
        P(None, "east", "north", None),
        P("east", "north", None),
        P("east", "north", None),
        P(),
        P(),
        P(),
        P(None, "east", "north", None),
    )
    out_specs = (P(None, "east", "north", None), P(), P())
    return jax.shard_map(
        per_device, mesh=mesh, in_specs=in_specs, out_specs=out_specs, check_vma=False
    )
```

```python
import functools
import math

import jax
import jax.numpy as jnp
from jax import lax
from jax.experimental import pallas as pl
from jax.experimental.pallas import tpu as pltpu
from jax.sharding import PartitionSpec as P

LANES = 128
HALO = 4
OFFSETS = 9
WIDE = OFFSETS * LANES
F32 = jnp.float32
BF16 = jnp.bfloat16


def rounds_of(axis):
    count = lax.axis_size(axis)
    me = lax.axis_index(axis)
    rounds = [([i ^ 1 for i in range(count)], me % 2, jnp.int32(1))]
    if count > 2:
        inside = ((me > 0) & (me < count - 1)).astype(jnp.int32)
        partners = [0] + [((i - 1) ^ 1) + 1 for i in range(1, count - 1)] + [count - 1]
        rounds.append((partners, (me + 1) % 2, inside))
    return rounds


def exchange(value, east, north):
    count = len(north)
    target = {(e, n): (f, m) for e, f in enumerate(east) for n, m in enumerate(north)}
    alone = [place for place, other in target.items() if place == other]
    while alone:
        e, n = alone.pop(0)
        near = [place for place in ((e, n ^ 1), (e ^ 1, n)) if place in alone]
        other = near[0] if near else alone[0]
        alone.remove(other)
        target[e, n], target[other] = other, (e, n)
    pairs = [(e * count + n, f * count + m) for (e, n), (f, m) in target.items()]
    return lax.ppermute(value, ("east", "north"), pairs)


def high_bit(axis, bit):
    return (lax.axis_index(axis) // bit) % 2


def bits_of(axis):
    size = lax.axis_size(axis)
    return [(axis, 1 << i) for i in range(size.bit_length() - 1)]


def place_in(group):
    return sum(high_bit(axis, bit) << i for i, (axis, bit) in enumerate(group))


def swap(value, group, change):
    masks = {"east": 0, "north": 0}
    for i, (axis, bit) in enumerate(group):
        if change >> i & 1:
            masks[axis] |= bit
    partners = [[i ^ masks[axis] for i in range(lax.axis_size(axis))] for axis in ("east", "north")]
    return exchange(value, *partners)


def share_sums(total, bits):
    total = total.astype(BF16)
    for bit in bits:
        total = (total.astype(F32) + swap(total, [bit], 1).astype(F32)).astype(BF16)
    return total


def gather_parts(mine, groups):
    for group in reversed(groups):
        ways = 1 << len(group)
        place = place_in(group)
        parts = [mine] + [swap(mine, group, change) for change in range(1, ways)]
        joined = []
        for row in range(ways):
            piece = parts[0]
            for change in range(1, ways):
                piece = jnp.where((place ^ row) == change, parts[change], piece)
            joined.append(piece)
        mine = jnp.concatenate(joined, 0)
    return mine


def lane_of(shape):
    return lax.broadcasted_iota(jnp.int32, shape, len(shape) - 1)


def put_stack(value, upward, stack, parity, index):
    even_ref, odd_ref = stack
    total = value.shape[0]
    rows = total - 2 * upward
    cubes = value.reshape(total // upward, upward, LANES)
    level = lax.broadcasted_iota(jnp.int32, cubes.shape, 1)
    below = jnp.where(level == 0, 0.0, pltpu.roll(cubes, 1, 1)).reshape(total, LANES)
    above = jnp.where(level == upward - 1, 0.0, pltpu.roll(cubes, upward - 1, 1)).reshape(total, LANES)
    for up, moved in enumerate((below, value, above)):
        lanes = slice(up * LANES, (up + 1) * LANES)
        even_ref[parity, index * total : (index + 1) * total, lanes] = moved.astype(BF16)
        odd_ref[parity, index * rows : (index + 1) * rows, lanes] = moved[upward : upward + rows].astype(BF16)


def shifts_of(stack, plane, rows, upward, start, size):
    even_ref, odd_ref = stack
    even = (plane // 2) * (rows + 2 * upward) + start
    odd = (plane // 2) * rows + start
    return jnp.concatenate(
        [
            even_ref[plane % 2, even : even + size, :],
            odd_ref[plane % 2, odd : odd + size, :],
            even_ref[plane % 2, even + 2 * upward : even + 2 * upward + size, :],
        ],
        1,
    )


def stack_shapes(planes, rows, upward):
    return [pltpu.VMEM((2, planes // 2 * (rows + extra), 3 * LANES), BF16) for extra in (2 * upward, 0)]


def grouped(pairs, size):
    count = max(1, pairs // size)
    edges = [pairs * i // count for i in range(count + 1)]
    return list(zip(edges, edges[1:]))


def convolve(stack, weight_ref, first, stop, rows, upward):
    fields = [
        jnp.concatenate([shifts_of(stack, 2 * pair + p, rows, upward, 0, rows) for p in range(4)], 1)
        for pair in range(first, stop)
    ]
    both = jnp.dot(jnp.concatenate(fields, 0), weight_ref[...], preferred_element_type=F32)
    return [
        (pair, parity, both[(pair - first) * rows : (pair - first + 1) * rows, parity * LANES : (parity + 1) * LANES])
        for pair in range(first, stop)
        for parity in range(2)
    ]


def unit_of(channels):
    row = lax.broadcasted_iota(jnp.int32, (channels, LANES), 0)
    return (row == lax.broadcasted_iota(jnp.int32, (channels, LANES), 1)).astype(BF16)


def put_back(back_ref, w_ref, channels):
    unit = unit_of(channels)
    border = jnp.zeros((LANES - channels, channels), BF16)
    for d in range(3):
        for j in range(OFFSETS):
            wide = jnp.concatenate([w_ref[d * OFFSETS + j], border], 0)
            block = jnp.dot(wide, unit, preferred_element_type=F32).astype(BF16)
            for q in range(2):
                row = ((2 - d + q) * OFFSETS + OFFSETS - 1 - j) * LANES
                back_ref[row : row + LANES, q * LANES : (q + 1) * LANES] = block
    put_zeros(back_ref)


def put_zeros(target_ref):
    run = OFFSETS * LANES
    target_ref[0:run, LANES : 2 * LANES] = jnp.zeros((run, LANES), BF16)
    target_ref[3 * run : 4 * run, 0:LANES] = jnp.zeros((run, LANES), BF16)


def put_ahead(ahead_ref, w_ref, channels):
    unit = unit_of(channels)
    border = jnp.zeros((LANES - channels, channels), BF16)
    for d in range(3):
        for j in range(OFFSETS):
            wide = jnp.concatenate([w_ref[d * OFFSETS + j], border], 0)
            turned = lax.dot_general(unit, wide, (((0,), (1,)), ((), ())), preferred_element_type=F32).astype(BF16)
            for q in range(2):
                row = ((d + q) * OFFSETS + j) * LANES
                ahead_ref[row : row + LANES, q * LANES : (q + 1) * LANES] = turned
    put_zeros(ahead_ref)


def weights_kernel(
    channels, classes,
    w1_in, w2_in, head_in,
    ahead1_ref, back2_ref, head_out,
    w1_ref, w2_ref, head_ref, arrived,
):
    copies = [
        pltpu.make_async_copy(source, target, arrived.at[i])
        for i, (source, target) in enumerate(((w1_in, w1_ref), (w2_in, w2_ref), (head_in, head_ref)))
    ]
    for copy in copies:
        copy.start()
    for copy in copies:
        copy.wait()
    put_ahead(ahead1_ref, w1_ref, channels)
    put_back(back2_ref, w2_ref, channels)
    head_out[...] = jnp.zeros_like(head_out)
    row = lax.broadcasted_iota(jnp.int32, (LANES, classes), 0)
    spread = (row == lax.broadcasted_iota(jnp.int32, (LANES, classes), 1) + channels + 1).astype(BF16)
    head_out[:, 0:channels] = jnp.dot(spread, head_ref[...], preferred_element_type=F32).astype(BF16)


def put_turned(turned_ref, value, plane, east, channels):
    turned = value.astype(BF16).T[0:channels]
    size = value.shape[0]
    for d in range(3):
        e = plane + d - 1
        if 0 <= e < east:
            turned_ref[d * channels : (d + 1) * channels, e * size : (e + 1) * size] = turned


def kernel_sum(turned_ref, stack, first, east, rows, upward, low, size, channels):
    fields = [shifts_of(stack, plane, rows, upward, low, size) for plane in range(first, first + east)]
    total = jnp.dot(turned_ref[...], jnp.concatenate(fields, 0), preferred_element_type=F32)
    blocks = [
        total[d * channels : (d + 1) * channels, j * LANES : (j + 1) * LANES]
        for d in range(3)
        for j in range(OFFSETS)
    ]
    blocks.append(jnp.zeros_like(blocks[0]))
    lane = lane_of(blocks[0].shape)
    spare = LANES - channels
    tiles = []
    for t in range(0, 28, 4):
        for r in range(3):
            tail = pltpu.roll(blocks[t + 3], channels - spare * r, 1)
            tiles.append(jnp.where(lane < channels, blocks[t + r], tail))
    return tiles


def prepare_kernel(
    channels, upward, edge,
    active_in, features_in, occupied_in, teacher_in,
    center_ref, *edge_refs,
):
    *edge_refs, active_ref, features_ref, occupied_ref, teacher_ref, arrived = edge_refs
    copies = [
        pltpu.make_async_copy(source, target, arrived.at[i])
        for i, (source, target) in enumerate(
            (
                (active_in, active_ref),
                (occupied_in, occupied_ref),
                (teacher_in, teacher_ref),
                (features_in, features_ref),
            )
        )
    ]
    for copy in copies:
        copy.start()
    for copy in copies[:-1]:
        copy.wait()
    east, size, _ = center_ref.shape
    north = size // upward
    classes = teacher_ref.shape[0]
    wide = (classes + 1) * upward
    row = lax.broadcasted_iota(jnp.int32, (size, north), 0) // upward
    spread = (row == lax.broadcasted_iota(jnp.int32, (size, north), 1)).astype(BF16)
    level = lax.broadcasted_iota(jnp.int32, (size, wide), 0) % upward
    same = level == lax.broadcasted_iota(jnp.int32, (size, wide), 1) % upward
    target = lax.broadcasted_iota(jnp.int32, (wide, LANES), 0) // upward + channels
    gather = (target == lax.broadcasted_iota(jnp.int32, (wide, LANES), 1)).astype(BF16)
    bricks = active_ref.shape
    up = lax.broadcasted_iota(jnp.int32, (upward, north), 0) // (upward // bricks[1])
    along = lax.broadcasted_iota(jnp.int32, (upward, north), 1) // (north // bricks[2])
    for e in range(east):
        mask = jnp.zeros((upward, north), jnp.int32)
        for b in range(bricks[2]):
            for c in range(bricks[1]):
                inside = (along == b) & (up == c)
                mask = jnp.where(inside, active_ref[e // (east // bricks[0]), c, b], mask)
        mask = (mask * occupied_ref[e]).astype(F32)
        goal = teacher_ref[:, e].astype(F32).reshape(classes * upward, north)
        field = jnp.concatenate([mask, goal], 0).astype(BF16)
        everywhere = lax.dot_general(spread, field, (((1,), (1,)), ((), ())), preferred_element_type=F32)
        own = jnp.where(same, everywhere, 0.0).astype(BF16)
        tail = jnp.dot(own, gather, preferred_element_type=F32).astype(BF16)
        center_ref[e, :, channels:LANES] = tail[:, channels:LANES]
    copies[-1].wait()
    center_ref[:, :, 0:channels] = features_ref[...]
    east_starts = [(1 - side) * (east - HALO) for _, side, _ in rounds_of("east")]
    north_starts = [pl.multiple_of((1 - side) * (size - edge), edge) for _, side, _ in rounds_of("north")]
    edge_refs = iter(edge_refs)
    for e in east_starts:
        next(edge_refs)[...] = center_ref[pl.ds(e, HALO)]
    for n in north_starts:
        next(edge_refs)[...] = center_ref[:, pl.ds(n, edge), :]
    for e in east_starts:
        for n in north_starts:
            next(edge_refs)[...] = center_ref[pl.ds(e, HALO), pl.ds(n, edge), :]


def place_edges(center_ref, edge_refs, edge, x_ref):
    east, size, _ = center_ref.shape
    x_ref[...] = jnp.zeros_like(x_ref)
    x_ref[HALO : HALO + east, edge : edge + size, :] = center_ref[...]
    edge_refs = iter(edge_refs)
    middle_east, middle_north = pl.ds(HALO, east), pl.ds(edge, size)
    east_places = [(pl.ds((1 - side) * (east + HALO), HALO), inside) for _, side, inside in rounds_of("east")]
    north_places = [
        (pl.ds(pl.multiple_of((1 - side) * (size + edge), edge), edge), inside)
        for _, side, inside in rounds_of("north")
    ]
    spots = [(e, middle_north, inside) for e, inside in east_places]
    spots += [(middle_east, n, inside) for n, inside in north_places]
    spots += [(e, n, a * b) for e, a in east_places for n, b in north_places]
    for e, n, inside in spots:
        ref = next(edge_refs)

        @pl.when(inside == 1)
        def _(ref=ref, e=e, n=n):
            x_ref[e, n, :] = ref[...]


def whole_kernel(
    channels, classes, east, north, upward, edges,
    ahead1_ref, w2_in, back2_ref, head_ref, center_ref, *refs,
):
    (
        grad_ref, kept_ref, sent_ref,
        x_ref, even0, odd0, even1, odd1, even2, odd2, mask_ref, slope_ref, turned_ref, ahead2_ref, w2_ref, arrived,
    ) = refs[edges:]
    stack0, stack1, stack2 = (even0, odd0), (even1, odd1), (even2, odd2)
    copy = pltpu.make_async_copy(w2_in, w2_ref, arrived)
    copy.start()
    rows = (north + 2 * HALO) * upward
    low, size = HALO * upward, north * upward
    planes = east + 2 * HALO
    lane = lane_of((rows, LANES))
    rows1, rows2, rows3 = rows - 2 * upward, rows - 4 * upward, rows - 6 * upward
    low1, low2, low3 = low - upward, low - 2 * upward, low - 3 * upward

    place_edges(center_ref, refs[:edges], low, x_ref)
    border = jnp.zeros((upward, LANES), F32)

    for plane in range(planes):
        x = x_ref[plane].astype(F32)
        mask = jnp.broadcast_to(x[:, channels : channels + 1], (rows, LANES))
        mask_ref[plane] = mask
        a0 = jnp.where((mask > 0) & (lane < channels), x, 0.0)
        put_stack(jnp.concatenate([border, a0, border], 0), upward, stack0, plane % 2, plane // 2)

    copy.wait()
    put_ahead(ahead2_ref, w2_ref, channels)
    for first, stop in grouped((planes - 2) // 2, 2):
        for i, parity, value in convolve(stack0, ahead1_ref, first, stop, rows, upward):
            plane = 2 * i + parity
            mask = mask_ref[plane + 1]
            p1 = mask * value
            sig = 0.5 * jnp.tanh(0.5 * p1) + 0.5
            slope_ref[plane] = mask * (sig * (1.0 + p1 * (1.0 - sig)))
            put_stack((p1 * sig)[upward : upward + rows1], upward, stack1, parity, i)

    head = head_ref[...]
    class_lane = (lane[0:rows2] > channels) & (lane[0:rows2] <= channels + classes)
    here = slice(2 * upward, 2 * upward + rows2)

    for first, stop in grouped((planes - 4) // 2, 2):
        for i, parity, value in convolve(stack1, ahead2_ref, first, stop, rows2, upward):
            plane = 2 * i + parity
            mask = mask_ref[plane + 2, here]
            p2 = mask * value
            sig = 0.5 * jnp.tanh(0.5 * p2) + 0.5
            a2 = (p2 * sig).astype(BF16)
            logits = lax.dot_general(a2, head, (((1,), (1,)), ((), ())), preferred_element_type=F32)
            g_logits = jnp.where(class_lane, mask * (logits - x_ref[plane + 2, here].astype(F32)), 0.0)
            coarse = g_logits.astype(BF16)
            fine = (g_logits - coarse.astype(F32)).astype(BF16)
            g_a2 = jnp.dot(
                jnp.concatenate([coarse, fine], 1), jnp.concatenate([head, head], 0), preferred_element_type=F32
            )
            g_p2 = mask * g_a2 * (sig * (1.0 + p2 * (1.0 - sig)))
            put_stack(g_p2, upward, stack2, parity, i)
            put_turned(turned_ref, g_p2[low2 : low2 + size], plane - 2, east, channels)

    upper = high_bit("east", 1) == 1
    for t, tile in enumerate(kernel_sum(turned_ref, stack1, 3, east, rows2, upward, low2, size, channels)):
        kept_ref[t * channels : (t + 1) * channels, :] = tile.astype(BF16)

    there = slice(2 * upward + upward, 2 * upward + upward + rows3)
    for first, stop in grouped((planes - 6) // 2, 2):
        for i, parity, value in convolve(stack2, back2_ref, first, stop, rows3, upward):
            plane = 2 * i + parity
            g_p1 = slope_ref[plane + 2, there] * value
            grad_ref[plane] = g_p1.astype(BF16)
            put_turned(turned_ref, g_p1[low3 : low3 + size], plane - 1, east, channels)

    tiles = kernel_sum(turned_ref, stack0, 4, east, rows, upward, low, size, channels)
    for t, tile in enumerate(tiles):
        place = slice(t * channels, (t + 1) * channels)
        first, second = tile.astype(BF16), kept_ref[place, :]
        sent_ref[place, :] = jnp.where(upper, second, first)
        kept_ref[place, :] = jnp.where(upper, first, second)
    filled = len(tiles) * channels
    if filled < kept_ref.shape[0]:
        kept_ref[filled:, :] = jnp.zeros((kept_ref.shape[0] - filled, LANES), BF16)
        sent_ref[filled:, :] = jnp.zeros((kept_ref.shape[0] - filled, LANES), BF16)


def last_kernel(
    channels, east, north, upward,
    center_ref, grad_ref, w1_in, kept_in,
    out_ref, kept_out,
    even_ref, odd_ref, back1_ref, w1_ref, arrived,
):
    size = north * upward
    copy = pltpu.make_async_copy(w1_in, w1_ref, arrived)
    copy.start()
    for plane in range(east + 2):
        put_stack(grad_ref[plane].astype(F32), upward, (even_ref, odd_ref), plane % 2, plane // 2)
    copy.wait()
    put_back(back1_ref, w1_ref, channels)
    for first, stop in grouped(east // 2, 4):
        for i, parity, value in convolve((even_ref, odd_ref), back1_ref, first, stop, size, upward):
            plane = 2 * i + parity
            mask = center_ref[plane, :, channels : channels + 1].astype(F32)
            out_ref[plane] = (mask * value)[:, 0:channels].astype(BF16)


def parts_kernel(place_ref, kept_ref, came_ref, total_ref, *sent_refs):
    part = total_ref.shape[0]
    for change, ref in enumerate((total_ref,) + sent_refs):
        start = pl.multiple_of((place_ref[0] ^ change) * part, part)
        rows = pl.ds(start, part)
        ref[...] = (kept_ref[rows, :].astype(F32) + came_ref[rows, :].astype(F32)).astype(ref.dtype)


def unpack_kernel(channels, scale, aliased, first_ref_flag, packed_ref, *refs):
    first_out, second_out, whole_ref, done = refs[2:] if aliased else refs
    spare = LANES - channels
    is_first = first_ref_flag[0] == 1
    spans = [(t, min(t + 4, 27)) for t in range(0, 27, 4)]

    def copy_of(target, i):
        a, b = spans[i]
        return pltpu.make_async_copy(whole_ref.at[a:b], target.at[a:b], done.at[i])

    for i, (t, stop) in enumerate(spans):
        tiles = []
        for r in range(3):
            start = (t // 4 * 3 + r) * channels
            tiles.append(packed_ref[start : start + channels, :].astype(F32) * scale)
        for r in range(3):
            whole_ref[t + r] = tiles[r][:, 0:channels]
        if stop - t == 4:
            lane = lane_of(tiles[0].shape)
            parts = [pltpu.roll(tiles[r], (spare * r - channels) % LANES, 1) for r in range(3)]
            last = jnp.where(lane < spare, parts[0], jnp.where(lane < 2 * spare, parts[1], parts[2]))
            whole_ref[t + 3] = last[:, 0:channels]

        @pl.when(is_first)
        def _(i=i):
            copy_of(first_out, i).start()

        @pl.when(jnp.logical_not(is_first))
        def _(i=i):
            copy_of(second_out, i).start()

    for i in range(len(spans)):
        copy_of(first_out, i).wait()


def per_device(
    features, brick_active, voxel_occupancy, first_weights, second_weights, head, teacher
):
    channels = features.shape[0]
    east, north, upward = features.shape[1:]
    classes = teacher.shape[0]
    devices = lax.axis_size("east") * lax.axis_size("north")
    scale = 1.0 / math.sqrt(devices * east * north * upward)
    planes = east + 2 * HALO
    rows = (north + 2 * HALO) * upward
    edge, size = HALO * upward, north * upward
    vmem = pl.BlockSpec(memory_space=pltpu.VMEM)
    smem = pl.BlockSpec(memory_space=pltpu.SMEM)
    anywhere = pl.BlockSpec(memory_space=pl.ANY)
    far = pl.BlockSpec(memory_space=pltpu.HBM)

    east_bits, north_bits = bits_of("east"), bits_of("north")
    rest = north_bits + east_bits[1:]
    near, others = rest[:2], rest[2:]
    upper = high_bit(*east_bits[0])
    easts, norths = rounds_of("east"), rounds_of("north")
    counts = (len(easts), len(norths))

    shapes = [(HALO, size, LANES)] * counts[0] + [(east, edge, LANES)] * counts[1]
    shapes += [(HALO, edge, LANES)] * (counts[0] * counts[1])
    center, *edges = pl.pallas_call(
        functools.partial(prepare_kernel, channels, upward, edge),
        out_shape=[jax.ShapeDtypeStruct(shape, BF16) for shape in [(east, size, LANES)] + shapes],
        in_specs=[far] * 4,
        out_specs=[vmem] * (1 + len(shapes)),
        scratch_shapes=[
            pltpu.SMEM((brick_active.shape[0], brick_active.shape[2], brick_active.shape[1]), jnp.int32),
            pltpu.VMEM((east, size, channels), BF16),
            pltpu.VMEM((east, upward, north), jnp.int32),
            pltpu.VMEM((classes, east, upward, north), BF16),
            pltpu.SemaphoreType.DMA((4,)),
        ],
        compiler_params=pltpu.CompilerParams(vmem_limit_bytes=6 * 1024 * 1024),
        name="prepare",
    )(
        *[
            pltpu.with_memory_space_constraint(value, pltpu.HBM)
            for value in (
                brick_active.transpose(0, 2, 1),
                features.transpose(1, 2, 3, 0).reshape(east, size, channels),
                voxel_occupancy.transpose(0, 2, 1),
                teacher.transpose(0, 1, 3, 2),
            )
        ]
    )
    stay = [list(range(lax.axis_size(axis))) for axis in ("east", "north")]
    routes = [(partners, stay[1]) for partners, _, _ in easts] + [(stay[0], partners) for partners, _, _ in norths]
    routes += [(a, b) for a, _, _ in easts for b, _, _ in norths]
    edges = [exchange(value, *route) for value, route in zip(edges, routes)]

    unit = devices // 2 * 16
    packed = -(-21 * channels // unit) * unit
    first_far, second_far, head_far = [
        pltpu.with_memory_space_constraint(value, pltpu.HBM) for value in (first_weights, second_weights, head)
    ]
    ahead1, back2, head_wide = pl.pallas_call(
        functools.partial(weights_kernel, channels, classes),
        out_shape=[jax.ShapeDtypeStruct(shape, BF16) for shape in ((4 * WIDE, 2 * LANES), (4 * WIDE, 2 * LANES), (LANES, LANES))],
        in_specs=[far] * 3,
        out_specs=[vmem] * 3,
        scratch_shapes=[
            pltpu.VMEM(first_weights.shape, BF16),
            pltpu.VMEM(second_weights.shape, BF16),
            pltpu.VMEM(head.shape, BF16),
            pltpu.SemaphoreType.DMA((3,)),
        ],
        compiler_params=pltpu.CompilerParams(vmem_limit_bytes=10 * 1024 * 1024),
        name="weights",
    )(first_far, second_far, head_far)
    grad, kept, sent = pl.pallas_call(
        functools.partial(whole_kernel, channels, classes, east, north, upward, len(edges)),
        out_shape=(
            jax.ShapeDtypeStruct((east + 2, rows - 6 * upward, LANES), BF16),
            jax.ShapeDtypeStruct((packed, LANES), BF16),
            jax.ShapeDtypeStruct((packed, LANES), BF16),
        ),
        in_specs=[vmem, far] + [vmem] * (3 + len(edges)),
        out_specs=(vmem, vmem, vmem),
        scratch_shapes=[
            pltpu.VMEM((planes, rows, LANES), BF16),
            *stack_shapes(planes, rows, upward),
            *stack_shapes(planes - 2, rows - 4 * upward, upward),
            *stack_shapes(planes - 4, rows - 6 * upward, upward),
            pltpu.VMEM((planes, rows, LANES), F32),
            pltpu.VMEM((planes - 2, rows, LANES), F32),
            pltpu.VMEM((3 * channels, east * size), BF16),
            pltpu.VMEM((4 * WIDE, 2 * LANES), BF16),
            pltpu.VMEM(second_weights.shape, BF16),
            pltpu.SemaphoreType.DMA(()),
        ],
        compiler_params=pltpu.CompilerParams(vmem_limit_bytes=28 * 1024 * 1024),
        name="fields",
    )(ahead1, second_far, back2, head_wide, center, *edges)

    features_out = []

    def beside(kept):
        out, kept = pl.pallas_call(
            functools.partial(last_kernel, channels, east, north, upward),
            out_shape=(
                jax.ShapeDtypeStruct((east, size, channels), BF16),
                jax.ShapeDtypeStruct(kept.shape, F32),
            ),
            in_specs=[vmem, vmem, far, anywhere],
            out_specs=(vmem, anywhere),
            input_output_aliases={3: 1},
            scratch_shapes=[
                *stack_shapes(east + 2, size, upward),
                pltpu.VMEM((4 * WIDE, 2 * LANES), BF16),
                pltpu.VMEM(first_weights.shape, BF16),
                pltpu.SemaphoreType.DMA(()),
            ],
            compiler_params=pltpu.CompilerParams(vmem_limit_bytes=10 * 1024 * 1024),
            name="features",
        )(center, grad, first_far, kept)
        features_out.append(out)
        return kept

    ways = 1 << len(near)
    part = packed // ways
    total, *parts = pl.pallas_call(
        parts_kernel,
        out_shape=[jax.ShapeDtypeStruct((part, LANES), F32)]
        + [jax.ShapeDtypeStruct((part, LANES), BF16)] * (ways - 1),
        in_specs=[smem] + [vmem] * 2,
        out_specs=[vmem] * ways,
        compiler_params=pltpu.CompilerParams(vmem_limit_bytes=4 * 1024 * 1024),
        name="parts",
    )(place_in(near).reshape(1).astype(jnp.int32), kept, swap(sent, east_bits[:1], 1))
    total = beside(total)
    for change in range(ways - 1, 0, -1):
        total = total + swap(parts[change - 1], near, change).astype(F32)
    mine = gather_parts(share_sums(total, others), [near])
    other = swap(mine, east_bits[:1], 1)

    def unpack(is_first, value, *aliased):
        return pl.pallas_call(
            functools.partial(unpack_kernel, channels, scale, bool(aliased)),
            out_shape=(
                jax.ShapeDtypeStruct(first_weights.shape, F32),
                jax.ShapeDtypeStruct(second_weights.shape, F32),
            ),
            in_specs=[smem, vmem] + [anywhere] * len(aliased),
            out_specs=(anywhere, anywhere),
            input_output_aliases={2: 0, 3: 1} if aliased else {},
            scratch_shapes=[pltpu.VMEM(first_weights.shape, F32), pltpu.SemaphoreType.DMA((7,))],
            compiler_params=pltpu.CompilerParams(vmem_limit_bytes=5 * 1024 * 1024),
            name="unpack",
        )(is_first.reshape(1).astype(jnp.int32), value, *aliased)

    outputs = unpack(upper, mine)
    grad_first, grad_second = unpack(1 - upper, other, *outputs)
    (grad_features,) = features_out
    grad_features = grad_features.reshape(east, north, upward, channels).transpose(3, 0, 1, 2)
    return (grad_features, grad_first, grad_second)


def solution(mesh):
    in_specs = (
        P(None, "east", "north", None),
        P("east", "north", None),
        P("east", "north", None),
        P(),
        P(),
        P(),
        P(None, "east", "north", None),
    )
    out_specs = (P(None, "east", "north", None), P(), P())
    return jax.shard_map(
        per_device, mesh=mesh, in_specs=in_specs, out_specs=out_specs, check_vma=False
    )
```

```python
import functools
import math

import jax
import jax.numpy as jnp
from jax import lax
from jax.experimental import pallas as pl
from jax.experimental.pallas import tpu as pltpu
from jax.sharding import PartitionSpec as P

LANES = 128
HALO = 4
OFFSETS = 9
WIDE = OFFSETS * LANES
F32 = jnp.float32
BF16 = jnp.bfloat16


def rounds_of(axis):
    count = lax.axis_size(axis)
    me = lax.axis_index(axis)
    rounds = [([i ^ 1 for i in range(count)], me % 2, jnp.int32(1))]
    if count > 2:
        inside = ((me > 0) & (me < count - 1)).astype(jnp.int32)
        partners = [0] + [((i - 1) ^ 1) + 1 for i in range(1, count - 1)] + [count - 1]
        rounds.append((partners, (me + 1) % 2, inside))
    return rounds


def exchange(value, east, north):
    count = len(north)
    target = {(e, n): (f, m) for e, f in enumerate(east) for n, m in enumerate(north)}
    alone = [place for place, other in target.items() if place == other]
    while alone:
        e, n = alone.pop(0)
        near = [place for place in ((e, n ^ 1), (e ^ 1, n)) if place in alone]
        other = near[0] if near else alone[0]
        alone.remove(other)
        target[e, n], target[other] = other, (e, n)
    pairs = [(e * count + n, f * count + m) for (e, n), (f, m) in target.items()]
    return lax.ppermute(value, ("east", "north"), pairs)


def high_bit(axis, bit):
    return (lax.axis_index(axis) // bit) % 2


def bits_of(axis):
    size = lax.axis_size(axis)
    return [(axis, 1 << i) for i in range(size.bit_length() - 1)]


def place_in(group):
    return sum(high_bit(axis, bit) << i for i, (axis, bit) in enumerate(group))


def swap(value, group, change):
    masks = {"east": 0, "north": 0}
    for i, (axis, bit) in enumerate(group):
        if change >> i & 1:
            masks[axis] |= bit
    partners = [[i ^ masks[axis] for i in range(lax.axis_size(axis))] for axis in ("east", "north")]
    return exchange(value, *partners)


def share_sums(total, bits):
    total = total.astype(BF16)
    for bit in bits:
        total = (total.astype(F32) + swap(total, [bit], 1).astype(F32)).astype(BF16)
    return total


def gather_parts(mine, groups):
    for group in reversed(groups):
        ways = 1 << len(group)
        place = place_in(group)
        parts = [mine] + [swap(mine, group, change) for change in range(1, ways)]
        joined = []
        for row in range(ways):
            piece = parts[0]
            for change in range(1, ways):
                piece = jnp.where((place ^ row) == change, parts[change], piece)
            joined.append(piece)
        mine = jnp.concatenate(joined, 0)
    return mine


def lane_of(shape):
    return lax.broadcasted_iota(jnp.int32, shape, len(shape) - 1)


def put_stack(value, upward, stack, parity, index):
    even_ref, odd_ref = stack
    total = value.shape[0]
    rows = total - 2 * upward
    cubes = value.reshape(total // upward, upward, LANES)
    level = lax.broadcasted_iota(jnp.int32, cubes.shape, 1)
    below = jnp.where(level == 0, 0.0, pltpu.roll(cubes, 1, 1)).reshape(total, LANES)
    above = jnp.where(level == upward - 1, 0.0, pltpu.roll(cubes, upward - 1, 1)).reshape(total, LANES)
    for up, moved in enumerate((below, value, above)):
        lanes = slice(up * LANES, (up + 1) * LANES)
        even_ref[parity, index * total : (index + 1) * total, lanes] = moved.astype(BF16)
        odd_ref[parity, index * rows : (index + 1) * rows, lanes] = moved[upward : upward + rows].astype(BF16)


def shifts_of(stack, plane, rows, upward, start, size):
    even_ref, odd_ref = stack
    even = (plane // 2) * (rows + 2 * upward) + start
    odd = (plane // 2) * rows + start
    return jnp.concatenate(
        [
            even_ref[plane % 2, even : even + size, :],
            odd_ref[plane % 2, odd : odd + size, :],
            even_ref[plane % 2, even + 2 * upward : even + 2 * upward + size, :],
        ],
        1,
    )


def stack_shapes(planes, rows, upward):
    return [pltpu.VMEM((2, planes // 2 * (rows + extra), 3 * LANES), BF16) for extra in (2 * upward, 0)]


def grouped(pairs, size):
    return [(first, min(first + size, pairs)) for first in range(0, pairs, size)]


def convolve(stack, weight_ref, first, stop, rows, upward):
    fields = [
        jnp.concatenate([shifts_of(stack, 2 * pair + p, rows, upward, 0, rows) for p in range(4)], 1)
        for pair in range(first, stop)
    ]
    both = jnp.dot(jnp.concatenate(fields, 0), weight_ref[...], preferred_element_type=F32)
    return [
        (pair, parity, both[(pair - first) * rows : (pair - first + 1) * rows, parity * LANES : (parity + 1) * LANES])
        for pair in range(first, stop)
        for parity in range(2)
    ]


def unit_of(channels):
    row = lax.broadcasted_iota(jnp.int32, (channels, LANES), 0)
    return (row == lax.broadcasted_iota(jnp.int32, (channels, LANES), 1)).astype(BF16)


def put_back(back_ref, w_ref, channels):
    unit = unit_of(channels)
    border = jnp.zeros((LANES - channels, channels), BF16)
    for d in range(3):
        for j in range(OFFSETS):
            wide = jnp.concatenate([w_ref[d * OFFSETS + j], border], 0)
            block = jnp.dot(wide, unit, preferred_element_type=F32).astype(BF16)
            for q in range(2):
                row = ((2 - d + q) * OFFSETS + OFFSETS - 1 - j) * LANES
                back_ref[row : row + LANES, q * LANES : (q + 1) * LANES] = block
    put_zeros(back_ref)


def put_zeros(target_ref):
    run = OFFSETS * LANES
    target_ref[0:run, LANES : 2 * LANES] = jnp.zeros((run, LANES), BF16)
    target_ref[3 * run : 4 * run, 0:LANES] = jnp.zeros((run, LANES), BF16)


def put_ahead(ahead_ref, w_ref, channels):
    unit = unit_of(channels)
    border = jnp.zeros((LANES - channels, channels), BF16)
    for d in range(3):
        for j in range(OFFSETS):
            wide = jnp.concatenate([w_ref[d * OFFSETS + j], border], 0)
            turned = lax.dot_general(unit, wide, (((0,), (1,)), ((), ())), preferred_element_type=F32).astype(BF16)
            for q in range(2):
                row = ((d + q) * OFFSETS + j) * LANES
                ahead_ref[row : row + LANES, q * LANES : (q + 1) * LANES] = turned
    put_zeros(ahead_ref)


def weights_kernel(
    channels, classes,
    w1_in, w2_in, head_in,
    ahead1_ref, back2_ref, head_out,
    w1_ref, w2_ref, head_ref, arrived,
):
    copies = [
        pltpu.make_async_copy(source, target, arrived.at[i])
        for i, (source, target) in enumerate(((w1_in, w1_ref), (w2_in, w2_ref), (head_in, head_ref)))
    ]
    for copy in copies:
        copy.start()
    for copy in copies:
        copy.wait()
    put_ahead(ahead1_ref, w1_ref, channels)
    put_back(back2_ref, w2_ref, channels)
    head_out[...] = jnp.zeros_like(head_out)
    row = lax.broadcasted_iota(jnp.int32, (LANES, classes), 0)
    spread = (row == lax.broadcasted_iota(jnp.int32, (LANES, classes), 1) + channels + 1).astype(BF16)
    head_out[:, 0:channels] = jnp.dot(spread, head_ref[...], preferred_element_type=F32).astype(BF16)


def put_turned(turned_ref, value, plane, east, channels):
    turned = value.astype(BF16).T[0:channels]
    size = value.shape[0]
    for d in range(3):
        e = plane + d - 1
        if 0 <= e < east:
            turned_ref[d * channels : (d + 1) * channels, e * size : (e + 1) * size] = turned


def kernel_sum(turned_ref, stack, first, east, rows, upward, low, size, channels):
    fields = [shifts_of(stack, plane, rows, upward, low, size) for plane in range(first, first + east)]
    total = jnp.dot(turned_ref[...], jnp.concatenate(fields, 0), preferred_element_type=F32)
    blocks = [
        total[d * channels : (d + 1) * channels, j * LANES : (j + 1) * LANES]
        for d in range(3)
        for j in range(OFFSETS)
    ]
    blocks.append(jnp.zeros_like(blocks[0]))
    lane = lane_of(blocks[0].shape)
    spare = LANES - channels
    tiles = []
    for t in range(0, 28, 4):
        for r in range(3):
            tail = pltpu.roll(blocks[t + 3], channels - spare * r, 1)
            tiles.append(jnp.where(lane < channels, blocks[t + r], tail))
    return tiles


def prepare_kernel(
    channels, upward, edge,
    active_in, features_in, occupied_in, teacher_in,
    center_ref, *edge_refs,
):
    *edge_refs, active_ref, features_ref, occupied_ref, teacher_ref, arrived = edge_refs
    copies = [
        pltpu.make_async_copy(source, target, arrived.at[i])
        for i, (source, target) in enumerate(
            (
                (active_in, active_ref),
                (occupied_in, occupied_ref),
                (teacher_in, teacher_ref),
                (features_in, features_ref),
            )
        )
    ]
    for copy in copies:
        copy.start()
    for copy in copies[:-1]:
        copy.wait()
    east, size, _ = center_ref.shape
    north = size // upward
    classes = teacher_ref.shape[0]
    wide = (classes + 1) * upward
    row = lax.broadcasted_iota(jnp.int32, (size, north), 0) // upward
    spread = (row == lax.broadcasted_iota(jnp.int32, (size, north), 1)).astype(BF16)
    level = lax.broadcasted_iota(jnp.int32, (size, wide), 0) % upward
    same = level == lax.broadcasted_iota(jnp.int32, (size, wide), 1) % upward
    target = lax.broadcasted_iota(jnp.int32, (wide, LANES), 0) // upward + channels
    gather = (target == lax.broadcasted_iota(jnp.int32, (wide, LANES), 1)).astype(BF16)
    bricks = active_ref.shape
    up = lax.broadcasted_iota(jnp.int32, (upward, north), 0) // (upward // bricks[1])
    along = lax.broadcasted_iota(jnp.int32, (upward, north), 1) // (north // bricks[2])
    for e in range(east):
        mask = jnp.zeros((upward, north), jnp.int32)
        for b in range(bricks[2]):
            for c in range(bricks[1]):
                inside = (along == b) & (up == c)
                mask = jnp.where(inside, active_ref[e // (east // bricks[0]), c, b], mask)
        mask = (mask * occupied_ref[e]).astype(F32)
        goal = teacher_ref[:, e].astype(F32).reshape(classes * upward, north)
        field = jnp.concatenate([mask, goal], 0).astype(BF16)
        everywhere = lax.dot_general(spread, field, (((1,), (1,)), ((), ())), preferred_element_type=F32)
        own = jnp.where(same, everywhere, 0.0).astype(BF16)
        tail = jnp.dot(own, gather, preferred_element_type=F32).astype(BF16)
        center_ref[e, :, channels:LANES] = tail[:, channels:LANES]
    copies[-1].wait()
    center_ref[:, :, 0:channels] = features_ref[...]
    east_starts = [(1 - side) * (east - HALO) for _, side, _ in rounds_of("east")]
    north_starts = [pl.multiple_of((1 - side) * (size - edge), edge) for _, side, _ in rounds_of("north")]
    edge_refs = iter(edge_refs)
    for e in east_starts:
        next(edge_refs)[...] = center_ref[pl.ds(e, HALO)]
    for n in north_starts:
        next(edge_refs)[...] = center_ref[:, pl.ds(n, edge), :]
    for e in east_starts:
        for n in north_starts:
            next(edge_refs)[...] = center_ref[pl.ds(e, HALO), pl.ds(n, edge), :]


def place_edges(center_ref, edge_refs, edge, x_ref):
    east, size, _ = center_ref.shape
    x_ref[...] = jnp.zeros_like(x_ref)
    x_ref[HALO : HALO + east, edge : edge + size, :] = center_ref[...]
    edge_refs = iter(edge_refs)
    middle_east, middle_north = pl.ds(HALO, east), pl.ds(edge, size)
    east_places = [(pl.ds((1 - side) * (east + HALO), HALO), inside) for _, side, inside in rounds_of("east")]
    north_places = [
        (pl.ds(pl.multiple_of((1 - side) * (size + edge), edge), edge), inside)
        for _, side, inside in rounds_of("north")
    ]
    spots = [(e, middle_north, inside) for e, inside in east_places]
    spots += [(middle_east, n, inside) for n, inside in north_places]
    spots += [(e, n, a * b) for e, a in east_places for n, b in north_places]
    for e, n, inside in spots:
        ref = next(edge_refs)

        @pl.when(inside == 1)
        def _(ref=ref, e=e, n=n):
            x_ref[e, n, :] = ref[...]


def whole_kernel(
    channels, classes, east, north, upward, edges,
    ahead1_ref, w2_in, back2_ref, head_ref, center_ref, *refs,
):
    (
        grad_ref, kept_ref, sent_ref,
        x_ref, even0, odd0, even1, odd1, even2, odd2, mask_ref, slope_ref, turned_ref, ahead2_ref, w2_ref, arrived,
    ) = refs[edges:]
    stack0, stack1, stack2 = (even0, odd0), (even1, odd1), (even2, odd2)
    copy = pltpu.make_async_copy(w2_in, w2_ref, arrived)
    copy.start()
    rows = (north + 2 * HALO) * upward
    low, size = HALO * upward, north * upward
    planes = east + 2 * HALO
    lane = lane_of((rows, LANES))
    rows1, rows2, rows3 = rows - 2 * upward, rows - 4 * upward, rows - 6 * upward
    low1, low2, low3 = low - upward, low - 2 * upward, low - 3 * upward

    place_edges(center_ref, refs[:edges], low, x_ref)
    border = jnp.zeros((upward, LANES), F32)

    for plane in range(planes):
        x = x_ref[plane].astype(F32)
        mask = jnp.broadcast_to(x[:, channels : channels + 1], (rows, LANES))
        mask_ref[plane] = mask
        a0 = jnp.where((mask > 0) & (lane < channels), x, 0.0)
        put_stack(jnp.concatenate([border, a0, border], 0), upward, stack0, plane % 2, plane // 2)

    copy.wait()
    put_ahead(ahead2_ref, w2_ref, channels)
    for first, stop in grouped((planes - 2) // 2, 2):
        for i, parity, value in convolve(stack0, ahead1_ref, first, stop, rows, upward):
            plane = 2 * i + parity
            mask = mask_ref[plane + 1]
            p1 = mask * value
            sig = 0.5 * jnp.tanh(0.5 * p1) + 0.5
            slope_ref[plane] = mask * (sig * (1.0 + p1 * (1.0 - sig)))
            put_stack((p1 * sig)[upward : upward + rows1], upward, stack1, parity, i)

    head = head_ref[...]
    class_lane = (lane[0:rows2] > channels) & (lane[0:rows2] <= channels + classes)
    here = slice(2 * upward, 2 * upward + rows2)

    for first, stop in grouped((planes - 4) // 2, 2):
        for i, parity, value in convolve(stack1, ahead2_ref, first, stop, rows2, upward):
            plane = 2 * i + parity
            mask = mask_ref[plane + 2, here]
            p2 = mask * value
            sig = 0.5 * jnp.tanh(0.5 * p2) + 0.5
            a2 = (p2 * sig).astype(BF16)
            logits = lax.dot_general(a2, head, (((1,), (1,)), ((), ())), preferred_element_type=F32)
            g_logits = jnp.where(class_lane, mask * (logits - x_ref[plane + 2, here].astype(F32)), 0.0)
            coarse = g_logits.astype(BF16)
            fine = (g_logits - coarse.astype(F32)).astype(BF16)
            g_a2 = jnp.dot(
                jnp.concatenate([coarse, fine], 1), jnp.concatenate([head, head], 0), preferred_element_type=F32
            )
            g_p2 = mask * g_a2 * (sig * (1.0 + p2 * (1.0 - sig)))
            put_stack(g_p2, upward, stack2, parity, i)
            put_turned(turned_ref, g_p2[low2 : low2 + size], plane - 2, east, channels)

    upper = high_bit("east", 1) == 1
    for t, tile in enumerate(kernel_sum(turned_ref, stack1, 3, east, rows2, upward, low2, size, channels)):
        kept_ref[t * channels : (t + 1) * channels, :] = tile.astype(BF16)

    there = slice(2 * upward + upward, 2 * upward + upward + rows3)
    for first, stop in grouped((planes - 6) // 2, 2):
        for i, parity, value in convolve(stack2, back2_ref, first, stop, rows3, upward):
            plane = 2 * i + parity
            g_p1 = slope_ref[plane + 2, there] * value
            grad_ref[plane] = g_p1.astype(BF16)
            put_turned(turned_ref, g_p1[low3 : low3 + size], plane - 1, east, channels)

    tiles = kernel_sum(turned_ref, stack0, 4, east, rows, upward, low, size, channels)
    for t, tile in enumerate(tiles):
        place = slice(t * channels, (t + 1) * channels)
        first, second = tile.astype(BF16), kept_ref[place, :]
        sent_ref[place, :] = jnp.where(upper, second, first)
        kept_ref[place, :] = jnp.where(upper, first, second)
    filled = len(tiles) * channels
    if filled < kept_ref.shape[0]:
        kept_ref[filled:, :] = jnp.zeros((kept_ref.shape[0] - filled, LANES), BF16)
        sent_ref[filled:, :] = jnp.zeros((kept_ref.shape[0] - filled, LANES), BF16)


def last_kernel(
    channels, east, north, upward,
    center_ref, grad_ref, w1_in, kept_in,
    out_ref, kept_out,
    even_ref, odd_ref, back1_ref, w1_ref, arrived,
):
    size = north * upward
    copy = pltpu.make_async_copy(w1_in, w1_ref, arrived)
    copy.start()
    for plane in range(east + 2):
        put_stack(grad_ref[plane].astype(F32), upward, (even_ref, odd_ref), plane % 2, plane // 2)
    copy.wait()
    put_back(back1_ref, w1_ref, channels)
    for first, stop in grouped(east // 2, 4):
        for i, parity, value in convolve((even_ref, odd_ref), back1_ref, first, stop, size, upward):
            plane = 2 * i + parity
            mask = center_ref[plane, :, channels : channels + 1].astype(F32)
            out_ref[plane] = (mask * value)[:, 0:channels].astype(BF16)


def parts_kernel(place_ref, kept_ref, came_ref, total_ref, *sent_refs):
    part = total_ref.shape[0]
    for change, ref in enumerate((total_ref,) + sent_refs):
        start = pl.multiple_of((place_ref[0] ^ change) * part, part)
        rows = pl.ds(start, part)
        ref[...] = (kept_ref[rows, :].astype(F32) + came_ref[rows, :].astype(F32)).astype(ref.dtype)


def unpack_kernel(channels, scale, aliased, first_ref_flag, packed_ref, *refs):
    first_out, second_out, whole_ref, done = refs[2:] if aliased else refs
    spare = LANES - channels
    is_first = first_ref_flag[0] == 1
    spans = [(t, min(t + 4, 27)) for t in range(0, 27, 4)]

    def copy_of(target, i):
        a, b = spans[i]
        return pltpu.make_async_copy(whole_ref.at[a:b], target.at[a:b], done.at[i])

    for i, (t, stop) in enumerate(spans):
        tiles = []
        for r in range(3):
            start = (t // 4 * 3 + r) * channels
            tiles.append(packed_ref[start : start + channels, :].astype(F32) * scale)
        for r in range(3):
            whole_ref[t + r] = tiles[r][:, 0:channels]
        if stop - t == 4:
            lane = lane_of(tiles[0].shape)
            parts = [pltpu.roll(tiles[r], (spare * r - channels) % LANES, 1) for r in range(3)]
            last = jnp.where(lane < spare, parts[0], jnp.where(lane < 2 * spare, parts[1], parts[2]))
            whole_ref[t + 3] = last[:, 0:channels]

        @pl.when(is_first)
        def _(i=i):
            copy_of(first_out, i).start()

        @pl.when(jnp.logical_not(is_first))
        def _(i=i):
            copy_of(second_out, i).start()

    for i in range(len(spans)):
        copy_of(first_out, i).wait()


def per_device(
    features, brick_active, voxel_occupancy, first_weights, second_weights, head, teacher
):
    channels = features.shape[0]
    east, north, upward = features.shape[1:]
    classes = teacher.shape[0]
    devices = lax.axis_size("east") * lax.axis_size("north")
    scale = 1.0 / math.sqrt(devices * east * north * upward)
    planes = east + 2 * HALO
    rows = (north + 2 * HALO) * upward
    edge, size = HALO * upward, north * upward
    vmem = pl.BlockSpec(memory_space=pltpu.VMEM)
    smem = pl.BlockSpec(memory_space=pltpu.SMEM)
    anywhere = pl.BlockSpec(memory_space=pl.ANY)
    far = pl.BlockSpec(memory_space=pltpu.HBM)

    east_bits, north_bits = bits_of("east"), bits_of("north")
    rest = north_bits + east_bits[1:]
    near, others = rest[:2], rest[2:]
    upper = high_bit(*east_bits[0])
    easts, norths = rounds_of("east"), rounds_of("north")
    counts = (len(easts), len(norths))

    shapes = [(HALO, size, LANES)] * counts[0] + [(east, edge, LANES)] * counts[1]
    shapes += [(HALO, edge, LANES)] * (counts[0] * counts[1])
    center, *edges = pl.pallas_call(
        functools.partial(prepare_kernel, channels, upward, edge),
        out_shape=[jax.ShapeDtypeStruct(shape, BF16) for shape in [(east, size, LANES)] + shapes],
        in_specs=[far] * 4,
        out_specs=[vmem] * (1 + len(shapes)),
        scratch_shapes=[
            pltpu.SMEM((brick_active.shape[0], brick_active.shape[2], brick_active.shape[1]), jnp.int32),
            pltpu.VMEM((east, size, channels), BF16),
            pltpu.VMEM((east, upward, north), jnp.int32),
            pltpu.VMEM((classes, east, upward, north), BF16),
            pltpu.SemaphoreType.DMA((4,)),
        ],
        compiler_params=pltpu.CompilerParams(vmem_limit_bytes=6 * 1024 * 1024),
        name="prepare",
    )(
        *[
            pltpu.with_memory_space_constraint(value, pltpu.HBM)
            for value in (
                brick_active.transpose(0, 2, 1),
                features.transpose(1, 2, 3, 0).reshape(east, size, channels),
                voxel_occupancy.transpose(0, 2, 1),
                teacher.transpose(0, 1, 3, 2),
            )
        ]
    )
    stay = [list(range(lax.axis_size(axis))) for axis in ("east", "north")]
    routes = [(partners, stay[1]) for partners, _, _ in easts] + [(stay[0], partners) for partners, _, _ in norths]
    routes += [(a, b) for a, _, _ in easts for b, _, _ in norths]
    came = {i: exchange(edges[i], *routes[i]) for i in [*range(1, len(edges)), 0]}
    edges = [came[i] for i in range(len(edges))]

    unit = devices // 2 * 16
    packed = -(-21 * channels // unit) * unit
    first_far, second_far, head_far = [
        pltpu.with_memory_space_constraint(value, pltpu.HBM) for value in (first_weights, second_weights, head)
    ]
    ahead1, back2, head_wide = pl.pallas_call(
        functools.partial(weights_kernel, channels, classes),
        out_shape=[jax.ShapeDtypeStruct(shape, BF16) for shape in ((4 * WIDE, 2 * LANES), (4 * WIDE, 2 * LANES), (LANES, LANES))],
        in_specs=[far] * 3,
        out_specs=[vmem] * 3,
        scratch_shapes=[
            pltpu.VMEM(first_weights.shape, BF16),
            pltpu.VMEM(second_weights.shape, BF16),
            pltpu.VMEM(head.shape, BF16),
            pltpu.SemaphoreType.DMA((3,)),
        ],
        compiler_params=pltpu.CompilerParams(vmem_limit_bytes=10 * 1024 * 1024),
        name="weights",
    )(first_far, second_far, head_far)
    grad, kept, sent = pl.pallas_call(
        functools.partial(whole_kernel, channels, classes, east, north, upward, len(edges)),
        out_shape=(
            jax.ShapeDtypeStruct((east + 2, rows - 6 * upward, LANES), BF16),
            jax.ShapeDtypeStruct((packed, LANES), BF16),
            jax.ShapeDtypeStruct((packed, LANES), BF16),
        ),
        in_specs=[vmem, far] + [vmem] * (3 + len(edges)),
        out_specs=(vmem, vmem, vmem),
        scratch_shapes=[
            pltpu.VMEM((planes, rows, LANES), BF16),
            *stack_shapes(planes, rows, upward),
            *stack_shapes(planes - 2, rows - 4 * upward, upward),
            *stack_shapes(planes - 4, rows - 6 * upward, upward),
            pltpu.VMEM((planes, rows, LANES), F32),
            pltpu.VMEM((planes - 2, rows, LANES), F32),
            pltpu.VMEM((3 * channels, east * size), BF16),
            pltpu.VMEM((4 * WIDE, 2 * LANES), BF16),
            pltpu.VMEM(second_weights.shape, BF16),
            pltpu.SemaphoreType.DMA(()),
        ],
        compiler_params=pltpu.CompilerParams(vmem_limit_bytes=28 * 1024 * 1024),
        name="fields",
    )(ahead1, second_far, back2, head_wide, center, *edges)

    features_out = []

    def beside(kept):
        out, kept = pl.pallas_call(
            functools.partial(last_kernel, channels, east, north, upward),
            out_shape=(
                jax.ShapeDtypeStruct((east, size, channels), BF16),
                jax.ShapeDtypeStruct(kept.shape, F32),
            ),
            in_specs=[vmem, vmem, far, anywhere],
            out_specs=(vmem, anywhere),
            input_output_aliases={3: 1},
            scratch_shapes=[
                *stack_shapes(east + 2, size, upward),
                pltpu.VMEM((4 * WIDE, 2 * LANES), BF16),
                pltpu.VMEM(first_weights.shape, BF16),
                pltpu.SemaphoreType.DMA(()),
            ],
            compiler_params=pltpu.CompilerParams(vmem_limit_bytes=10 * 1024 * 1024),
            name="features",
        )(center, grad, first_far, kept)
        features_out.append(out)
        return kept

    ways = 1 << len(near)
    part = packed // ways
    total, *parts = pl.pallas_call(
        parts_kernel,
        out_shape=[jax.ShapeDtypeStruct((part, LANES), F32)]
        + [jax.ShapeDtypeStruct((part, LANES), BF16)] * (ways - 1),
        in_specs=[smem] + [vmem] * 2,
        out_specs=[vmem] * ways,
        compiler_params=pltpu.CompilerParams(vmem_limit_bytes=4 * 1024 * 1024),
        name="parts",
    )(place_in(near).reshape(1).astype(jnp.int32), kept, swap(sent, east_bits[:1], 1))
    total = beside(total)
    for change in range(ways - 1, 0, -1):
        total = total + swap(parts[change - 1], near, change).astype(F32)
    mine = gather_parts(share_sums(total, others), [near])
    other = swap(mine, east_bits[:1], 1)

    def unpack(is_first, value, *aliased):
        return pl.pallas_call(
            functools.partial(unpack_kernel, channels, scale, bool(aliased)),
            out_shape=(
                jax.ShapeDtypeStruct(first_weights.shape, F32),
                jax.ShapeDtypeStruct(second_weights.shape, F32),
            ),
            in_specs=[smem, vmem] + [anywhere] * len(aliased),
            out_specs=(anywhere, anywhere),
            input_output_aliases={2: 0, 3: 1} if aliased else {},
            scratch_shapes=[pltpu.VMEM(first_weights.shape, F32), pltpu.SemaphoreType.DMA((7,))],
            compiler_params=pltpu.CompilerParams(vmem_limit_bytes=5 * 1024 * 1024),
            name="unpack",
        )(is_first.reshape(1).astype(jnp.int32), value, *aliased)

    outputs = unpack(upper, mine)
    grad_first, grad_second = unpack(1 - upper, other, *outputs)
    (grad_features,) = features_out
    grad_features = grad_features.reshape(east, north, upward, channels).transpose(3, 0, 1, 2)
    return (grad_features, grad_first, grad_second)


def solution(mesh):
    in_specs = (
        P(None, "east", "north", None),
        P("east", "north", None),
        P("east", "north", None),
        P(),
        P(),
        P(),
        P(None, "east", "north", None),
    )
    out_specs = (P(None, "east", "north", None), P(), P())
    return jax.shard_map(
        per_device, mesh=mesh, in_specs=in_specs, out_specs=out_specs, check_vma=False
    )
```

```python
import functools
import math

import jax
import jax.numpy as jnp
from jax import lax
from jax.experimental import pallas as pl
from jax.experimental.pallas import tpu as pltpu
from jax.sharding import PartitionSpec as P

LANES = 128
HALO = 4
OFFSETS = 9
WIDE = OFFSETS * LANES
F32 = jnp.float32
BF16 = jnp.bfloat16


def rounds_of(axis):
    count = lax.axis_size(axis)
    me = lax.axis_index(axis)
    rounds = [([i ^ 1 for i in range(count)], me % 2, jnp.int32(1))]
    if count > 2:
        inside = ((me > 0) & (me < count - 1)).astype(jnp.int32)
        partners = [0] + [((i - 1) ^ 1) + 1 for i in range(1, count - 1)] + [count - 1]
        rounds.append((partners, (me + 1) % 2, inside))
    return rounds


def exchange(value, east, north):
    count = len(north)
    target = {(e, n): (f, m) for e, f in enumerate(east) for n, m in enumerate(north)}
    alone = [place for place, other in target.items() if place == other]
    while alone:
        e, n = alone.pop(0)
        near = [place for place in ((e, n ^ 1), (e ^ 1, n)) if place in alone]
        other = near[0] if near else alone[0]
        alone.remove(other)
        target[e, n], target[other] = other, (e, n)
    pairs = [(e * count + n, f * count + m) for (e, n), (f, m) in target.items()]
    return lax.ppermute(value, ("east", "north"), pairs)


def high_bit(axis, bit):
    return (lax.axis_index(axis) // bit) % 2


def bits_of(axis):
    size = lax.axis_size(axis)
    return [(axis, 1 << i) for i in range(size.bit_length() - 1)]


def place_in(group):
    return sum(high_bit(axis, bit) << i for i, (axis, bit) in enumerate(group))


def swap(value, group, change):
    masks = {"east": 0, "north": 0}
    for i, (axis, bit) in enumerate(group):
        if change >> i & 1:
            masks[axis] |= bit
    partners = [[i ^ masks[axis] for i in range(lax.axis_size(axis))] for axis in ("east", "north")]
    return exchange(value, *partners)


def share_sums(total, bits):
    total = total.astype(BF16)
    for bit in bits:
        total = (total.astype(F32) + swap(total, [bit], 1).astype(F32)).astype(BF16)
    return total


def gather_parts(mine, groups):
    for group in reversed(groups):
        ways = 1 << len(group)
        place = place_in(group)
        parts = [mine] + [swap(mine, group, change) for change in range(1, ways)]
        joined = []
        for row in range(ways):
            piece = parts[0]
            for change in range(1, ways):
                piece = jnp.where((place ^ row) == change, parts[change], piece)
            joined.append(piece)
        mine = jnp.concatenate(joined, 0)
    return mine


def lane_of(shape):
    return lax.broadcasted_iota(jnp.int32, shape, len(shape) - 1)


def put_stack(value, upward, stack, parity, index):
    even_ref, odd_ref = stack
    total = value.shape[0]
    rows = total - 2 * upward
    cubes = value.reshape(total // upward, upward, LANES)
    level = lax.broadcasted_iota(jnp.int32, cubes.shape, 1)
    below = jnp.where(level == 0, 0.0, pltpu.roll(cubes, 1, 1)).reshape(total, LANES)
    above = jnp.where(level == upward - 1, 0.0, pltpu.roll(cubes, upward - 1, 1)).reshape(total, LANES)
    for up, moved in enumerate((below, value, above)):
        lanes = slice(up * LANES, (up + 1) * LANES)
        even_ref[parity, index * total : (index + 1) * total, lanes] = moved.astype(BF16)
        odd_ref[parity, index * rows : (index + 1) * rows, lanes] = moved[upward : upward + rows].astype(BF16)


def shifts_of(stack, plane, rows, upward, start, size):
    even_ref, odd_ref = stack
    even = (plane // 2) * (rows + 2 * upward) + start
    odd = (plane // 2) * rows + start
    return jnp.concatenate(
        [
            even_ref[plane % 2, even : even + size, :],
            odd_ref[plane % 2, odd : odd + size, :],
            even_ref[plane % 2, even + 2 * upward : even + 2 * upward + size, :],
        ],
        1,
    )


def stack_shapes(planes, rows, upward):
    return [pltpu.VMEM((2, planes // 2 * (rows + extra), 3 * LANES), BF16) for extra in (2 * upward, 0)]


def grouped(pairs, size):
    count = max(1, pairs // size)
    edges = [pairs * i // count for i in range(count + 1)]
    return list(zip(edges, edges[1:]))


def convolve(stack, weight_ref, first, stop, rows, upward):
    fields = [
        jnp.concatenate([shifts_of(stack, 2 * pair + p, rows, upward, 0, rows) for p in range(4)], 1)
        for pair in range(first, stop)
    ]
    both = jnp.dot(jnp.concatenate(fields, 0), weight_ref[...], preferred_element_type=F32)
    return [
        (pair, parity, both[(pair - first) * rows : (pair - first + 1) * rows, parity * LANES : (parity + 1) * LANES])
        for pair in range(first, stop)
        for parity in range(2)
    ]


def ahead_of(runs, product):
    held = product(*runs[0])
    for run in runs[1:]:
        coming = product(*run)
        yield from held
        held = coming
    yield from held


def unit_of(channels):
    row = lax.broadcasted_iota(jnp.int32, (channels, LANES), 0)
    return (row == lax.broadcasted_iota(jnp.int32, (channels, LANES), 1)).astype(BF16)


def put_back(back_ref, w_ref, channels):
    unit = unit_of(channels)
    border = jnp.zeros((LANES - channels, channels), BF16)
    for d in range(3):
        for j in range(OFFSETS):
            wide = jnp.concatenate([w_ref[d * OFFSETS + j], border], 0)
            block = jnp.dot(wide, unit, preferred_element_type=F32).astype(BF16)
            for q in range(2):
                row = ((2 - d + q) * OFFSETS + OFFSETS - 1 - j) * LANES
                back_ref[row : row + LANES, q * LANES : (q + 1) * LANES] = block
    put_zeros(back_ref)


def put_zeros(target_ref):
    run = OFFSETS * LANES
    target_ref[0:run, LANES : 2 * LANES] = jnp.zeros((run, LANES), BF16)
    target_ref[3 * run : 4 * run, 0:LANES] = jnp.zeros((run, LANES), BF16)


def put_ahead(ahead_ref, w_ref, channels):
    unit = unit_of(channels)
    border = jnp.zeros((LANES - channels, channels), BF16)
    for d in range(3):
        for j in range(OFFSETS):
            wide = jnp.concatenate([w_ref[d * OFFSETS + j], border], 0)
            turned = lax.dot_general(unit, wide, (((0,), (1,)), ((), ())), preferred_element_type=F32).astype(BF16)
            for q in range(2):
                row = ((d + q) * OFFSETS + j) * LANES
                ahead_ref[row : row + LANES, q * LANES : (q + 1) * LANES] = turned
    put_zeros(ahead_ref)


def weights_kernel(
    channels, classes,
    w1_in, w2_in, head_in,
    ahead1_ref, back2_ref, head_out,
    w1_ref, w2_ref, head_ref, arrived,
):
    copies = [
        pltpu.make_async_copy(source, target, arrived.at[i])
        for i, (source, target) in enumerate(((w1_in, w1_ref), (w2_in, w2_ref), (head_in, head_ref)))
    ]
    for copy in copies:
        copy.start()
    for copy in copies:
        copy.wait()
    put_ahead(ahead1_ref, w1_ref, channels)
    put_back(back2_ref, w2_ref, channels)
    head_out[...] = jnp.zeros_like(head_out)
    row = lax.broadcasted_iota(jnp.int32, (LANES, classes), 0)
    spread = (row == lax.broadcasted_iota(jnp.int32, (LANES, classes), 1) + channels + 1).astype(BF16)
    head_out[:, 0:channels] = jnp.dot(spread, head_ref[...], preferred_element_type=F32).astype(BF16)


def put_turned(turned_ref, value, plane, east, channels):
    turned = value.astype(BF16).T[0:channels]
    size = value.shape[0]
    for d in range(3):
        e = plane + d - 1
        if 0 <= e < east:
            turned_ref[d * channels : (d + 1) * channels, e * size : (e + 1) * size] = turned


def kernel_sum(turned_ref, stack, first, east, rows, upward, low, size, channels):
    fields = [shifts_of(stack, plane, rows, upward, low, size) for plane in range(first, first + east)]
    total = jnp.dot(turned_ref[...], jnp.concatenate(fields, 0), preferred_element_type=F32)
    blocks = [
        total[d * channels : (d + 1) * channels, j * LANES : (j + 1) * LANES]
        for d in range(3)
        for j in range(OFFSETS)
    ]
    blocks.append(jnp.zeros_like(blocks[0]))
    lane = lane_of(blocks[0].shape)
    spare = LANES - channels
    tiles = []
    for t in range(0, 28, 4):
        for r in range(3):
            tail = pltpu.roll(blocks[t + 3], channels - spare * r, 1)
            tiles.append(jnp.where(lane < channels, blocks[t + r], tail))
    return tiles


def prepare_kernel(
    channels, upward, edge,
    active_in, features_in, occupied_in, teacher_in,
    center_ref, *edge_refs,
):
    *edge_refs, active_ref, features_ref, occupied_ref, teacher_ref, arrived = edge_refs
    copies = [
        pltpu.make_async_copy(source, target, arrived.at[i])
        for i, (source, target) in enumerate(
            (
                (active_in, active_ref),
                (occupied_in, occupied_ref),
                (teacher_in, teacher_ref),
                (features_in, features_ref),
            )
        )
    ]
    for copy in copies:
        copy.start()
    for copy in copies[:-1]:
        copy.wait()
    east, size, _ = center_ref.shape
    north = size // upward
    classes = teacher_ref.shape[0]
    wide = (classes + 1) * upward
    row = lax.broadcasted_iota(jnp.int32, (size, north), 0) // upward
    spread = (row == lax.broadcasted_iota(jnp.int32, (size, north), 1)).astype(BF16)
    level = lax.broadcasted_iota(jnp.int32, (size, wide), 0) % upward
    same = level == lax.broadcasted_iota(jnp.int32, (size, wide), 1) % upward
    target = lax.broadcasted_iota(jnp.int32, (wide, LANES), 0) // upward + channels
    gather = (target == lax.broadcasted_iota(jnp.int32, (wide, LANES), 1)).astype(BF16)
    bricks = active_ref.shape
    up = lax.broadcasted_iota(jnp.int32, (upward, north), 0) // (upward // bricks[1])
    along = lax.broadcasted_iota(jnp.int32, (upward, north), 1) // (north // bricks[2])
    for e in range(east):
        mask = jnp.zeros((upward, north), jnp.int32)
        for b in range(bricks[2]):
            for c in range(bricks[1]):
                inside = (along == b) & (up == c)
                mask = jnp.where(inside, active_ref[e // (east // bricks[0]), c, b], mask)
        mask = (mask * occupied_ref[e]).astype(F32)
        goal = teacher_ref[:, e].astype(F32).reshape(classes * upward, north)
        field = jnp.concatenate([mask, goal], 0).astype(BF16)
        everywhere = lax.dot_general(spread, field, (((1,), (1,)), ((), ())), preferred_element_type=F32)
        own = jnp.where(same, everywhere, 0.0).astype(BF16)
        tail = jnp.dot(own, gather, preferred_element_type=F32).astype(BF16)
        center_ref[e, :, channels:LANES] = tail[:, channels:LANES]
    copies[-1].wait()
    center_ref[:, :, 0:channels] = features_ref[...]
    east_starts = [(1 - side) * (east - HALO) for _, side, _ in rounds_of("east")]
    north_starts = [pl.multiple_of((1 - side) * (size - edge), edge) for _, side, _ in rounds_of("north")]
    edge_refs = iter(edge_refs)
    for e in east_starts:
        next(edge_refs)[...] = center_ref[pl.ds(e, HALO)]
    for n in north_starts:
        next(edge_refs)[...] = center_ref[:, pl.ds(n, edge), :]
    for e in east_starts:
        for n in north_starts:
            next(edge_refs)[...] = center_ref[pl.ds(e, HALO), pl.ds(n, edge), :]


def place_edges(center_ref, edge_refs, edge, x_ref):
    east, size, _ = center_ref.shape
    x_ref[...] = jnp.zeros_like(x_ref)
    x_ref[HALO : HALO + east, edge : edge + size, :] = center_ref[...]
    edge_refs = iter(edge_refs)
    middle_east, middle_north = pl.ds(HALO, east), pl.ds(edge, size)
    east_places = [(pl.ds((1 - side) * (east + HALO), HALO), inside) for _, side, inside in rounds_of("east")]
    north_places = [
        (pl.ds(pl.multiple_of((1 - side) * (size + edge), edge), edge), inside)
        for _, side, inside in rounds_of("north")
    ]
    spots = [(e, middle_north, inside) for e, inside in east_places]
    spots += [(middle_east, n, inside) for n, inside in north_places]
    spots += [(e, n, a * b) for e, a in east_places for n, b in north_places]
    for e, n, inside in spots:
        ref = next(edge_refs)

        @pl.when(inside == 1)
        def _(ref=ref, e=e, n=n):
            x_ref[e, n, :] = ref[...]


def whole_kernel(
    channels, classes, east, north, upward, edges,
    ahead1_ref, w2_in, back2_ref, head_ref, center_ref, *refs,
):
    (
        grad_ref, kept_ref, sent_ref,
        x_ref, even0, odd0, even1, odd1, even2, odd2, mask_ref, slope_ref, turned_ref, ahead2_ref, w2_ref, arrived,
    ) = refs[edges:]
    stack0, stack1, stack2 = (even0, odd0), (even1, odd1), (even2, odd2)
    copy = pltpu.make_async_copy(w2_in, w2_ref, arrived)
    copy.start()
    rows = (north + 2 * HALO) * upward
    low, size = HALO * upward, north * upward
    planes = east + 2 * HALO
    lane = lane_of((rows, LANES))
    rows1, rows2, rows3 = rows - 2 * upward, rows - 4 * upward, rows - 6 * upward
    low1, low2, low3 = low - upward, low - 2 * upward, low - 3 * upward

    place_edges(center_ref, refs[:edges], low, x_ref)
    border = jnp.zeros((upward, LANES), F32)

    for plane in range(planes):
        x = x_ref[plane].astype(F32)
        mask = jnp.broadcast_to(x[:, channels : channels + 1], (rows, LANES))
        mask_ref[plane] = mask
        a0 = jnp.where((mask > 0) & (lane < channels), x, 0.0)
        put_stack(jnp.concatenate([border, a0, border], 0), upward, stack0, plane % 2, plane // 2)

    copy.wait()
    put_ahead(ahead2_ref, w2_ref, channels)
    product = functools.partial(convolve, stack0, ahead1_ref, rows=rows, upward=upward)
    for i, parity, value in ahead_of(grouped((planes - 2) // 2, 2), product):
        plane = 2 * i + parity
        mask = mask_ref[plane + 1]
        p1 = mask * value
        sig = 0.5 * jnp.tanh(0.5 * p1) + 0.5
        slope_ref[plane] = mask * (sig * (1.0 + p1 * (1.0 - sig)))
        put_stack((p1 * sig)[upward : upward + rows1], upward, stack1, parity, i)

    head = head_ref[...]
    class_lane = (lane[0:rows2] > channels) & (lane[0:rows2] <= channels + classes)
    here = slice(2 * upward, 2 * upward + rows2)

    product = functools.partial(convolve, stack1, ahead2_ref, rows=rows2, upward=upward)
    for i, parity, value in ahead_of(grouped((planes - 4) // 2, 2), product):
        plane = 2 * i + parity
        mask = mask_ref[plane + 2, here]
        p2 = mask * value
        sig = 0.5 * jnp.tanh(0.5 * p2) + 0.5
        a2 = (p2 * sig).astype(BF16)
        logits = lax.dot_general(a2, head, (((1,), (1,)), ((), ())), preferred_element_type=F32)
        g_logits = jnp.where(class_lane, mask * (logits - x_ref[plane + 2, here].astype(F32)), 0.0)
        coarse = g_logits.astype(BF16)
        fine = (g_logits - coarse.astype(F32)).astype(BF16)
        g_a2 = jnp.dot(
            jnp.concatenate([coarse, fine], 1), jnp.concatenate([head, head], 0), preferred_element_type=F32
        )
        g_p2 = mask * g_a2 * (sig * (1.0 + p2 * (1.0 - sig)))
        put_stack(g_p2, upward, stack2, parity, i)
        put_turned(turned_ref, g_p2[low2 : low2 + size], plane - 2, east, channels)

    upper = high_bit("east", 1) == 1
    for t, tile in enumerate(kernel_sum(turned_ref, stack1, 3, east, rows2, upward, low2, size, channels)):
        kept_ref[t * channels : (t + 1) * channels, :] = tile.astype(BF16)

    there = slice(2 * upward + upward, 2 * upward + upward + rows3)
    product = functools.partial(convolve, stack2, back2_ref, rows=rows3, upward=upward)
    for i, parity, value in ahead_of(grouped((planes - 6) // 2, 2), product):
        plane = 2 * i + parity
        g_p1 = slope_ref[plane + 2, there] * value
        grad_ref[plane] = g_p1.astype(BF16)
        put_turned(turned_ref, g_p1[low3 : low3 + size], plane - 1, east, channels)

    tiles = kernel_sum(turned_ref, stack0, 4, east, rows, upward, low, size, channels)
    for t, tile in enumerate(tiles):
        place = slice(t * channels, (t + 1) * channels)
        first, second = tile.astype(BF16), kept_ref[place, :]
        sent_ref[place, :] = jnp.where(upper, second, first)
        kept_ref[place, :] = jnp.where(upper, first, second)
    filled = len(tiles) * channels
    if filled < kept_ref.shape[0]:
        kept_ref[filled:, :] = jnp.zeros((kept_ref.shape[0] - filled, LANES), BF16)
        sent_ref[filled:, :] = jnp.zeros((kept_ref.shape[0] - filled, LANES), BF16)


def last_kernel(
    channels, east, north, upward,
    center_ref, grad_ref, w1_in, kept_in,
    out_ref, kept_out,
    even_ref, odd_ref, back1_ref, w1_ref, arrived,
):
    size = north * upward
    copy = pltpu.make_async_copy(w1_in, w1_ref, arrived)
    copy.start()
    for plane in range(east + 2):
        put_stack(grad_ref[plane].astype(F32), upward, (even_ref, odd_ref), plane % 2, plane // 2)
    copy.wait()
    put_back(back1_ref, w1_ref, channels)
    for first, stop in grouped(east // 2, 4):
        for i, parity, value in convolve((even_ref, odd_ref), back1_ref, first, stop, size, upward):
            plane = 2 * i + parity
            mask = center_ref[plane, :, channels : channels + 1].astype(F32)
            out_ref[plane] = (mask * value)[:, 0:channels].astype(BF16)


def parts_kernel(place_ref, kept_ref, came_ref, total_ref, *sent_refs):
    part = total_ref.shape[0]
    for change, ref in enumerate((total_ref,) + sent_refs):
        start = pl.multiple_of((place_ref[0] ^ change) * part, part)
        rows = pl.ds(start, part)
        ref[...] = (kept_ref[rows, :].astype(F32) + came_ref[rows, :].astype(F32)).astype(ref.dtype)


def unpack_kernel(channels, scale, aliased, first_ref_flag, packed_ref, *refs):
    first_out, second_out, whole_ref, done = refs[2:] if aliased else refs
    spare = LANES - channels
    is_first = first_ref_flag[0] == 1
    spans = [(t, min(t + 4, 27)) for t in range(0, 27, 4)]

    def copy_of(target, i):
        a, b = spans[i]
        return pltpu.make_async_copy(whole_ref.at[a:b], target.at[a:b], done.at[i])

    for i, (t, stop) in enumerate(spans):
        tiles = []
        for r in range(3):
            start = (t // 4 * 3 + r) * channels
            tiles.append(packed_ref[start : start + channels, :].astype(F32) * scale)
        for r in range(3):
            whole_ref[t + r] = tiles[r][:, 0:channels]
        if stop - t == 4:
            lane = lane_of(tiles[0].shape)
            parts = [pltpu.roll(tiles[r], (spare * r - channels) % LANES, 1) for r in range(3)]
            last = jnp.where(lane < spare, parts[0], jnp.where(lane < 2 * spare, parts[1], parts[2]))
            whole_ref[t + 3] = last[:, 0:channels]

        @pl.when(is_first)
        def _(i=i):
            copy_of(first_out, i).start()

        @pl.when(jnp.logical_not(is_first))
        def _(i=i):
            copy_of(second_out, i).start()

    for i in range(len(spans)):
        copy_of(first_out, i).wait()


def per_device(
    features, brick_active, voxel_occupancy, first_weights, second_weights, head, teacher
):
    channels = features.shape[0]
    east, north, upward = features.shape[1:]
    classes = teacher.shape[0]
    devices = lax.axis_size("east") * lax.axis_size("north")
    scale = 1.0 / math.sqrt(devices * east * north * upward)
    planes = east + 2 * HALO
    rows = (north + 2 * HALO) * upward
    edge, size = HALO * upward, north * upward
    vmem = pl.BlockSpec(memory_space=pltpu.VMEM)
    smem = pl.BlockSpec(memory_space=pltpu.SMEM)
    anywhere = pl.BlockSpec(memory_space=pl.ANY)
    far = pl.BlockSpec(memory_space=pltpu.HBM)

    east_bits, north_bits = bits_of("east"), bits_of("north")
    rest = north_bits + east_bits[1:]
    near, others = rest[:2], rest[2:]
    upper = high_bit(*east_bits[0])
    easts, norths = rounds_of("east"), rounds_of("north")
    counts = (len(easts), len(norths))

    shapes = [(HALO, size, LANES)] * counts[0] + [(east, edge, LANES)] * counts[1]
    shapes += [(HALO, edge, LANES)] * (counts[0] * counts[1])
    center, *edges = pl.pallas_call(
        functools.partial(prepare_kernel, channels, upward, edge),
        out_shape=[jax.ShapeDtypeStruct(shape, BF16) for shape in [(east, size, LANES)] + shapes],
        in_specs=[far] * 4,
        out_specs=[vmem] * (1 + len(shapes)),
        scratch_shapes=[
            pltpu.SMEM((brick_active.shape[0], brick_active.shape[2], brick_active.shape[1]), jnp.int32),
            pltpu.VMEM((east, size, channels), BF16),
            pltpu.VMEM((east, upward, north), jnp.int32),
            pltpu.VMEM((classes, east, upward, north), BF16),
            pltpu.SemaphoreType.DMA((4,)),
        ],
        compiler_params=pltpu.CompilerParams(vmem_limit_bytes=6 * 1024 * 1024),
        name="prepare",
    )(
        *[
            pltpu.with_memory_space_constraint(value, pltpu.HBM)
            for value in (
                brick_active.transpose(0, 2, 1),
                features.transpose(1, 2, 3, 0).reshape(east, size, channels),
                voxel_occupancy.transpose(0, 2, 1),
                teacher.transpose(0, 1, 3, 2),
            )
        ]
    )
    stay = [list(range(lax.axis_size(axis))) for axis in ("east", "north")]
    routes = [(partners, stay[1]) for partners, _, _ in easts] + [(stay[0], partners) for partners, _, _ in norths]
    routes += [(a, b) for a, _, _ in easts for b, _, _ in norths]
    edges = [exchange(value, *route) for value, route in zip(edges, routes)]

    unit = devices // 2 * 16
    packed = -(-21 * channels // unit) * unit
    first_far, second_far, head_far = [
        pltpu.with_memory_space_constraint(value, pltpu.HBM) for value in (first_weights, second_weights, head)
    ]
    ahead1, back2, head_wide = pl.pallas_call(
        functools.partial(weights_kernel, channels, classes),
        out_shape=[jax.ShapeDtypeStruct(shape, BF16) for shape in ((4 * WIDE, 2 * LANES), (4 * WIDE, 2 * LANES), (LANES, LANES))],
        in_specs=[far] * 3,
        out_specs=[vmem] * 3,
        scratch_shapes=[
            pltpu.VMEM(first_weights.shape, BF16),
            pltpu.VMEM(second_weights.shape, BF16),
            pltpu.VMEM(head.shape, BF16),
            pltpu.SemaphoreType.DMA((3,)),
        ],
        compiler_params=pltpu.CompilerParams(vmem_limit_bytes=10 * 1024 * 1024),
        name="weights",
    )(first_far, second_far, head_far)
    grad, kept, sent = pl.pallas_call(
        functools.partial(whole_kernel, channels, classes, east, north, upward, len(edges)),
        out_shape=(
            jax.ShapeDtypeStruct((east + 2, rows - 6 * upward, LANES), BF16),
            jax.ShapeDtypeStruct((packed, LANES), BF16),
            jax.ShapeDtypeStruct((packed, LANES), BF16),
        ),
        in_specs=[vmem, far] + [vmem] * (3 + len(edges)),
        out_specs=(vmem, vmem, vmem),
        scratch_shapes=[
            pltpu.VMEM((planes, rows, LANES), BF16),
            *stack_shapes(planes, rows, upward),
            *stack_shapes(planes - 2, rows - 4 * upward, upward),
            *stack_shapes(planes - 4, rows - 6 * upward, upward),
            pltpu.VMEM((planes, rows, LANES), F32),
            pltpu.VMEM((planes - 2, rows, LANES), F32),
            pltpu.VMEM((3 * channels, east * size), BF16),
            pltpu.VMEM((4 * WIDE, 2 * LANES), BF16),
            pltpu.VMEM(second_weights.shape, BF16),
            pltpu.SemaphoreType.DMA(()),
        ],
        compiler_params=pltpu.CompilerParams(vmem_limit_bytes=28 * 1024 * 1024),
        name="fields",
    )(ahead1, second_far, back2, head_wide, center, *edges)

    features_out = []

    def beside(kept):
        out, kept = pl.pallas_call(
            functools.partial(last_kernel, channels, east, north, upward),
            out_shape=(
                jax.ShapeDtypeStruct((east, size, channels), BF16),
                jax.ShapeDtypeStruct(kept.shape, F32),
            ),
            in_specs=[vmem, vmem, far, anywhere],
            out_specs=(vmem, anywhere),
            input_output_aliases={3: 1},
            scratch_shapes=[
                *stack_shapes(east + 2, size, upward),
                pltpu.VMEM((4 * WIDE, 2 * LANES), BF16),
                pltpu.VMEM(first_weights.shape, BF16),
                pltpu.SemaphoreType.DMA(()),
            ],
            compiler_params=pltpu.CompilerParams(vmem_limit_bytes=10 * 1024 * 1024),
            name="features",
        )(center, grad, first_far, kept)
        features_out.append(out)
        return kept

    ways = 1 << len(near)
    part = packed // ways
    total, *parts = pl.pallas_call(
        parts_kernel,
        out_shape=[jax.ShapeDtypeStruct((part, LANES), F32)]
        + [jax.ShapeDtypeStruct((part, LANES), BF16)] * (ways - 1),
        in_specs=[smem] + [vmem] * 2,
        out_specs=[vmem] * ways,
        compiler_params=pltpu.CompilerParams(vmem_limit_bytes=4 * 1024 * 1024),
        name="parts",
    )(place_in(near).reshape(1).astype(jnp.int32), kept, swap(sent, east_bits[:1], 1))
    total = beside(total)
    for change in range(ways - 1, 0, -1):
        total = total + swap(parts[change - 1], near, change).astype(F32)
    mine = gather_parts(share_sums(total, others), [near])
    other = swap(mine, east_bits[:1], 1)

    def unpack(is_first, value, *aliased):
        return pl.pallas_call(
            functools.partial(unpack_kernel, channels, scale, bool(aliased)),
            out_shape=(
                jax.ShapeDtypeStruct(first_weights.shape, F32),
                jax.ShapeDtypeStruct(second_weights.shape, F32),
            ),
            in_specs=[smem, vmem] + [anywhere] * len(aliased),
            out_specs=(anywhere, anywhere),
            input_output_aliases={2: 0, 3: 1} if aliased else {},
            scratch_shapes=[pltpu.VMEM(first_weights.shape, F32), pltpu.SemaphoreType.DMA((7,))],
            compiler_params=pltpu.CompilerParams(vmem_limit_bytes=5 * 1024 * 1024),
            name="unpack",
        )(is_first.reshape(1).astype(jnp.int32), value, *aliased)

    outputs = unpack(upper, mine)
    grad_first, grad_second = unpack(1 - upper, other, *outputs)
    (grad_features,) = features_out
    grad_features = grad_features.reshape(east, north, upward, channels).transpose(3, 0, 1, 2)
    return (grad_features, grad_first, grad_second)


def solution(mesh):
    in_specs = (
        P(None, "east", "north", None),
        P("east", "north", None),
        P("east", "north", None),
        P(),
        P(),
        P(),
        P(None, "east", "north", None),
    )
    out_specs = (P(None, "east", "north", None), P(), P())
    return jax.shard_map(
        per_device, mesh=mesh, in_specs=in_specs, out_specs=out_specs, check_vma=False
    )
```

```python
import functools
import math

import jax
import jax.numpy as jnp
from jax import lax
from jax.experimental import pallas as pl
from jax.experimental.pallas import tpu as pltpu
from jax.sharding import PartitionSpec as P

LANES = 128
HALO = 4
OFFSETS = 9
WIDE = OFFSETS * LANES
F32 = jnp.float32
BF16 = jnp.bfloat16


def rounds_of(axis):
    count = lax.axis_size(axis)
    me = lax.axis_index(axis)
    rounds = [([i ^ 1 for i in range(count)], me % 2, jnp.int32(1))]
    if count > 2:
        inside = ((me > 0) & (me < count - 1)).astype(jnp.int32)
        partners = [0] + [((i - 1) ^ 1) + 1 for i in range(1, count - 1)] + [count - 1]
        rounds.append((partners, (me + 1) % 2, inside))
    return rounds


def exchange(value, east, north):
    count = len(north)
    target = {(e, n): (f, m) for e, f in enumerate(east) for n, m in enumerate(north)}
    alone = [place for place, other in target.items() if place == other]
    while alone:
        e, n = alone.pop(0)
        near = [place for place in ((e, n ^ 1), (e ^ 1, n)) if place in alone]
        other = near[0] if near else alone[0]
        alone.remove(other)
        target[e, n], target[other] = other, (e, n)
    pairs = [(e * count + n, f * count + m) for (e, n), (f, m) in target.items()]
    return lax.ppermute(value, ("east", "north"), pairs)


def high_bit(axis, bit):
    return (lax.axis_index(axis) // bit) % 2


def bits_of(axis):
    size = lax.axis_size(axis)
    return [(axis, 1 << i) for i in range(size.bit_length() - 1)]


def place_in(group):
    return sum(high_bit(axis, bit) << i for i, (axis, bit) in enumerate(group))


def swap(value, group, change):
    masks = {"east": 0, "north": 0}
    for i, (axis, bit) in enumerate(group):
        if change >> i & 1:
            masks[axis] |= bit
    partners = [[i ^ masks[axis] for i in range(lax.axis_size(axis))] for axis in ("east", "north")]
    return exchange(value, *partners)


def share_sums(total, bits):
    total = total.astype(BF16)
    for bit in bits:
        total = (total.astype(F32) + swap(total, [bit], 1).astype(F32)).astype(BF16)
    return total


def gather_parts(mine, groups):
    for group in reversed(groups):
        ways = 1 << len(group)
        place = place_in(group)
        parts = [mine] + [swap(mine, group, change) for change in range(1, ways)]
        joined = []
        for row in range(ways):
            piece = parts[0]
            for change in range(1, ways):
                piece = jnp.where((place ^ row) == change, parts[change], piece)
            joined.append(piece)
        mine = jnp.concatenate(joined, 0)
    return mine


def lane_of(shape):
    return lax.broadcasted_iota(jnp.int32, shape, len(shape) - 1)


def put_stack(value, upward, stack, parity, index):
    even_ref, odd_ref = stack
    total = value.shape[0]
    rows = total - 2 * upward
    cubes = value.reshape(total // upward, upward, LANES)
    level = lax.broadcasted_iota(jnp.int32, cubes.shape, 1)
    below = jnp.where(level == 0, 0.0, pltpu.roll(cubes, 1, 1)).reshape(total, LANES)
    above = jnp.where(level == upward - 1, 0.0, pltpu.roll(cubes, upward - 1, 1)).reshape(total, LANES)
    for up, moved in enumerate((below, value, above)):
        lanes = slice(up * LANES, (up + 1) * LANES)
        even_ref[parity, index * total : (index + 1) * total, lanes] = moved.astype(BF16)
        odd_ref[parity, index * rows : (index + 1) * rows, lanes] = moved[upward : upward + rows].astype(BF16)


def shifts_of(stack, plane, rows, upward, start, size):
    even_ref, odd_ref = stack
    even = (plane // 2) * (rows + 2 * upward) + start
    odd = (plane // 2) * rows + start
    return jnp.concatenate(
        [
            even_ref[plane % 2, even : even + size, :],
            odd_ref[plane % 2, odd : odd + size, :],
            even_ref[plane % 2, even + 2 * upward : even + 2 * upward + size, :],
        ],
        1,
    )


def stack_shapes(planes, rows, upward):
    return [pltpu.VMEM((2, planes // 2 * (rows + extra), 3 * LANES), BF16) for extra in (2 * upward, 0)]


def grouped(pairs, size):
    count = max(1, pairs // size)
    edges = [pairs * i // count for i in range(count + 1)]
    return list(zip(edges, edges[1:]))


def convolve(stack, weight_ref, first, stop, rows, upward):
    fields = [
        jnp.concatenate([shifts_of(stack, 2 * pair + p, rows, upward, 0, rows) for p in range(4)], 1)
        for pair in range(first, stop)
    ]
    both = jnp.dot(jnp.concatenate(fields, 0), weight_ref[...], preferred_element_type=F32)
    return [
        (pair, parity, both[(pair - first) * rows : (pair - first + 1) * rows, parity * LANES : (parity + 1) * LANES])
        for pair in range(first, stop)
        for parity in range(2)
    ]


def staged(stages):
    held, done = None, [0] * len(stages)

    def finish():
        number, last, outcome = held
        stages[number][2](outcome, last)
        done[number] += len(outcome)

    for number, (runs, product, _) in enumerate(stages):
        for run in runs:
            if number > 0 and done[number - 1] < 2 * run[1] + 2:
                finish()
                held = None
            coming = (number, run == runs[-1], product(*run))
            if held is not None:
                finish()
            held = coming
    finish()


def unit_of(channels):
    row = lax.broadcasted_iota(jnp.int32, (channels, LANES), 0)
    return (row == lax.broadcasted_iota(jnp.int32, (channels, LANES), 1)).astype(BF16)


def put_back(back_ref, w_ref, channels):
    unit = unit_of(channels)
    border = jnp.zeros((LANES - channels, channels), BF16)
    for d in range(3):
        for j in range(OFFSETS):
            wide = jnp.concatenate([w_ref[d * OFFSETS + j], border], 0)
            block = jnp.dot(wide, unit, preferred_element_type=F32).astype(BF16)
            for q in range(2):
                row = ((2 - d + q) * OFFSETS + OFFSETS - 1 - j) * LANES
                back_ref[row : row + LANES, q * LANES : (q + 1) * LANES] = block
    put_zeros(back_ref)


def put_zeros(target_ref):
    run = OFFSETS * LANES
    target_ref[0:run, LANES : 2 * LANES] = jnp.zeros((run, LANES), BF16)
    target_ref[3 * run : 4 * run, 0:LANES] = jnp.zeros((run, LANES), BF16)


def put_ahead(ahead_ref, w_ref, channels):
    unit = unit_of(channels)
    border = jnp.zeros((LANES - channels, channels), BF16)
    for d in range(3):
        for j in range(OFFSETS):
            wide = jnp.concatenate([w_ref[d * OFFSETS + j], border], 0)
            turned = lax.dot_general(unit, wide, (((0,), (1,)), ((), ())), preferred_element_type=F32).astype(BF16)
            for q in range(2):
                row = ((d + q) * OFFSETS + j) * LANES
                ahead_ref[row : row + LANES, q * LANES : (q + 1) * LANES] = turned
    put_zeros(ahead_ref)


def weights_kernel(
    channels, classes,
    w1_in, w2_in, head_in,
    ahead1_ref, back2_ref, head_out,
    w1_ref, w2_ref, head_ref, arrived,
):
    copies = [
        pltpu.make_async_copy(source, target, arrived.at[i])
        for i, (source, target) in enumerate(((w1_in, w1_ref), (w2_in, w2_ref), (head_in, head_ref)))
    ]
    for copy in copies:
        copy.start()
    for copy in copies:
        copy.wait()
    put_ahead(ahead1_ref, w1_ref, channels)
    put_back(back2_ref, w2_ref, channels)
    head_out[...] = jnp.zeros_like(head_out)
    row = lax.broadcasted_iota(jnp.int32, (LANES, classes), 0)
    spread = (row == lax.broadcasted_iota(jnp.int32, (LANES, classes), 1) + channels + 1).astype(BF16)
    head_out[:, 0:channels] = jnp.dot(spread, head_ref[...], preferred_element_type=F32).astype(BF16)


def put_turned(turned_ref, value, plane, east, channels):
    turned = value.astype(BF16).T[0:channels]
    size = value.shape[0]
    for d in range(3):
        e = plane + d - 1
        if 0 <= e < east:
            turned_ref[d * channels : (d + 1) * channels, e * size : (e + 1) * size] = turned


def kernel_sum(turned_ref, stack, first, east, rows, upward, low, size, channels):
    fields = [shifts_of(stack, plane, rows, upward, low, size) for plane in range(first, first + east)]
    total = jnp.dot(turned_ref[...], jnp.concatenate(fields, 0), preferred_element_type=F32)
    blocks = [
        total[d * channels : (d + 1) * channels, j * LANES : (j + 1) * LANES]
        for d in range(3)
        for j in range(OFFSETS)
    ]
    blocks.append(jnp.zeros_like(blocks[0]))
    lane = lane_of(blocks[0].shape)
    spare = LANES - channels
    tiles = []
    for t in range(0, 28, 4):
        for r in range(3):
            tail = pltpu.roll(blocks[t + 3], channels - spare * r, 1)
            tiles.append(jnp.where(lane < channels, blocks[t + r], tail))
    return tiles


def prepare_kernel(
    channels, upward, edge,
    active_in, features_in, occupied_in, teacher_in,
    center_ref, *edge_refs,
):
    *edge_refs, active_ref, features_ref, occupied_ref, teacher_ref, arrived = edge_refs
    copies = [
        pltpu.make_async_copy(source, target, arrived.at[i])
        for i, (source, target) in enumerate(
            (
                (active_in, active_ref),
                (occupied_in, occupied_ref),
                (teacher_in, teacher_ref),
                (features_in, features_ref),
            )
        )
    ]
    for copy in copies:
        copy.start()
    for copy in copies[:-1]:
        copy.wait()
    east, size, _ = center_ref.shape
    north = size // upward
    classes = teacher_ref.shape[0]
    wide = (classes + 1) * upward
    row = lax.broadcasted_iota(jnp.int32, (size, north), 0) // upward
    spread = (row == lax.broadcasted_iota(jnp.int32, (size, north), 1)).astype(BF16)
    level = lax.broadcasted_iota(jnp.int32, (size, wide), 0) % upward
    same = level == lax.broadcasted_iota(jnp.int32, (size, wide), 1) % upward
    target = lax.broadcasted_iota(jnp.int32, (wide, LANES), 0) // upward + channels
    gather = (target == lax.broadcasted_iota(jnp.int32, (wide, LANES), 1)).astype(BF16)
    bricks = active_ref.shape
    up = lax.broadcasted_iota(jnp.int32, (upward, north), 0) // (upward // bricks[1])
    along = lax.broadcasted_iota(jnp.int32, (upward, north), 1) // (north // bricks[2])
    for e in range(east):
        mask = jnp.zeros((upward, north), jnp.int32)
        for b in range(bricks[2]):
            for c in range(bricks[1]):
                inside = (along == b) & (up == c)
                mask = jnp.where(inside, active_ref[e // (east // bricks[0]), c, b], mask)
        mask = (mask * occupied_ref[e]).astype(F32)
        goal = teacher_ref[:, e].astype(F32).reshape(classes * upward, north)
        field = jnp.concatenate([mask, goal], 0).astype(BF16)
        everywhere = lax.dot_general(spread, field, (((1,), (1,)), ((), ())), preferred_element_type=F32)
        own = jnp.where(same, everywhere, 0.0).astype(BF16)
        tail = jnp.dot(own, gather, preferred_element_type=F32).astype(BF16)
        center_ref[e, :, channels:LANES] = tail[:, channels:LANES]
    copies[-1].wait()
    center_ref[:, :, 0:channels] = features_ref[...]
    east_starts = [(1 - side) * (east - HALO) for _, side, _ in rounds_of("east")]
    north_starts = [pl.multiple_of((1 - side) * (size - edge), edge) for _, side, _ in rounds_of("north")]
    edge_refs = iter(edge_refs)
    for e in east_starts:
        next(edge_refs)[...] = center_ref[pl.ds(e, HALO)]
    for n in north_starts:
        next(edge_refs)[...] = center_ref[:, pl.ds(n, edge), :]
    for e in east_starts:
        for n in north_starts:
            next(edge_refs)[...] = center_ref[pl.ds(e, HALO), pl.ds(n, edge), :]


def place_edges(center_ref, edge_refs, edge, x_ref):
    east, size, _ = center_ref.shape
    x_ref[...] = jnp.zeros_like(x_ref)
    x_ref[HALO : HALO + east, edge : edge + size, :] = center_ref[...]
    edge_refs = iter(edge_refs)
    middle_east, middle_north = pl.ds(HALO, east), pl.ds(edge, size)
    east_places = [(pl.ds((1 - side) * (east + HALO), HALO), inside) for _, side, inside in rounds_of("east")]
    north_places = [
        (pl.ds(pl.multiple_of((1 - side) * (size + edge), edge), edge), inside)
        for _, side, inside in rounds_of("north")
    ]
    spots = [(e, middle_north, inside) for e, inside in east_places]
    spots += [(middle_east, n, inside) for n, inside in north_places]
    spots += [(e, n, a * b) for e, a in east_places for n, b in north_places]
    for e, n, inside in spots:
        ref = next(edge_refs)

        @pl.when(inside == 1)
        def _(ref=ref, e=e, n=n):
            x_ref[e, n, :] = ref[...]


def whole_kernel(
    channels, classes, east, north, upward, edges,
    ahead1_ref, w2_in, back2_ref, head_ref, center_ref, *refs,
):
    (
        grad_ref, kept_ref, sent_ref,
        x_ref, even0, odd0, even1, odd1, even2, odd2, mask_ref, slope_ref, turned_ref, ahead2_ref, w2_ref, arrived,
    ) = refs[edges:]
    stack0, stack1, stack2 = (even0, odd0), (even1, odd1), (even2, odd2)
    copy = pltpu.make_async_copy(w2_in, w2_ref, arrived)
    copy.start()
    rows = (north + 2 * HALO) * upward
    low, size = HALO * upward, north * upward
    planes = east + 2 * HALO
    lane = lane_of((rows, LANES))
    rows1, rows2, rows3 = rows - 2 * upward, rows - 4 * upward, rows - 6 * upward
    low1, low2, low3 = low - upward, low - 2 * upward, low - 3 * upward

    place_edges(center_ref, refs[:edges], low, x_ref)
    border = jnp.zeros((upward, LANES), F32)

    for plane in range(planes):
        x = x_ref[plane].astype(F32)
        mask = jnp.broadcast_to(x[:, channels : channels + 1], (rows, LANES))
        mask_ref[plane] = mask
        a0 = jnp.where((mask > 0) & (lane < channels), x, 0.0)
        put_stack(jnp.concatenate([border, a0, border], 0), upward, stack0, plane % 2, plane // 2)

    head = head_ref[...]
    class_lane = (lane[0:rows2] > channels) & (lane[0:rows2] <= channels + classes)
    here = slice(2 * upward, 2 * upward + rows2)
    there = slice(2 * upward + upward, 2 * upward + upward + rows3)

    def first_forward(outcome, last):
        if outcome[0][0] == 0:
            copy.wait()
            put_ahead(ahead2_ref, w2_ref, channels)
        for i, parity, value in outcome:
            plane = 2 * i + parity
            mask = mask_ref[plane + 1]
            p1 = mask * value
            sig = 0.5 * jnp.tanh(0.5 * p1) + 0.5
            slope_ref[plane] = mask * (sig * (1.0 + p1 * (1.0 - sig)))
            put_stack((p1 * sig)[upward : upward + rows1], upward, stack1, parity, i)

    def second_forward(outcome, last):
        a2, slopes, errors = [], [], []
        for i, parity, value in outcome:
            mask = mask_ref[2 * i + parity + 2, here]
            p2 = mask * value
            sig = 0.5 * jnp.tanh(0.5 * p2) + 0.5
            a2.append((p2 * sig).astype(BF16))
            slopes.append(mask * (sig * (1.0 + p2 * (1.0 - sig))))
        logits = lax.dot_general(
            jnp.concatenate(a2, 0), head, (((1,), (1,)), ((), ())), preferred_element_type=F32
        )
        for number, (i, parity, _) in enumerate(outcome):
            plane = 2 * i + parity + 2
            own = logits[number * rows2 : (number + 1) * rows2]
            error = jnp.where(class_lane, mask_ref[plane, here] * (own - x_ref[plane, here].astype(F32)), 0.0)
            coarse = error.astype(BF16)
            fine = (error - coarse.astype(F32)).astype(BF16)
            errors.append(jnp.concatenate([coarse, fine], 1))
        g_a2 = jnp.dot(jnp.concatenate(errors, 0), jnp.concatenate([head, head], 0), preferred_element_type=F32)
        for number, (i, parity, _) in enumerate(outcome):
            g_p2 = g_a2[number * rows2 : (number + 1) * rows2] * slopes[number]
            put_stack(g_p2, upward, stack2, parity, i)
            put_turned(turned_ref, g_p2[low2 : low2 + size], 2 * i + parity - 2, east, channels)
        if last:
            for t, tile in enumerate(kernel_sum(turned_ref, stack1, 3, east, rows2, upward, low2, size, channels)):
                kept_ref[t * channels : (t + 1) * channels, :] = tile.astype(BF16)

    def second_backward(outcome, last):
        for i, parity, value in outcome:
            plane = 2 * i + parity
            g_p1 = slope_ref[plane + 2, there] * value
            grad_ref[plane] = g_p1.astype(BF16)
            put_turned(turned_ref, g_p1[low3 : low3 + size], plane - 1, east, channels)

    steps = (
        (2, stack0, ahead1_ref, rows, first_forward),
        (4, stack1, ahead2_ref, rows2, second_forward),
        (6, stack2, back2_ref, rows3, second_backward),
    )
    staged(
        [
            (
                grouped((planes - margin) // 2, 2),
                functools.partial(convolve, stack, weight_ref, rows=height, upward=upward),
                handler,
            )
            for margin, stack, weight_ref, height, handler in steps
        ]
    )
    upper = high_bit("east", 1) == 1
    tiles = kernel_sum(turned_ref, stack0, 4, east, rows, upward, low, size, channels)
    for t, tile in enumerate(tiles):
        place = slice(t * channels, (t + 1) * channels)
        first, second = tile.astype(BF16), kept_ref[place, :]
        sent_ref[place, :] = jnp.where(upper, second, first)
        kept_ref[place, :] = jnp.where(upper, first, second)
    filled = len(tiles) * channels
    if filled < kept_ref.shape[0]:
        kept_ref[filled:, :] = jnp.zeros((kept_ref.shape[0] - filled, LANES), BF16)
        sent_ref[filled:, :] = jnp.zeros((kept_ref.shape[0] - filled, LANES), BF16)


def last_kernel(
    channels, east, north, upward,
    center_ref, grad_ref, w1_in, kept_in,
    out_ref, kept_out,
    even_ref, odd_ref, back1_ref, w1_ref, arrived,
):
    size = north * upward
    copy = pltpu.make_async_copy(w1_in, w1_ref, arrived)
    copy.start()
    for plane in range(east + 2):
        put_stack(grad_ref[plane].astype(F32), upward, (even_ref, odd_ref), plane % 2, plane // 2)
    copy.wait()
    put_back(back1_ref, w1_ref, channels)
    for first, stop in grouped(east // 2, 4):
        for i, parity, value in convolve((even_ref, odd_ref), back1_ref, first, stop, size, upward):
            plane = 2 * i + parity
            mask = center_ref[plane, :, channels : channels + 1].astype(F32)
            out_ref[plane] = (mask * value)[:, 0:channels].astype(BF16)


def parts_kernel(place_ref, kept_ref, came_ref, total_ref, *sent_refs):
    part = total_ref.shape[0]
    for change, ref in enumerate((total_ref,) + sent_refs):
        start = pl.multiple_of((place_ref[0] ^ change) * part, part)
        rows = pl.ds(start, part)
        ref[...] = (kept_ref[rows, :].astype(F32) + came_ref[rows, :].astype(F32)).astype(ref.dtype)


def unpack_kernel(channels, scale, aliased, first_ref_flag, packed_ref, *refs):
    first_out, second_out, whole_ref, done = refs[2:] if aliased else refs
    spare = LANES - channels
    is_first = first_ref_flag[0] == 1
    spans = [(t, min(t + 4, 27)) for t in range(0, 27, 4)]

    def copy_of(target, i):
        a, b = spans[i]
        return pltpu.make_async_copy(whole_ref.at[a:b], target.at[a:b], done.at[i])

    for i, (t, stop) in enumerate(spans):
        tiles = []
        for r in range(3):
            start = (t // 4 * 3 + r) * channels
            tiles.append(packed_ref[start : start + channels, :].astype(F32) * scale)
        for r in range(3):
            whole_ref[t + r] = tiles[r][:, 0:channels]
        if stop - t == 4:
            lane = lane_of(tiles[0].shape)
            parts = [pltpu.roll(tiles[r], (spare * r - channels) % LANES, 1) for r in range(3)]
            last = jnp.where(lane < spare, parts[0], jnp.where(lane < 2 * spare, parts[1], parts[2]))
            whole_ref[t + 3] = last[:, 0:channels]

        @pl.when(is_first)
        def _(i=i):
            copy_of(first_out, i).start()

        @pl.when(jnp.logical_not(is_first))
        def _(i=i):
            copy_of(second_out, i).start()

    for i in range(len(spans)):
        copy_of(first_out, i).wait()


def per_device(
    features, brick_active, voxel_occupancy, first_weights, second_weights, head, teacher
):
    channels = features.shape[0]
    east, north, upward = features.shape[1:]
    classes = teacher.shape[0]
    devices = lax.axis_size("east") * lax.axis_size("north")
    scale = 1.0 / math.sqrt(devices * east * north * upward)
    planes = east + 2 * HALO
    rows = (north + 2 * HALO) * upward
    edge, size = HALO * upward, north * upward
    vmem = pl.BlockSpec(memory_space=pltpu.VMEM)
    smem = pl.BlockSpec(memory_space=pltpu.SMEM)
    anywhere = pl.BlockSpec(memory_space=pl.ANY)
    far = pl.BlockSpec(memory_space=pltpu.HBM)

    east_bits, north_bits = bits_of("east"), bits_of("north")
    rest = north_bits + east_bits[1:]
    near, others = rest[:2], rest[2:]
    upper = high_bit(*east_bits[0])
    easts, norths = rounds_of("east"), rounds_of("north")
    counts = (len(easts), len(norths))

    shapes = [(HALO, size, LANES)] * counts[0] + [(east, edge, LANES)] * counts[1]
    shapes += [(HALO, edge, LANES)] * (counts[0] * counts[1])
    center, *edges = pl.pallas_call(
        functools.partial(prepare_kernel, channels, upward, edge),
        out_shape=[jax.ShapeDtypeStruct(shape, BF16) for shape in [(east, size, LANES)] + shapes],
        in_specs=[far] * 4,
        out_specs=[vmem] * (1 + len(shapes)),
        scratch_shapes=[
            pltpu.SMEM((brick_active.shape[0], brick_active.shape[2], brick_active.shape[1]), jnp.int32),
            pltpu.VMEM((east, size, channels), BF16),
            pltpu.VMEM((east, upward, north), jnp.int32),
            pltpu.VMEM((classes, east, upward, north), BF16),
            pltpu.SemaphoreType.DMA((4,)),
        ],
        compiler_params=pltpu.CompilerParams(vmem_limit_bytes=6 * 1024 * 1024),
        name="prepare",
    )(
        *[
            pltpu.with_memory_space_constraint(value, pltpu.HBM)
            for value in (
                brick_active.transpose(0, 2, 1),
                features.transpose(1, 2, 3, 0).reshape(east, size, channels),
                voxel_occupancy.transpose(0, 2, 1),
                teacher.transpose(0, 1, 3, 2),
            )
        ]
    )
    stay = [list(range(lax.axis_size(axis))) for axis in ("east", "north")]
    routes = [(partners, stay[1]) for partners, _, _ in easts] + [(stay[0], partners) for partners, _, _ in norths]
    routes += [(a, b) for a, _, _ in easts for b, _, _ in norths]
    edges = [exchange(value, *route) for value, route in zip(edges, routes)]

    unit = devices // 2 * 16
    packed = -(-21 * channels // unit) * unit
    first_far, second_far, head_far = [
        pltpu.with_memory_space_constraint(value, pltpu.HBM) for value in (first_weights, second_weights, head)
    ]
    ahead1, back2, head_wide = pl.pallas_call(
        functools.partial(weights_kernel, channels, classes),
        out_shape=[jax.ShapeDtypeStruct(shape, BF16) for shape in ((4 * WIDE, 2 * LANES), (4 * WIDE, 2 * LANES), (LANES, LANES))],
        in_specs=[far] * 3,
        out_specs=[vmem] * 3,
        scratch_shapes=[
            pltpu.VMEM(first_weights.shape, BF16),
            pltpu.VMEM(second_weights.shape, BF16),
            pltpu.VMEM(head.shape, BF16),
            pltpu.SemaphoreType.DMA((3,)),
        ],
        compiler_params=pltpu.CompilerParams(vmem_limit_bytes=10 * 1024 * 1024),
        name="weights",
    )(first_far, second_far, head_far)
    grad, kept, sent = pl.pallas_call(
        functools.partial(whole_kernel, channels, classes, east, north, upward, len(edges)),
        out_shape=(
            jax.ShapeDtypeStruct((east + 2, rows - 6 * upward, LANES), BF16),
            jax.ShapeDtypeStruct((packed, LANES), BF16),
            jax.ShapeDtypeStruct((packed, LANES), BF16),
        ),
        in_specs=[vmem, far] + [vmem] * (3 + len(edges)),
        out_specs=(vmem, vmem, vmem),
        scratch_shapes=[
            pltpu.VMEM((planes, rows, LANES), BF16),
            *stack_shapes(planes, rows, upward),
            *stack_shapes(planes - 2, rows - 4 * upward, upward),
            *stack_shapes(planes - 4, rows - 6 * upward, upward),
            pltpu.VMEM((planes, rows, LANES), F32),
            pltpu.VMEM((planes - 2, rows, LANES), F32),
            pltpu.VMEM((3 * channels, east * size), BF16),
            pltpu.VMEM((4 * WIDE, 2 * LANES), BF16),
            pltpu.VMEM(second_weights.shape, BF16),
            pltpu.SemaphoreType.DMA(()),
        ],
        compiler_params=pltpu.CompilerParams(vmem_limit_bytes=28 * 1024 * 1024),
        name="fields",
    )(ahead1, second_far, back2, head_wide, center, *edges)

    features_out = []

    def beside(kept):
        out, kept = pl.pallas_call(
            functools.partial(last_kernel, channels, east, north, upward),
            out_shape=(
                jax.ShapeDtypeStruct((east, size, channels), BF16),
                jax.ShapeDtypeStruct(kept.shape, F32),
            ),
            in_specs=[vmem, vmem, far, anywhere],
            out_specs=(vmem, anywhere),
            input_output_aliases={3: 1},
            scratch_shapes=[
                *stack_shapes(east + 2, size, upward),
                pltpu.VMEM((4 * WIDE, 2 * LANES), BF16),
                pltpu.VMEM(first_weights.shape, BF16),
                pltpu.SemaphoreType.DMA(()),
            ],
            compiler_params=pltpu.CompilerParams(vmem_limit_bytes=10 * 1024 * 1024),
            name="features",
        )(center, grad, first_far, kept)
        features_out.append(out)
        return kept

    ways = 1 << len(near)
    part = packed // ways
    total, *parts = pl.pallas_call(
        parts_kernel,
        out_shape=[jax.ShapeDtypeStruct((part, LANES), F32)]
        + [jax.ShapeDtypeStruct((part, LANES), BF16)] * (ways - 1),
        in_specs=[smem] + [vmem] * 2,
        out_specs=[vmem] * ways,
        compiler_params=pltpu.CompilerParams(vmem_limit_bytes=4 * 1024 * 1024),
        name="parts",
    )(place_in(near).reshape(1).astype(jnp.int32), kept, swap(sent, east_bits[:1], 1))
    total = beside(total)
    for change in range(ways - 1, 0, -1):
        total = total + swap(parts[change - 1], near, change).astype(F32)
    mine = gather_parts(share_sums(total, others), [near])
    other = swap(mine, east_bits[:1], 1)

    def unpack(is_first, value, *aliased):
        return pl.pallas_call(
            functools.partial(unpack_kernel, channels, scale, bool(aliased)),
            out_shape=(
                jax.ShapeDtypeStruct(first_weights.shape, F32),
                jax.ShapeDtypeStruct(second_weights.shape, F32),
            ),
            in_specs=[smem, vmem] + [anywhere] * len(aliased),
            out_specs=(anywhere, anywhere),
            input_output_aliases={2: 0, 3: 1} if aliased else {},
            scratch_shapes=[pltpu.VMEM(first_weights.shape, F32), pltpu.SemaphoreType.DMA((7,))],
            compiler_params=pltpu.CompilerParams(vmem_limit_bytes=5 * 1024 * 1024),
            name="unpack",
        )(is_first.reshape(1).astype(jnp.int32), value, *aliased)

    outputs = unpack(upper, mine)
    grad_first, grad_second = unpack(1 - upper, other, *outputs)
    (grad_features,) = features_out
    grad_features = grad_features.reshape(east, north, upward, channels).transpose(3, 0, 1, 2)
    return (grad_features, grad_first, grad_second)


def solution(mesh):
    in_specs = (
        P(None, "east", "north", None),
        P("east", "north", None),
        P("east", "north", None),
        P(),
        P(),
        P(),
        P(None, "east", "north", None),
    )
    out_specs = (P(None, "east", "north", None), P(), P())
    return jax.shard_map(
        per_device, mesh=mesh, in_specs=in_specs, out_specs=out_specs, check_vma=False
    )
```

```python
import functools
import math

import jax
import jax.numpy as jnp
from jax import lax
from jax.experimental import pallas as pl
from jax.experimental.pallas import tpu as pltpu
from jax.sharding import PartitionSpec as P

LANES = 128
HALO = 4
OFFSETS = 9
WIDE = OFFSETS * LANES
F32 = jnp.float32
BF16 = jnp.bfloat16


def rounds_of(axis):
    count = lax.axis_size(axis)
    me = lax.axis_index(axis)
    rounds = [([i ^ 1 for i in range(count)], me % 2, jnp.int32(1))]
    if count > 2:
        inside = ((me > 0) & (me < count - 1)).astype(jnp.int32)
        partners = [0] + [((i - 1) ^ 1) + 1 for i in range(1, count - 1)] + [count - 1]
        rounds.append((partners, (me + 1) % 2, inside))
    return rounds


def exchange(value, east, north):
    count = len(north)
    target = {(e, n): (f, m) for e, f in enumerate(east) for n, m in enumerate(north)}
    alone = [place for place, other in target.items() if place == other]
    while alone:
        e, n = alone.pop(0)
        near = [place for place in ((e, n ^ 1), (e ^ 1, n)) if place in alone]
        other = near[0] if near else alone[0]
        alone.remove(other)
        target[e, n], target[other] = other, (e, n)
    pairs = [(e * count + n, f * count + m) for (e, n), (f, m) in target.items()]
    return lax.ppermute(value, ("east", "north"), pairs)


def high_bit(axis, bit):
    return (lax.axis_index(axis) // bit) % 2


def bits_of(axis):
    size = lax.axis_size(axis)
    return [(axis, 1 << i) for i in range(size.bit_length() - 1)]


def place_in(group):
    return sum(high_bit(axis, bit) << i for i, (axis, bit) in enumerate(group))


def swap(value, group, change):
    masks = {"east": 0, "north": 0}
    for i, (axis, bit) in enumerate(group):
        if change >> i & 1:
            masks[axis] |= bit
    partners = [[i ^ masks[axis] for i in range(lax.axis_size(axis))] for axis in ("east", "north")]
    return exchange(value, *partners)


def share_sums(total, bits):
    total = total.astype(BF16)
    for bit in bits:
        total = (total.astype(F32) + swap(total, [bit], 1).astype(F32)).astype(BF16)
    return total


def gather_parts(mine, groups):
    for group in reversed(groups):
        ways = 1 << len(group)
        place = place_in(group)
        parts = [mine] + [swap(mine, group, change) for change in range(1, ways)]
        joined = []
        for row in range(ways):
            piece = parts[0]
            for change in range(1, ways):
                piece = jnp.where((place ^ row) == change, parts[change], piece)
            joined.append(piece)
        mine = jnp.concatenate(joined, 0)
    return mine


def lane_of(shape):
    return lax.broadcasted_iota(jnp.int32, shape, len(shape) - 1)


def put_stack(value, upward, stack, parity, index):
    even_ref, odd_ref = stack
    total = value.shape[0]
    rows = total - 2 * upward
    cubes = value.reshape(total // upward, upward, LANES)
    level = lax.broadcasted_iota(jnp.int32, cubes.shape, 1)
    below = jnp.where(level == 0, 0.0, pltpu.roll(cubes, 1, 1)).reshape(total, LANES)
    above = jnp.where(level == upward - 1, 0.0, pltpu.roll(cubes, upward - 1, 1)).reshape(total, LANES)
    for up, moved in enumerate((below, value, above)):
        lanes = slice(up * LANES, (up + 1) * LANES)
        even_ref[parity, index * total : (index + 1) * total, lanes] = moved.astype(BF16)
        odd_ref[parity, index * rows : (index + 1) * rows, lanes] = moved[upward : upward + rows].astype(BF16)


def shifts_of(stack, plane, rows, upward, start, size):
    even_ref, odd_ref = stack
    even = (plane // 2) * (rows + 2 * upward) + start
    odd = (plane // 2) * rows + start
    return jnp.concatenate(
        [
            even_ref[plane % 2, even : even + size, :],
            odd_ref[plane % 2, odd : odd + size, :],
            even_ref[plane % 2, even + 2 * upward : even + 2 * upward + size, :],
        ],
        1,
    )


def stack_shapes(planes, rows, upward):
    return [pltpu.VMEM((2, planes // 2 * (rows + extra), 3 * LANES), BF16) for extra in (2 * upward, 0)]


def grouped(pairs, size):
    count = max(1, pairs // size)
    edges = [pairs * i // count for i in range(count + 1)]
    return list(zip(edges, edges[1:]))


def convolve(stack, weight_ref, first, stop, rows, upward):
    fields = [
        jnp.concatenate([shifts_of(stack, 2 * pair + p, rows, upward, 0, rows) for p in range(4)], 1)
        for pair in range(first, stop)
    ]
    both = jnp.dot(jnp.concatenate(fields, 0), weight_ref[...], preferred_element_type=F32)
    return [
        (pair, parity, both[(pair - first) * rows : (pair - first + 1) * rows, parity * LANES : (parity + 1) * LANES])
        for pair in range(first, stop)
        for parity in range(2)
    ]


def staged(stages):
    held, done = None, [0] * len(stages)

    def finish():
        number, last, outcome = held
        stages[number][2](outcome, last)
        done[number] += len(outcome)

    for number, (runs, product, _) in enumerate(stages):
        for run in runs:
            if number > 0 and done[number - 1] < 2 * run[1] + 2:
                finish()
                held = None
            coming = (number, run == runs[-1], product(*run))
            if held is not None:
                finish()
            held = coming
    finish()


def unit_of(channels):
    row = lax.broadcasted_iota(jnp.int32, (channels, LANES), 0)
    return (row == lax.broadcasted_iota(jnp.int32, (channels, LANES), 1)).astype(BF16)


def put_back(back_ref, w_ref, channels):
    unit = unit_of(channels)
    border = jnp.zeros((LANES - channels, channels), BF16)
    for d in range(3):
        for j in range(OFFSETS):
            wide = jnp.concatenate([w_ref[d * OFFSETS + j], border], 0)
            block = jnp.dot(wide, unit, preferred_element_type=F32).astype(BF16)
            for q in range(2):
                row = ((2 - d + q) * OFFSETS + OFFSETS - 1 - j) * LANES
                back_ref[row : row + LANES, q * LANES : (q + 1) * LANES] = block
    put_zeros(back_ref)


def put_zeros(target_ref):
    run = OFFSETS * LANES
    target_ref[0:run, LANES : 2 * LANES] = jnp.zeros((run, LANES), BF16)
    target_ref[3 * run : 4 * run, 0:LANES] = jnp.zeros((run, LANES), BF16)


def put_ahead(ahead_ref, w_ref, channels):
    unit = unit_of(channels)
    border = jnp.zeros((LANES - channels, channels), BF16)
    for d in range(3):
        for j in range(OFFSETS):
            wide = jnp.concatenate([w_ref[d * OFFSETS + j], border], 0)
            turned = lax.dot_general(unit, wide, (((0,), (1,)), ((), ())), preferred_element_type=F32).astype(BF16)
            for q in range(2):
                row = ((d + q) * OFFSETS + j) * LANES
                ahead_ref[row : row + LANES, q * LANES : (q + 1) * LANES] = turned
    put_zeros(ahead_ref)


def weights_kernel(
    channels, classes,
    w1_in, w2_in, head_in,
    ahead1_ref, back2_ref, head_out,
    w1_ref, w2_ref, head_ref, arrived,
):
    copies = [
        pltpu.make_async_copy(source, target, arrived.at[i])
        for i, (source, target) in enumerate(((w1_in, w1_ref), (w2_in, w2_ref), (head_in, head_ref)))
    ]
    for copy in copies:
        copy.start()
    for copy in copies:
        copy.wait()
    put_ahead(ahead1_ref, w1_ref, channels)
    put_back(back2_ref, w2_ref, channels)
    head_out[...] = jnp.zeros_like(head_out)
    row = lax.broadcasted_iota(jnp.int32, (LANES, classes), 0)
    spread = (row == lax.broadcasted_iota(jnp.int32, (LANES, classes), 1) + channels + 1).astype(BF16)
    head_out[:, 0:channels] = jnp.dot(spread, head_ref[...], preferred_element_type=F32).astype(BF16)


def put_turned(turned_ref, value, plane, east, channels):
    turned = value.astype(BF16).T[0:channels]
    size = value.shape[0]
    for d in range(3):
        e = plane + d - 1
        if 0 <= e < east:
            turned_ref[d * channels : (d + 1) * channels, e * size : (e + 1) * size] = turned


def kernel_sum(turned_ref, stack, first, east, rows, upward, low, size, channels):
    fields = [shifts_of(stack, plane, rows, upward, low, size) for plane in range(first, first + east)]
    total = jnp.dot(turned_ref[...], jnp.concatenate(fields, 0), preferred_element_type=F32)
    blocks = [
        total[d * channels : (d + 1) * channels, j * LANES : (j + 1) * LANES]
        for d in range(3)
        for j in range(OFFSETS)
    ]
    blocks.append(jnp.zeros_like(blocks[0]))
    lane = lane_of(blocks[0].shape)
    spare = LANES - channels
    tiles = []
    for t in range(0, 28, 4):
        for r in range(3):
            tail = pltpu.roll(blocks[t + 3], channels - spare * r, 1)
            tiles.append(jnp.where(lane < channels, blocks[t + r], tail))
    return tiles


def prepare_kernel(
    channels, upward, edge,
    active_in, features_in, occupied_in, teacher_in,
    center_ref, *edge_refs,
):
    *edge_refs, active_ref, features_ref, occupied_ref, teacher_ref, arrived = edge_refs
    copies = [
        pltpu.make_async_copy(source, target, arrived.at[i])
        for i, (source, target) in enumerate(
            (
                (active_in, active_ref),
                (occupied_in, occupied_ref),
                (teacher_in, teacher_ref),
                (features_in, features_ref),
            )
        )
    ]
    for copy in copies:
        copy.start()
    for copy in copies[:-1]:
        copy.wait()
    east, size, _ = center_ref.shape
    north = size // upward
    classes = teacher_ref.shape[0]
    wide = (classes + 1) * upward
    row = lax.broadcasted_iota(jnp.int32, (size, north), 0) // upward
    spread = (row == lax.broadcasted_iota(jnp.int32, (size, north), 1)).astype(BF16)
    level = lax.broadcasted_iota(jnp.int32, (size, wide), 0) % upward
    same = level == lax.broadcasted_iota(jnp.int32, (size, wide), 1) % upward
    target = lax.broadcasted_iota(jnp.int32, (wide, LANES), 0) // upward + channels
    gather = (target == lax.broadcasted_iota(jnp.int32, (wide, LANES), 1)).astype(BF16)
    bricks = active_ref.shape
    up = lax.broadcasted_iota(jnp.int32, (upward, north), 0) // (upward // bricks[1])
    along = lax.broadcasted_iota(jnp.int32, (upward, north), 1) // (north // bricks[2])
    for e in range(east):
        mask = jnp.zeros((upward, north), jnp.int32)
        for b in range(bricks[2]):
            for c in range(bricks[1]):
                inside = (along == b) & (up == c)
                mask = jnp.where(inside, active_ref[e // (east // bricks[0]), c, b], mask)
        mask = (mask * occupied_ref[e]).astype(F32)
        goal = teacher_ref[:, e].astype(F32).reshape(classes * upward, north)
        field = jnp.concatenate([mask, goal], 0).astype(BF16)
        everywhere = lax.dot_general(spread, field, (((1,), (1,)), ((), ())), preferred_element_type=F32)
        own = jnp.where(same, everywhere, 0.0).astype(BF16)
        tail = jnp.dot(own, gather, preferred_element_type=F32).astype(BF16)
        center_ref[e, :, channels:LANES] = tail[:, channels:LANES]
    copies[-1].wait()
    center_ref[:, :, 0:channels] = features_ref[...]
    east_starts = [(1 - side) * (east - HALO) for _, side, _ in rounds_of("east")]
    north_starts = [pl.multiple_of((1 - side) * (size - edge), edge) for _, side, _ in rounds_of("north")]
    edge_refs = iter(edge_refs)
    for e in east_starts:
        next(edge_refs)[...] = center_ref[pl.ds(e, HALO)]
    for n in north_starts:
        next(edge_refs)[...] = center_ref[:, pl.ds(n, edge), :]
    for e in east_starts:
        for n in north_starts:
            next(edge_refs)[...] = center_ref[pl.ds(e, HALO), pl.ds(n, edge), :]


def place_edges(center_ref, edge_refs, edge, x_ref):
    east, size, _ = center_ref.shape
    x_ref[...] = jnp.zeros_like(x_ref)
    x_ref[HALO : HALO + east, edge : edge + size, :] = center_ref[...]
    edge_refs = iter(edge_refs)
    middle_east, middle_north = pl.ds(HALO, east), pl.ds(edge, size)
    east_places = [(pl.ds((1 - side) * (east + HALO), HALO), inside) for _, side, inside in rounds_of("east")]
    north_places = [
        (pl.ds(pl.multiple_of((1 - side) * (size + edge), edge), edge), inside)
        for _, side, inside in rounds_of("north")
    ]
    spots = [(e, middle_north, inside) for e, inside in east_places]
    spots += [(middle_east, n, inside) for n, inside in north_places]
    spots += [(e, n, a * b) for e, a in east_places for n, b in north_places]
    for e, n, inside in spots:
        ref = next(edge_refs)

        @pl.when(inside == 1)
        def _(ref=ref, e=e, n=n):
            x_ref[e, n, :] = ref[...]


def whole_kernel(
    channels, classes, east, north, upward, edges,
    ahead1_ref, w2_in, back2_ref, head_ref, center_ref, *refs,
):
    (
        grad_ref, kept_ref, sent_ref,
        x_ref, even0, odd0, even1, odd1, even2, odd2, mask_ref, slope_ref, turned_ref, ahead2_ref, w2_ref, arrived,
    ) = refs[edges:]
    stack0, stack1, stack2 = (even0, odd0), (even1, odd1), (even2, odd2)
    copy = pltpu.make_async_copy(w2_in, w2_ref, arrived)
    copy.start()
    rows = (north + 2 * HALO) * upward
    low, size = HALO * upward, north * upward
    planes = east + 2 * HALO
    lane = lane_of((rows, LANES))
    rows1, rows2, rows3 = rows - 2 * upward, rows - 4 * upward, rows - 6 * upward
    low1, low2, low3 = low - upward, low - 2 * upward, low - 3 * upward

    place_edges(center_ref, refs[:edges], low, x_ref)
    border = jnp.zeros((upward, LANES), F32)

    built = []

    def build(plane):
        x = x_ref[plane].astype(F32)
        mask = jnp.broadcast_to(x[:, channels : channels + 1], (rows, LANES))
        mask_ref[plane] = mask
        a0 = jnp.where((mask > 0) & (lane < channels), x, 0.0)
        put_stack(jnp.concatenate([border, a0, border], 0), upward, stack0, plane % 2, plane // 2)
        built.append(plane)

    def first_product(first, stop):
        while len(built) < 2 * stop + 2:
            build(len(built))
        return convolve(stack0, ahead1_ref, first, stop, rows, upward)

    head = head_ref[...]
    class_lane = (lane[0:rows2] > channels) & (lane[0:rows2] <= channels + classes)
    here = slice(2 * upward, 2 * upward + rows2)
    there = slice(2 * upward + upward, 2 * upward + upward + rows3)

    def first_forward(outcome, last):
        if outcome[0][0] == 0:
            copy.wait()
            put_ahead(ahead2_ref, w2_ref, channels)
        for i, parity, value in outcome:
            plane = 2 * i + parity
            mask = mask_ref[plane + 1]
            p1 = mask * value
            sig = 0.5 * jnp.tanh(0.5 * p1) + 0.5
            slope_ref[plane] = mask * (sig * (1.0 + p1 * (1.0 - sig)))
            put_stack((p1 * sig)[upward : upward + rows1], upward, stack1, parity, i)

    def second_forward(outcome, last):
        a2, slopes, errors = [], [], []
        for i, parity, value in outcome:
            mask = mask_ref[2 * i + parity + 2, here]
            p2 = mask * value
            sig = 0.5 * jnp.tanh(0.5 * p2) + 0.5
            a2.append((p2 * sig).astype(BF16))
            slopes.append(mask * (sig * (1.0 + p2 * (1.0 - sig))))
        logits = lax.dot_general(
            jnp.concatenate(a2, 0), head, (((1,), (1,)), ((), ())), preferred_element_type=F32
        )
        for number, (i, parity, _) in enumerate(outcome):
            plane = 2 * i + parity + 2
            own = logits[number * rows2 : (number + 1) * rows2]
            error = jnp.where(class_lane, mask_ref[plane, here] * (own - x_ref[plane, here].astype(F32)), 0.0)
            coarse = error.astype(BF16)
            fine = (error - coarse.astype(F32)).astype(BF16)
            errors.append(jnp.concatenate([coarse, fine], 1))
        g_a2 = jnp.dot(jnp.concatenate(errors, 0), jnp.concatenate([head, head], 0), preferred_element_type=F32)
        for number, (i, parity, _) in enumerate(outcome):
            g_p2 = g_a2[number * rows2 : (number + 1) * rows2] * slopes[number]
            put_stack(g_p2, upward, stack2, parity, i)
            put_turned(turned_ref, g_p2[low2 : low2 + size], 2 * i + parity - 2, east, channels)
        if last:
            for t, tile in enumerate(kernel_sum(turned_ref, stack1, 3, east, rows2, upward, low2, size, channels)):
                kept_ref[t * channels : (t + 1) * channels, :] = tile.astype(BF16)

    def second_backward(outcome, last):
        for i, parity, value in outcome:
            plane = 2 * i + parity
            g_p1 = slope_ref[plane + 2, there] * value
            grad_ref[plane] = g_p1.astype(BF16)
            put_turned(turned_ref, g_p1[low3 : low3 + size], plane - 1, east, channels)

    staged(
        [
            (grouped((planes - 2) // 2, 2), first_product, first_forward),
            (
                grouped((planes - 4) // 2, 2),
                functools.partial(convolve, stack1, ahead2_ref, rows=rows2, upward=upward),
                second_forward,
            ),
            (
                grouped((planes - 6) // 2, 2),
                functools.partial(convolve, stack2, back2_ref, rows=rows3, upward=upward),
                second_backward,
            ),
        ]
    )
    upper = high_bit("east", 1) == 1
    tiles = kernel_sum(turned_ref, stack0, 4, east, rows, upward, low, size, channels)
    for t, tile in enumerate(tiles):
        place = slice(t * channels, (t + 1) * channels)
        first, second = tile.astype(BF16), kept_ref[place, :]
        sent_ref[place, :] = jnp.where(upper, second, first)
        kept_ref[place, :] = jnp.where(upper, first, second)
    filled = len(tiles) * channels
    if filled < kept_ref.shape[0]:
        kept_ref[filled:, :] = jnp.zeros((kept_ref.shape[0] - filled, LANES), BF16)
        sent_ref[filled:, :] = jnp.zeros((kept_ref.shape[0] - filled, LANES), BF16)


def last_kernel(
    channels, east, north, upward,
    center_ref, grad_ref, w1_in, kept_in,
    out_ref, kept_out,
    even_ref, odd_ref, back1_ref, w1_ref, arrived,
):
    size = north * upward
    copy = pltpu.make_async_copy(w1_in, w1_ref, arrived)
    copy.start()
    for plane in range(east + 2):
        put_stack(grad_ref[plane].astype(F32), upward, (even_ref, odd_ref), plane % 2, plane // 2)
    copy.wait()
    put_back(back1_ref, w1_ref, channels)
    for first, stop in grouped(east // 2, 4):
        for i, parity, value in convolve((even_ref, odd_ref), back1_ref, first, stop, size, upward):
            plane = 2 * i + parity
            mask = center_ref[plane, :, channels : channels + 1].astype(F32)
            out_ref[plane] = (mask * value)[:, 0:channels].astype(BF16)


def parts_kernel(place_ref, kept_ref, came_ref, total_ref, *sent_refs):
    part = total_ref.shape[0]
    for change, ref in enumerate((total_ref,) + sent_refs):
        start = pl.multiple_of((place_ref[0] ^ change) * part, part)
        rows = pl.ds(start, part)
        ref[...] = (kept_ref[rows, :].astype(F32) + came_ref[rows, :].astype(F32)).astype(ref.dtype)


def unpack_kernel(channels, scale, aliased, first_ref_flag, packed_ref, *refs):
    first_out, second_out, whole_ref, done = refs[2:] if aliased else refs
    spare = LANES - channels
    is_first = first_ref_flag[0] == 1
    spans = [(t, min(t + 4, 27)) for t in range(0, 27, 4)]

    def copy_of(target, i):
        a, b = spans[i]
        return pltpu.make_async_copy(whole_ref.at[a:b], target.at[a:b], done.at[i])

    for i, (t, stop) in enumerate(spans):
        tiles = []
        for r in range(3):
            start = (t // 4 * 3 + r) * channels
            tiles.append(packed_ref[start : start + channels, :].astype(F32) * scale)
        for r in range(3):
            whole_ref[t + r] = tiles[r][:, 0:channels]
        if stop - t == 4:
            lane = lane_of(tiles[0].shape)
            parts = [pltpu.roll(tiles[r], (spare * r - channels) % LANES, 1) for r in range(3)]
            last = jnp.where(lane < spare, parts[0], jnp.where(lane < 2 * spare, parts[1], parts[2]))
            whole_ref[t + 3] = last[:, 0:channels]

        @pl.when(is_first)
        def _(i=i):
            copy_of(first_out, i).start()

        @pl.when(jnp.logical_not(is_first))
        def _(i=i):
            copy_of(second_out, i).start()

    for i in range(len(spans)):
        copy_of(first_out, i).wait()


def per_device(
    features, brick_active, voxel_occupancy, first_weights, second_weights, head, teacher
):
    channels = features.shape[0]
    east, north, upward = features.shape[1:]
    classes = teacher.shape[0]
    devices = lax.axis_size("east") * lax.axis_size("north")
    scale = 1.0 / math.sqrt(devices * east * north * upward)
    planes = east + 2 * HALO
    rows = (north + 2 * HALO) * upward
    edge, size = HALO * upward, north * upward
    vmem = pl.BlockSpec(memory_space=pltpu.VMEM)
    smem = pl.BlockSpec(memory_space=pltpu.SMEM)
    anywhere = pl.BlockSpec(memory_space=pl.ANY)
    far = pl.BlockSpec(memory_space=pltpu.HBM)

    east_bits, north_bits = bits_of("east"), bits_of("north")
    rest = north_bits + east_bits[1:]
    near, others = rest[:2], rest[2:]
    upper = high_bit(*east_bits[0])
    easts, norths = rounds_of("east"), rounds_of("north")
    counts = (len(easts), len(norths))

    shapes = [(HALO, size, LANES)] * counts[0] + [(east, edge, LANES)] * counts[1]
    shapes += [(HALO, edge, LANES)] * (counts[0] * counts[1])
    center, *edges = pl.pallas_call(
        functools.partial(prepare_kernel, channels, upward, edge),
        out_shape=[jax.ShapeDtypeStruct(shape, BF16) for shape in [(east, size, LANES)] + shapes],
        in_specs=[far] * 4,
        out_specs=[vmem] * (1 + len(shapes)),
        scratch_shapes=[
            pltpu.SMEM((brick_active.shape[0], brick_active.shape[2], brick_active.shape[1]), jnp.int32),
            pltpu.VMEM((east, size, channels), BF16),
            pltpu.VMEM((east, upward, north), jnp.int32),
            pltpu.VMEM((classes, east, upward, north), BF16),
            pltpu.SemaphoreType.DMA((4,)),
        ],
        compiler_params=pltpu.CompilerParams(vmem_limit_bytes=6 * 1024 * 1024),
        name="prepare",
    )(
        *[
            pltpu.with_memory_space_constraint(value, pltpu.HBM)
            for value in (
                brick_active.transpose(0, 2, 1),
                features.transpose(1, 2, 3, 0).reshape(east, size, channels),
                voxel_occupancy.transpose(0, 2, 1),
                teacher.transpose(0, 1, 3, 2),
            )
        ]
    )
    stay = [list(range(lax.axis_size(axis))) for axis in ("east", "north")]
    routes = [(partners, stay[1]) for partners, _, _ in easts] + [(stay[0], partners) for partners, _, _ in norths]
    routes += [(a, b) for a, _, _ in easts for b, _, _ in norths]
    edges = [exchange(value, *route) for value, route in zip(edges, routes)]

    unit = devices // 2 * 16
    packed = -(-21 * channels // unit) * unit
    first_far, second_far, head_far = [
        pltpu.with_memory_space_constraint(value, pltpu.HBM) for value in (first_weights, second_weights, head)
    ]
    ahead1, back2, head_wide = pl.pallas_call(
        functools.partial(weights_kernel, channels, classes),
        out_shape=[jax.ShapeDtypeStruct(shape, BF16) for shape in ((4 * WIDE, 2 * LANES), (4 * WIDE, 2 * LANES), (LANES, LANES))],
        in_specs=[far] * 3,
        out_specs=[vmem] * 3,
        scratch_shapes=[
            pltpu.VMEM(first_weights.shape, BF16),
            pltpu.VMEM(second_weights.shape, BF16),
            pltpu.VMEM(head.shape, BF16),
            pltpu.SemaphoreType.DMA((3,)),
        ],
        compiler_params=pltpu.CompilerParams(vmem_limit_bytes=10 * 1024 * 1024),
        name="weights",
    )(first_far, second_far, head_far)
    grad, kept, sent = pl.pallas_call(
        functools.partial(whole_kernel, channels, classes, east, north, upward, len(edges)),
        out_shape=(
            jax.ShapeDtypeStruct((east + 2, rows - 6 * upward, LANES), BF16),
            jax.ShapeDtypeStruct((packed, LANES), BF16),
            jax.ShapeDtypeStruct((packed, LANES), BF16),
        ),
        in_specs=[vmem, far] + [vmem] * (3 + len(edges)),
        out_specs=(vmem, vmem, vmem),
        scratch_shapes=[
            pltpu.VMEM((planes, rows, LANES), BF16),
            *stack_shapes(planes, rows, upward),
            *stack_shapes(planes - 2, rows - 4 * upward, upward),
            *stack_shapes(planes - 4, rows - 6 * upward, upward),
            pltpu.VMEM((planes, rows, LANES), F32),
            pltpu.VMEM((planes - 2, rows, LANES), F32),
            pltpu.VMEM((3 * channels, east * size), BF16),
            pltpu.VMEM((4 * WIDE, 2 * LANES), BF16),
            pltpu.VMEM(second_weights.shape, BF16),
            pltpu.SemaphoreType.DMA(()),
        ],
        compiler_params=pltpu.CompilerParams(vmem_limit_bytes=28 * 1024 * 1024),
        name="fields",
    )(ahead1, second_far, back2, head_wide, center, *edges)

    features_out = []

    def beside(kept):
        out, kept = pl.pallas_call(
            functools.partial(last_kernel, channels, east, north, upward),
            out_shape=(
                jax.ShapeDtypeStruct((east, size, channels), BF16),
                jax.ShapeDtypeStruct(kept.shape, F32),
            ),
            in_specs=[vmem, vmem, far, anywhere],
            out_specs=(vmem, anywhere),
            input_output_aliases={3: 1},
            scratch_shapes=[
                *stack_shapes(east + 2, size, upward),
                pltpu.VMEM((4 * WIDE, 2 * LANES), BF16),
                pltpu.VMEM(first_weights.shape, BF16),
                pltpu.SemaphoreType.DMA(()),
            ],
            compiler_params=pltpu.CompilerParams(vmem_limit_bytes=10 * 1024 * 1024),
            name="features",
        )(center, grad, first_far, kept)
        features_out.append(out)
        return kept

    ways = 1 << len(near)
    part = packed // ways
    total, *parts = pl.pallas_call(
        parts_kernel,
        out_shape=[jax.ShapeDtypeStruct((part, LANES), F32)]
        + [jax.ShapeDtypeStruct((part, LANES), BF16)] * (ways - 1),
        in_specs=[smem] + [vmem] * 2,
        out_specs=[vmem] * ways,
        compiler_params=pltpu.CompilerParams(vmem_limit_bytes=4 * 1024 * 1024),
        name="parts",
    )(place_in(near).reshape(1).astype(jnp.int32), kept, swap(sent, east_bits[:1], 1))
    total = beside(total)
    for change in range(ways - 1, 0, -1):
        total = total + swap(parts[change - 1], near, change).astype(F32)
    mine = gather_parts(share_sums(total, others), [near])
    other = swap(mine, east_bits[:1], 1)

    def unpack(is_first, value, *aliased):
        return pl.pallas_call(
            functools.partial(unpack_kernel, channels, scale, bool(aliased)),
            out_shape=(
                jax.ShapeDtypeStruct(first_weights.shape, F32),
                jax.ShapeDtypeStruct(second_weights.shape, F32),
            ),
            in_specs=[smem, vmem] + [anywhere] * len(aliased),
            out_specs=(anywhere, anywhere),
            input_output_aliases={2: 0, 3: 1} if aliased else {},
            scratch_shapes=[pltpu.VMEM(first_weights.shape, F32), pltpu.SemaphoreType.DMA((7,))],
            compiler_params=pltpu.CompilerParams(vmem_limit_bytes=5 * 1024 * 1024),
            name="unpack",
        )(is_first.reshape(1).astype(jnp.int32), value, *aliased)

    outputs = unpack(upper, mine)
    grad_first, grad_second = unpack(1 - upper, other, *outputs)
    (grad_features,) = features_out
    grad_features = grad_features.reshape(east, north, upward, channels).transpose(3, 0, 1, 2)
    return (grad_features, grad_first, grad_second)


def solution(mesh):
    in_specs = (
        P(None, "east", "north", None),
        P("east", "north", None),
        P("east", "north", None),
        P(),
        P(),
        P(),
        P(None, "east", "north", None),
    )
    out_specs = (P(None, "east", "north", None), P(), P())
    return jax.shard_map(
        per_device, mesh=mesh, in_specs=in_specs, out_specs=out_specs, check_vma=False
    )
```

```python
import functools
import math

import jax
import jax.numpy as jnp
from jax import lax
from jax.experimental import pallas as pl
from jax.experimental.pallas import tpu as pltpu
from jax.sharding import PartitionSpec as P

LANES = 128
HALO = 4
OFFSETS = 9
WIDE = OFFSETS * LANES
F32 = jnp.float32
BF16 = jnp.bfloat16


def rounds_of(axis):
    count = lax.axis_size(axis)
    me = lax.axis_index(axis)
    rounds = [([i ^ 1 for i in range(count)], me % 2, jnp.int32(1))]
    if count > 2:
        inside = ((me > 0) & (me < count - 1)).astype(jnp.int32)
        partners = [0] + [((i - 1) ^ 1) + 1 for i in range(1, count - 1)] + [count - 1]
        rounds.append((partners, (me + 1) % 2, inside))
    return rounds


def exchange(value, east, north):
    count = len(north)
    target = {(e, n): (f, m) for e, f in enumerate(east) for n, m in enumerate(north)}
    alone = [place for place, other in target.items() if place == other]
    while alone:
        e, n = alone.pop(0)
        near = [place for place in ((e, n ^ 1), (e ^ 1, n)) if place in alone]
        other = near[0] if near else alone[0]
        alone.remove(other)
        target[e, n], target[other] = other, (e, n)
    pairs = [(e * count + n, f * count + m) for (e, n), (f, m) in target.items()]
    return lax.ppermute(value, ("east", "north"), pairs)


def high_bit(axis, bit):
    return (lax.axis_index(axis) // bit) % 2


def bits_of(axis):
    size = lax.axis_size(axis)
    return [(axis, 1 << i) for i in range(size.bit_length() - 1)]


def place_in(group):
    return sum(high_bit(axis, bit) << i for i, (axis, bit) in enumerate(group))


def swap(value, group, change):
    masks = {"east": 0, "north": 0}
    for i, (axis, bit) in enumerate(group):
        if change >> i & 1:
            masks[axis] |= bit
    partners = [[i ^ masks[axis] for i in range(lax.axis_size(axis))] for axis in ("east", "north")]
    return exchange(value, *partners)


def share_sums(total, bits):
    total = total.astype(BF16)
    for bit in bits:
        total = (total.astype(F32) + swap(total, [bit], 1).astype(F32)).astype(BF16)
    return total


def gather_parts(mine, groups):
    for group in reversed(groups):
        ways = 1 << len(group)
        place = place_in(group)
        parts = [mine] + [swap(mine, group, change) for change in range(1, ways)]
        joined = []
        for row in range(ways):
            piece = parts[0]
            for change in range(1, ways):
                piece = jnp.where((place ^ row) == change, parts[change], piece)
            joined.append(piece)
        mine = jnp.concatenate(joined, 0)
    return mine


def lane_of(shape):
    return lax.broadcasted_iota(jnp.int32, shape, len(shape) - 1)


def put_stack(value, upward, stack, parity, index):
    even_ref, odd_ref = stack
    total = value.shape[0]
    rows = total - 2 * upward
    cubes = value.reshape(total // upward, upward, LANES)
    level = lax.broadcasted_iota(jnp.int32, cubes.shape, 1)
    below = jnp.where(level == 0, 0.0, pltpu.roll(cubes, 1, 1)).reshape(total, LANES)
    above = jnp.where(level == upward - 1, 0.0, pltpu.roll(cubes, upward - 1, 1)).reshape(total, LANES)
    for up, moved in enumerate((below, value, above)):
        lanes = slice(up * LANES, (up + 1) * LANES)
        even_ref[parity, index * total : (index + 1) * total, lanes] = moved.astype(BF16)
        odd_ref[parity, index * rows : (index + 1) * rows, lanes] = moved[upward : upward + rows].astype(BF16)


def shifts_of(stack, plane, rows, upward, start, size):
    even_ref, odd_ref = stack
    even = (plane // 2) * (rows + 2 * upward) + start
    odd = (plane // 2) * rows + start
    return jnp.concatenate(
        [
            even_ref[plane % 2, even : even + size, :],
            odd_ref[plane % 2, odd : odd + size, :],
            even_ref[plane % 2, even + 2 * upward : even + 2 * upward + size, :],
        ],
        1,
    )


def stack_shapes(planes, rows, upward):
    return [pltpu.VMEM((2, planes // 2 * (rows + extra), 3 * LANES), BF16) for extra in (2 * upward, 0)]


def grouped(pairs, size):
    count = max(1, pairs // size)
    edges = [pairs * i // count for i in range(count + 1)]
    return list(zip(edges, edges[1:]))


def convolve(stack, weight_ref, first, stop, rows, upward):
    fields = [
        jnp.concatenate([shifts_of(stack, 2 * pair + p, rows, upward, 0, rows) for p in range(4)], 1)
        for pair in range(first, stop)
    ]
    both = jnp.dot(jnp.concatenate(fields, 0), weight_ref[...], preferred_element_type=F32)
    return [
        (pair, parity, both[(pair - first) * rows : (pair - first + 1) * rows, parity * LANES : (parity + 1) * LANES])
        for pair in range(first, stop)
        for parity in range(2)
    ]


def staged(stages):
    held, done = None, [0] * len(stages)

    def finish():
        number, last, outcome = held
        stages[number][2](outcome, last)
        done[number] += len(outcome)

    for number, (runs, product, _) in enumerate(stages):
        for run in runs:
            if number > 0 and done[number - 1] < 2 * run[1] + 2:
                finish()
                held = None
            coming = (number, run == runs[-1], product(*run))
            if held is not None:
                finish()
            held = coming
    finish()


def unit_of(channels):
    row = lax.broadcasted_iota(jnp.int32, (channels, LANES), 0)
    return (row == lax.broadcasted_iota(jnp.int32, (channels, LANES), 1)).astype(BF16)


def put_back(back_ref, w_ref, channels):
    unit = unit_of(channels)
    border = jnp.zeros((LANES - channels, channels), BF16)
    for d in range(3):
        for j in range(OFFSETS):
            wide = jnp.concatenate([w_ref[d * OFFSETS + j], border], 0)
            block = jnp.dot(wide, unit, preferred_element_type=F32).astype(BF16)
            for q in range(2):
                row = ((2 - d + q) * OFFSETS + OFFSETS - 1 - j) * LANES
                back_ref[row : row + LANES, q * LANES : (q + 1) * LANES] = block
    put_zeros(back_ref)


def put_zeros(target_ref):
    run = OFFSETS * LANES
    target_ref[0:run, LANES : 2 * LANES] = jnp.zeros((run, LANES), BF16)
    target_ref[3 * run : 4 * run, 0:LANES] = jnp.zeros((run, LANES), BF16)


def put_ahead(ahead_ref, w_ref, channels):
    unit = unit_of(channels)
    border = jnp.zeros((LANES - channels, channels), BF16)
    for d in range(3):
        for j in range(OFFSETS):
            wide = jnp.concatenate([w_ref[d * OFFSETS + j], border], 0)
            turned = lax.dot_general(unit, wide, (((0,), (1,)), ((), ())), preferred_element_type=F32).astype(BF16)
            for q in range(2):
                row = ((d + q) * OFFSETS + j) * LANES
                ahead_ref[row : row + LANES, q * LANES : (q + 1) * LANES] = turned
    put_zeros(ahead_ref)


def weights_kernel(
    channels, classes,
    w1_in, w2_in, head_in,
    ahead1_ref, back2_ref, head_out,
    w1_ref, w2_ref, head_ref, arrived,
):
    copies = [
        pltpu.make_async_copy(source, target, arrived.at[i])
        for i, (source, target) in enumerate(((w1_in, w1_ref), (w2_in, w2_ref), (head_in, head_ref)))
    ]
    for copy in copies:
        copy.start()
    for copy in copies:
        copy.wait()
    put_ahead(ahead1_ref, w1_ref, channels)
    put_back(back2_ref, w2_ref, channels)
    head_out[...] = jnp.zeros_like(head_out)
    row = lax.broadcasted_iota(jnp.int32, (LANES, classes), 0)
    spread = (row == lax.broadcasted_iota(jnp.int32, (LANES, classes), 1) + channels + 1).astype(BF16)
    head_out[:, 0:channels] = jnp.dot(spread, head_ref[...], preferred_element_type=F32).astype(BF16)


def put_turned(turned_ref, value, plane, east, channels):
    turned = value.astype(BF16).T[0:channels]
    size = value.shape[0]
    for d in range(3):
        e = plane + d - 1
        if 0 <= e < east:
            turned_ref[d * channels : (d + 1) * channels, e * size : (e + 1) * size] = turned


def kernel_sum(turned_ref, stack, first, east, rows, upward, low, size, channels):
    fields = [shifts_of(stack, plane, rows, upward, low, size) for plane in range(first, first + east)]
    total = jnp.dot(turned_ref[...], jnp.concatenate(fields, 0), preferred_element_type=F32)
    blocks = [
        total[d * channels : (d + 1) * channels, j * LANES : (j + 1) * LANES]
        for d in range(3)
        for j in range(OFFSETS)
    ]
    blocks.append(jnp.zeros_like(blocks[0]))
    lane = lane_of(blocks[0].shape)
    spare = LANES - channels
    tiles = []
    for t in range(0, 28, 4):
        for r in range(3):
            tail = pltpu.roll(blocks[t + 3], channels - spare * r, 1)
            tiles.append(jnp.where(lane < channels, blocks[t + r], tail))
    return tiles


def prepare_kernel(
    channels, upward, edge,
    active_in, features_in, occupied_in, teacher_in,
    center_ref, *edge_refs,
):
    *edge_refs, active_ref, features_ref, occupied_ref, teacher_ref, arrived = edge_refs
    copies = [
        pltpu.make_async_copy(source, target, arrived.at[i])
        for i, (source, target) in enumerate(
            (
                (active_in, active_ref),
                (occupied_in, occupied_ref),
                (teacher_in, teacher_ref),
                (features_in, features_ref),
            )
        )
    ]
    for copy in copies:
        copy.start()
    for copy in copies[:-1]:
        copy.wait()
    east, size, _ = center_ref.shape
    north = size // upward
    classes = teacher_ref.shape[0]
    wide = (classes + 1) * upward
    row = lax.broadcasted_iota(jnp.int32, (size, north), 0) // upward
    spread = (row == lax.broadcasted_iota(jnp.int32, (size, north), 1)).astype(BF16)
    level = lax.broadcasted_iota(jnp.int32, (size, wide), 0) % upward
    same = level == lax.broadcasted_iota(jnp.int32, (size, wide), 1) % upward
    target = lax.broadcasted_iota(jnp.int32, (wide, LANES), 0) // upward + channels
    gather = (target == lax.broadcasted_iota(jnp.int32, (wide, LANES), 1)).astype(BF16)
    bricks = active_ref.shape
    up = lax.broadcasted_iota(jnp.int32, (upward, north), 0) // (upward // bricks[1])
    along = lax.broadcasted_iota(jnp.int32, (upward, north), 1) // (north // bricks[2])
    for e in range(east):
        mask = jnp.zeros((upward, north), jnp.int32)
        for b in range(bricks[2]):
            for c in range(bricks[1]):
                inside = (along == b) & (up == c)
                mask = jnp.where(inside, active_ref[e // (east // bricks[0]), c, b], mask)
        mask = (mask * occupied_ref[e]).astype(F32)
        goal = teacher_ref[:, e].astype(F32).reshape(classes * upward, north)
        field = jnp.concatenate([mask, goal], 0).astype(BF16)
        everywhere = lax.dot_general(spread, field, (((1,), (1,)), ((), ())), preferred_element_type=F32)
        own = jnp.where(same, everywhere, 0.0).astype(BF16)
        tail = jnp.dot(own, gather, preferred_element_type=F32).astype(BF16)
        center_ref[e, :, channels:LANES] = tail[:, channels:LANES]
    copies[-1].wait()
    center_ref[:, :, 0:channels] = features_ref[...]
    east_starts = [(1 - side) * (east - HALO) for _, side, _ in rounds_of("east")]
    north_starts = [pl.multiple_of((1 - side) * (size - edge), edge) for _, side, _ in rounds_of("north")]
    edge_refs = iter(edge_refs)
    for e in east_starts:
        next(edge_refs)[...] = center_ref[pl.ds(e, HALO)]
    for n in north_starts:
        next(edge_refs)[...] = center_ref[:, pl.ds(n, edge), :]
    for e in east_starts:
        for n in north_starts:
            next(edge_refs)[...] = center_ref[pl.ds(e, HALO), pl.ds(n, edge), :]


def place_edges(center_ref, edge_refs, edge, x_ref):
    east, size, _ = center_ref.shape
    x_ref[...] = jnp.zeros_like(x_ref)
    x_ref[HALO : HALO + east, edge : edge + size, :] = center_ref[...]
    edge_refs = iter(edge_refs)
    middle_east, middle_north = pl.ds(HALO, east), pl.ds(edge, size)
    east_places = [(pl.ds((1 - side) * (east + HALO), HALO), inside) for _, side, inside in rounds_of("east")]
    north_places = [
        (pl.ds(pl.multiple_of((1 - side) * (size + edge), edge), edge), inside)
        for _, side, inside in rounds_of("north")
    ]
    spots = [(e, middle_north, inside) for e, inside in east_places]
    spots += [(middle_east, n, inside) for n, inside in north_places]
    spots += [(e, n, a * b) for e, a in east_places for n, b in north_places]
    for e, n, inside in spots:
        ref = next(edge_refs)

        @pl.when(inside == 1)
        def _(ref=ref, e=e, n=n):
            x_ref[e, n, :] = ref[...]


def whole_kernel(
    channels, classes, east, north, upward, edges,
    ahead1_ref, w2_in, back2_ref, head_ref, center_ref, *refs,
):
    (
        grad_ref, kept_ref, sent_ref,
        x_ref, even0, odd0, even1, odd1, even2, odd2, mask_ref, slope_ref, turned_ref, ahead2_ref, w2_ref, arrived,
    ) = refs[edges:]
    stack0, stack1, stack2 = (even0, odd0), (even1, odd1), (even2, odd2)
    copy = pltpu.make_async_copy(w2_in, w2_ref, arrived)
    copy.start()
    rows = (north + 2 * HALO) * upward
    low, size = HALO * upward, north * upward
    planes = east + 2 * HALO
    lane = lane_of((rows, LANES))
    rows1, rows2, rows3 = rows - 2 * upward, rows - 4 * upward, rows - 6 * upward
    low1, low2, low3 = low - upward, low - 2 * upward, low - 3 * upward

    place_edges(center_ref, refs[:edges], low, x_ref)
    border = jnp.zeros((upward, LANES), F32)

    built = []

    def build(plane):
        x = x_ref[plane].astype(F32)
        mask = jnp.broadcast_to(x[:, channels : channels + 1], (rows, LANES))
        mask_ref[plane] = mask
        a0 = jnp.where((mask > 0) & (lane < channels), x, 0.0)
        put_stack(jnp.concatenate([border, a0, border], 0), upward, stack0, plane % 2, plane // 2)
        built.append(plane)

    def first_product(first, stop):
        while len(built) < 2 * stop + 2:
            build(len(built))
        return convolve(stack0, ahead1_ref, first, stop, rows, upward)

    head = head_ref[...]
    class_lane = (lane[0:rows2] > channels) & (lane[0:rows2] <= channels + classes)
    here = slice(2 * upward, 2 * upward + rows2)
    there = slice(2 * upward + upward, 2 * upward + upward + rows3)

    def first_forward(outcome, last):
        if outcome[0][0] == 0:
            copy.wait()
            put_ahead(ahead2_ref, w2_ref, channels)
        for i, parity, value in outcome:
            plane = 2 * i + parity
            mask = mask_ref[plane + 1]
            p1 = mask * value
            sig = 0.5 * jnp.tanh(0.5 * p1) + 0.5
            slope_ref[plane] = mask * (sig * (1.0 + p1 * (1.0 - sig)))
            put_stack((p1 * sig)[upward : upward + rows1], upward, stack1, parity, i)

    def second_forward(outcome, last):
        a2, slopes, errors = [], [], []
        for i, parity, value in outcome:
            mask = mask_ref[2 * i + parity + 2, here]
            p2 = mask * value
            sig = 0.5 * jnp.tanh(0.5 * p2) + 0.5
            a2.append((p2 * sig).astype(BF16))
            slopes.append(mask * (sig * (1.0 + p2 * (1.0 - sig))))
        logits = lax.dot_general(
            jnp.concatenate(a2, 0), head, (((1,), (1,)), ((), ())), preferred_element_type=F32
        )
        for number, (i, parity, _) in enumerate(outcome):
            plane = 2 * i + parity + 2
            own = logits[number * rows2 : (number + 1) * rows2]
            error = jnp.where(class_lane, mask_ref[plane, here] * (own - x_ref[plane, here].astype(F32)), 0.0)
            coarse = error.astype(BF16)
            fine = (error - coarse.astype(F32)).astype(BF16)
            errors.append(jnp.concatenate([coarse, fine], 1))
        g_a2 = jnp.dot(jnp.concatenate(errors, 0), jnp.concatenate([head, head], 0), preferred_element_type=F32)
        for number, (i, parity, _) in enumerate(outcome):
            g_p2 = g_a2[number * rows2 : (number + 1) * rows2] * slopes[number]
            put_stack(g_p2, upward, stack2, parity, i)
            put_turned(turned_ref, g_p2[low2 : low2 + size], 2 * i + parity - 2, east, channels)
        if last:
            for t, tile in enumerate(kernel_sum(turned_ref, stack1, 3, east, rows2, upward, low2, size, channels)):
                kept_ref[t * channels : (t + 1) * channels, :] = tile.astype(BF16)

    def second_backward(outcome, last):
        for i, parity, value in outcome:
            plane = 2 * i + parity
            g_p1 = slope_ref[plane + 2, there] * value
            grad_ref[plane] = g_p1.astype(BF16)
            put_turned(turned_ref, g_p1[low3 : low3 + size], plane - 1, east, channels)

    staged(
        [
            (grouped((planes - 2) // 2, 2), first_product, first_forward),
            (
                grouped((planes - 4) // 2, 3),
                functools.partial(convolve, stack1, ahead2_ref, rows=rows2, upward=upward),
                second_forward,
            ),
            (
                grouped((planes - 6) // 2, 2),
                functools.partial(convolve, stack2, back2_ref, rows=rows3, upward=upward),
                second_backward,
            ),
        ]
    )
    upper = high_bit("east", 1) == 1
    tiles = kernel_sum(turned_ref, stack0, 4, east, rows, upward, low, size, channels)
    for t, tile in enumerate(tiles):
        place = slice(t * channels, (t + 1) * channels)
        first, second = tile.astype(BF16), kept_ref[place, :]
        sent_ref[place, :] = jnp.where(upper, second, first)
        kept_ref[place, :] = jnp.where(upper, first, second)
    filled = len(tiles) * channels
    if filled < kept_ref.shape[0]:
        kept_ref[filled:, :] = jnp.zeros((kept_ref.shape[0] - filled, LANES), BF16)
        sent_ref[filled:, :] = jnp.zeros((kept_ref.shape[0] - filled, LANES), BF16)


def last_kernel(
    channels, east, north, upward,
    center_ref, grad_ref, w1_in, kept_in,
    out_ref, kept_out,
    even_ref, odd_ref, back1_ref, w1_ref, arrived,
):
    size = north * upward
    copy = pltpu.make_async_copy(w1_in, w1_ref, arrived)
    copy.start()
    for plane in range(east + 2):
        put_stack(grad_ref[plane].astype(F32), upward, (even_ref, odd_ref), plane % 2, plane // 2)
    copy.wait()
    put_back(back1_ref, w1_ref, channels)
    for first, stop in grouped(east // 2, 4):
        for i, parity, value in convolve((even_ref, odd_ref), back1_ref, first, stop, size, upward):
            plane = 2 * i + parity
            mask = center_ref[plane, :, channels : channels + 1].astype(F32)
            out_ref[plane] = (mask * value)[:, 0:channels].astype(BF16)


def parts_kernel(place_ref, kept_ref, came_ref, total_ref, *sent_refs):
    part = total_ref.shape[0]
    for change, ref in enumerate((total_ref,) + sent_refs):
        start = pl.multiple_of((place_ref[0] ^ change) * part, part)
        rows = pl.ds(start, part)
        ref[...] = (kept_ref[rows, :].astype(F32) + came_ref[rows, :].astype(F32)).astype(ref.dtype)


def unpack_kernel(channels, scale, aliased, first_ref_flag, packed_ref, *refs):
    first_out, second_out, whole_ref, done = refs[2:] if aliased else refs
    spare = LANES - channels
    is_first = first_ref_flag[0] == 1
    spans = [(t, min(t + 4, 27)) for t in range(0, 27, 4)]

    def copy_of(target, i):
        a, b = spans[i]
        return pltpu.make_async_copy(whole_ref.at[a:b], target.at[a:b], done.at[i])

    for i, (t, stop) in enumerate(spans):
        tiles = []
        for r in range(3):
            start = (t // 4 * 3 + r) * channels
            tiles.append(packed_ref[start : start + channels, :].astype(F32) * scale)
        for r in range(3):
            whole_ref[t + r] = tiles[r][:, 0:channels]
        if stop - t == 4:
            lane = lane_of(tiles[0].shape)
            parts = [pltpu.roll(tiles[r], (spare * r - channels) % LANES, 1) for r in range(3)]
            last = jnp.where(lane < spare, parts[0], jnp.where(lane < 2 * spare, parts[1], parts[2]))
            whole_ref[t + 3] = last[:, 0:channels]

        @pl.when(is_first)
        def _(i=i):
            copy_of(first_out, i).start()

        @pl.when(jnp.logical_not(is_first))
        def _(i=i):
            copy_of(second_out, i).start()

    for i in range(len(spans)):
        copy_of(first_out, i).wait()


def per_device(
    features, brick_active, voxel_occupancy, first_weights, second_weights, head, teacher
):
    channels = features.shape[0]
    east, north, upward = features.shape[1:]
    classes = teacher.shape[0]
    devices = lax.axis_size("east") * lax.axis_size("north")
    scale = 1.0 / math.sqrt(devices * east * north * upward)
    planes = east + 2 * HALO
    rows = (north + 2 * HALO) * upward
    edge, size = HALO * upward, north * upward
    vmem = pl.BlockSpec(memory_space=pltpu.VMEM)
    smem = pl.BlockSpec(memory_space=pltpu.SMEM)
    anywhere = pl.BlockSpec(memory_space=pl.ANY)
    far = pl.BlockSpec(memory_space=pltpu.HBM)

    east_bits, north_bits = bits_of("east"), bits_of("north")
    rest = north_bits + east_bits[1:]
    near, others = rest[:2], rest[2:]
    upper = high_bit(*east_bits[0])
    easts, norths = rounds_of("east"), rounds_of("north")
    counts = (len(easts), len(norths))

    shapes = [(HALO, size, LANES)] * counts[0] + [(east, edge, LANES)] * counts[1]
    shapes += [(HALO, edge, LANES)] * (counts[0] * counts[1])
    center, *edges = pl.pallas_call(
        functools.partial(prepare_kernel, channels, upward, edge),
        out_shape=[jax.ShapeDtypeStruct(shape, BF16) for shape in [(east, size, LANES)] + shapes],
        in_specs=[far] * 4,
        out_specs=[vmem] * (1 + len(shapes)),
        scratch_shapes=[
            pltpu.SMEM((brick_active.shape[0], brick_active.shape[2], brick_active.shape[1]), jnp.int32),
            pltpu.VMEM((east, size, channels), BF16),
            pltpu.VMEM((east, upward, north), jnp.int32),
            pltpu.VMEM((classes, east, upward, north), BF16),
            pltpu.SemaphoreType.DMA((4,)),
        ],
        compiler_params=pltpu.CompilerParams(vmem_limit_bytes=6 * 1024 * 1024),
        name="prepare",
    )(
        *[
            pltpu.with_memory_space_constraint(value, pltpu.HBM)
            for value in (
                brick_active.transpose(0, 2, 1),
                features.transpose(1, 2, 3, 0).reshape(east, size, channels),
                voxel_occupancy.transpose(0, 2, 1),
                teacher.transpose(0, 1, 3, 2),
            )
        ]
    )
    stay = [list(range(lax.axis_size(axis))) for axis in ("east", "north")]
    routes = [(partners, stay[1]) for partners, _, _ in easts] + [(stay[0], partners) for partners, _, _ in norths]
    routes += [(a, b) for a, _, _ in easts for b, _, _ in norths]
    edges = [exchange(value, *route) for value, route in zip(edges, routes)]

    unit = devices // 2 * 16
    packed = -(-21 * channels // unit) * unit
    first_far, second_far, head_far = [
        pltpu.with_memory_space_constraint(value, pltpu.HBM) for value in (first_weights, second_weights, head)
    ]
    ahead1, back2, head_wide = pl.pallas_call(
        functools.partial(weights_kernel, channels, classes),
        out_shape=[jax.ShapeDtypeStruct(shape, BF16) for shape in ((4 * WIDE, 2 * LANES), (4 * WIDE, 2 * LANES), (LANES, LANES))],
        in_specs=[far] * 3,
        out_specs=[vmem] * 3,
        scratch_shapes=[
            pltpu.VMEM(first_weights.shape, BF16),
            pltpu.VMEM(second_weights.shape, BF16),
            pltpu.VMEM(head.shape, BF16),
            pltpu.SemaphoreType.DMA((3,)),
        ],
        compiler_params=pltpu.CompilerParams(vmem_limit_bytes=10 * 1024 * 1024),
        name="weights",
    )(first_far, second_far, head_far)
    grad, kept, sent = pl.pallas_call(
        functools.partial(whole_kernel, channels, classes, east, north, upward, len(edges)),
        out_shape=(
            jax.ShapeDtypeStruct((east + 2, rows - 6 * upward, LANES), BF16),
            jax.ShapeDtypeStruct((packed, LANES), BF16),
            jax.ShapeDtypeStruct((packed, LANES), BF16),
        ),
        in_specs=[vmem, far] + [vmem] * (3 + len(edges)),
        out_specs=(vmem, vmem, vmem),
        scratch_shapes=[
            pltpu.VMEM((planes, rows, LANES), BF16),
            *stack_shapes(planes, rows, upward),
            *stack_shapes(planes - 2, rows - 4 * upward, upward),
            *stack_shapes(planes - 4, rows - 6 * upward, upward),
            pltpu.VMEM((planes, rows, LANES), F32),
            pltpu.VMEM((planes - 2, rows, LANES), F32),
            pltpu.VMEM((3 * channels, east * size), BF16),
            pltpu.VMEM((4 * WIDE, 2 * LANES), BF16),
            pltpu.VMEM(second_weights.shape, BF16),
            pltpu.SemaphoreType.DMA(()),
        ],
        compiler_params=pltpu.CompilerParams(vmem_limit_bytes=28 * 1024 * 1024),
        name="fields",
    )(ahead1, second_far, back2, head_wide, center, *edges)

    features_out = []

    def beside(kept):
        out, kept = pl.pallas_call(
            functools.partial(last_kernel, channels, east, north, upward),
            out_shape=(
                jax.ShapeDtypeStruct((east, size, channels), BF16),
                jax.ShapeDtypeStruct(kept.shape, F32),
            ),
            in_specs=[vmem, vmem, far, anywhere],
            out_specs=(vmem, anywhere),
            input_output_aliases={3: 1},
            scratch_shapes=[
                *stack_shapes(east + 2, size, upward),
                pltpu.VMEM((4 * WIDE, 2 * LANES), BF16),
                pltpu.VMEM(first_weights.shape, BF16),
                pltpu.SemaphoreType.DMA(()),
            ],
            compiler_params=pltpu.CompilerParams(vmem_limit_bytes=10 * 1024 * 1024),
            name="features",
        )(center, grad, first_far, kept)
        features_out.append(out)
        return kept

    ways = 1 << len(near)
    part = packed // ways
    total, *parts = pl.pallas_call(
        parts_kernel,
        out_shape=[jax.ShapeDtypeStruct((part, LANES), F32)]
        + [jax.ShapeDtypeStruct((part, LANES), BF16)] * (ways - 1),
        in_specs=[smem] + [vmem] * 2,
        out_specs=[vmem] * ways,
        compiler_params=pltpu.CompilerParams(vmem_limit_bytes=4 * 1024 * 1024),
        name="parts",
    )(place_in(near).reshape(1).astype(jnp.int32), kept, swap(sent, east_bits[:1], 1))
    total = beside(total)
    for change in range(ways - 1, 0, -1):
        total = total + swap(parts[change - 1], near, change).astype(F32)
    mine = gather_parts(share_sums(total, others), [near])
    other = swap(mine, east_bits[:1], 1)

    def unpack(is_first, value, *aliased):
        return pl.pallas_call(
            functools.partial(unpack_kernel, channels, scale, bool(aliased)),
            out_shape=(
                jax.ShapeDtypeStruct(first_weights.shape, F32),
                jax.ShapeDtypeStruct(second_weights.shape, F32),
            ),
            in_specs=[smem, vmem] + [anywhere] * len(aliased),
            out_specs=(anywhere, anywhere),
            input_output_aliases={2: 0, 3: 1} if aliased else {},
            scratch_shapes=[pltpu.VMEM(first_weights.shape, F32), pltpu.SemaphoreType.DMA((7,))],
            compiler_params=pltpu.CompilerParams(vmem_limit_bytes=5 * 1024 * 1024),
            name="unpack",
        )(is_first.reshape(1).astype(jnp.int32), value, *aliased)

    outputs = unpack(upper, mine)
    grad_first, grad_second = unpack(1 - upper, other, *outputs)
    (grad_features,) = features_out
    grad_features = grad_features.reshape(east, north, upward, channels).transpose(3, 0, 1, 2)
    return (grad_features, grad_first, grad_second)


def solution(mesh):
    in_specs = (
        P(None, "east", "north", None),
        P("east", "north", None),
        P("east", "north", None),
        P(),
        P(),
        P(),
        P(None, "east", "north", None),
    )
    out_specs = (P(None, "east", "north", None), P(), P())
    return jax.shard_map(
        per_device, mesh=mesh, in_specs=in_specs, out_specs=out_specs, check_vma=False
    )
```
